32 devices in a mesh: dp: 8 (over z, y), shard: 4 (over x, core).
Axes of the slice: x: 2, y: 2, z: 4, core: 2. Of those that a mesh axis runs over, the one named last changes fastest.
Arguments:
- tokens: bfloat16 [16, 4096, 512], P('dp', 'shard'), may hold values from -6 to 6
- cotangent: bfloat16 [16, 4096, 512], P('dp', 'shard'), may hold values from -6 to 6
- segments: int32 [16, 4096], P('dp', 'shard'), may hold values from 0 to 4, as said below
- log_decay: float32 [2], replicated, may hold values from -0.034 to 0, as said below
- w_qk: float32 [2, 512, 512], P(None, 'shard'), may hold values from -0.25 to 0.25
- w_vg: float32 [2, 512, 864], P(None, 'shard'), may hold values from -0.25 to 0.25
- w_out: float32 [864, 512], P(None, 'shard'), may hold values from -0.21875 to 0.21875
- w_gu: float32 [2, 512, 864], P(None, 'shard'), may hold values from -0.25 to 0.25
- w_down: float32 [864, 512], P(None, 'shard'), may hold values from -0.21875 to 0.21875
- norm_gains: float32 [2, 512], P(None, 'shard'), may hold values from 0.5 to 1.4
- m_qk: float32 [2, 512, 512], P(None, 'shard'), may hold values from -0.0007324219 to 0.0007324219
- m_vg: float32 [2, 512, 864], P(None, 'shard'), may hold values from -0.0007324219 to 0.0007324219
- m_out: float32 [864, 512], P(None, 'shard'), may hold values from -0.0009765625 to 0.0009765625
- m_gu: float32 [2, 512, 864], P(None, 'shard'), may hold values from -0.0009765625 to 0.0009765625
- m_down: float32 [864, 512], P(None, 'shard'), may hold values from -0.0012207031 to 0.0012207031
- m_gains: float32 [2, 512], P(None, 'shard'), may hold values from -0.0014648438 to 0.0014648438
- v_qk: float32 [2, 512, 512], P(None, 'shard'), may hold values from 1.0693438e-08 to 4.2459238e-08
- v_vg: float32 [2, 512, 864], P(None, 'shard'), may hold values from 1.0693438e-08 to 4.2459238e-08
- v_out: float32 [864, 512], P(None, 'shard'), may hold values from 2.390298e-08 to 9.4353865e-08
- v_gu: float32 [2, 512, 864], P(None, 'shard'), may hold values from 1.6669183e-08 to 6.6047704e-08
- v_down: float32 [864, 512], P(None, 'shard'), may hold values from 2.7991646e-08 to 1.1322464e-07
- v_gains: float32 [2, 512], P(None, 'shard'), may hold values from 4.2459238e-08 to 1.6983695e-07
Outputs:
- tokens_out: bfloat16 [16, 4096, 512], P('dp', 'shard')
- grad_input: bfloat16 [16, 4096, 512], P('dp', 'shard')
- new_w_qk: float32 [2, 512, 512], P(None, 'shard')
- new_w_vg: float32 [2, 512, 864], P(None, 'shard')
- new_w_out: float32 [864, 512], P(None, 'shard')
- new_w_gu: float32 [2, 512, 864], P(None, 'shard')
- new_w_down: float32 [864, 512], P(None, 'shard')
- new_gains: float32 [2, 512], P(None, 'shard')
- new_m_qk: float32 [2, 512, 512], P(None, 'shard')
- new_m_vg: float32 [2, 512, 864], P(None, 'shard')
- new_m_out: float32 [864, 512], P(None, 'shard')
- new_m_gu: float32 [2, 512, 864], P(None, 'shard')
- new_m_down: float32 [864, 512], P(None, 'shard')
- new_m_gains: float32 [2, 512], P(None, 'shard')
- new_v_qk: float32 [2, 512, 512], P(None, 'shard')
- new_v_vg: float32 [2, 512, 864], P(None, 'shard')
- new_v_out: float32 [864, 512], P(None, 'shard')
- new_v_gu: float32 [2, 512, 864], P(None, 'shard')
- new_v_down: float32 [864, 512], P(None, 'shard')
- new_v_gains: float32 [2, 512], P(None, 'shard')
- grad_norm: float32 [], replicated
The draws below stay inside these ranges and needn't reach their ends.
Inputs may be any that keep to these rules, and one draw needn't show every extreme that they name: `segments`: document numbers never fall along a sequence; each sequence holds exactly five documents, one of which begins before position 1024 and ends after position 3072. `log_decay`: negative.
All inputs are finite; a program needn't handle non-finite values.
Results may differ from the reference program's by a relative error of at most 0.02.
The reference program's roundings to bfloat16 on the way count: a program that leaves them out, or rounds other values in their place, can miss the bound.
Values may be sent and summed in bfloat16 or wider, within the bound.
No kernel may reach another device: no remote copies, remote signals or barrier semaphores. Data moves between devices by JAX's collectives and lax.ppermute only.
A program may use at most 256 MiB of HBM per device.

```python
import math
import jax
import jax.numpy as jnp
from jax import lax

D = 512
H = 2
KD = 256
VD = 432
FF = 864
LEN_DEV = 1024
BLOCK = 512
STEP = 10
NSEQ = 16
LEN = 4096
NPARAM = 3179520


def draw_segments(key, part):
    key = jax.random.fold_in(key, 37)
    keys = jax.random.split(key, 4)
    begin = jax.random.randint(keys[0], (NSEQ, 1), 2, LEN_DEV)
    early = jax.random.randint(keys[1], (NSEQ, 1), 1, begin)
    finish = LEN - jax.random.randint(keys[2], (NSEQ, 1), 2, LEN_DEV)
    late = jax.random.randint(keys[3], (NSEQ, 1), finish + 1, LEN)
    places = jnp.arange(LEN)[None, :]
    return (places >= early).astype(jnp.int32) + (places >= begin).astype(jnp.int32) + (places >= finish).astype(jnp.int32) + (places >= late).astype(jnp.int32)


def draw_log_decay(key, part):
    key = jax.random.fold_in(key, 11)
    fast_key, slow_key, pick_key = jax.random.split(key, 3)
    slow = -jax.random.uniform(slow_key, (H,), jnp.float32, 0.3, 1.5) / LEN
    fast = -jax.random.uniform(fast_key, (H,), jnp.float32, 1.0 / 50.0, 1.0 / 30.0)
    chosen = jax.random.randint(pick_key, (), 0, H)
    return jnp.where(jnp.arange(H) == chosen, fast, slow)


def draw_norm_gains(key, part):
    key = jax.random.fold_in(key, 23)
    rising = 0.6 + 0.6 * jnp.arange(D).astype(jnp.float32) / D
    factor = jax.random.uniform(key, (2, D), jnp.float32, 0.85, 1.15)
    return rising[None, :] * factor


def level_of(own_key, extent, cuts, smallest, largest):
    def one(dim, parts):
        heights = jax.random.uniform(jax.random.fold_in(jax.random.fold_in(own_key, 6), dim), (parts,), jnp.float32, smallest / len(cuts), largest / len(cuts))
        return jnp.repeat(jnp.exp(heights), extent[dim] // parts).reshape((-1,) + (1,) * (len(extent) - dim - 1))

    factor_of = one(*cuts[0])
    for cut in cuts[1:]:
        factor_of = factor_of * one(*cut)
    return factor_of


def noise(rng, dims, scale, most, shards=(), held_as=jnp.bfloat16):
    factor_of = level_of(rng, dims, shards, -0.22, 0.18) if shards else 1.0
    drawn = jax.random.normal(rng, dims, jnp.float32) * scale * factor_of
    return jnp.minimum(jnp.maximum(drawn, -most), most).astype(held_as)


def setup_inputs(seed: int = 0) -> dict:
    streams_of = jax.random.split(jax.random.key(seed), 23)
    return {
        "tokens": noise(streams_of[0], (NSEQ, LEN, D), 1.0, 6.0, ((0, 8), (1, 4))),
        "cotangent": noise(streams_of[1], (NSEQ, LEN, D), 1.0, 6.0, ((0, 8), (1, 4))),
        "segments": draw_segments(jax.random.fold_in(streams_of[22], 71), 0),
        "log_decay": draw_log_decay(jax.random.fold_in(streams_of[22], 71), 0),
        "w_qk": noise(streams_of[4], (2, D, H * KD), D ** -0.5, 0.25, ((1, 4),), jnp.float32),
        "w_vg": noise(streams_of[5], (2, D, H * VD), D ** -0.5, 0.25, ((1, 4),), jnp.float32),
        "w_out": noise(streams_of[6], (H * VD, D), (H * VD) ** -0.5, 0.21875, ((1, 4),), jnp.float32),
        "w_gu": noise(streams_of[7], (2, D, FF), D ** -0.5, 0.25, ((1, 4),), jnp.float32),
        "w_down": noise(streams_of[8], (FF, D), FF ** -0.5, 0.21875, ((1, 4),), jnp.float32),
        "norm_gains": draw_norm_gains(jax.random.fold_in(streams_of[22], 71), 0),
        "m_qk": noise(streams_of[10], (2, D, H * KD), (0.09 * NPARAM ** -0.5), 0.0007324219, ((1, 4),), jnp.float32),
        "m_vg": noise(streams_of[11], (2, D, H * VD), (0.09 * NPARAM ** -0.5), 0.0007324219, ((1, 4),), jnp.float32),
        "m_out": noise(streams_of[12], (H * VD, D), (0.13 * NPARAM ** -0.5), 0.0009765625, ((1, 4),), jnp.float32),
        "m_gu": noise(streams_of[13], (2, D, FF), (0.11 * NPARAM ** -0.5), 0.0009765625, ((1, 4),), jnp.float32),
        "m_down": noise(streams_of[14], (FF, D), (0.14 * NPARAM ** -0.5), 0.0012207031, ((1, 4),), jnp.float32),
        "m_gains": noise(streams_of[15], (2, D), (0.18 * NPARAM ** -0.5), 0.0014648438, ((1, 4),), jnp.float32),
        "v_qk": jnp.clip(jnp.exp(math.log(4.245923790335837e-08) - 1.3789142 * jax.random.uniform(streams_of[16], (2, D, H * KD), jnp.float32) ** level_of(streams_of[16], (2, D, H * KD), ((1, 4),), -0.2, 0.2)), 1.0693438134978805e-08, 4.245923790335837e-08),
        "v_vg": jnp.clip(jnp.exp(math.log(4.245923790335837e-08) - 1.3789142 * jax.random.uniform(streams_of[17], (2, D, H * VD), jnp.float32) ** level_of(streams_of[17], (2, D, H * VD), ((1, 4),), -0.2, 0.2)), 1.0693438134978805e-08, 4.245923790335837e-08),
        "v_out": jnp.clip(jnp.exp(math.log(9.435386516543076e-08) - 1.3730491 * jax.random.uniform(streams_of[18], (H * VD, D), jnp.float32) ** level_of(streams_of[18], (H * VD, D), ((1, 4),), -0.2, 0.2)), 2.3902979151557702e-08, 9.435386516543076e-08),
        "v_gu": jnp.clip(jnp.exp(math.log(6.604770419471606e-08) - 1.3768156 * jax.random.uniform(streams_of[19], (2, D, FF), jnp.float32) ** level_of(streams_of[19], (2, D, FF), ((1, 4),), -0.2, 0.2)), 1.666918336695744e-08, 6.604770419471606e-08),
        "v_down": jnp.clip(jnp.exp(math.log(1.1322463677743144e-07) - 1.39746766 * jax.random.uniform(streams_of[20], (FF, D), jnp.float32) ** level_of(streams_of[20], (FF, D), ((1, 4),), -0.2, 0.2)), 2.799164633415785e-08, 1.1322463677743144e-07),
        "v_gains": jnp.clip(jnp.exp(math.log(1.6983695161343348e-07) - 1.3862944 * jax.random.uniform(streams_of[21], (2, D), jnp.float32) ** level_of(streams_of[21], (2, D), ((1, 4),), -0.2, 0.2)), 4.245923790335837e-08, 1.6983695161343348e-07),
    }


EPS = 1e-05
ADAM_EPS = 1e-08
BETA_ONE = 0.9
BETA_TWO = 0.95
MATRIX_RATE = 0.15
GAIN_RATE = 1.0
DECAY_WEIGHT = 0.1
CLIP = 1.0
PRECISION_TOP = lax.Precision.HIGHEST

@jax.custom_vjp
def low(v):
    return lax.optimization_barrier(v.astype(jnp.bfloat16)).astype(jnp.float32)

@jax.custom_vjp
def low_back(v):
    return v

def low_keep(v):
    return (low(v), None)

def low_pass(kept, grad):
    return (grad,)

def back_keep(v):
    return (v, None)

def back_low(kept, grad):
    return (low(grad),)
low.defvjp(low_keep, low_pass)
low_back.defvjp(back_keep, back_low)

def matmul(left, right):
    return jnp.dot(left, right, precision=PRECISION_TOP)

def rms_norm(values, gain):
    return values * lax.rsqrt(lax.optimization_barrier(jnp.mean(values * values, axis=-1, keepdims=True)) + EPS) * gain

def gated_norm(retained, gate):
    grouped = retained.reshape(retained.shape[:-1] + (H, VD))
    centered = grouped - lax.optimization_barrier(jnp.mean(grouped, axis=-1, keepdims=True))
    normed = centered * lax.rsqrt(lax.optimization_barrier(jnp.mean(centered * centered, axis=-1, keepdims=True)) + 1.0 * KD)
    return normed.reshape(retained.shape) * jax.nn.silu(gate)

def gelu_gate(gate_ff, up_ff):
    return jax.nn.gelu(gate_ff, approximate=False) * up_ff

def rotation_tables(positions):
    half_width = KD // 2
    freq_rates = jnp.exp(-math.log(10000.0) * jnp.arange(half_width).astype(jnp.float32) / half_width)
    angles = positions[:, None] * freq_rates[None, :]
    return (jnp.cos(angles)[:, None, :], jnp.sin(angles)[:, None, :])

def rotate(values, cosine, sine):
    shaped = values.reshape(values.shape[:-1] + (H, 2, KD // 2))
    former = shaped[..., 0, :]
    latter = shaped[..., 1, :]
    turned = jnp.stack([former * cosine - latter * sine, latter * cosine + former * sine], axis=-2)
    return turned.reshape(values.shape)

def decay_matrix(seg_block, log_decay):
    steps_in = jnp.arange(seg_block.shape[-1])
    offset = steps_in[:, None] - steps_in[None, :]
    allowed = (offset >= 0) & (seg_block[..., :, None] == seg_block[..., None, :])
    distance = jnp.maximum(offset, 0).astype(jnp.float32)
    return jnp.where(allowed[..., None, :, :], jnp.exp(log_decay[:, None, None] * distance), 0.0)

def retention(query, key, value, segment_row, log_decay):
    length = segment_row.shape[0]
    count = length // BLOCK

    def block_step(carry, block):
        running_state, last = carry
        query_section, key_section, value_section, seg_c = block
        size = seg_c.shape[0]
        steps_in = jnp.arange(size).astype(jnp.float32)
        mixing = decay_matrix(seg_c, log_decay)
        scores = low_back(jnp.einsum('nhk,mhk->hnm', query_section, key_section, precision=PRECISION_TOP))
        weights = low(scores * mixing)
        intra = jnp.einsum('hnm,mhv->nhv', weights, value_section, precision=PRECISION_TOP)
        query_matrix = jnp.exp(log_decay[None, :] * (steps_in[:, None] + 1.0)) * (seg_c == last)[:, None].astype(jnp.float32)
        cross_section_part = jnp.einsum('stc,tca->sta', query_section * query_matrix[:, :, None], running_state, precision=PRECISION_TOP)
        key_matrix = jnp.exp(log_decay[None, :] * (size - 1.0 - steps_in[:, None])) * (seg_c == seg_c[-1])[:, None].astype(jnp.float32)
        keep = (seg_c[0] == seg_c[-1]) & (seg_c[0] == last)
        carried_over = jnp.where(keep, jnp.exp(log_decay * size)[:, None, None] * running_state, 0.0)
        next_state = carried_over + jnp.einsum('jqo,jqs->qos', key_section * key_matrix[:, :, None], value_section, precision=PRECISION_TOP)
        return ((next_state, seg_c[-1]), intra + cross_section_part)
    blocks = (query.reshape(count, BLOCK, H, KD), key.reshape(count, BLOCK, H, KD), value.reshape(count, BLOCK, H, VD), segment_row.reshape(count, BLOCK))
    start = (jnp.zeros((H, KD, VD), jnp.float32), jnp.int32(-1))
    final, outputs = lax.scan(jax.checkpoint(block_step), start, blocks)
    return outputs.reshape(length, H, VD)

def layer(params, inputs, segment_row, log_decay):
    w_qk, w_vg, w_out, w_gu, w_down, gains = params
    length = inputs.shape[0]
    hidden_one = low(rms_norm(inputs, gains[0]))
    query_pre = low_back(matmul(hidden_one, w_qk[0]))
    key_pre = low_back(matmul(hidden_one, w_qk[1]))
    value_pre = low_back(matmul(hidden_one, w_vg[0]))
    gate_pre = low_back(matmul(hidden_one, w_vg[1]))
    positions = jnp.arange(length).astype(jnp.float32)
    cosine, sine = rotation_tables(positions)
    query = low(rotate(query_pre, cosine, sine)).reshape(length, H, KD)
    key = low(rotate(key_pre, cosine, sine)).reshape(length, H, KD)
    value = low(value_pre).reshape(length, H, VD)
    retained = low_back(retention(query, key, value, segment_row, log_decay).reshape(length, H * VD))
    mixed = low(gated_norm(retained, gate_pre))
    resid = inputs + low_back(matmul(mixed, w_out))
    hidden_two = low(rms_norm(resid, gains[1]))
    gate_ff = low_back(matmul(hidden_two, w_gu[0]))
    up_ff = low_back(matmul(hidden_two, w_gu[1]))
    product = low(gelu_gate(gate_ff, up_ff))
    return resid + low_back(matmul(product, w_down))

def adam_step(master, moment, second, grad, scale, rate, decay_weight):
    clipped = grad * scale
    moment_new = BETA_ONE * moment + (1.0 - BETA_ONE) * clipped
    second_new = BETA_TWO * second + (1.0 - BETA_TWO) * clipped * clipped
    corrected = moment_new / (1.0 - BETA_ONE ** STEP) / (jnp.sqrt(second_new / (1.0 - BETA_TWO ** STEP)) + ADAM_EPS)
    return (master - rate * (corrected + decay_weight * master), moment_new, second_new)

def reference(tokens, cotangent, segments, log_decay, w_qk, w_vg, w_out, w_gu, w_down, norm_gains, m_qk, m_vg, m_out, m_gu, m_down, m_gains, v_qk, v_vg, v_out, v_gu, v_down, v_gains):
    masters = (w_qk, w_vg, w_out, w_gu, w_down, norm_gains)
    params = tuple((item.astype(jnp.bfloat16).astype(jnp.float32) for item in masters))

    def one_sequence(totals, items):
        inputs, grads_in, segment_row = items
        outputs, pull = jax.vjp(lambda weights, values: layer(weights, values, segment_row, log_decay), params, inputs.astype(jnp.float32))
        weight_grads, input_grad = pull(grads_in.astype(jnp.float32))
        totals = tuple((running + addition for running, addition in zip(totals, weight_grads)))
        return (totals, (outputs.astype(jnp.bfloat16), input_grad.astype(jnp.bfloat16)))
    zeros = tuple((jnp.zeros_like(item) for item in params))
    grads, (tokens_out, grad_input) = lax.scan(one_sequence, zeros, (tokens, cotangent, segments))
    squares = jnp.float32(0.0)
    for item in grads:
        squares = squares + jnp.sum(item * item)
    grad_norm = jnp.sqrt(squares)
    scale = jnp.minimum(1.0, CLIP / (grad_norm + 1e-06))
    moments = (m_qk, m_vg, m_out, m_gu, m_down, m_gains)
    seconds = (v_qk, v_vg, v_out, v_gu, v_down, v_gains)
    rates = (MATRIX_RATE,) * 5 + (GAIN_RATE,)
    decays = (DECAY_WEIGHT,) * 5 + (0.0,)
    results = [adam_step(masters[index], moments[index], seconds[index], grads[index], scale, rates[index], decays[index]) for index in range(6)]
    new_w = [entry[0] for entry in results]
    new_m = [entry[1] for entry in results]
    new_v = [entry[2] for entry in results]
    return (tokens_out, grad_input, new_w[0], new_w[1], new_w[2], new_w[3], new_w[4], new_w[5], new_m[0], new_m[1], new_m[2], new_m[3], new_m[4], new_m[5], new_v[0], new_v[1], new_v[2], new_v[3], new_v[4], new_v[5], grad_norm)
```

```python
import math

import jax
import jax.numpy as jnp
from jax import lax
from jax.sharding import PartitionSpec as P

H = 2
KD = 256
VD = 432
BLOCK = 512
STEP = 10


EPS = 1e-05
ADAM_EPS = 1e-08
BETA_ONE = 0.9
BETA_TWO = 0.95
MATRIX_RATE = 0.15
GAIN_RATE = 1.0
DECAY_WEIGHT = 0.1
CLIP = 1.0
PRECISION_TOP = lax.Precision.HIGHEST


def bits_of(axis):
    return (lax.axis_size(axis) - 1).bit_length()


def exchange(value, axis, bit):
    size = lax.axis_size(axis)
    return lax.ppermute(value, axis, [(i, i ^ (1 << bit)) for i in range(size)])


def gather_shards(own):
    held = own[None]
    for bit in reversed(range(bits_of("shard"))):
        held = jnp.concatenate([held, exchange(held, "shard", bit)])
    count = bits_of("shard")
    mine = lax.axis_index("shard")
    order = [int(format(p, "0%db" % count)[::-1], 2) if count else 0 for p in range(1 << count)]
    where = jnp.array(order, jnp.int32)
    slots = jnp.bitwise_xor(jnp.arange(1 << count), mine)
    inverse = jnp.argsort(where)
    return jnp.stack([lax.dynamic_index_in_dim(held, inverse[slots[j]], 0, False) for j in range(1 << count)])


def add_low(one, two):
    return (one.astype(jnp.float32) + two.astype(jnp.float32)).astype(jnp.bfloat16)


def reduce_owned(parts):
    mine = lax.axis_index("shard")
    held = parts
    for bit in range(bits_of("shard")):
        half = (mine >> bit) & 1
        split = held.reshape((held.shape[0] // 2, 2) + held.shape[1:])
        keep = lax.dynamic_index_in_dim(split, half, 1, False)
        send = lax.dynamic_index_in_dim(split, 1 - half, 1, False)
        held = add_low(keep, exchange(send, "shard", bit))
    held = held[0]
    place = lax.axis_index("dp")
    count = bits_of("dp")
    for bit in range(count):
        half = (place >> bit) & 1
        rows = held.shape[0] // 2
        keep = lax.dynamic_slice_in_dim(held, half * rows, rows, 0)
        send = lax.dynamic_slice_in_dim(held, (1 - half) * rows, rows, 0)
        held = add_low(keep, exchange(send, "dp", bit))
    for bit in reversed(range(count)):
        half = (place >> bit) & 1
        other = exchange(held, "dp", bit)
        held = jnp.where(half == 0, jnp.concatenate([held, other]), jnp.concatenate([other, held]))
    return held


def pass_on(local, first, last, decay, reverse):
    size = lax.axis_size("shard")
    mine = lax.axis_index("shard")
    order = list(range(size))
    if reverse:
        order = order[::-1]
    entering = jnp.zeros_like(local)
    for here, there in zip(order[:-1], order[1:]):
        keep = (first == last)[:, None, None, None]
        leaving = local + jnp.where(keep, decay[None, :, None, None] * entering, 0.0)
        got = lax.ppermute(leaving.astype(jnp.bfloat16), "shard", [(here, there)])
        entering = jnp.where(mine == there, got.astype(jnp.float32), entering)
    return entering


def matmul(left, right):
    return jnp.dot(left, right, preferred_element_type=jnp.float32)


def rms_norm(values, gain):
    return values * lax.rsqrt(jnp.mean(values * values, axis=-1, keepdims=True) + EPS) * gain


def gated_norm(retained, gate):
    grouped = retained.reshape(retained.shape[:-1] + (H, VD))
    centered = grouped - jnp.mean(grouped, axis=-1, keepdims=True)
    normed = centered * lax.rsqrt(jnp.mean(centered * centered, axis=-1, keepdims=True) + 1.0 * KD)
    return normed.reshape(retained.shape) * jax.nn.silu(gate)


def gelu_gate(gate_ff, up_ff):
    return jax.nn.gelu(gate_ff, approximate=False) * up_ff


def rotation_tables(positions):
    half_width = KD // 2
    freq_rates = jnp.exp(
        -math.log(10000.0) * jnp.arange(half_width).astype(jnp.float32) / half_width
    )
    angles = positions[:, None] * freq_rates[None, :]
    return (jnp.cos(angles)[:, None, :], jnp.sin(angles)[:, None, :])


def rotate(values, cosine, sine):
    shaped = values.reshape(values.shape[:-1] + (H, 2, KD // 2))
    former = shaped[..., 0, :]
    latter = shaped[..., 1, :]
    turned = jnp.stack([former * cosine - latter * sine, latter * cosine + former * sine], axis=-2)
    return turned.reshape(values.shape)


def decay_matrix(seg_block, log_decay):
    steps_in = jnp.arange(seg_block.shape[-1])
    offset = steps_in[:, None] - steps_in[None, :]
    allowed = (offset >= 0) & (seg_block[..., :, None] == seg_block[..., None, :])
    distance = jnp.maximum(offset, 0).astype(jnp.float32)
    return jnp.where(allowed[..., None, :, :], jnp.exp(log_decay[:, None, None] * distance), 0.0)


def block_weights(seg_c, last, log_decay):
    size = seg_c.shape[1]
    steps_in = jnp.arange(size).astype(jnp.float32)
    query_matrix = (
        jnp.exp(log_decay[None, :] * (steps_in[:, None] + 1.0))
        * (seg_c == last[:, None]).astype(jnp.float32)[..., None]
    )
    key_matrix = (
        jnp.exp(log_decay[None, :] * (size - 1.0 - steps_in[:, None]))
        * (seg_c == seg_c[:, -1:]).astype(jnp.float32)[..., None]
    )
    keep = (seg_c[:, 0] == seg_c[:, -1]) & (seg_c[:, 0] == last)
    return (query_matrix, key_matrix, keep)


def block_forward(query_section, key_section, value_section, seg_c, running_state, last, log_decay):
    size = seg_c.shape[1]
    mixing = decay_matrix(seg_c, log_decay)
    scores = jnp.einsum(
        "snhk,smhk->shnm", query_section, key_section, preferred_element_type=jnp.float32
    )
    weights = (scores * mixing).astype(jnp.bfloat16)
    intra = jnp.einsum(
        "shnm,smhv->snhv", weights, value_section, preferred_element_type=jnp.float32
    )
    query_matrix, key_matrix, keep = block_weights(seg_c, last, log_decay)
    cross_section_part = jnp.einsum(
        "snhk,shkv->snhv",
        query_section.astype(jnp.float32) * query_matrix[..., None],
        running_state,
        precision=PRECISION_TOP,
    )
    carried_over = jnp.where(
        keep[:, None, None, None],
        jnp.exp(log_decay * size)[None, :, None, None] * running_state,
        0.0,
    )
    next_state = carried_over + jnp.einsum(
        "smhk,smhv->shkv",
        key_section.astype(jnp.float32) * key_matrix[..., None],
        value_section.astype(jnp.float32),
        precision=PRECISION_TOP,
    )
    return (intra + cross_section_part, next_state)


def block_backward(
    query_section,
    key_section,
    value_section,
    seg_c,
    grad_c,
    running_state,
    last,
    grad_after,
    log_decay,
):
    size = seg_c.shape[1]
    mixing = decay_matrix(seg_c, log_decay)
    scores = jnp.einsum(
        "snhk,smhk->shnm", query_section, key_section, preferred_element_type=jnp.float32
    )
    weights = (scores * mixing).astype(jnp.bfloat16)
    grad_weights = jnp.einsum(
        "snhv,smhv->shnm", grad_c, value_section, preferred_element_type=jnp.float32
    )
    grad_scores = (grad_weights * mixing).astype(jnp.bfloat16)
    grad_query = jnp.einsum(
        "shnm,smhk->snhk", grad_scores, key_section, preferred_element_type=jnp.float32
    )
    grad_key = jnp.einsum(
        "shnm,snhk->smhk", grad_scores, query_section, preferred_element_type=jnp.float32
    )
    grad_value = jnp.einsum("shnm,snhv->smhv", weights, grad_c, preferred_element_type=jnp.float32)
    query_matrix, key_matrix, keep = block_weights(seg_c, last, log_decay)
    grad_float = grad_c.astype(jnp.float32)
    grad_query = grad_query + query_matrix[..., None] * jnp.einsum(
        "snhv,shkv->snhk", grad_float, running_state, precision=PRECISION_TOP
    )
    grad_key = grad_key + key_matrix[..., None] * jnp.einsum(
        "smhv,shkv->smhk", value_section.astype(jnp.float32), grad_after, precision=PRECISION_TOP
    )
    grad_value = grad_value + jnp.einsum(
        "smhk,shkv->smhv",
        key_section.astype(jnp.float32) * key_matrix[..., None],
        grad_after,
        precision=PRECISION_TOP,
    )
    grad_enter = jnp.where(
        keep[:, None, None, None], jnp.exp(log_decay * size)[None, :, None, None] * grad_after, 0.0
    )
    grad_enter = grad_enter + jnp.einsum(
        "snhk,snhv->shkv",
        query_section.astype(jnp.float32) * query_matrix[..., None],
        grad_float,
        precision=PRECISION_TOP,
    )
    return (grad_query, grad_key, grad_value, grad_enter)


def local_retention(query, key, value, segments, log_decay):
    seqs, length = segments.shape
    count = length // BLOCK

    def advance(carry, index):
        running_state, last, output = carry
        start = index * BLOCK
        pieces = [
            lax.dynamic_slice_in_dim(item, start, BLOCK, 1)
            for item in (query, key, value, segments)
        ]
        result, next_state = block_forward(
            pieces[0], pieces[1], pieces[2], pieces[3], running_state, last, log_decay
        )
        output = lax.dynamic_update_slice_in_dim(output, result, start, 1)
        return ((next_state, pieces[3][:, -1], output), (running_state, last))

    initial = (
        jnp.zeros((seqs, H, KD, VD), jnp.float32),
        jnp.full((seqs,), -1, jnp.int32),
        jnp.zeros((seqs, length, H, VD), jnp.float32),
    )
    final, kept = lax.scan(advance, initial, jnp.arange(count))
    return (final[2], kept[0], kept[1], final[0])


def local_backward(
    query, key, value, segments, log_decay, grad_ret, entering, entering_last, own_grad
):
    seqs, length = segments.shape
    count = length // BLOCK

    def retreat(carry, index):
        grad_state, query_buf, key_buf, value_buf = carry
        start = index * BLOCK
        pieces = [
            lax.dynamic_slice_in_dim(item, start, BLOCK, 1)
            for item in (query, key, value, segments, grad_ret)
        ]
        grad_query, grad_key, grad_value, grad_enter = block_backward(
            pieces[0],
            pieces[1],
            pieces[2],
            pieces[3],
            pieces[4],
            entering[index],
            entering_last[index],
            grad_state,
            log_decay,
        )
        query_buf = lax.dynamic_update_slice_in_dim(query_buf, grad_query, start, 1)
        key_buf = lax.dynamic_update_slice_in_dim(key_buf, grad_key, start, 1)
        value_buf = lax.dynamic_update_slice_in_dim(value_buf, grad_value, start, 1)
        return ((grad_enter, query_buf, key_buf, value_buf), None)

    initial = (
        own_grad,
        jnp.zeros((seqs, length, H, KD), jnp.float32),
        jnp.zeros((seqs, length, H, KD), jnp.float32),
        jnp.zeros((seqs, length, H, VD), jnp.float32),
    )
    final, unused = lax.scan(retreat, initial, jnp.arange(count), reverse=True)
    return (final[1], final[2], final[3])


def adam_step(master, moment, second, grad, scale, rate, decay_weight):
    clipped = grad * scale
    moment_new = BETA_ONE * moment + (1.0 - BETA_ONE) * clipped
    second_new = BETA_TWO * second + (1.0 - BETA_TWO) * clipped * clipped
    corrected = (
        moment_new
        / (1.0 - BETA_ONE**STEP)
        / (jnp.sqrt(second_new / (1.0 - BETA_TWO**STEP)) + ADAM_EPS)
    )
    return (master - rate * (corrected + decay_weight * master), moment_new, second_new)


def on_device(
    tokens,
    cotangent,
    segments,
    log_decay,
    w_qk,
    w_vg,
    w_out,
    w_gu,
    w_down,
    norm_gains,
    m_qk,
    m_vg,
    m_out,
    m_gu,
    m_down,
    m_gains,
    v_qk,
    v_vg,
    v_out,
    v_gu,
    v_down,
    v_gains,
):
    low = jnp.bfloat16
    slices = jnp.concatenate(
        [
            w_qk.astype(low).transpose(0, 2, 1).reshape(-1, w_qk.shape[1]),
            w_vg.astype(low).transpose(0, 2, 1).reshape(-1, w_qk.shape[1]),
            w_out.astype(low),
            w_gu.astype(low).transpose(0, 2, 1).reshape(-1, w_qk.shape[1]),
            w_down.astype(low),
            norm_gains.astype(low),
        ]
    )
    whole = gather_shards(slices).transpose(1, 0, 2).reshape(slices.shape[0], -1)
    kd, vd, ff = H * KD, H * VD, w_down.shape[0]
    cuts = [0, kd, kd, vd, vd, vd, ff, ff, ff, 2]
    edges = [sum(cuts[: i + 1]) for i in range(len(cuts))]
    q_t, k_t, v_t, g_t, full_out, gate_t, up_t, full_down, full_gains = [
        whole[edges[i] : edges[i + 1]] for i in range(9)
    ]
    full_qk = (q_t.T, k_t.T)
    full_vg = (v_t.T, g_t.T)
    full_gu = (gate_t.T, up_t.T)
    seqs, length, width = tokens.shape
    rows = seqs * length
    inputs = tokens.astype(jnp.float32).reshape(rows, width)
    gain_one = full_gains[0].astype(jnp.float32)
    gain_two = full_gains[1].astype(jnp.float32)
    normed_one, pull_one = jax.vjp(rms_norm, inputs, gain_one)
    hidden_one = normed_one.astype(jnp.bfloat16)
    query_pre = matmul(hidden_one, full_qk[0])
    key_pre = matmul(hidden_one, full_qk[1])
    value_pre = matmul(hidden_one, full_vg[0])
    gate_pre = matmul(hidden_one, full_vg[1])
    positions = (lax.axis_index("shard") * length + jnp.arange(length)).astype(jnp.float32)
    cosine, sine = rotation_tables(positions)
    query = (
        rotate(query_pre.reshape(seqs, length, H * KD), cosine, sine)
        .astype(jnp.bfloat16)
        .reshape(seqs, length, H, KD)
    )
    key = (
        rotate(key_pre.reshape(seqs, length, H * KD), cosine, sine)
        .astype(jnp.bfloat16)
        .reshape(seqs, length, H, KD)
    )
    value = value_pre.astype(jnp.bfloat16).reshape(seqs, length, H, VD)
    local_out, entering, entering_last, local_state = local_retention(
        query, key, value, segments, log_decay
    )
    link_decay = jnp.exp(log_decay * length)
    first_seg, last_seg = segments[:, 0], segments[:, -1]
    size = lax.axis_size("shard")
    near = lax.ppermute(
        last_seg.astype(jnp.float32), "shard", [(i, i + 1) for i in range(size - 1)]
    )
    in_last = jnp.where(lax.axis_index("shard") > 0, near.astype(jnp.int32), -1)
    joined = jnp.where(in_last == first_seg, first_seg, -2)
    in_state = pass_on(local_state, joined, last_seg, link_decay, False)
    device_steps = jnp.arange(length).astype(jnp.float32)
    device_weight = (
        jnp.exp(log_decay[None, :] * (device_steps[:, None] + 1.0))
        * (segments == in_last[:, None]).astype(jnp.float32)[..., None]
    )
    query_float = query.astype(jnp.float32)
    retained = local_out + jnp.einsum(
        "snhk,shkv->snhv", query_float * device_weight[..., None], in_state, precision=PRECISION_TOP
    )
    mixed_attn, pull_gate = jax.vjp(gated_norm, retained.reshape(rows, H * VD), gate_pre)
    mixed_low = mixed_attn.astype(jnp.bfloat16)
    resid = inputs + matmul(mixed_low, full_out)
    normed_two, pull_two = jax.vjp(rms_norm, resid, gain_two)
    hidden_two = normed_two.astype(jnp.bfloat16)
    gate_ff = matmul(hidden_two, full_gu[0])
    up_ff = matmul(hidden_two, full_gu[1])
    product, pull_ff = jax.vjp(gelu_gate, gate_ff, up_ff)
    product_low = product.astype(jnp.bfloat16)
    output = resid + matmul(product_low, full_down)
    tokens_out = output.astype(jnp.bfloat16).reshape(tokens.shape)
    grad_out = cotangent.reshape(rows, width)
    grad_down = matmul(product_low.T, grad_out)
    grad_product = matmul(grad_out, full_down.T)
    grad_gate_ff, grad_up_ff = pull_ff(grad_product)
    grad_gate_low = grad_gate_ff.astype(jnp.bfloat16)
    grad_up_low = grad_up_ff.astype(jnp.bfloat16)
    grad_gu = [matmul(grad_gate_low.T, hidden_two), matmul(grad_up_low.T, hidden_two)]
    grad_hidden_two = matmul(grad_gate_low, full_gu[0].T) + matmul(grad_up_low, full_gu[1].T)
    grad_resid_norm, grad_gain_two = pull_two(grad_hidden_two)
    grad_resid = grad_out.astype(jnp.float32) + grad_resid_norm
    grad_resid_low = grad_resid.astype(jnp.bfloat16)
    grad_out_proj = matmul(mixed_low.T, grad_resid_low)
    grad_mixed = matmul(grad_resid_low, full_out.T)
    grad_retained, grad_gate = pull_gate(grad_mixed)
    grad_gate_attn = grad_gate.astype(jnp.bfloat16)
    grad_ret_low = grad_retained.astype(jnp.bfloat16).reshape(seqs, length, H, VD)
    grad_ret_float = grad_ret_low.astype(jnp.float32)
    device_grad = jnp.einsum(
        "snhk,snhv->shkv",
        query_float * device_weight[..., None],
        grad_ret_float,
        precision=PRECISION_TOP,
    )
    grad_query_device = device_weight[..., None] * jnp.einsum(
        "snhv,shkv->snhk", grad_ret_float, in_state, precision=PRECISION_TOP
    )
    own_grad = pass_on(device_grad, joined, last_seg, link_decay, True)
    grad_query, grad_key, grad_value = local_backward(
        query, key, value, segments, log_decay, grad_ret_low, entering, entering_last, own_grad
    )
    grad_query = grad_query + grad_query_device
    grad_query_pre = (
        rotate(grad_query.reshape(seqs, length, H * KD), cosine, -sine)
        .reshape(rows, H * KD)
        .astype(jnp.bfloat16)
    )
    grad_key_pre = (
        rotate(grad_key.reshape(seqs, length, H * KD), cosine, -sine)
        .reshape(rows, H * KD)
        .astype(jnp.bfloat16)
    )
    grad_value_pre = grad_value.reshape(rows, H * VD).astype(jnp.bfloat16)
    grad_qk = [matmul(grad_query_pre.T, hidden_one), matmul(grad_key_pre.T, hidden_one)]
    grad_vg = [matmul(grad_value_pre.T, hidden_one), matmul(grad_gate_attn.T, hidden_one)]
    grad_hidden_one = (
        matmul(grad_query_pre, full_qk[0].T)
        + matmul(grad_key_pre, full_qk[1].T)
        + matmul(grad_value_pre, full_vg[0].T)
        + matmul(grad_gate_attn, full_vg[1].T)
    )
    grad_input_norm, grad_gain_one = pull_one(grad_hidden_one)
    grad_input = (grad_resid + grad_input_norm).astype(jnp.bfloat16).reshape(tokens.shape)
    grad_gains = jnp.stack([grad_gain_one, grad_gain_two])
    def packed(items):
        rows = sum(item.shape[0] for item in items)
        quantum = 16 * lax.axis_size("dp")
        fill = -rows % quantum
        stacked = jnp.concatenate(
            [item.astype(low) for item in items] + [jnp.zeros((fill, width), low)]
        )
        return stacked.reshape(stacked.shape[0], -1, width // size).transpose(1, 0, 2)

    early = reduce_owned(packed([grad_down, grad_out_proj, grad_gu[0], grad_gu[1], grad_vg[1]]))
    late = reduce_owned(packed([grad_qk[0], grad_qk[1], grad_vg[0], grad_gains]))
    early = early.astype(jnp.float32)
    late = late.astype(jnp.float32)
    squares = jnp.sum(early * early) + jnp.sum(late * late)
    total = squares
    for bit in range(bits_of("shard")):
        total = total + exchange(total, "shard", bit)
    e = [early[:ff], early[ff : ff + vd], early[ff + vd : 2 * ff + vd]]
    e += [early[2 * ff + vd : 3 * ff + vd], early[3 * ff + vd : 3 * ff + 2 * vd]]
    l = [late[:kd], late[kd : 2 * kd], late[2 * kd : 2 * kd + vd]]
    owned = (
        jnp.stack([l[0].T, l[1].T]),
        jnp.stack([l[2].T, e[4].T]),
        e[1],
        jnp.stack([e[2].T, e[3].T]),
        e[0],
        late[2 * kd + vd : 2 * kd + vd + 2],
    )
    grad_norm = jnp.sqrt(total)
    scale = jnp.minimum(1.0, CLIP / (grad_norm + 1e-06))
    masters = (w_qk, w_vg, w_out, w_gu, w_down, norm_gains)
    moments = (m_qk, m_vg, m_out, m_gu, m_down, m_gains)
    seconds = (v_qk, v_vg, v_out, v_gu, v_down, v_gains)
    rates = (MATRIX_RATE,) * 5 + (GAIN_RATE,)
    decays = (DECAY_WEIGHT,) * 5 + (0.0,)
    results = [
        adam_step(
            masters[index],
            moments[index],
            seconds[index],
            owned[index],
            scale,
            rates[index],
            decays[index],
        )
        for index in range(6)
    ]
    new_w = [entry[0] for entry in results]
    new_m = [entry[1] for entry in results]
    new_v = [entry[2] for entry in results]
    return (
        tokens_out,
        grad_input,
        new_w[0],
        new_w[1],
        new_w[2],
        new_w[3],
        new_w[4],
        new_w[5],
        new_m[0],
        new_m[1],
        new_m[2],
        new_m[3],
        new_m[4],
        new_m[5],
        new_v[0],
        new_v[1],
        new_v[2],
        new_v[3],
        new_v[4],
        new_v[5],
        grad_norm,
    )


def solution(mesh):
    in_specs = (
        P("dp", "shard", None),
        P("dp", "shard", None),
        P("dp", "shard"),
        P(),
        P(None, "shard", None),
        P(None, "shard", None),
        P(None, "shard"),
        P(None, "shard", None),
        P(None, "shard"),
        P(None, "shard"),
        P(None, "shard", None),
        P(None, "shard", None),
        P(None, "shard"),
        P(None, "shard", None),
        P(None, "shard"),
        P(None, "shard"),
        P(None, "shard", None),
        P(None, "shard", None),
        P(None, "shard"),
        P(None, "shard", None),
        P(None, "shard"),
        P(None, "shard"),
    )
    out_specs = (
        P("dp", "shard", None),
        P("dp", "shard", None),
        P(None, "shard", None),
        P(None, "shard", None),
        P(None, "shard"),
        P(None, "shard", None),
        P(None, "shard"),
        P(None, "shard"),
        P(None, "shard", None),
        P(None, "shard", None),
        P(None, "shard"),
        P(None, "shard", None),
        P(None, "shard"),
        P(None, "shard"),
        P(None, "shard", None),
        P(None, "shard", None),
        P(None, "shard"),
        P(None, "shard", None),
        P(None, "shard"),
        P(None, "shard"),
        P(),
    )
    return jax.shard_map(
        on_device, mesh=mesh, in_specs=in_specs, out_specs=out_specs, check_vma=False
    )
```

```python
import functools
import math

import jax
import jax.numpy as jnp
from jax import lax
from jax.experimental import pallas as pl
from jax.experimental.pallas import tpu as pltpu
from jax.sharding import PartitionSpec as P

H = 2
KD = 256
VD = 432
VP = 512
BLOCK = 512
STEP = 10

EPS = 1e-05
ADAM_EPS = 1e-08
BETA_ONE = 0.9
BETA_TWO = 0.95
MATRIX_RATE = 0.15
GAIN_RATE = 1.0
DECAY_WEIGHT = 0.1
CLIP = 1.0

LOW = jnp.bfloat16
WIDE = jnp.float32
VMEM = pltpu.VMEM
SMEM = pltpu.SMEM
LIMIT = 56 * 1024 * 1024


def dot(a, b):
    return jnp.dot(a, b, preferred_element_type=WIDE)


def dot_nt(a, b):
    return lax.dot_general(a, b, (((1,), (1,)), ((), ())), preferred_element_type=WIDE)


def dot_tn(a, b):
    return lax.dot_general(a, b, (((0,), (0,)), ((), ())), preferred_element_type=WIDE)


def params(**more):
    return pltpu.CompilerParams(vmem_limit_bytes=LIMIT, **more)


def cost(flops, moved):
    return pl.CostEstimate(flops=int(flops), bytes_accessed=int(moved), transcendentals=0)


def smem():
    return pl.BlockSpec(memory_space=SMEM)


def whole(shape):
    return pl.BlockSpec(shape, lambda *at: (0,) * len(shape))


def shape(dims, kind):
    return jax.ShapeDtypeStruct(dims, kind)


def bits_of(axis):
    return (lax.axis_size(axis) - 1).bit_length()


def exchange(value, axis, bit):
    size = lax.axis_size(axis)
    return lax.ppermute(value, axis, [(i, i ^ (1 << bit)) for i in range(size)])


def gather_shards(own):
    held = [(0, own)]
    for bit in reversed(range(bits_of("shard"))):
        held += [(mask | (1 << bit), exchange(part, "shard", bit)) for mask, part in held]
    return held


def add_low(one, two):
    return (one.astype(WIDE) + two.astype(WIDE)).astype(LOW)


def reduce_owned(keep, send):
    near = exchange(send, "shard", 0)
    far = exchange(add_low(keep[1], near[1]), "shard", 1)
    held = (keep[0].astype(WIDE) + near[0].astype(WIDE) + far.astype(WIDE)).astype(LOW)
    place = lax.axis_index("dp")
    count = bits_of("dp")
    for bit in range(count):
        half = (place >> bit) & 1
        rows = held.shape[0] // 2
        keep = lax.dynamic_slice_in_dim(held, half * rows, rows, 0)
        send = lax.dynamic_slice_in_dim(held, (1 - half) * rows, rows, 0)
        held = add_low(keep, exchange(send, "dp", bit))
    for bit in reversed(range(count)):
        half = (place >> bit) & 1
        other = exchange(held, "dp", bit)
        held = jnp.where(half == 0, jnp.concatenate([held, other]), jnp.concatenate([other, held]))
    return held


def pass_on(local, decay, reverse):
    mine = lax.axis_index("shard")
    decay = decay[:, None, None]
    total = local
    entering = jnp.zeros(local.shape, WIDE)
    reach = jnp.ones_like(decay)
    span = decay
    count = bits_of("shard")
    for bit in range(count):
        got = exchange(total, "shard", bit).astype(WIDE)
        side = (mine >> bit) & 1
        later = (side == 0) if reverse else (side == 1)
        entering = jnp.where(later, entering + reach * got, entering)
        if bit + 1 < count:
            wide = total.astype(WIDE)
            total = jnp.where(later, wide + span * got, got + span * wide).astype(LOW)
            reach = jnp.where(later, reach * span, reach)
            span = span * span
    return entering.astype(LOW)


def assemble_kernel(plan, fills, masks, me_ref, *refs):
    sources, out = refs[:-1], refs[-1]
    lanes = sources[0].shape[1]
    for row, size in fills:
        out[row : row + size, :] = jnp.zeros((size, out.shape[1]), out.dtype)
    for mask, source in zip(masks, sources):
        lane = pl.multiple_of(jnp.bitwise_xor(me_ref[0], mask) * lanes, lanes)
        for start, row, size in plan:
            out[row : row + size, pl.ds(lane, lanes)] = source[start : start + size, :]


def assemble(held, plan, fills, rows, width, me):
    masks = [mask for mask, part in held]
    parts = [part for mask, part in held]
    return pl.pallas_call(
        functools.partial(assemble_kernel, plan, fills, masks),
        out_shape=shape((rows, width), LOW),
        in_specs=[smem()] + [pl.BlockSpec(memory_space=VMEM)] * len(parts),
        out_specs=pl.BlockSpec(memory_space=VMEM),
        compiler_params=params(),
        cost_estimate=cost(0, 4 * rows * width),
    )(me, *parts)


def rotated(flat, cosine, sine):
    half = KD // 2
    parts = []
    for h in range(H):
        u = flat[:, h * KD : h * KD + half]
        w = flat[:, h * KD + half : (h + 1) * KD]
        parts += [u * cosine - w * sine, w * cosine + u * sine]
    return jnp.concatenate(parts, axis=1)


def column(size):
    return lax.broadcasted_iota(jnp.int32, (size, 1), 0).astype(WIDE)


def front_kernel(
    seq, count, decay, seg_s, tok, w, gains, cos, sin, seg, *rest
):
    hid, q, k, v, kv, out_state, state = rest[-7:]
    c = pl.program_id(0)
    x = tok[...].astype(WIDE)
    r = lax.rsqrt(jnp.mean(x * x, axis=1, keepdims=True) + EPS)
    h1 = (x * r * gains[0:1, :].astype(WIDE)).astype(LOW)
    hid[...] = h1
    kd = H * KD
    q[...] = rotated(dot_nt(h1, w[0:kd, :]), cos[...], sin[...]).astype(LOW)
    key = rotated(dot_nt(h1, w[kd : 2 * kd, :]), cos[...], sin[...]).astype(LOW)
    k[...] = key
    val = dot_nt(h1, w[2 * kd : 2 * kd + H * VP, :]).astype(LOW)
    v[...] = val
    first = seg_s[seq, c * BLOCK]
    last = seg_s[seq, c * BLOCK + BLOCK - 1]
    before = seg_s[seq, jnp.maximum(c * BLOCK - 1, 0)]
    here = (seg[...] == last).astype(WIDE)
    joined = jnp.logical_and(jnp.logical_and(first == last, first == before), c > 0)
    for h in range(H):
        a = decay[h]
        kw = jnp.exp(a * (BLOCK - 1.0 - column(BLOCK))) * here
        kk = (key[:, h * KD : (h + 1) * KD].astype(WIDE) * kw).astype(LOW)
        add = dot_tn(kk, val[:, h * VP : (h + 1) * VP])
        kv[h] = add
        factor = jnp.exp(jnp.full((1, 1), a * BLOCK, WIDE))
        total = jnp.where(joined, factor * state[h], 0.0) + add
        state[h] = total
        out_state[h] = total.astype(LOW)


def seq_block(seqs, width, seq, count):
    return pl.BlockSpec((BLOCK, width), lambda c: (seq * count + c, 0))


def front(seq, seqs, length, tokens, seg_col, segments, decay, w, gains, cos, sin, earlier):
    count = length // BLOCK
    rows = seqs * length
    width = tokens.shape[-1]
    block = lambda n: seq_block(seqs, n, seq, count)
    outs = [(width, LOW), (H * KD, LOW), (H * KD, LOW), (H * VP, LOW)]
    many = len(outs)
    table = pl.BlockSpec((BLOCK, KD // 2), lambda c: (c, 0))
    inputs = [decay, segments, tokens, w, gains, cos, sin, seg_col]
    specs = [smem(), smem(), block(width), whole(w.shape), whole(gains.shape), table, table, block(1)]
    aliases = {}
    if earlier is not None:
        aliases = {len(inputs) + i: i for i in range(many)}
        inputs += list(earlier)
        specs += [pl.BlockSpec(memory_space=pl.ANY)] * many
    return pl.pallas_call(
        functools.partial(front_kernel, seq, count),
        grid=(count,),
        out_shape=[shape((rows, n), kind) for n, kind in outs]
        + [shape((count, H, KD, VP), WIDE), shape((H, KD, VP), LOW)],
        in_specs=specs,
        out_specs=[block(n) for n, kind in outs]
        + [pl.BlockSpec((None, H, KD, VP), lambda c: (c, 0, 0, 0)), whole((H, KD, VP))],
        scratch_shapes=[VMEM((H, KD, VP), WIDE)],
        input_output_aliases=aliases,
        compiler_params=params(),
        cost_estimate=cost(2 * length * width * w.shape[0], 12 * length * width),
    )(*inputs)


def mixing_tables(decay, table):
    n = lax.broadcasted_iota(jnp.int32, (BLOCK, BLOCK), 0)
    m = lax.broadcasted_iota(jnp.int32, (BLOCK, BLOCK), 1)
    offset = n - m
    for h in range(H):
        table[h] = jnp.where(
            offset >= 0, jnp.exp(decay[h] * jnp.maximum(offset, 0).astype(WIDE)), 0.0
        )


TILE = 256


def inner_kernel(decay, q, k, v, hid, wg, seg, seg_row, intra, gate, table):
    @pl.when(pl.program_id(0) == 0)
    def _():
        mixing_tables(decay, table)

    gate[...] = dot_nt(hid[...], wg[...])
    for i in range(BLOCK // TILE):
        top, reach = i * TILE, (i + 1) * TILE
        same = seg[top:reach, :] == seg_row[:, :reach]
        for h in range(H):
            s = dot_nt(q[top:reach, h * KD : (h + 1) * KD], k[:reach, h * KD : (h + 1) * KD])
            weights = jnp.where(same, s * table[h, top:reach, :reach], 0.0).astype(LOW)
            intra[top:reach, h * VP : (h + 1) * VP] = dot(
                weights, v[:reach, h * VP : (h + 1) * VP]
            )


def inner(q, k, v, hid, wtwo, seg_col, seg_row, decay):
    rows, width = hid.shape
    block = lambda n: pl.BlockSpec((BLOCK, n), lambda t: (t, 0))
    return pl.pallas_call(
        inner_kernel,
        grid=(rows // BLOCK,),
        out_shape=[shape((rows, H * VP), WIDE)] * 2,
        in_specs=[
            smem(),
            block(H * KD),
            block(H * KD),
            block(H * VP),
            block(width),
            pl.BlockSpec((H * VP, width), lambda t: (0, 0)),
            block(1),
            pl.BlockSpec((None, 1, BLOCK), lambda t: (t, 0, 0)),
        ],
        out_specs=[block(H * VP)] * 2,
        scratch_shapes=[VMEM((H, BLOCK, BLOCK), WIDE)],
        compiler_params=params(),
        cost_estimate=cost(rows * (2 * width * H * VP + 2 * BLOCK * H * VP), 8 * rows * H * VP),
    )(decay, q, k, v, hid, wtwo, seg_col, seg_row)


def middle_kernel(seq, count, ff, decay, seg_s, in_last, *refs):
    (intra, gate, q, tok, cot, seg, w, gains, entering, kv) = refs[:10]
    (tok_out, hid2, prod, dgate, dup, mixed, glow, ggate, gret, st_out, dst, leave, state) = refs[-13:]
    t = pl.program_id(0)
    per = BLOCK // TILE
    c = t // per
    start = c * BLOCK
    vp = H * VP
    before = jnp.where(c > 0, seg_s[seq, jnp.maximum(start - 1, 0)], in_last[seq])

    @pl.when(t == 0)
    def _():
        state[...] = entering[...].astype(WIDE)
        st_out[0] = entering[...]

    for b in range(1, count):

        @pl.when(t == b * per)
        def _():
            prev = seg_s[seq, (b - 1) * BLOCK - 1] if b > 1 else in_last[seq]
            first = seg_s[seq, (b - 1) * BLOCK]
            last = seg_s[seq, b * BLOCK - 1]
            joined = jnp.logical_and(first == last, first == prev)
            for h in range(H):
                factor = jnp.exp(jnp.full((1, 1), decay[h] * BLOCK, WIDE))
                total = jnp.where(joined, factor * state[h], 0.0) + kv[b - 1, h]
                state[h] = total
                st_out[b, h] = total.astype(LOW)

    here = (seg[...] == before).astype(WIDE)
    within = ((t % per) * TILE).astype(WIDE) + 1.0 + column(TILE)
    lane = lax.broadcasted_iota(jnp.int32, (1, VP), 1)
    real = (lane < VD).astype(WIDE)
    normed, silu, slope, inverse, weighted = [], [], [], [], []
    for h in range(H):
        qw = jnp.exp(decay[h] * within) * here
        qh = q[:, h * KD : (h + 1) * KD]
        weighted.append((qh.astype(WIDE) * qw).astype(LOW))
        cross = dot(qh, st_out[c, h])
        ret = intra[:, h * VP : (h + 1) * VP] + qw * cross
        mean = jnp.sum(ret, axis=1, keepdims=True) * (1.0 / VD)
        centered = (ret - mean) * real
        var = jnp.sum(centered * centered, axis=1, keepdims=True) * (1.0 / VD)
        inv = lax.rsqrt(var + 1.0 * KD)
        nh = centered * inv
        g = gate[:, h * VP : (h + 1) * VP]
        sg = 0.5 * jnp.tanh(0.5 * g) + 0.5
        sl = g * sg
        mixed[:, h * VP : (h + 1) * VP] = (nh * sl).astype(LOW)
        normed.append(nh)
        silu.append(sl)
        slope.append(sg + sl * (1.0 - sg))
        inverse.append(inv)
    x = tok[...].astype(WIDE)
    w_out = w[vp : 2 * vp, :]
    wg = w[2 * vp : 2 * vp + ff, :]
    wu = w[2 * vp + ff : 2 * vp + 2 * ff, :]
    wd = w[2 * vp + 2 * ff : 2 * vp + 3 * ff, :]
    resid = x + dot(mixed[...], w_out)
    r2 = lax.rsqrt(jnp.mean(resid * resid, axis=1, keepdims=True) + EPS)
    gain = gains[1:2, :].astype(WIDE)
    xhat = resid * r2
    h2 = (xhat * gain).astype(LOW)
    hid2[...] = h2
    gf = dot_nt(h2, wg)
    uf = dot_nt(h2, wu)
    e = jnp.exp(-0.5 * gf * gf)
    d = 1.0 / (1.0 + (0.3275911 * math.sqrt(0.5)) * jnp.abs(gf))
    poly = d * (
        0.254829592
        + d * (-0.284496736 + d * (1.421413741 + d * (-1.453152027 + d * 1.061405429)))
    )
    tail = 0.5 * poly * e
    cdf = jnp.where(gf >= 0.0, 1.0 - tail, tail)
    ge = gf * cdf
    dge = cdf + gf * e * (1.0 / math.sqrt(2.0 * math.pi))
    p = (ge * uf).astype(LOW)
    prod[...] = p
    ct = cot[...]
    tok_out[...] = (resid + dot(p, wd)).astype(LOW)
    gp = dot_nt(ct, wd)
    dg = (gp * uf * dge).astype(LOW)
    du = (gp * ge).astype(LOW)
    dgate[...] = dg
    dup[...] = du
    gh = (dot(dg, wg) + dot(du, wu)) * gain
    inner_product = jnp.mean(gh * xhat, axis=1, keepdims=True)
    gl = (ct.astype(WIDE) + r2 * (gh - xhat * inner_product)).astype(LOW)
    glow[...] = gl
    gm_all = dot_nt(gl, w_out)
    for h in range(H):
        gm = gm_all[:, h * VP : (h + 1) * VP]
        ggate[:, h * VP : (h + 1) * VP] = (gm * normed[h] * slope[h]).astype(LOW)
        gn = gm * silu[h]
        one = jnp.sum(gn, axis=1, keepdims=True) * (1.0 / VD)
        two = jnp.sum(gn * normed[h], axis=1, keepdims=True) * (1.0 / VD)
        gr = (inverse[h] * (gn - one - normed[h] * two) * real).astype(LOW)
        gret[:, h * VP : (h + 1) * VP] = gr
        add = dot_tn(weighted[h], gr)

        @pl.when(t % per == 0)
        def _():
            dst[c, h] = add

        @pl.when(t % per != 0)
        def _():
            dst[c, h] += add

    @pl.when(t == count * per - 1)
    def _():
        for h in range(H):
            total = dst[count - 1, h]
            for b in reversed(range(count - 1)):
                prev = seg_s[seq, b * BLOCK - 1] if b > 0 else in_last[seq]
                first = seg_s[seq, b * BLOCK]
                last = seg_s[seq, (b + 1) * BLOCK - 1]
                joined = jnp.logical_and(first == last, first == prev)
                factor = jnp.exp(jnp.full((1, 1), decay[h] * BLOCK, WIDE))
                total = jnp.where(joined, factor * total, 0.0) + dst[b, h]
            leave[h] = total.astype(LOW)


def middle(seq, seqs, length, ff, data, seg_col, segments, in_last, decay, w, gains, entering, kv, earlier):
    intra, gate, q, tokens, cotangent = data
    rows, width = tokens.shape
    count = length // BLOCK
    tiles = length // TILE
    block = lambda n: pl.BlockSpec((TILE, n), lambda t: (seq * tiles + t, 0))
    vp = H * VP
    outs = [width, width, ff, ff, ff, vp, width, vp, vp]
    many = len(outs)
    inputs = [decay, segments, in_last, intra, gate, q, tokens, cotangent, seg_col, w, gains, entering, kv]
    specs = [smem()] * 3 + [block(vp), block(vp), block(H * KD), block(width), block(width), block(1)]
    specs += [whole(w.shape), whole(gains.shape), whole(entering.shape), whole(kv.shape)]
    aliases = {}
    if earlier is not None:
        aliases = {len(inputs) + i: i for i in range(many)}
        inputs += list(earlier)
        specs += [pl.BlockSpec(memory_space=pl.ANY)] * many
    states = (count, H, KD, VP)
    return pl.pallas_call(
        functools.partial(middle_kernel, seq, count, ff),
        grid=(tiles,),
        out_shape=[shape((rows, n), LOW) for n in outs]
        + [shape(states, LOW), shape(states, WIDE), shape(states[1:], LOW)],
        in_specs=specs,
        out_specs=[block(n) for n in outs] + [whole(states), whole(states), whole(states[1:])],
        scratch_shapes=[VMEM(states[1:], WIDE)],
        input_output_aliases=aliases,
        compiler_params=params(),
        cost_estimate=cost(2 * length * width * (2 * vp + 6 * ff), 30 * length * width),
    )(*inputs)


def weight_kernel(plan, me_ref, *refs):
    count = len({i for pair in plan for i in pair[:2]})
    ins, (keep, send, total) = refs[:count], refs[count:]
    t = pl.program_id(0)
    last = pl.num_programs(0) - 1
    for left, right, cuts in plan:
        a, b = ins[left], ins[right]
        for source, row, size in cuts:
            add = dot_tn(a[:, source : source + size], b[...])

            @pl.when(t == 0)
            def _():
                total[row : row + size, :] = add

            @pl.when(t > 0)
            def _():
                total[row : row + size, :] += add

    @pl.when(t == last)
    def _():
        lanes = keep.shape[2]
        used = max(row + size for left, right, cuts in plan for source, row, size in cuts)
        for part in range(2 * keep.shape[0]):
            target = (keep, send)[part & 1]
            lane = pl.multiple_of(jnp.bitwise_xor(me_ref[0], part) * lanes, lanes)
            target[part >> 1, :used, :] = total[:, pl.ds(lane, lanes)].astype(LOW)
            if used < keep.shape[1]:
                target[part >> 1, used:, :] = jnp.zeros((keep.shape[1] - used, lanes), LOW)


def weight_grads(arrays, plan, rows_out, me, shards):
    rows = arrays[0].shape[0]
    width = 512
    used = max(row + size for left, right, cuts in plan for source, row, size in cuts)
    block = lambda n: pl.BlockSpec((BLOCK, n), lambda t: (t, 0))
    lanes = arrays[plan[0][1]].shape[1] // shards
    return pl.pallas_call(
        functools.partial(weight_kernel, plan),
        grid=(rows // BLOCK,),
        out_shape=[shape((shards // 2, rows_out, lanes), LOW)] * 2,
        in_specs=[smem()] + [block(item.shape[1]) for item in arrays],
        out_specs=[whole((shards // 2, rows_out, lanes))] * 2,
        scratch_shapes=[VMEM((used, lanes * shards), WIDE)],
        compiler_params=params(),
        cost_estimate=cost(2 * rows * used * lanes * shards, 2 * rows * sum(i.shape[1] for i in arrays)),
    )(me, *arrays)


def back_kernel(seq, count, decay, seg_s, in_last, *refs):
    (q, k, v, gret, cos, sin, seg, seg_row, st, dst, after) = refs[:11]
    (dq, dk, dv, state, table, weights, grads) = refs[-7:]
    t = pl.program_id(0)
    c = count - 1 - t

    @pl.when(t == 0)
    def _():
        mixing_tables(decay, table)
        state[...] = after[...].astype(WIDE)
        weights[...] = jnp.zeros(weights.shape, LOW)
        grads[...] = jnp.zeros(grads.shape, LOW)

    for b in range(1, count):

        @pl.when(c == b - 1)
        def _():
            prev = seg_s[seq, b * BLOCK - 1]
            first = seg_s[seq, b * BLOCK]
            last = seg_s[seq, (b + 1) * BLOCK - 1]
            joined = jnp.logical_and(first == last, first == prev)
            for h in range(H):
                factor = jnp.exp(jnp.full((1, 1), decay[h] * BLOCK, WIDE))
                state[h] = jnp.where(joined, factor * state[h], 0.0) + dst[b, h]

    start = c * BLOCK
    before = jnp.where(c > 0, seg_s[seq, jnp.maximum(start - 1, 0)], in_last[seq])
    final = seg_s[seq, start + BLOCK - 1]
    here = (seg[...] == before).astype(WIDE)
    ends = (seg[...] == final).astype(WIDE)
    place = column(BLOCK)
    dqs, dks = [], []
    for h in range(H):
        a = decay[h]
        qh = q[:, h * KD : (h + 1) * KD]
        kh = k[:, h * KD : (h + 1) * KD]
        vh = v[:, h * VP : (h + 1) * VP]
        gh = gret[:, h * VP : (h + 1) * VP]
        qw = jnp.exp(a * (place + 1.0)) * here
        kw = jnp.exp(a * (BLOCK - 1.0 - place)) * ends
        parts = []
        for i in range(BLOCK // TILE):
            top, reach = i * TILE, (i + 1) * TILE
            same = seg[top:reach, :] == seg_row[:, :reach]
            mix = jnp.where(same, table[h, top:reach, :reach], 0.0)
            s = dot_nt(qh[top:reach, :], kh[:reach, :])
            weights[top:reach, :reach] = (s * mix).astype(LOW)
            gs = (dot_nt(gh[top:reach, :], vh[:reach, :]) * mix).astype(LOW)
            grads[top:reach, :reach] = gs
            parts.append(dot(gs, kh[:reach, :]))
        late = state[h].astype(LOW)
        dqs.append(jnp.concatenate(parts) + qw * dot_nt(gh, st[c, h]))
        parts, values = [], []
        for i in range(BLOCK // TILE):
            top, reach = i * TILE, (i + 1) * TILE
            parts.append(dot_tn(grads[top:, top:reach], qh[top:, :]))
            values.append(dot_tn(weights[top:, top:reach], gh[top:, :]))
        dks.append(jnp.concatenate(parts) + kw * dot_nt(vh, late))
        dv[:, h * VP : (h + 1) * VP] = (jnp.concatenate(values) + kw * dot(kh, late)).astype(LOW)
    dq[...] = rotated(jnp.concatenate(dqs, axis=1), cos[...], -sin[...]).astype(LOW)
    dk[...] = rotated(jnp.concatenate(dks, axis=1), cos[...], -sin[...]).astype(LOW)


def back(seq, length, data, cos, sin, seg_col, seg_row, segments, in_last, decay, st, dst, after, earlier):
    rows = data[0].shape[0]
    count = length // BLOCK
    block = lambda n: pl.BlockSpec((BLOCK, n), lambda t: (seq * count + count - 1 - t, 0))
    table = pl.BlockSpec((BLOCK, KD // 2), lambda t: (count - 1 - t, 0))
    outs = [H * KD, H * KD, H * VP]
    many = len(outs)
    inputs = [decay, segments, in_last, *data, cos, sin, seg_col, seg_row, st, dst, after]
    specs = [smem()] * 3 + [block(item.shape[1]) for item in data] + [table, table, block(1)]
    specs += [pl.BlockSpec((None, 1, BLOCK), lambda t: (seq * count + count - 1 - t, 0, 0))]
    specs += [whole(st.shape), whole(dst.shape), whole(after.shape)]
    aliases = {}
    if earlier is not None:
        aliases = {len(inputs) + i: i for i in range(many)}
        inputs += list(earlier)
        specs += [pl.BlockSpec(memory_space=pl.ANY)] * many
    return pl.pallas_call(
        functools.partial(back_kernel, seq, count),
        grid=(count,),
        out_shape=[shape((rows, n), LOW) for n in outs],
        in_specs=specs,
        out_specs=[block(n) for n in outs],
        scratch_shapes=[
            VMEM((H, KD, VP), WIDE),
            VMEM((H, BLOCK, BLOCK), WIDE),
            VMEM((BLOCK, BLOCK), LOW),
            VMEM((BLOCK, BLOCK), LOW),
        ],
        input_output_aliases=aliases,
        compiler_params=params(),
        cost_estimate=cost(length * H * 2 * BLOCK * 3 * (KD + VP), 16 * length * H * VP),
    )(*inputs)


def input_kernel(dq, dk, dv, ggate, tok, glow, w, wg, gains, out):
    kd, vp = H * KD, H * VP
    gh = dot(dq[...], w[:kd, :]) + dot(dk[...], w[kd : 2 * kd, :])
    gh += dot(dv[...], w[2 * kd : 2 * kd + vp, :]) + dot(ggate[...], wg[...])
    x = tok[...].astype(WIDE)
    r = lax.rsqrt(jnp.mean(x * x, axis=1, keepdims=True) + EPS)
    xhat = x * r
    gh = gh * gains[0:1, :].astype(WIDE)
    inner_product = jnp.mean(gh * xhat, axis=1, keepdims=True)
    out[...] = (glow[...].astype(WIDE) + r * (gh - xhat * inner_product)).astype(LOW)


def input_grad(dq, dk, dv, ggate, tokens, glow, w, wtwo, gains):
    rows, width = tokens.shape
    block = lambda item: pl.BlockSpec((BLOCK, item.shape[1]), lambda t: (t, 0))
    return pl.pallas_call(
        input_kernel,
        grid=(rows // BLOCK,),
        out_shape=shape((rows, width), LOW),
        in_specs=[block(item) for item in (dq, dk, dv, ggate, tokens, glow)]
        + [whole(w.shape), pl.BlockSpec((H * VP, width), lambda t: (0, 0)), whole(gains.shape)],
        out_specs=block(tokens),
        compiler_params=params(),
        cost_estimate=cost(2 * rows * width * (w.shape[0] + H * VP), 20 * rows * width),
    )(dq, dk, dv, ggate, tokens, glow, w, wtwo, gains)


def adam_step(master, moment, second, grad, scale, rate, decay_weight):
    clipped = grad * scale
    moment_new = BETA_ONE * moment + (1.0 - BETA_ONE) * clipped
    second_new = BETA_TWO * second + (1.0 - BETA_TWO) * clipped * clipped
    corrected = (
        moment_new
        * (1.0 / (1.0 - BETA_ONE**STEP))
        / (jnp.sqrt(second_new * (1.0 / (1.0 - BETA_TWO**STEP))) + ADAM_EPS)
    )
    return (master - rate * (corrected + decay_weight * master), moment_new, second_new)


def squares_kernel(vd, ff, early, late, w_qk, w_vg, w_gu, low_gains, grad_gains, total):
    kd = H * KD
    used_e = 2 * vd + 3 * ff
    used_l = 2 * kd + vd
    e = early[:used_e, :].astype(WIDE)
    l = late[:used_l, :].astype(WIDE)

    def product(weight, grad):
        turned = weight.astype(LOW).astype(WIDE).T
        return jnp.sum(turned * grad, axis=0, keepdims=True)

    one = product(w_qk[0], l[:kd, :]) + product(w_qk[1], l[kd : 2 * kd, :])
    one += product(w_vg[0], l[2 * kd : 2 * kd + vd, :])
    one += product(w_vg[1], e[ff + vd + 2 * ff : 2 * vd + 3 * ff, :])
    two = product(w_gu[0], e[ff + vd : 2 * ff + vd, :])
    two += product(w_gu[1], e[2 * ff + vd : 3 * ff + vd, :])
    gains = jnp.concatenate([one, two]) / low_gains[...].astype(LOW).astype(WIDE)
    grad_gains[...] = gains
    sums = jnp.sum(e * e, axis=0, keepdims=True) + jnp.sum(l * l, axis=0, keepdims=True)
    sums += jnp.sum(gains * gains, axis=0, keepdims=True)
    total[...] = jnp.broadcast_to(jnp.sum(sums, axis=1, keepdims=True), total.shape)


def squares(vd, ff, early, late, w_qk, w_vg, w_gu, gains):
    return pl.pallas_call(
        functools.partial(squares_kernel, vd, ff),
        out_shape=[shape(gains.shape, WIDE), shape((8, 128), WIDE)],
        in_specs=[pl.BlockSpec(memory_space=VMEM)] * 6,
        out_specs=[pl.BlockSpec(memory_space=VMEM)] * 2,
        compiler_params=params(),
    )(early, late, w_qk, w_vg, w_gu, gains)


def update_kernel(vd, ff, scale_ref, early, late, gain_grads, *refs):
    ins, outs = refs[:18], refs[18:]
    kd = H * KD
    scale = scale_ref[0]

    def step(place, at, grad, rate, decay_weight):
        results = adam_step(
            ins[place][at], ins[6 + place][at], ins[12 + place][at], grad, scale, rate, decay_weight
        )
        for group, result in enumerate(results):
            outs[6 * group + place][at] = result

    def rows(source, start, size):
        return source[start : start + size, :].astype(WIDE)

    step(0, 0, rows(late, 0, kd).T, MATRIX_RATE, DECAY_WEIGHT)
    step(0, 1, rows(late, kd, kd).T, MATRIX_RATE, DECAY_WEIGHT)
    step(1, 0, rows(late, 2 * kd, vd).T, MATRIX_RATE, DECAY_WEIGHT)
    step(1, 1, rows(early, vd + 3 * ff, vd).T, MATRIX_RATE, DECAY_WEIGHT)
    step(2, ..., rows(early, ff, vd), MATRIX_RATE, DECAY_WEIGHT)
    step(3, 0, rows(early, ff + vd, ff).T, MATRIX_RATE, DECAY_WEIGHT)
    step(3, 1, rows(early, 2 * ff + vd, ff).T, MATRIX_RATE, DECAY_WEIGHT)
    step(4, ..., rows(early, 0, ff), MATRIX_RATE, DECAY_WEIGHT)
    step(5, ..., gain_grads[...], GAIN_RATE, 0.0)


def update(vd, ff, scale, early, late, gain_grads, masters, moments, seconds):
    arrays = (*masters, *moments, *seconds)
    return pl.pallas_call(
        functools.partial(update_kernel, vd, ff),
        out_shape=[shape(item.shape, WIDE) for item in arrays],
        in_specs=[smem()] + [pl.BlockSpec(memory_space=VMEM)] * 21,
        out_specs=[pl.BlockSpec(memory_space=VMEM)] * 18,
        compiler_params=params(),
    )(scale, early, late, gain_grads, *arrays)


def on_device(
    tokens,
    cotangent,
    segments,
    log_decay,
    w_qk,
    w_vg,
    w_out,
    w_gu,
    w_down,
    norm_gains,
    *states,
):
    moments, seconds = states[:6], states[6:]
    masters = (w_qk, w_vg, w_out, w_gu, w_down, norm_gains)
    shards = lax.axis_size("shard")
    me = lax.axis_index("shard").reshape(1)
    seqs, length, width = tokens.shape
    rows = seqs * length
    kd, vd, ff = H * KD, H * VD, w_down.shape[0]
    vp = H * VP

    first = jnp.concatenate(
        [
            w_qk[0].astype(LOW).T,
            w_qk[1].astype(LOW).T,
            w_vg[0].astype(LOW).T,
            jnp.pad(norm_gains.astype(LOW), ((0, 14), (0, 0))),
        ]
    )
    rest = jnp.concatenate(
        [
            w_vg[1].astype(LOW).T,
            w_out.astype(LOW),
            w_gu[0].astype(LOW).T,
            w_gu[1].astype(LOW).T,
            w_down.astype(LOW),
        ]
    )
    first_held = gather_shards(first)
    rest_held = gather_shards(rest)

    def padded(start, row):
        return [(start + h * VD, row + h * VP, VD) for h in range(H)]

    def fills(row):
        return [(row + h * VP + VD, VP - VD) for h in range(H)]

    plan = [(0, 0, 2 * kd)] + padded(2 * kd, 2 * kd) + [(2 * kd + vd, 2 * kd + vp, 16)]
    w_one = assemble(first_held, plan, fills(2 * kd), 2 * kd + vp + 16, width, me)
    gains = w_one[2 * kd + vp :]
    w_one = w_one[: 2 * kd + vp]
    plan = padded(0, 0) + padded(vd, vp) + [(2 * vd, 2 * vp, 3 * ff)]
    w_two = assemble(rest_held, plan, fills(0) + fills(vp), 2 * vp + 3 * ff, width, me)

    half_width = KD // 2
    freq_rates = jnp.exp(-math.log(10000.0) * jnp.arange(half_width).astype(WIDE) / half_width)
    positions = (lax.axis_index("shard") * length + jnp.arange(length)).astype(WIDE)
    angles = positions[:, None] * freq_rates[None, :]
    cos, sin = jnp.cos(angles), jnp.sin(angles)

    tok = tokens.reshape(rows, width)
    cot = cotangent.reshape(rows, width)
    seg_col = segments.reshape(rows, 1)
    seg_row = segments.reshape(rows // BLOCK, 1, BLOCK)
    in_last = jnp.where(lax.axis_index("shard") > 0, segments[:, 0], -1)
    span = jnp.exp(log_decay * length)

    flat, kvs, entering = None, [], []
    for seq in range(seqs):
        *flat, kv, leaving = front(
            seq, seqs, length, tok, seg_col, segments, log_decay, w_one, gains, cos, sin, flat
        )
        kvs.append(kv)
        entering.append(pass_on(leaving, span, False))
    hid, q, k, v = flat
    intra, gate = inner(q, k, v, hid, w_two, seg_col, seg_row, log_decay)
    data = (intra, gate, q, tok, cot)
    flat, sts, dsts, after = None, [], [], []
    for seq in range(seqs):
        *flat, st, dst, leaving = middle(
            seq, seqs, length, ff, data, seg_col, segments, in_last, log_decay,
            w_two, gains, entering[seq], kvs[seq], flat,
        )
        sts.append(st)
        dsts.append(dst)
        after.append(pass_on(leaving, span, True))
    tokens_out, hid2, prod, dgate, dup, mixed, glow, ggate, gret = flat

    quantum = 16 * lax.axis_size("dp")
    fit = lambda used: used + -used % quantum

    def halves(row):
        return [(h * VP, row + h * VD, VD) for h in range(H)]

    plan = [
        (0, 1, [(0, 0, ff)]),
        (2, 3, halves(ff)),
        (4, 5, [(0, ff + vd, ff)]),
        (6, 5, [(0, 2 * ff + vd, ff)]),
        (7, 8, halves(3 * ff + vd)),
    ]
    early = weight_grads(
        [prod, cot, mixed, glow, dgate, hid2, dup, ggate, hid], plan, fit(3 * ff + 2 * vd), me, shards
    )
    early = reduce_owned(*early)
    flat = None
    for seq in range(seqs):
        flat = back(
            seq, length, (q, k, v, gret), cos, sin, seg_col, seg_row, segments, in_last, log_decay,
            sts[seq], dsts[seq], after[seq], flat,
        )
    dq, dk, dv = flat
    plan = [(0, 3, [(0, 0, kd)]), (1, 3, [(0, kd, kd)]), (2, 3, halves(2 * kd))]
    late = weight_grads([dq, dk, dv, hid], plan, fit(2 * kd + vd), me, shards)
    late = reduce_owned(*late)
    grad_input = input_grad(dq, dk, dv, ggate, tok, glow, w_one, w_two, gains)

    gain_grads, total = squares(vd, ff, early, late, w_qk, w_vg, w_gu, norm_gains)
    total = total[0, 0]
    for bit in range(bits_of("shard")):
        total = total + exchange(total, "shard", bit)
    grad_norm = jnp.sqrt(total)
    scale = jnp.minimum(1.0, CLIP / (grad_norm + 1e-06))
    results = update(
        vd, ff, scale.reshape(1), early, late, gain_grads, masters, moments, seconds
    )
    return (
        tokens_out.reshape(tokens.shape),
        grad_input.reshape(tokens.shape),
        *results,
        grad_norm,
    )


def solution(mesh):
    split = P("dp", "shard", None)
    rows, columns = P(None, "shard", None), P(None, "shard")
    group = (rows, rows, columns, rows, columns, columns)
    in_specs = (split, split, P("dp", "shard"), P()) + group * 3
    out_specs = (split, split) + group * 3 + (P(),)
    return jax.shard_map(
        on_device, mesh=mesh, in_specs=in_specs, out_specs=out_specs, check_vma=False
    )
```

```python
import functools
import math

import jax
import jax.numpy as jnp
from jax import lax
from jax.experimental import pallas as pl
from jax.experimental.pallas import tpu as pltpu
from jax.sharding import PartitionSpec as P

H = 2
KD = 256
VD = 432
VP = 512
BLOCK = 512
STEP = 10

EPS = 1e-05
ADAM_EPS = 1e-08
BETA_ONE = 0.9
BETA_TWO = 0.95
MATRIX_RATE = 0.15
GAIN_RATE = 1.0
DECAY_WEIGHT = 0.1
CLIP = 1.0

LOW = jnp.bfloat16
WIDE = jnp.float32
VMEM = pltpu.VMEM
SMEM = pltpu.SMEM
LIMIT = 56 * 1024 * 1024


def dot(a, b):
    return jnp.dot(a, b, preferred_element_type=WIDE)


def dot_nt(a, b):
    return lax.dot_general(a, b, (((1,), (1,)), ((), ())), preferred_element_type=WIDE)


def dot_tn(a, b):
    return lax.dot_general(a, b, (((0,), (0,)), ((), ())), preferred_element_type=WIDE)


def params(**more):
    return pltpu.CompilerParams(vmem_limit_bytes=LIMIT, **more)


def cost(flops, moved):
    return pl.CostEstimate(flops=int(flops), bytes_accessed=int(moved), transcendentals=0)


def smem():
    return pl.BlockSpec(memory_space=SMEM)


def whole(shape):
    return pl.BlockSpec(shape, lambda *at: (0,) * len(shape))


def shape(dims, kind):
    return jax.ShapeDtypeStruct(dims, kind)


def bits_of(axis):
    return (lax.axis_size(axis) - 1).bit_length()


def exchange(value, axis, bit):
    size = lax.axis_size(axis)
    return lax.ppermute(value, axis, [(i, i ^ (1 << bit)) for i in range(size)])


def gather_shards(own):
    held = [(0, own)]
    for bit in reversed(range(bits_of("shard"))):
        held += [(mask | (1 << bit), exchange(part, "shard", bit)) for mask, part in held]
    return held


def add_low(one, two):
    return (one.astype(WIDE) + two.astype(WIDE)).astype(LOW)


class Reduction:
    def __init__(self, keep, send):
        self.keep = keep
        self.near = exchange(send, "shard", 0)

    def cross(self):
        low = add_low(self.keep[1], self.near[1])
        self.far = exchange(low, "shard", 1)
        return low

    def scatter(self):
        own = self.keep[0].astype(WIDE) + self.near[0].astype(WIDE) + self.far.astype(WIDE)
        own = own.astype(LOW)
        copies = lax.axis_size("dp")
        own = own.reshape(copies, own.shape[0] // copies, own.shape[1])
        self.parts = lax.all_to_all(own, "dp", 0, 0)
        return own

    def gather(self):
        part = jnp.sum(self.parts.astype(WIDE), axis=0).astype(LOW)
        spread = jnp.broadcast_to(part[None], self.parts.shape)
        self.full = lax.all_to_all(spread, "dp", 0, 0)
        return spread

    def result(self):
        return self.full.reshape(-1, self.full.shape[2])


class Passing:
    def __init__(self, local, decay, reverse):
        self.reverse = reverse
        self.total = local
        self.entering = jnp.zeros(local.shape, WIDE)
        self.span = decay[:, None, None]
        self.reach = jnp.ones_like(self.span)
        self.bit = 0
        self.got = exchange(local, "shard", 0)

    def turn(self):
        got = self.got.astype(WIDE)
        side = (lax.axis_index("shard") >> self.bit) & 1
        later = (side == 0) if self.reverse else (side == 1)
        self.entering = jnp.where(later, self.entering + self.reach * got, self.entering)
        self.bit += 1
        if self.bit == bits_of("shard"):
            return self.entering.astype(LOW)
        wide = self.total.astype(WIDE)
        self.total = jnp.where(later, wide + self.span * got, got + self.span * wide).astype(LOW)
        self.reach = jnp.where(later, self.reach * self.span, self.reach)
        self.span = self.span * self.span
        self.got = exchange(self.total, "shard", self.bit)
        return self.total


def after(value, *others):
    return lax.optimization_barrier((value, *others))[0]


def assemble_kernel(plan, fills, masks, me_ref, *refs):
    sources, outs = refs[: len(masks)], refs[len(masks) :]
    lanes = sources[0].shape[1]
    for index, row, size in fills:
        outs[index][row : row + size, :] = jnp.zeros((size, outs[index].shape[1]), LOW)
    for mask, source in zip(masks, sources):
        lane = pl.multiple_of(jnp.bitwise_xor(me_ref[0], mask) * lanes, lanes)
        for start, index, row, size in plan:
            outs[index][row : row + size, pl.ds(lane, lanes)] = source[start : start + size, :]


def assemble(held, plan, fills, heights, width, me):
    masks = [mask for mask, part in held]
    parts = [part for mask, part in held]
    return pl.pallas_call(
        functools.partial(assemble_kernel, plan, fills, masks),
        out_shape=[shape((rows, width), LOW) for rows in heights],
        in_specs=[smem()] + [pl.BlockSpec(memory_space=VMEM)] * len(parts),
        out_specs=[pl.BlockSpec(memory_space=VMEM)] * len(heights),
        compiler_params=params(),
        cost_estimate=cost(0, 4 * sum(heights) * width),
    )(me, *parts)


def rotated(flat, cosine, sine):
    half = KD // 2
    parts = []
    for h in range(H):
        u = flat[:, h * KD : h * KD + half]
        w = flat[:, h * KD + half : (h + 1) * KD]
        parts += [u * cosine - w * sine, w * cosine + u * sine]
    return jnp.concatenate(parts, axis=1)


def column(size):
    return lax.broadcasted_iota(jnp.int32, (size, 1), 0).astype(WIDE)


def front_kernel(
    seq, count, decay, seg_s, tok, w, gains, cos, sin, seg, *rest
):
    hid, k, v, kv, out_state, state = rest[-6:]
    c = pl.program_id(0)
    x = tok[...].astype(WIDE)
    r = lax.rsqrt(jnp.mean(x * x, axis=1, keepdims=True) + EPS)
    h1 = (x * r * gains[0:1, :].astype(WIDE)).astype(LOW)
    hid[...] = h1
    kd = H * KD
    key = rotated(dot_nt(h1, w[:kd, :]), cos[...], sin[...]).astype(LOW)
    k[...] = key
    val = dot_nt(h1, w[kd : kd + H * VP, :]).astype(LOW)
    v[...] = val
    first = seg_s[seq, c * BLOCK]
    last = seg_s[seq, c * BLOCK + BLOCK - 1]
    before = seg_s[seq, jnp.maximum(c * BLOCK - 1, 0)]
    here = (seg[...] == last).astype(WIDE)
    joined = jnp.logical_and(jnp.logical_and(first == last, first == before), c > 0)
    for h in range(H):
        a = decay[h]
        kw = jnp.exp(a * (BLOCK - 1.0 - column(BLOCK))) * here
        kk = (key[:, h * KD : (h + 1) * KD].astype(WIDE) * kw).astype(LOW)
        add = dot_tn(kk, val[:, h * VP : (h + 1) * VP])
        kv[h] = add
        factor = jnp.exp(jnp.full((1, 1), a * BLOCK, WIDE))
        total = jnp.where(joined, factor * state[h], 0.0) + add
        state[h] = total
        out_state[h] = total.astype(LOW)


def seq_block(seqs, width, seq, count):
    return pl.BlockSpec((BLOCK, width), lambda c: (seq * count + c, 0))


def front(seq, seqs, length, tokens, seg_col, segments, decay, w, gains, cos, sin, earlier):
    count = length // BLOCK
    rows = seqs * length
    width = tokens.shape[-1]
    block = lambda n: seq_block(seqs, n, seq, count)
    outs = [(width, LOW), (H * KD, LOW), (H * VP, LOW)]
    many = len(outs)
    table = pl.BlockSpec((BLOCK, KD // 2), lambda c: (c, 0))
    inputs = [decay, segments, tokens, w, gains, cos, sin, seg_col]
    specs = [smem(), smem(), block(width), whole(w.shape), whole(gains.shape), table, table, block(1)]
    aliases = {}
    if earlier is not None:
        aliases = {len(inputs) + i: i for i in range(many)}
        inputs += list(earlier)
        specs += [pl.BlockSpec(memory_space=pl.ANY)] * many
    return pl.pallas_call(
        functools.partial(front_kernel, seq, count),
        grid=(count,),
        out_shape=[shape((rows, n), kind) for n, kind in outs]
        + [shape((count, H, KD, VP), WIDE), shape((H, KD, VP), LOW)],
        in_specs=specs,
        out_specs=[block(n) for n, kind in outs]
        + [pl.BlockSpec((None, H, KD, VP), lambda c: (c, 0, 0, 0)), whole((H, KD, VP))],
        scratch_shapes=[VMEM((H, KD, VP), WIDE)],
        input_output_aliases=aliases,
        compiler_params=params(),
        cost_estimate=cost(2 * length * width * w.shape[0], 12 * length * width),
    )(*inputs)


def decay_row(a):
    return jnp.exp(-a * lax.broadcasted_iota(jnp.int32, (1, BLOCK), 1).astype(WIDE))


def mixing(a, top, size, seg, seg_row):
    reach = top + size
    rows = jnp.exp(a * (column(size) + float(top)))
    same = seg[top:reach, :] == seg_row[:, :reach]
    n = lax.broadcasted_iota(jnp.int32, (size, reach), 0) + top
    m = lax.broadcasted_iota(jnp.int32, (size, reach), 1)
    return jnp.where(jnp.logical_and(same, n >= m), rows * decay_row(a)[:, :reach], 0.0)


TILE = 256


def inner_kernel(decay, k, v, hid, w, cos, sin, seg, seg_row, q, intra, gate):
    kd = H * KD
    query = rotated(dot_nt(hid[...], w[:kd, :]), cos[...], sin[...]).astype(LOW)
    q[...] = query
    gate[...] = dot_nt(hid[...], w[kd:, :]).astype(LOW)
    for i in range(BLOCK // TILE):
        top, reach = i * TILE, (i + 1) * TILE
        for h in range(H):
            s = dot_nt(query[top:reach, h * KD : (h + 1) * KD], k[:reach, h * KD : (h + 1) * KD])
            weights = (s * mixing(decay[h], top, TILE, seg, seg_row)).astype(LOW)
            intra[top:reach, h * VP : (h + 1) * VP] = dot(
                weights, v[:reach, h * VP : (h + 1) * VP]
            ).astype(LOW)


def inner(k, v, hid, w, cos, sin, seg_col, seg_row, decay, length):
    rows, width = hid.shape
    count = length // BLOCK
    block = lambda n: pl.BlockSpec((BLOCK, n), lambda t: (t, 0))
    table = pl.BlockSpec((BLOCK, KD // 2), lambda t: (t % count, 0))
    return pl.pallas_call(
        inner_kernel,
        grid=(rows // BLOCK,),
        out_shape=[shape((rows, n), LOW) for n in (H * KD, H * VP, H * VP)],
        in_specs=[
            smem(),
            block(H * KD),
            block(H * VP),
            block(width),
            whole(w.shape),
            table,
            table,
            block(1),
            pl.BlockSpec((None, 1, BLOCK), lambda t: (t, 0, 0)),
        ],
        out_specs=[block(n) for n in (H * KD, H * VP, H * VP)],
        compiler_params=params(),
        cost_estimate=cost(rows * (2 * width * 1536 + 2 * BLOCK * H * VP), 8 * rows * H * VP),
    )(decay, k, v, hid, w, cos, sin, seg_col, seg_row)


def middle_kernel(seq, count, ff, decay, seg_s, in_last, *refs):
    (intra, gate, q, tok, cot, seg, w, gains, entering, kv) = refs[:10]
    (tok_out, hid2, prod, dgate, dup, mixed, glow, ggate, gret, st_out, dst, leave, state) = refs[-13:]
    t = pl.program_id(0)
    per = BLOCK // TILE
    c = t // per
    start = c * BLOCK
    vp = H * VP
    before = jnp.where(c > 0, seg_s[seq, jnp.maximum(start - 1, 0)], in_last[seq])

    @pl.when(t == 0)
    def _():
        state[...] = entering[...].astype(WIDE)
        st_out[0] = entering[...]

    for b in range(1, count):

        @pl.when(t == b * per)
        def _():
            prev = seg_s[seq, (b - 1) * BLOCK - 1] if b > 1 else in_last[seq]
            first = seg_s[seq, (b - 1) * BLOCK]
            last = seg_s[seq, b * BLOCK - 1]
            joined = jnp.logical_and(first == last, first == prev)
            for h in range(H):
                factor = jnp.exp(jnp.full((1, 1), decay[h] * BLOCK, WIDE))
                total = jnp.where(joined, factor * state[h], 0.0) + kv[b - 1, h]
                state[h] = total
                st_out[b, h] = total.astype(LOW)

    here = (seg[...] == before).astype(WIDE)
    within = ((t % per) * TILE).astype(WIDE) + 1.0 + column(TILE)
    lane = lax.broadcasted_iota(jnp.int32, (1, VP), 1)
    real = (lane < VD).astype(WIDE)
    normed, silu, slope, inverse, weighted = [], [], [], [], []
    for h in range(H):
        qw = jnp.exp(decay[h] * within) * here
        qh = q[:, h * KD : (h + 1) * KD]
        weighted.append((qh.astype(WIDE) * qw).astype(LOW))
        cross = dot(qh, st_out[c, h])
        ret = intra[:, h * VP : (h + 1) * VP].astype(WIDE) + qw * cross
        mean = jnp.sum(ret, axis=1, keepdims=True) * (1.0 / VD)
        centered = (ret - mean) * real
        var = jnp.sum(centered * centered, axis=1, keepdims=True) * (1.0 / VD)
        inv = lax.rsqrt(var + 1.0 * KD)
        nh = centered * inv
        g = gate[:, h * VP : (h + 1) * VP].astype(WIDE)
        sg = 0.5 * jnp.tanh(0.5 * g) + 0.5
        sl = g * sg
        mixed[:, h * VP : (h + 1) * VP] = (nh * sl).astype(LOW)
        normed.append(nh)
        silu.append(sl)
        slope.append(sg + sl * (1.0 - sg))
        inverse.append(inv)
    x = tok[...].astype(WIDE)
    w_out = w[:vp, :]
    wg = w[vp : vp + ff, :]
    wu = w[vp + ff : vp + 2 * ff, :]
    wd = w[vp + 2 * ff : vp + 3 * ff, :]
    resid = x + dot(mixed[...], w_out)
    r2 = lax.rsqrt(jnp.mean(resid * resid, axis=1, keepdims=True) + EPS)
    gain = gains[1:2, :].astype(WIDE)
    xhat = resid * r2
    h2 = (xhat * gain).astype(LOW)
    hid2[...] = h2
    gf = dot_nt(h2, wg)
    uf = dot_nt(h2, wu)
    e = jnp.exp(-0.5 * gf * gf)
    d = 1.0 / (1.0 + (0.3275911 * math.sqrt(0.5)) * jnp.abs(gf))
    poly = d * (
        0.254829592
        + d * (-0.284496736 + d * (1.421413741 + d * (-1.453152027 + d * 1.061405429)))
    )
    tail = 0.5 * poly * e
    cdf = jnp.where(gf >= 0.0, 1.0 - tail, tail)
    ge = gf * cdf
    dge = cdf + gf * e * (1.0 / math.sqrt(2.0 * math.pi))
    p = (ge * uf).astype(LOW)
    prod[...] = p
    ct = cot[...]
    tok_out[...] = (resid + dot(p, wd)).astype(LOW)
    gp = dot_nt(ct, wd)
    dg = (gp * uf * dge).astype(LOW)
    du = (gp * ge).astype(LOW)
    dgate[...] = dg
    dup[...] = du
    gh = (dot(dg, wg) + dot(du, wu)) * gain
    inner_product = jnp.mean(gh * xhat, axis=1, keepdims=True)
    gl = (ct.astype(WIDE) + r2 * (gh - xhat * inner_product)).astype(LOW)
    glow[...] = gl
    gm_all = dot_nt(gl, w_out)
    for h in range(H):
        gm = gm_all[:, h * VP : (h + 1) * VP]
        ggate[:, h * VP : (h + 1) * VP] = (gm * normed[h] * slope[h]).astype(LOW)
        gn = gm * silu[h]
        one = jnp.sum(gn, axis=1, keepdims=True) * (1.0 / VD)
        two = jnp.sum(gn * normed[h], axis=1, keepdims=True) * (1.0 / VD)
        gr = (inverse[h] * (gn - one - normed[h] * two) * real).astype(LOW)
        gret[:, h * VP : (h + 1) * VP] = gr
        add = dot_tn(weighted[h], gr)

        @pl.when(t % per == 0)
        def _():
            dst[c, h] = add

        @pl.when(t % per != 0)
        def _():
            dst[c, h] += add

    @pl.when(t == count * per - 1)
    def _():
        for h in range(H):
            total = dst[count - 1, h]
            for b in reversed(range(count - 1)):
                prev = seg_s[seq, b * BLOCK - 1] if b > 0 else in_last[seq]
                first = seg_s[seq, b * BLOCK]
                last = seg_s[seq, (b + 1) * BLOCK - 1]
                joined = jnp.logical_and(first == last, first == prev)
                factor = jnp.exp(jnp.full((1, 1), decay[h] * BLOCK, WIDE))
                total = jnp.where(joined, factor * total, 0.0) + dst[b, h]
            leave[h] = total.astype(LOW)


def middle(seq, seqs, length, ff, data, seg_col, segments, in_last, decay, w, gains, entering, kv, earlier):
    intra, gate, q, tokens, cotangent = data
    rows, width = tokens.shape
    count = length // BLOCK
    tiles = length // TILE
    block = lambda n: pl.BlockSpec((TILE, n), lambda t: (seq * tiles + t, 0))
    vp = H * VP
    outs = [width, width, ff, ff, ff, vp, width, vp, vp]
    many = len(outs)
    inputs = [decay, segments, in_last, intra, gate, q, tokens, cotangent, seg_col, w, gains, entering, kv]
    specs = [smem()] * 3 + [block(vp), block(vp), block(H * KD), block(width), block(width), block(1)]
    specs += [whole(w.shape), whole(gains.shape), whole(entering.shape), whole(kv.shape)]
    aliases = {}
    if earlier is not None:
        aliases = {len(inputs) + i: i for i in range(many)}
        inputs += list(earlier)
        specs += [pl.BlockSpec(memory_space=pl.ANY)] * many
    states = (count, H, KD, VP)
    return pl.pallas_call(
        functools.partial(middle_kernel, seq, count, ff),
        grid=(tiles,),
        out_shape=[shape((rows, n), LOW) for n in outs]
        + [shape(states, LOW), shape(states, WIDE), shape(states[1:], LOW)],
        in_specs=specs,
        out_specs=[block(n) for n in outs] + [whole(states), whole(states), whole(states[1:])],
        scratch_shapes=[VMEM(states[1:], WIDE)],
        input_output_aliases=aliases,
        compiler_params=params(),
        cost_estimate=cost(2 * length * width * (2 * vp + 6 * ff), 30 * length * width),
    )(*inputs)


def weight_kernel(plan, me_ref, *refs):
    count = len({i for pair in plan for i in pair[:2]})
    ins, (keep, send, total) = refs[:count], refs[count:]
    t = pl.program_id(0)
    last = pl.num_programs(0) - 1
    for left, right, cuts in plan:
        a, b = ins[left], ins[right]
        for source, row, size in cuts:
            add = dot_tn(a[:, source : source + size], b[...])

            @pl.when(t == 0)
            def _():
                total[row : row + size, :] = add

            @pl.when(t > 0)
            def _():
                total[row : row + size, :] += add

    @pl.when(t == last)
    def _():
        lanes = keep.shape[2]
        used = max(row + size for left, right, cuts in plan for source, row, size in cuts)
        for part in range(2 * keep.shape[0]):
            target = (keep, send)[part & 1]
            lane = pl.multiple_of(jnp.bitwise_xor(me_ref[0], part) * lanes, lanes)
            target[part >> 1, :used, :] = total[:, pl.ds(lane, lanes)].astype(LOW)
            if used < keep.shape[1]:
                target[part >> 1, used:, :] = jnp.zeros((keep.shape[1] - used, lanes), LOW)


def weight_grads(arrays, plan, rows_out, me, shards):
    rows = arrays[0].shape[0]
    width = 512
    used = max(row + size for left, right, cuts in plan for source, row, size in cuts)
    block = lambda n: pl.BlockSpec((BLOCK, n), lambda t: (t, 0))
    lanes = arrays[plan[0][1]].shape[1] // shards
    return pl.pallas_call(
        functools.partial(weight_kernel, plan),
        grid=(rows // BLOCK,),
        out_shape=[shape((shards // 2, rows_out, lanes), LOW)] * 2,
        in_specs=[smem()] + [block(item.shape[1]) for item in arrays],
        out_specs=[whole((shards // 2, rows_out, lanes))] * 2,
        scratch_shapes=[VMEM((used, lanes * shards), WIDE)],
        compiler_params=params(),
        cost_estimate=cost(2 * rows * used * lanes * shards, 2 * rows * sum(i.shape[1] for i in arrays)),
    )(me, *arrays)


def back_kernel(seq, count, decay, seg_s, in_last, *refs):
    (q, k, v, gret, cos, sin, seg, seg_row, st, dst, after) = refs[:11]
    (dq, dk, dv, state, weights, grads) = refs[-6:]
    t = pl.program_id(0)
    c = count - 1 - t

    @pl.when(t == 0)
    def _():
        state[...] = after[...].astype(WIDE)

    for b in range(1, count):

        @pl.when(c == b - 1)
        def _():
            prev = seg_s[seq, b * BLOCK - 1]
            first = seg_s[seq, b * BLOCK]
            last = seg_s[seq, (b + 1) * BLOCK - 1]
            joined = jnp.logical_and(first == last, first == prev)
            for h in range(H):
                factor = jnp.exp(jnp.full((1, 1), decay[h] * BLOCK, WIDE))
                state[h] = jnp.where(joined, factor * state[h], 0.0) + dst[b, h]

    start = c * BLOCK
    before = jnp.where(c > 0, seg_s[seq, jnp.maximum(start - 1, 0)], in_last[seq])
    final = seg_s[seq, start + BLOCK - 1]
    here = (seg[...] == before).astype(WIDE)
    ends = (seg[...] == final).astype(WIDE)
    place = column(BLOCK)
    dqs, dks = [], []
    for h in range(H):
        a = decay[h]
        qh = q[:, h * KD : (h + 1) * KD]
        kh = k[:, h * KD : (h + 1) * KD]
        vh = v[:, h * VP : (h + 1) * VP]
        gh = gret[:, h * VP : (h + 1) * VP]
        qw = jnp.exp(a * (place + 1.0)) * here
        kw = jnp.exp(a * (BLOCK - 1.0 - place)) * ends
        parts = []
        for i in range(BLOCK // TILE):
            top, reach = i * TILE, (i + 1) * TILE
            mix = mixing(a, top, TILE, seg, seg_row)
            s = dot_nt(qh[top:reach, :], kh[:reach, :])
            weights[top:reach, :reach] = (s * mix).astype(LOW)
            gs = (dot_nt(gh[top:reach, :], vh[:reach, :]) * mix).astype(LOW)
            grads[top:reach, :reach] = gs
            parts.append(dot(gs, kh[:reach, :]))
        late = state[h].astype(LOW)
        dqs.append(jnp.concatenate(parts) + qw * dot_nt(gh, st[c, h]))
        parts, values = [], []
        for i in range(BLOCK // TILE):
            top, reach = i * TILE, (i + 1) * TILE
            parts.append(dot_tn(grads[top:, top:reach], qh[top:, :]))
            values.append(dot_tn(weights[top:, top:reach], gh[top:, :]))
        dks.append(jnp.concatenate(parts) + kw * dot_nt(vh, late))
        dv[:, h * VP : (h + 1) * VP] = (jnp.concatenate(values) + kw * dot(kh, late)).astype(LOW)
    dq[...] = rotated(jnp.concatenate(dqs, axis=1), cos[...], -sin[...]).astype(LOW)
    dk[...] = rotated(jnp.concatenate(dks, axis=1), cos[...], -sin[...]).astype(LOW)


def back(seq, length, data, cos, sin, seg_col, seg_row, segments, in_last, decay, st, dst, after, earlier):
    rows = data[0].shape[0]
    count = length // BLOCK
    block = lambda n: pl.BlockSpec((BLOCK, n), lambda t: (seq * count + count - 1 - t, 0))
    table = pl.BlockSpec((BLOCK, KD // 2), lambda t: (count - 1 - t, 0))
    outs = [H * KD, H * KD, H * VP]
    many = len(outs)
    inputs = [decay, segments, in_last, *data, cos, sin, seg_col, seg_row, st, dst, after]
    specs = [smem()] * 3 + [block(item.shape[1]) for item in data] + [table, table, block(1)]
    specs += [pl.BlockSpec((None, 1, BLOCK), lambda t: (seq * count + count - 1 - t, 0, 0))]
    specs += [whole(st.shape), whole(dst.shape), whole(after.shape)]
    aliases = {}
    if earlier is not None:
        aliases = {len(inputs) + i: i for i in range(many)}
        inputs += list(earlier)
        specs += [pl.BlockSpec(memory_space=pl.ANY)] * many
    return pl.pallas_call(
        functools.partial(back_kernel, seq, count),
        grid=(count,),
        out_shape=[shape((rows, n), LOW) for n in outs],
        in_specs=specs,
        out_specs=[block(n) for n in outs],
        scratch_shapes=[
            VMEM((H, KD, VP), WIDE),
            VMEM((BLOCK, BLOCK), LOW),
            VMEM((BLOCK, BLOCK), LOW),
        ],
        input_output_aliases=aliases,
        compiler_params=params(),
        cost_estimate=cost(length * H * 2 * BLOCK * 3 * (KD + VP), 16 * length * H * VP),
    )(*inputs)


def input_kernel(dq, dk, dv, ggate, tok, glow, w_kv, w_qg, gains, out):
    kd = H * KD
    gh = dot(dq[...], w_qg[:kd, :]) + dot(dk[...], w_kv[:kd, :])
    gh += dot(dv[...], w_kv[kd:, :]) + dot(ggate[...], w_qg[kd:, :])
    x = tok[...].astype(WIDE)
    r = lax.rsqrt(jnp.mean(x * x, axis=1, keepdims=True) + EPS)
    xhat = x * r
    gh = gh * gains[0:1, :].astype(WIDE)
    inner_product = jnp.mean(gh * xhat, axis=1, keepdims=True)
    out[...] = (glow[...].astype(WIDE) + r * (gh - xhat * inner_product)).astype(LOW)


def input_grad(dq, dk, dv, ggate, tokens, glow, w_kv, w_qg, gains):
    rows, width = tokens.shape
    block = lambda item: pl.BlockSpec((BLOCK, item.shape[1]), lambda t: (t, 0))
    return pl.pallas_call(
        input_kernel,
        grid=(rows // BLOCK,),
        out_shape=shape((rows, width), LOW),
        in_specs=[block(item) for item in (dq, dk, dv, ggate, tokens, glow)]
        + [whole(w_kv.shape), whole(w_qg.shape), whole(gains.shape)],
        out_specs=block(tokens),
        compiler_params=params(),
        cost_estimate=cost(2 * rows * width * 2 * w_kv.shape[0], 20 * rows * width),
    )(dq, dk, dv, ggate, tokens, glow, w_kv, w_qg, gains)


def adam_step(master, moment, second, grad, scale, rate, decay_weight):
    clipped = grad * scale
    moment_new = BETA_ONE * moment + (1.0 - BETA_ONE) * clipped
    second_new = BETA_TWO * second + (1.0 - BETA_TWO) * clipped * clipped
    corrected = (
        moment_new
        * (1.0 / (1.0 - BETA_ONE**STEP))
        / (jnp.sqrt(second_new * (1.0 / (1.0 - BETA_TWO**STEP))) + ADAM_EPS)
    )
    return (master - rate * (corrected + decay_weight * master), moment_new, second_new)


def squares_kernel(vd, ff, one, two, three, w_qk, w_vg, w_gu, low_gains, grad_gains, total):
    kd = H * KD

    def rows(source, start, size):
        return source[start : start + size, :].astype(WIDE)

    def product(weight, grad):
        return jnp.sum(weight.astype(LOW).astype(WIDE) * grad, axis=0, keepdims=True)

    sums = []

    def square(item):
        sums.append(jnp.sum(item * item, axis=0, keepdims=True))
        return item

    first = jnp.zeros((1, low_gains.shape[1]), WIDE)
    for i in range(2):
        grad = square(rows(three, i * kd, kd))
        first += jnp.sum(w_qk[i].astype(LOW).astype(WIDE).T * grad, axis=0, keepdims=True)
    first += product(w_vg[0], square(rows(three, 2 * kd, vd)))
    first += product(w_vg[1], square(rows(two, vd, vd)))
    square(rows(two, 0, vd))
    square(rows(one, 0, ff))
    second = product(w_gu[0], square(rows(one, ff, ff)))
    second += product(w_gu[1], square(rows(one, 2 * ff, ff)))
    gains = jnp.concatenate([first, second]) / low_gains[...].astype(LOW).astype(WIDE)
    grad_gains[...] = gains
    sums.append(jnp.sum(gains * gains, axis=0, keepdims=True))
    total[...] = jnp.broadcast_to(jnp.sum(sum(sums), axis=1, keepdims=True), total.shape)


def squares(vd, ff, grads, w_qk, w_vg, w_gu, gains):
    return pl.pallas_call(
        functools.partial(squares_kernel, vd, ff),
        out_shape=[shape(gains.shape, WIDE), shape((8, 128), WIDE)],
        in_specs=[pl.BlockSpec(memory_space=VMEM)] * 7,
        out_specs=[pl.BlockSpec(memory_space=VMEM)] * 2,
        compiler_params=params(),
    )(*grads, w_qk, w_vg, w_gu, gains)


def update_kernel(vd, ff, here, there, one, two, three, gain_grads, *refs):
    ins, outs = refs[:18], refs[18:36]
    norm_out = refs[36]
    kd = H * KD
    norm = jnp.sqrt(here[...] + there[...])
    norm_out[...] = norm
    scale = jnp.minimum(1.0, CLIP / (norm + 1e-06))[0:1, 0:1]

    def step(place, at, grad, rate, decay_weight):
        results = adam_step(
            ins[place][at], ins[6 + place][at], ins[12 + place][at], grad, scale, rate, decay_weight
        )
        for group, result in enumerate(results):
            outs[6 * group + place][at] = result

    def rows(source, start, size):
        return source[start : start + size, :].astype(WIDE)

    step(4, ..., rows(one, 0, ff), MATRIX_RATE, DECAY_WEIGHT)
    step(3, 0, rows(one, ff, ff), MATRIX_RATE, DECAY_WEIGHT)
    step(3, 1, rows(one, 2 * ff, ff), MATRIX_RATE, DECAY_WEIGHT)
    step(2, ..., rows(two, 0, vd), MATRIX_RATE, DECAY_WEIGHT)
    step(1, 1, rows(two, vd, vd), MATRIX_RATE, DECAY_WEIGHT)
    step(1, 0, rows(three, 2 * kd, vd), MATRIX_RATE, DECAY_WEIGHT)
    step(0, 0, rows(three, 0, kd).T, MATRIX_RATE, DECAY_WEIGHT)
    step(0, 1, rows(three, kd, kd).T, MATRIX_RATE, DECAY_WEIGHT)
    step(5, ..., gain_grads[...], GAIN_RATE, 0.0)


def update(vd, ff, here, there, grads, gain_grads, arrays):
    return pl.pallas_call(
        functools.partial(update_kernel, vd, ff),
        out_shape=[shape(item.shape, WIDE) for item in arrays] + [shape(here.shape, WIDE)],
        in_specs=[pl.BlockSpec(memory_space=VMEM)] * 24,
        out_specs=[pl.BlockSpec(memory_space=VMEM)] * 19,
        compiler_params=params(),
    )(here, there, *grads, gain_grads, *arrays)


def on_device(
    tokens,
    cotangent,
    segments,
    log_decay,
    w_qk,
    w_vg,
    w_out,
    w_gu,
    w_down,
    norm_gains,
    *states,
):
    turned = lambda item: jnp.swapaxes(item, 1, 2)
    shards = lax.axis_size("shard")
    me = lax.axis_index("shard").reshape(1)
    seqs, length, width = tokens.shape
    rows = seqs * length
    kd, vd, ff = H * KD, H * VD, w_down.shape[0]
    vp = H * VP
    vg_t, gu_t = turned(w_vg), turned(w_gu)

    low = lambda item: item.astype(LOW)
    first = jnp.concatenate(
        [low(w_qk[1]).T, low(vg_t[0]), jnp.pad(low(norm_gains), ((0, 14), (0, 0)))]
    )
    second = jnp.concatenate([low(w_qk[0]).T, low(vg_t[1])])
    third = jnp.concatenate([low(w_out), low(gu_t[0]), low(gu_t[1]), low(w_down)])
    first_held = gather_shards(first)
    second_held = gather_shards(second)
    third_held = gather_shards(after(third, first_held[1][1]))

    def padded(start, row):
        return [(start + h * VD, 0, row + h * VP, VD) for h in range(H)]

    def fills(row):
        return [(0, row + h * VP + VD, VP - VD) for h in range(H)]

    plan = [(0, 0, 0, kd)] + padded(kd, kd) + [(kd + vd, 1, 0, 16)]
    w_kv, gains = assemble(first_held, plan, fills(kd), [kd + vp, 16], width, after(me, second))
    plan = [(0, 0, 0, kd)] + padded(kd, kd)
    (w_qg,) = assemble(second_held, plan, fills(kd), [kd + vp], width, me)
    plan = padded(0, 0) + [(vd, 0, vp, 3 * ff)]
    (w_rest,) = assemble(third_held, plan, fills(0), [vp + 3 * ff], width, me)

    half_width = KD // 2
    freq_rates = jnp.exp(-math.log(10000.0) * jnp.arange(half_width).astype(WIDE) / half_width)
    positions = (lax.axis_index("shard") * length + jnp.arange(length)).astype(WIDE)
    angles = positions[:, None] * freq_rates[None, :]
    cos, sin = jnp.cos(angles), jnp.sin(angles)

    tok = tokens.reshape(rows, width)
    cot = cotangent.reshape(rows, width)
    seg_col = segments.reshape(rows, 1)
    seg_row = segments.reshape(rows // BLOCK, 1, BLOCK)
    in_last = jnp.where(lax.axis_index("shard") > 0, segments[:, 0], -1)
    span = jnp.exp(log_decay * length)

    flat, kvs, passing = None, [], []
    for seq in range(seqs):
        *flat, kv, leaving = front(
            seq, seqs, length, tok, seg_col, segments, log_decay, w_kv, gains, cos, sin, flat
        )
        kvs.append(kv)
        passing.append(Passing(leaving, span, False))
    hid, k, v = flat
    decay = log_decay
    for item in passing[:-1]:
        decay = after(decay, item.turn())
    q, intra, gate = inner(k, v, hid, w_qg, cos, sin, seg_col, seg_row, decay, length)
    decay = after(decay, passing[-1].turn(), q)
    data = (intra, gate, q, tok, cot)
    flat, sts, dsts, returning = None, [], [], []
    for seq in range(seqs):
        *flat, st, dst, leaving = middle(
            seq, seqs, length, ff, data, seg_col, segments, in_last, decay,
            w_rest, gains, passing[seq].turn(), kvs[seq], flat,
        )
        sts.append(st)
        dsts.append(dst)
        returning.append(Passing(leaving, span, True))
    tokens_out, hid2, prod, dgate, dup, mixed, glow, ggate, gret = flat

    quantum = 16 * lax.axis_size("dp")
    fit = lambda used: used + -used % quantum

    def halves(row):
        return [(h * VP, row + h * VD, VD) for h in range(H)]

    place = me
    for item in returning[:-1]:
        place = after(place, item.turn())
    plan = [(0, 1, [(0, 0, ff)]), (2, 3, [(0, ff, ff)]), (4, 3, [(0, 2 * ff, ff)])]
    one = Reduction(*weight_grads([prod, cot, dgate, hid2, dup], plan, fit(3 * ff), place, shards))
    place = after(place, returning[-1].turn())
    plan = [(0, 1, halves(0)), (2, 3, halves(vd))]
    two = Reduction(*weight_grads([mixed, glow, ggate, hid], plan, fit(2 * vd), place, shards))
    decay = after(decay, one.cross())
    flat = None
    for seq in range(seqs):
        flat = back(
            seq, length, (q, k, v, gret), cos, sin, seg_col, seg_row, segments, in_last, decay,
            sts[seq], dsts[seq], returning[seq].turn(), flat,
        )
        if seq == 0:
            decay = after(decay, two.cross(), flat[0])
    dq, dk, dv = flat
    plan = [(0, 3, [(0, 0, kd)]), (1, 3, [(0, kd, kd)]), (2, 3, halves(2 * kd))]
    place = after(place, one.scatter(), dq)
    three = Reduction(*weight_grads([dq, dk, dv, hid], plan, fit(2 * kd + vd), place, shards))
    two.scatter()
    three.cross()
    grad_input = input_grad(dq, dk, dv, ggate, tok, glow, w_kv, w_qg, gains)
    one.gather()
    three.scatter()
    two.gather()
    three.gather()
    grads = (one.result(), two.result(), three.result())

    gain_grads, total = squares(vd, ff, grads, w_qk, vg_t, gu_t, norm_gains)
    count = bits_of("shard")
    for bit in range(count - 1):
        total = total + exchange(total, "shard", bit)
    arrays = []
    for group in ((w_qk, w_vg, w_out, w_gu, w_down, norm_gains), states[:6], states[6:]):
        arrays += [turned(item) if i in (1, 3) else item for i, item in enumerate(group)]
    *results, norm = update(
        vd, ff, total, exchange(total, "shard", count - 1), grads, gain_grads, arrays
    )
    results = [turned(item) if i % 6 in (1, 3) else item for i, item in enumerate(results)]
    return (
        tokens_out.reshape(tokens.shape),
        grad_input.reshape(tokens.shape),
        *results,
        norm[0, 0],
    )


def solution(mesh):
    split = P("dp", "shard", None)
    rows, columns = P(None, "shard", None), P(None, "shard")
    group = (rows, rows, columns, rows, columns, columns)
    in_specs = (split, split, P("dp", "shard"), P()) + group * 3
    out_specs = (split, split) + group * 3 + (P(),)
    return jax.shard_map(
        on_device, mesh=mesh, in_specs=in_specs, out_specs=out_specs, check_vma=False
    )
```

```python
import functools
import math

import jax
import jax.numpy as jnp
from jax import lax
from jax.experimental import pallas as pl
from jax.experimental.pallas import tpu as pltpu
from jax.sharding import PartitionSpec as P

H = 2
KD = 256
VD = 432
VP = 512
BLOCK = 512
STEP = 10

EPS = 1e-05
ADAM_EPS = 1e-08
BETA_ONE = 0.9
BETA_TWO = 0.95
MATRIX_RATE = 0.15
GAIN_RATE = 1.0
DECAY_WEIGHT = 0.1
CLIP = 1.0

LOW = jnp.bfloat16
WIDE = jnp.float32
VMEM = pltpu.VMEM
SMEM = pltpu.SMEM
LIMIT = 56 * 1024 * 1024


def dot(a, b):
    return jnp.dot(a, b, preferred_element_type=WIDE)


def dot_nt(a, b):
    return lax.dot_general(a, b, (((1,), (1,)), ((), ())), preferred_element_type=WIDE)


def dot_tn(a, b):
    return lax.dot_general(a, b, (((0,), (0,)), ((), ())), preferred_element_type=WIDE)


def params(**more):
    return pltpu.CompilerParams(vmem_limit_bytes=LIMIT, **more)


def cost(flops, moved):
    return pl.CostEstimate(flops=int(flops), bytes_accessed=int(moved), transcendentals=0)


def smem():
    return pl.BlockSpec(memory_space=SMEM)


def whole(shape):
    return pl.BlockSpec(shape, lambda *at: (0,) * len(shape))


def shape(dims, kind):
    return jax.ShapeDtypeStruct(dims, kind)


def bits_of(axis):
    return (lax.axis_size(axis) - 1).bit_length()


def exchange(value, axis, bit):
    size = lax.axis_size(axis)
    return lax.ppermute(value, axis, [(i, i ^ (1 << bit)) for i in range(size)])


def gather_shards(own):
    held = [(0, own)]
    for bit in reversed(range(bits_of("shard"))):
        held += [(mask | (1 << bit), exchange(part, "shard", bit)) for mask, part in held]
    return [(mask, None, part) for mask, part in held]


def gather_halves(own, side, first):
    rows = own.shape[0] // 2
    send = after(lax.dynamic_slice_in_dim(own, side[0] * rows, rows, 0), first)
    here = exchange(send, "shard", 1)
    there = exchange(here, "dp", 0)
    held = [(0, None, own), (1, None, exchange(own, "shard", 0))]
    held += [(2, 0, here), (2, 1, there)]
    held += [(3, 0, exchange(here, "shard", 0)), (3, 1, exchange(there, "shard", 0))]
    return held, send


def add_low(one, two):
    return (one.astype(WIDE) + two.astype(WIDE)).astype(LOW)


def spread(part, copies):
    return jnp.broadcast_to(part[None], (copies, *part.shape))


def summed(parts):
    return jnp.sum(parts.astype(WIDE), axis=0).astype(LOW)


class Reduction:
    def __init__(self, keep, send):
        self.keep = keep
        self.near = exchange(send, "shard", 0)

    def cross(self):
        low = add_low(self.keep[1], self.near[1])
        self.far = exchange(low, "shard", 1)
        return low

    def own(self):
        total = self.keep[0].astype(WIDE) + self.near[0].astype(WIDE) + self.far.astype(WIDE)
        return total.astype(LOW)

    def scatter(self):
        own = self.own()
        copies = lax.axis_size("dp")
        self.parts = lax.all_to_all(own.reshape(copies, -1, own.shape[1]), "dp", 0, 0)
        return own

    def gather(self):
        part = summed(self.parts)
        self.full = lax.all_to_all(spread(part, lax.axis_size("dp")), "dp", 0, 0)
        return part

    def result(self):
        return self.full.reshape(-1, self.full.shape[2])


class Staged(Reduction):
    def groups(self):
        size = lax.axis_size("dp")
        return [list(range(0, size, 2)), list(range(1, size, 2))]

    def halve(self):
        own = self.own()
        self.side = lax.axis_index("dp") & 1
        rows = own.shape[0] // 2
        self.mine = lax.dynamic_slice_in_dim(own, self.side * rows, rows, 0)
        send = lax.dynamic_slice_in_dim(own, (1 - self.side) * rows, rows, 0)
        self.other = exchange(send, "dp", 0)
        return send

    def scatter(self):
        half = add_low(self.mine, self.other)
        self.copies = lax.axis_size("dp") // 2
        half = half.reshape(self.copies, -1, half.shape[1])
        self.parts = lax.all_to_all(half, "dp", 0, 0, axis_index_groups=self.groups())
        return half

    def gather(self):
        part = summed(self.parts)
        half = lax.all_to_all(spread(part, self.copies), "dp", 0, 0, axis_index_groups=self.groups())
        self.half = half.reshape(-1, half.shape[2])
        return part

    def double(self):
        self.other = exchange(self.half, "dp", 0)

    def result(self):
        here, there = self.half, self.other
        return jnp.where(
            self.side == 0, jnp.concatenate([here, there]), jnp.concatenate([there, here])
        )


class Passing:
    def __init__(self, local, reverse):
        self.local = local
        near = [(0, 1), (2, 3)]
        steps = [near, [(1, 2)], [(2, 3)]]
        if reverse:
            steps = [[(3 - a, 3 - b) for a, b in step] for step in steps]
        self.steps = steps
        self.got = [lax.ppermute(local, "shard", steps[0])]

    def turn(self, decay, length):
        total = combine(decay, length, self.local, self.got[0])
        self.got.append(lax.ppermute(total, "shard", self.steps[1]))
        self.got.append(lax.ppermute(self.got[1], "shard", self.steps[2]))
        return total


def entering(decay, length, h, got):
    factor = jnp.exp(jnp.full((1, 1), decay[h] * length, WIDE))
    wide = [item[h].astype(WIDE) for item in got]
    return wide[0] + wide[1] + factor * wide[2]


def after(value, *others):
    return lax.optimization_barrier((value, *others))[0]


def combine_kernel(length, decay, local, got, out):
    for h in range(H):
        factor = jnp.exp(jnp.full((1, 1), decay[h] * length, WIDE))
        out[h] = (local[h].astype(WIDE) + factor * got[h].astype(WIDE)).astype(LOW)


def combine(decay, length, local, got):
    return pl.pallas_call(
        functools.partial(combine_kernel, length),
        out_shape=shape(local.shape, LOW),
        in_specs=[smem()] + [pl.BlockSpec(memory_space=VMEM)] * 2,
        out_specs=pl.BlockSpec(memory_space=VMEM),
        compiler_params=params(),
        cost_estimate=cost(local.size, 6 * local.size),
    )(decay, local, got)


def assemble_kernel(plan, fills, sources_of, me_ref, side_ref, *refs):
    sources, outs = refs[: len(sources_of)], refs[len(sources_of) :]
    lanes = sources[0].shape[1]
    for index, row, size in fills:
        outs[index][row : row + size, :] = jnp.zeros((size, outs[index].shape[1]), LOW)

    def place(source, lane, low, high):
        for start, index, row, size in plan:
            begin, end = max(start, low), min(start + size, high)
            if begin < end:
                to = row + begin - start
                outs[index][to : to + end - begin, pl.ds(lane, lanes)] = source[
                    begin - low : end - low, :
                ]

    for (mask, half), source in zip(sources_of, sources):
        lane = pl.multiple_of(jnp.bitwise_xor(me_ref[0], mask) * lanes, lanes)
        rows = source.shape[0]
        if half is None:
            place(source, lane, 0, rows)
            continue
        for side in range(2):

            @pl.when(side_ref[0] == side)
            def _():
                low = (side ^ half) * rows
                place(source, lane, low, low + rows)


def assemble(held, plan, fills, heights, width, me, side):
    sources_of = [(mask, half) for mask, half, part in held]
    parts = [part for mask, half, part in held]
    return pl.pallas_call(
        functools.partial(assemble_kernel, plan, fills, sources_of),
        out_shape=[shape((rows, width), LOW) for rows in heights],
        in_specs=[smem()] * 2 + [pl.BlockSpec(memory_space=VMEM)] * len(parts),
        out_specs=[pl.BlockSpec(memory_space=VMEM)] * len(heights),
        compiler_params=params(),
        cost_estimate=cost(0, 4 * sum(heights) * width),
    )(me, side, *parts)


def rotated(flat, cosine, sine):
    half = KD // 2
    parts = []
    for h in range(H):
        u = flat[:, h * KD : h * KD + half]
        w = flat[:, h * KD + half : (h + 1) * KD]
        parts += [u * cosine - w * sine, w * cosine + u * sine]
    return jnp.concatenate(parts, axis=1)


def column(size):
    return lax.broadcasted_iota(jnp.int32, (size, 1), 0).astype(WIDE)


def front_kernel(
    seq, count, decay, seg_s, tok, w, gains, cos, sin, seg, *rest
):
    hid, k, v, kv, out_state, state = rest[-6:]
    c = pl.program_id(0)
    x = tok[...].astype(WIDE)
    r = lax.rsqrt(jnp.mean(x * x, axis=1, keepdims=True) + EPS)
    h1 = (x * r * gains[0:1, :].astype(WIDE)).astype(LOW)
    hid[...] = h1
    kd = H * KD
    key = rotated(dot_nt(h1, w[:kd, :]), cos[...], sin[...]).astype(LOW)
    k[...] = key
    val = dot_nt(h1, w[kd : kd + H * VP, :]).astype(LOW)
    v[...] = val
    first = seg_s[seq, c * BLOCK]
    last = seg_s[seq, c * BLOCK + BLOCK - 1]
    before = seg_s[seq, jnp.maximum(c * BLOCK - 1, 0)]
    here = (seg[...] == last).astype(WIDE)
    joined = jnp.logical_and(jnp.logical_and(first == last, first == before), c > 0)
    for h in range(H):
        a = decay[h]
        kw = jnp.exp(a * (BLOCK - 1.0 - column(BLOCK))) * here
        kk = (key[:, h * KD : (h + 1) * KD].astype(WIDE) * kw).astype(LOW)
        add = dot_tn(kk, val[:, h * VP : (h + 1) * VP])
        kv[h] = add
        factor = jnp.exp(jnp.full((1, 1), a * BLOCK, WIDE))
        total = jnp.where(joined, factor * state[h], 0.0) + add
        state[h] = total
        out_state[h] = total.astype(LOW)


def seq_block(seqs, width, seq, count):
    return pl.BlockSpec((BLOCK, width), lambda c: (seq * count + c, 0))


def front(seq, seqs, length, tokens, seg_col, segments, decay, w, gains, cos, sin, earlier):
    count = length // BLOCK
    rows = seqs * length
    width = tokens.shape[-1]
    block = lambda n: seq_block(seqs, n, seq, count)
    outs = [(width, LOW), (H * KD, LOW), (H * VP, LOW)]
    many = len(outs)
    table = pl.BlockSpec((BLOCK, KD // 2), lambda c: (c, 0))
    inputs = [decay, segments, tokens, w, gains, cos, sin, seg_col]
    specs = [smem(), smem(), block(width), whole(w.shape), whole(gains.shape), table, table, block(1)]
    aliases = {}
    if earlier is not None:
        aliases = {len(inputs) + i: i for i in range(many)}
        inputs += list(earlier)
        specs += [pl.BlockSpec(memory_space=pl.ANY)] * many
    return pl.pallas_call(
        functools.partial(front_kernel, seq, count),
        grid=(count,),
        out_shape=[shape((rows, n), kind) for n, kind in outs]
        + [shape((count, H, KD, VP), WIDE), shape((H, KD, VP), LOW)],
        in_specs=specs,
        out_specs=[block(n) for n, kind in outs]
        + [pl.BlockSpec((None, H, KD, VP), lambda c: (c, 0, 0, 0)), whole((H, KD, VP))],
        scratch_shapes=[VMEM((H, KD, VP), WIDE)],
        input_output_aliases=aliases,
        compiler_params=params(),
        cost_estimate=cost(2 * length * width * w.shape[0], 12 * length * width),
    )(*inputs)


def decay_row(a):
    return jnp.exp(-a * lax.broadcasted_iota(jnp.int32, (1, BLOCK), 1).astype(WIDE))


def mixing(a, top, size, seg, seg_row):
    reach = top + size
    rows = jnp.exp(a * (column(size) + float(top)))
    same = seg[top:reach, :] == seg_row[:, :reach]
    n = lax.broadcasted_iota(jnp.int32, (size, reach), 0) + top
    m = lax.broadcasted_iota(jnp.int32, (size, reach), 1)
    return jnp.where(jnp.logical_and(same, n >= m), rows * decay_row(a)[:, :reach], 0.0)


TILE = 256


def inner_kernel(decay, k, v, hid, w, cos, sin, seg, seg_row, q, intra, gate):
    kd = H * KD
    query = rotated(dot_nt(hid[...], w[:kd, :]), cos[...], sin[...]).astype(LOW)
    q[...] = query
    gate[...] = dot_nt(hid[...], w[kd:, :]).astype(LOW)
    for i in range(BLOCK // TILE):
        top, reach = i * TILE, (i + 1) * TILE
        for h in range(H):
            s = dot_nt(query[top:reach, h * KD : (h + 1) * KD], k[:reach, h * KD : (h + 1) * KD])
            weights = (s * mixing(decay[h], top, TILE, seg, seg_row)).astype(LOW)
            intra[top:reach, h * VP : (h + 1) * VP] = dot(
                weights, v[:reach, h * VP : (h + 1) * VP]
            ).astype(LOW)


def inner(k, v, hid, w, cos, sin, seg_col, seg_row, decay, length):
    rows, width = hid.shape
    count = length // BLOCK
    block = lambda n: pl.BlockSpec((BLOCK, n), lambda t: (t, 0))
    table = pl.BlockSpec((BLOCK, KD // 2), lambda t: (t % count, 0))
    return pl.pallas_call(
        inner_kernel,
        grid=(rows // BLOCK,),
        out_shape=[shape((rows, n), LOW) for n in (H * KD, H * VP, H * VP)],
        in_specs=[
            smem(),
            block(H * KD),
            block(H * VP),
            block(width),
            whole(w.shape),
            table,
            table,
            block(1),
            pl.BlockSpec((None, 1, BLOCK), lambda t: (t, 0, 0)),
        ],
        out_specs=[block(n) for n in (H * KD, H * VP, H * VP)],
        compiler_params=params(),
        cost_estimate=cost(rows * (2 * width * 1536 + 2 * BLOCK * H * VP), 8 * rows * H * VP),
    )(decay, k, v, hid, w, cos, sin, seg_col, seg_row)


def middle_kernel(seq, count, ff, decay, seg_s, in_last, *refs):
    (intra, gate, q, tok, cot, seg, w, gains, *got, kv) = refs[:12]
    (tok_out, hid2, prod, dgate, dup, mixed, glow, ggate, gret, st_out, dst, leave, state) = refs[-13:]
    t = pl.program_id(0)
    per = BLOCK // TILE
    c = t // per
    start = c * BLOCK
    vp = H * VP
    before = jnp.where(c > 0, seg_s[seq, jnp.maximum(start - 1, 0)], in_last[seq])

    @pl.when(t == 0)
    def _():
        for h in range(H):
            total = entering(decay, count * BLOCK, h, got)
            state[h] = total
            st_out[0, h] = total.astype(LOW)

    for b in range(1, count):

        @pl.when(t == b * per)
        def _():
            prev = seg_s[seq, (b - 1) * BLOCK - 1] if b > 1 else in_last[seq]
            first = seg_s[seq, (b - 1) * BLOCK]
            last = seg_s[seq, b * BLOCK - 1]
            joined = jnp.logical_and(first == last, first == prev)
            for h in range(H):
                factor = jnp.exp(jnp.full((1, 1), decay[h] * BLOCK, WIDE))
                total = jnp.where(joined, factor * state[h], 0.0) + kv[b - 1, h]
                state[h] = total
                st_out[b, h] = total.astype(LOW)

    here = (seg[...] == before).astype(WIDE)
    within = ((t % per) * TILE).astype(WIDE) + 1.0 + column(TILE)
    lane = lax.broadcasted_iota(jnp.int32, (1, VP), 1)
    real = (lane < VD).astype(WIDE)
    normed, silu, slope, inverse, weighted = [], [], [], [], []
    for h in range(H):
        qw = jnp.exp(decay[h] * within) * here
        qh = q[:, h * KD : (h + 1) * KD]
        weighted.append((qh.astype(WIDE) * qw).astype(LOW))
        cross = dot(qh, st_out[c, h])
        ret = intra[:, h * VP : (h + 1) * VP].astype(WIDE) + qw * cross
        mean = jnp.sum(ret, axis=1, keepdims=True) * (1.0 / VD)
        centered = (ret - mean) * real
        var = jnp.sum(centered * centered, axis=1, keepdims=True) * (1.0 / VD)
        inv = lax.rsqrt(var + 1.0 * KD)
        nh = centered * inv
        g = gate[:, h * VP : (h + 1) * VP].astype(WIDE)
        sg = 0.5 * jnp.tanh(0.5 * g) + 0.5
        sl = g * sg
        mixed[:, h * VP : (h + 1) * VP] = (nh * sl).astype(LOW)
        normed.append(nh)
        silu.append(sl)
        slope.append(sg + sl * (1.0 - sg))
        inverse.append(inv)
    x = tok[...].astype(WIDE)
    w_out = w[:vp, :]
    wg = w[vp : vp + ff, :]
    wu = w[vp + ff : vp + 2 * ff, :]
    wd = w[vp + 2 * ff : vp + 3 * ff, :]
    resid = x + dot(mixed[...], w_out)
    r2 = lax.rsqrt(jnp.mean(resid * resid, axis=1, keepdims=True) + EPS)
    gain = gains[1:2, :].astype(WIDE)
    xhat = resid * r2
    h2 = (xhat * gain).astype(LOW)
    hid2[...] = h2
    gf = dot_nt(h2, wg)
    uf = dot_nt(h2, wu)
    e = jnp.exp(-0.5 * gf * gf)
    d = 1.0 / (1.0 + (0.3275911 * math.sqrt(0.5)) * jnp.abs(gf))
    poly = d * (
        0.254829592
        + d * (-0.284496736 + d * (1.421413741 + d * (-1.453152027 + d * 1.061405429)))
    )
    tail = 0.5 * poly * e
    cdf = jnp.where(gf >= 0.0, 1.0 - tail, tail)
    ge = gf * cdf
    dge = cdf + gf * e * (1.0 / math.sqrt(2.0 * math.pi))
    p = (ge * uf).astype(LOW)
    prod[...] = p
    ct = cot[...]
    tok_out[...] = (resid + dot(p, wd)).astype(LOW)
    gp = dot_nt(ct, wd)
    dg = (gp * uf * dge).astype(LOW)
    du = (gp * ge).astype(LOW)
    dgate[...] = dg
    dup[...] = du
    gh = (dot(dg, wg) + dot(du, wu)) * gain
    inner_product = jnp.mean(gh * xhat, axis=1, keepdims=True)
    gl = (ct.astype(WIDE) + r2 * (gh - xhat * inner_product)).astype(LOW)
    glow[...] = gl
    gm_all = dot_nt(gl, w_out)
    for h in range(H):
        gm = gm_all[:, h * VP : (h + 1) * VP]
        ggate[:, h * VP : (h + 1) * VP] = (gm * normed[h] * slope[h]).astype(LOW)
        gn = gm * silu[h]
        one = jnp.sum(gn, axis=1, keepdims=True) * (1.0 / VD)
        two = jnp.sum(gn * normed[h], axis=1, keepdims=True) * (1.0 / VD)
        gr = (inverse[h] * (gn - one - normed[h] * two) * real).astype(LOW)
        gret[:, h * VP : (h + 1) * VP] = gr
        add = dot_tn(weighted[h], gr)

        @pl.when(t % per == 0)
        def _():
            dst[c, h] = add

        @pl.when(t % per != 0)
        def _():
            dst[c, h] += add

    @pl.when(t == count * per - 1)
    def _():
        for h in range(H):
            total = dst[count - 1, h]
            for b in reversed(range(count - 1)):
                prev = seg_s[seq, b * BLOCK - 1] if b > 0 else in_last[seq]
                first = seg_s[seq, b * BLOCK]
                last = seg_s[seq, (b + 1) * BLOCK - 1]
                joined = jnp.logical_and(first == last, first == prev)
                factor = jnp.exp(jnp.full((1, 1), decay[h] * BLOCK, WIDE))
                total = jnp.where(joined, factor * total, 0.0) + dst[b, h]
            leave[h] = total.astype(LOW)


def middle(seq, seqs, length, ff, data, seg_col, segments, in_last, decay, w, gains, got, kv, earlier):
    intra, gate, q, tokens, cotangent = data
    rows, width = tokens.shape
    count = length // BLOCK
    tiles = length // TILE
    block = lambda n: pl.BlockSpec((TILE, n), lambda t: (seq * tiles + t, 0))
    vp = H * VP
    outs = [width, width, ff, ff, ff, vp, width, vp, vp]
    many = len(outs)
    inputs = [decay, segments, in_last, intra, gate, q, tokens, cotangent, seg_col, w, gains, *got, kv]
    specs = [smem()] * 3 + [block(vp), block(vp), block(H * KD), block(width), block(width), block(1)]
    specs += [whole(w.shape), whole(gains.shape), *(whole(item.shape) for item in got), whole(kv.shape)]
    aliases = {}
    if earlier is not None:
        aliases = {len(inputs) + i: i for i in range(many)}
        inputs += list(earlier)
        specs += [pl.BlockSpec(memory_space=pl.ANY)] * many
    states = (count, H, KD, VP)
    return pl.pallas_call(
        functools.partial(middle_kernel, seq, count, ff),
        grid=(tiles,),
        out_shape=[shape((rows, n), LOW) for n in outs]
        + [shape(states, LOW), shape(states, WIDE), shape(states[1:], LOW)],
        in_specs=specs,
        out_specs=[block(n) for n in outs] + [whole(states), whole(states), whole(states[1:])],
        scratch_shapes=[VMEM(states[1:], WIDE)],
        input_output_aliases=aliases,
        compiler_params=params(),
        cost_estimate=cost(2 * length * width * (2 * vp + 6 * ff), 30 * length * width),
    )(*inputs)


def weight_kernel(plan, me_ref, *refs):
    count = len({i for pair in plan for i in pair[:2]})
    ins, (keep, send, total) = refs[:count], refs[count:]
    t = pl.program_id(0)
    last = pl.num_programs(0) - 1
    for left, right, cuts in plan:
        a, b = ins[left], ins[right]
        for source, row, size in cuts:
            add = dot_tn(a[:, source : source + size], b[...])

            @pl.when(t == 0)
            def _():
                total[row : row + size, :] = add

            @pl.when(t > 0)
            def _():
                total[row : row + size, :] += add

    @pl.when(t == last)
    def _():
        lanes = keep.shape[2]
        used = max(row + size for left, right, cuts in plan for source, row, size in cuts)
        for part in range(2 * keep.shape[0]):
            target = (keep, send)[part & 1]
            lane = pl.multiple_of(jnp.bitwise_xor(me_ref[0], part) * lanes, lanes)
            target[part >> 1, :used, :] = total[:, pl.ds(lane, lanes)].astype(LOW)
            if used < keep.shape[1]:
                target[part >> 1, used:, :] = jnp.zeros((keep.shape[1] - used, lanes), LOW)


def weight_grads(arrays, plan, rows_out, me, shards):
    rows = arrays[0].shape[0]
    width = 512
    used = max(row + size for left, right, cuts in plan for source, row, size in cuts)
    block = lambda n: pl.BlockSpec((BLOCK, n), lambda t: (t, 0))
    lanes = arrays[plan[0][1]].shape[1] // shards
    return pl.pallas_call(
        functools.partial(weight_kernel, plan),
        grid=(rows // BLOCK,),
        out_shape=[shape((shards // 2, rows_out, lanes), LOW)] * 2,
        in_specs=[smem()] + [block(item.shape[1]) for item in arrays],
        out_specs=[whole((shards // 2, rows_out, lanes))] * 2,
        scratch_shapes=[VMEM((used, lanes * shards), WIDE)],
        compiler_params=params(),
        cost_estimate=cost(2 * rows * used * lanes * shards, 2 * rows * sum(i.shape[1] for i in arrays)),
    )(me, *arrays)


def back_kernel(seq, count, decay, seg_s, in_last, *refs):
    (q, k, v, gret, cos, sin, seg, seg_row, st, dst, *got) = refs[:13]
    (dq, dk, dv, state, weights, grads) = refs[-6:]
    t = pl.program_id(0)
    c = count - 1 - t

    @pl.when(t == 0)
    def _():
        for h in range(H):
            state[h] = entering(decay, count * BLOCK, h, got)

    for b in range(1, count):

        @pl.when(c == b - 1)
        def _():
            prev = seg_s[seq, b * BLOCK - 1]
            first = seg_s[seq, b * BLOCK]
            last = seg_s[seq, (b + 1) * BLOCK - 1]
            joined = jnp.logical_and(first == last, first == prev)
            for h in range(H):
                factor = jnp.exp(jnp.full((1, 1), decay[h] * BLOCK, WIDE))
                state[h] = jnp.where(joined, factor * state[h], 0.0) + dst[b, h]

    start = c * BLOCK
    before = jnp.where(c > 0, seg_s[seq, jnp.maximum(start - 1, 0)], in_last[seq])
    final = seg_s[seq, start + BLOCK - 1]
    here = (seg[...] == before).astype(WIDE)
    ends = (seg[...] == final).astype(WIDE)
    place = column(BLOCK)
    dqs, dks = [], []
    for h in range(H):
        a = decay[h]
        qh = q[:, h * KD : (h + 1) * KD]
        kh = k[:, h * KD : (h + 1) * KD]
        vh = v[:, h * VP : (h + 1) * VP]
        gh = gret[:, h * VP : (h + 1) * VP]
        qw = jnp.exp(a * (place + 1.0)) * here
        kw = jnp.exp(a * (BLOCK - 1.0 - place)) * ends
        parts = []
        for i in range(BLOCK // TILE):
            top, reach = i * TILE, (i + 1) * TILE
            mix = mixing(a, top, TILE, seg, seg_row)
            s = dot_nt(qh[top:reach, :], kh[:reach, :])
            weights[top:reach, :reach] = (s * mix).astype(LOW)
            gs = (dot_nt(gh[top:reach, :], vh[:reach, :]) * mix).astype(LOW)
            grads[top:reach, :reach] = gs
            parts.append(dot(gs, kh[:reach, :]))
        late = state[h].astype(LOW)
        dqs.append(jnp.concatenate(parts) + qw * dot_nt(gh, st[c, h]))
        parts, values = [], []
        for i in range(BLOCK // TILE):
            top, reach = i * TILE, (i + 1) * TILE
            parts.append(dot_tn(grads[top:, top:reach], qh[top:, :]))
            values.append(dot_tn(weights[top:, top:reach], gh[top:, :]))
        dks.append(jnp.concatenate(parts) + kw * dot_nt(vh, late))
        dv[:, h * VP : (h + 1) * VP] = (jnp.concatenate(values) + kw * dot(kh, late)).astype(LOW)
    dq[...] = rotated(jnp.concatenate(dqs, axis=1), cos[...], -sin[...]).astype(LOW)
    dk[...] = rotated(jnp.concatenate(dks, axis=1), cos[...], -sin[...]).astype(LOW)


def back(seq, length, data, cos, sin, seg_col, seg_row, segments, in_last, decay, st, dst, got, earlier):
    rows = data[0].shape[0]
    count = length // BLOCK
    block = lambda n: pl.BlockSpec((BLOCK, n), lambda t: (seq * count + count - 1 - t, 0))
    table = pl.BlockSpec((BLOCK, KD // 2), lambda t: (count - 1 - t, 0))
    outs = [H * KD, H * KD, H * VP]
    many = len(outs)
    inputs = [decay, segments, in_last, *data, cos, sin, seg_col, seg_row, st, dst, *got]
    specs = [smem()] * 3 + [block(item.shape[1]) for item in data] + [table, table, block(1)]
    specs += [pl.BlockSpec((None, 1, BLOCK), lambda t: (seq * count + count - 1 - t, 0, 0))]
    specs += [whole(st.shape), whole(dst.shape), *(whole(item.shape) for item in got)]
    aliases = {}
    if earlier is not None:
        aliases = {len(inputs) + i: i for i in range(many)}
        inputs += list(earlier)
        specs += [pl.BlockSpec(memory_space=pl.ANY)] * many
    return pl.pallas_call(
        functools.partial(back_kernel, seq, count),
        grid=(count,),
        out_shape=[shape((rows, n), LOW) for n in outs],
        in_specs=specs,
        out_specs=[block(n) for n in outs],
        scratch_shapes=[
            VMEM((H, KD, VP), WIDE),
            VMEM((BLOCK, BLOCK), LOW),
            VMEM((BLOCK, BLOCK), LOW),
        ],
        input_output_aliases=aliases,
        compiler_params=params(),
        cost_estimate=cost(length * H * 2 * BLOCK * 3 * (KD + VP), 16 * length * H * VP),
    )(*inputs)


def input_kernel(dq, dk, dv, ggate, tok, glow, w_kv, w_qg, gains, out):
    kd = H * KD
    gh = dot(dq[...], w_qg[:kd, :]) + dot(dk[...], w_kv[:kd, :])
    gh += dot(dv[...], w_kv[kd:, :]) + dot(ggate[...], w_qg[kd:, :])
    x = tok[...].astype(WIDE)
    r = lax.rsqrt(jnp.mean(x * x, axis=1, keepdims=True) + EPS)
    xhat = x * r
    gh = gh * gains[0:1, :].astype(WIDE)
    inner_product = jnp.mean(gh * xhat, axis=1, keepdims=True)
    out[...] = (glow[...].astype(WIDE) + r * (gh - xhat * inner_product)).astype(LOW)


def input_grad(dq, dk, dv, ggate, tokens, glow, w_kv, w_qg, gains):
    rows, width = tokens.shape
    block = lambda item: pl.BlockSpec((BLOCK, item.shape[1]), lambda t: (t, 0))
    return pl.pallas_call(
        input_kernel,
        grid=(rows // BLOCK,),
        out_shape=shape((rows, width), LOW),
        in_specs=[block(item) for item in (dq, dk, dv, ggate, tokens, glow)]
        + [whole(w_kv.shape), whole(w_qg.shape), whole(gains.shape)],
        out_specs=block(tokens),
        compiler_params=params(),
        cost_estimate=cost(2 * rows * width * 2 * w_kv.shape[0], 20 * rows * width),
    )(dq, dk, dv, ggate, tokens, glow, w_kv, w_qg, gains)


def adam_step(master, moment, second, grad, scale, rate, decay_weight):
    clipped = grad * scale
    moment_new = BETA_ONE * moment + (1.0 - BETA_ONE) * clipped
    second_new = BETA_TWO * second + (1.0 - BETA_TWO) * clipped * clipped
    corrected = (
        moment_new
        * (1.0 / (1.0 - BETA_ONE**STEP))
        / (jnp.sqrt(second_new * (1.0 / (1.0 - BETA_TWO**STEP))) + ADAM_EPS)
    )
    return (master - rate * (corrected + decay_weight * master), moment_new, second_new)


def squares_kernel(vd, ff, one, two, three, w_qk, w_vg, w_gu, low_gains, grad_gains, total):
    kd = H * KD

    def rows(source, start, size):
        return source[start : start + size, :].astype(WIDE)

    def product(weight, grad):
        return jnp.sum(weight.astype(LOW).astype(WIDE) * grad, axis=0, keepdims=True)

    sums = []

    def square(item):
        sums.append(jnp.sum(item * item, axis=0, keepdims=True))
        return item

    first = jnp.zeros((1, low_gains.shape[1]), WIDE)
    for i in range(2):
        grad = square(rows(three, i * kd, kd))
        first += jnp.sum(w_qk[i].astype(LOW).astype(WIDE).T * grad, axis=0, keepdims=True)
    first += product(w_vg[0], square(rows(three, 2 * kd, vd)))
    first += product(w_vg[1], square(rows(two, vd, vd)))
    square(rows(two, 0, vd))
    square(rows(one, 0, ff))
    second = product(w_gu[0], square(rows(one, ff, ff)))
    second += product(w_gu[1], square(rows(one, 2 * ff, ff)))
    gains = jnp.concatenate([first, second]) / low_gains[...].astype(LOW).astype(WIDE)
    grad_gains[...] = gains
    sums.append(jnp.sum(gains * gains, axis=0, keepdims=True))
    total[...] = jnp.broadcast_to(jnp.sum(sum(sums), axis=1, keepdims=True), total.shape)


def squares(vd, ff, grads, w_qk, w_vg, w_gu, gains):
    return pl.pallas_call(
        functools.partial(squares_kernel, vd, ff),
        out_shape=[shape(gains.shape, WIDE), shape((8, 128), WIDE)],
        in_specs=[pl.BlockSpec(memory_space=VMEM)] * 7,
        out_specs=[pl.BlockSpec(memory_space=VMEM)] * 2,
        compiler_params=params(),
    )(*grads, w_qk, w_vg, w_gu, gains)


def update_kernel(vd, ff, here, there, one, two, three, gain_grads, *refs):
    ins, outs = refs[:18], refs[18:36]
    norm_out = refs[36]
    kd = H * KD
    norm = jnp.sqrt(here[...] + there[...])
    norm_out[...] = norm
    scale = jnp.minimum(1.0, CLIP / (norm + 1e-06))[0:1, 0:1]

    def step(place, at, grad, rate, decay_weight):
        results = adam_step(
            ins[place][at], ins[6 + place][at], ins[12 + place][at], grad, scale, rate, decay_weight
        )
        for group, result in enumerate(results):
            outs[6 * group + place][at] = result

    def rows(source, start, size):
        return source[start : start + size, :].astype(WIDE)

    step(4, ..., rows(one, 0, ff), MATRIX_RATE, DECAY_WEIGHT)
    step(3, 0, rows(one, ff, ff), MATRIX_RATE, DECAY_WEIGHT)
    step(3, 1, rows(one, 2 * ff, ff), MATRIX_RATE, DECAY_WEIGHT)
    step(2, ..., rows(two, 0, vd), MATRIX_RATE, DECAY_WEIGHT)
    step(1, 1, rows(two, vd, vd), MATRIX_RATE, DECAY_WEIGHT)
    step(1, 0, rows(three, 2 * kd, vd), MATRIX_RATE, DECAY_WEIGHT)
    step(0, 0, rows(three, 0, kd).T, MATRIX_RATE, DECAY_WEIGHT)
    step(0, 1, rows(three, kd, kd).T, MATRIX_RATE, DECAY_WEIGHT)
    step(5, ..., gain_grads[...], GAIN_RATE, 0.0)


def update(vd, ff, here, there, grads, gain_grads, arrays):
    return pl.pallas_call(
        functools.partial(update_kernel, vd, ff),
        out_shape=[shape(item.shape, WIDE) for item in arrays] + [shape(here.shape, WIDE)],
        in_specs=[pl.BlockSpec(memory_space=VMEM)] * 24,
        out_specs=[pl.BlockSpec(memory_space=VMEM)] * 19,
        compiler_params=params(),
    )(here, there, *grads, gain_grads, *arrays)


def on_device(
    tokens,
    cotangent,
    segments,
    log_decay,
    w_qk,
    w_vg,
    w_out,
    w_gu,
    w_down,
    norm_gains,
    *states,
):
    turned = lambda item: jnp.swapaxes(item, 1, 2)
    shards = lax.axis_size("shard")
    me = lax.axis_index("shard").reshape(1)
    seqs, length, width = tokens.shape
    rows = seqs * length
    kd, vd, ff = H * KD, H * VD, w_down.shape[0]
    vp = H * VP
    vg_t, gu_t = turned(w_vg), turned(w_gu)

    low = lambda item: item.astype(LOW)
    first = jnp.concatenate(
        [low(w_qk[1]).T, low(vg_t[0]), jnp.pad(low(norm_gains), ((0, 14), (0, 0)))]
    )
    second = jnp.concatenate([low(w_qk[0]).T, low(vg_t[1])])
    third = jnp.concatenate([low(w_out), low(gu_t[0]), low(gu_t[1]), low(w_down)])
    side = (lax.axis_index("dp") & 1).reshape(1)
    first_held = gather_shards(first)
    second_held = gather_shards(second)
    third_held, sent = gather_halves(third, side, second_held[1][2])

    def padded(start, row):
        return [(start + h * VD, 0, row + h * VP, VD) for h in range(H)]

    def fills(row):
        return [(0, row + h * VP + VD, VP - VD) for h in range(H)]

    half_width = KD // 2
    freq_rates = jnp.exp(-math.log(10000.0) * jnp.arange(half_width).astype(WIDE) / half_width)
    positions = (lax.axis_index("shard") * length + jnp.arange(length)).astype(WIDE)
    angles = positions[:, None] * freq_rates[None, :]
    cos, sin = jnp.cos(angles), jnp.sin(angles)

    tok = tokens.reshape(rows, width)
    cot = cotangent.reshape(rows, width)
    seg_col = segments.reshape(rows, 1)
    seg_row = segments.reshape(rows // BLOCK, 1, BLOCK)
    in_last = jnp.where(lax.axis_index("shard") > 0, segments[:, 0], -1)
    decay = log_decay

    def tick(*done):
        nonlocal decay, me, gains
        decay, me, gains = lax.optimization_barrier((decay, me, gains, *done))[:3]

    plan = [(0, 0, 0, kd)] + padded(kd, kd) + [(kd + vd, 1, 0, 16)]
    w_kv, gains = assemble(first_held, plan, fills(kd), [kd + vp, 16], width, me, side)
    tick(sent)
    flat, kvs, passing = None, [], []
    for seq in range(seqs):
        *flat, kv, leaving = front(
            seq, seqs, length, tok, seg_col, segments, decay, w_kv, gains, cos, sin, flat
        )
        kvs.append(kv)
        passing.append(Passing(leaving, False))
        tick(leaving)
    hid, k, v = flat
    for item in passing[:-1]:
        tick(item.turn(decay, length))
    plan = [(0, 0, 0, kd)] + padded(kd, kd)
    (w_qg,) = assemble(second_held, plan, fills(kd), [kd + vp], width, me, side)
    tick(w_qg)
    tick(passing[-1].turn(decay, length))
    q, intra, gate = inner(k, v, hid, w_qg, cos, sin, seg_col, seg_row, decay, length)
    tick(q)
    plan = padded(0, 0) + [(vd, 0, vp, 3 * ff)]
    (w_rest,) = assemble(third_held, plan, fills(0), [vp + 3 * ff], width, me, side)
    tick(w_rest)
    data = (intra, gate, q, tok, cot)
    flat, sts, dsts, returning = None, [], [], []
    for seq in range(seqs):
        *flat, st, dst, leaving = middle(
            seq, seqs, length, ff, data, seg_col, segments, in_last, decay,
            w_rest, gains, passing[seq].got, kvs[seq], flat,
        )
        sts.append(st)
        dsts.append(dst)
        returning.append(Passing(leaving, True))
        tick(leaving)
    tokens_out, hid2, prod, dgate, dup, mixed, glow, ggate, gret = flat

    quantum = 16 * lax.axis_size("dp")
    fit = lambda used: used + -used % quantum

    def halves(row):
        return [(h * VP, row + h * VD, VD) for h in range(H)]

    for item in returning[:-1]:
        tick(item.turn(decay, length))
    plan = [(0, 1, [(0, 0, ff)]), (2, 3, [(0, ff, ff)]), (4, 3, [(0, 2 * ff, ff)])]
    made = weight_grads([prod, cot, dgate, hid2, dup], plan, fit(3 * ff), me, shards)
    one = Staged(*made)
    tick(made[0])
    tick(returning[-1].turn(decay, length))
    plan = [(0, 1, halves(0)), (2, 3, halves(vd))]
    made = weight_grads([mixed, glow, ggate, hid], plan, fit(2 * vd), me, shards)
    two = Staged(*made)
    tick(made[0])
    tick(one.cross())
    flat = None
    for seq in range(seqs):
        flat = back(
            seq, length, (q, k, v, gret), cos, sin, seg_col, seg_row, segments, in_last, decay,
            sts[seq], dsts[seq], returning[seq].got, flat,
        )
        tick(flat[0])
        if seq == 0:
            tick(two.cross())
    dq, dk, dv = flat
    tick(one.halve())
    plan = [(0, 3, [(0, 0, kd)]), (1, 3, [(0, kd, kd)]), (2, 3, halves(2 * kd))]
    made = weight_grads([dq, dk, dv, hid], plan, fit(2 * kd + vd), me, shards)
    three = Reduction(*made)
    tick(made[0])
    tick(one.scatter())
    tick(two.halve())
    tick(three.cross())
    grad_input = input_grad(dq, dk, dv, ggate, tok, glow, w_kv, w_qg, gains)
    one.gather()
    two.scatter()
    three.scatter()
    two.gather()
    one.double()
    three.gather()
    two.double()
    grads = (one.result(), two.result(), three.result())

    gain_grads, total = squares(vd, ff, grads, w_qk, vg_t, gu_t, norm_gains)
    count = bits_of("shard")
    for bit in range(count - 1):
        total = total + exchange(total, "shard", bit)
    arrays = []
    for group in ((w_qk, w_vg, w_out, w_gu, w_down, norm_gains), states[:6], states[6:]):
        arrays += [turned(item) if i in (1, 3) else item for i, item in enumerate(group)]
    *results, norm = update(
        vd, ff, total, exchange(total, "shard", count - 1), grads, gain_grads, arrays
    )
    results = [turned(item) if i % 6 in (1, 3) else item for i, item in enumerate(results)]
    return (
        tokens_out.reshape(tokens.shape),
        grad_input.reshape(tokens.shape),
        *results,
        norm[0, 0],
    )


def solution(mesh):
    split = P("dp", "shard", None)
    rows, columns = P(None, "shard", None), P(None, "shard")
    group = (rows, rows, columns, rows, columns, columns)
    in_specs = (split, split, P("dp", "shard"), P()) + group * 3
    out_specs = (split, split) + group * 3 + (P(),)
    return jax.shard_map(
        on_device, mesh=mesh, in_specs=in_specs, out_specs=out_specs, check_vma=False
    )
```

```python
import functools
import math

import jax
import jax.numpy as jnp
from jax import lax
from jax.experimental import pallas as pl
from jax.experimental.pallas import tpu as pltpu
from jax.sharding import PartitionSpec as P

H = 2
KD = 256
VD = 432
VP = 512
BLOCK = 512
STEP = 10

EPS = 1e-05
ADAM_EPS = 1e-08
BETA_ONE = 0.9
BETA_TWO = 0.95
MATRIX_RATE = 0.15
GAIN_RATE = 1.0
DECAY_WEIGHT = 0.1
CLIP = 1.0

LOW = jnp.bfloat16
WIDE = jnp.float32
VMEM = pltpu.VMEM
SMEM = pltpu.SMEM
LIMIT = 56 * 1024 * 1024


def dot(a, b):
    return jnp.dot(a, b, preferred_element_type=WIDE)


def dot_nt(a, b):
    return lax.dot_general(a, b, (((1,), (1,)), ((), ())), preferred_element_type=WIDE)


def dot_tn(a, b):
    return lax.dot_general(a, b, (((0,), (0,)), ((), ())), preferred_element_type=WIDE)


def params(**more):
    return pltpu.CompilerParams(vmem_limit_bytes=LIMIT, **more)


def cost(flops, moved):
    return pl.CostEstimate(flops=int(flops), bytes_accessed=int(moved), transcendentals=0)


def smem():
    return pl.BlockSpec(memory_space=SMEM)


def whole(shape):
    return pl.BlockSpec(shape, lambda *at: (0,) * len(shape))


def shape(dims, kind):
    return jax.ShapeDtypeStruct(dims, kind)


def bits_of(axis):
    return (lax.axis_size(axis) - 1).bit_length()


def exchange(value, axis, bit):
    size = lax.axis_size(axis)
    return lax.ppermute(value, axis, [(i, i ^ (1 << bit)) for i in range(size)])


def gather_shards(own):
    held = [(0, own)]
    for bit in reversed(range(bits_of("shard"))):
        held += [(mask | (1 << bit), exchange(part, "shard", bit)) for mask, part in held]
    return [(mask, None, part) for mask, part in held]


def gather_halves(own, side, first):
    rows = own.shape[0] // 2
    send = after(lax.dynamic_slice_in_dim(own, side[0] * rows, rows, 0), first)
    here = exchange(send, "shard", 1)
    there = exchange(here, "dp", 0)
    held = [(0, None, own), (1, None, exchange(own, "shard", 0))]
    held += [(2, 0, here), (2, 1, there)]
    held += [(3, 0, exchange(here, "shard", 0)), (3, 1, exchange(there, "shard", 0))]
    return held, send


def add_low(one, two):
    return (one.astype(WIDE) + two.astype(WIDE)).astype(LOW)


def spread(part, copies):
    return jnp.broadcast_to(part[None], (copies, *part.shape))


def summed(parts):
    return jnp.sum(parts.astype(WIDE), axis=0).astype(LOW)


class Reduction:
    def __init__(self, keep, send):
        self.keep = keep
        self.near = exchange(send, "shard", 0)

    def cross(self):
        low = add_low(self.keep[1], self.near[1])
        self.far = exchange(low, "shard", 1)
        return low

    def own(self):
        total = self.keep[0].astype(WIDE) + self.near[0].astype(WIDE) + self.far.astype(WIDE)
        return total.astype(LOW)

    def scatter(self):
        own = self.own()
        copies = lax.axis_size("dp")
        self.parts = lax.all_to_all(own.reshape(copies, -1, own.shape[1]), "dp", 0, 0)
        return own

    def gather(self):
        part = summed(self.parts)
        self.full = lax.all_to_all(spread(part, lax.axis_size("dp")), "dp", 0, 0)
        return part

    def result(self):
        return self.full.reshape(-1, self.full.shape[2])


class Staged(Reduction):
    def groups(self):
        size = lax.axis_size("dp")
        return [list(range(0, size, 2)), list(range(1, size, 2))]

    def halve(self):
        own = self.own()
        self.side = lax.axis_index("dp") & 1
        rows = own.shape[0] // 2
        self.mine = lax.dynamic_slice_in_dim(own, self.side * rows, rows, 0)
        send = lax.dynamic_slice_in_dim(own, (1 - self.side) * rows, rows, 0)
        self.other = exchange(send, "dp", 0)
        return send

    def scatter(self):
        half = add_low(self.mine, self.other)
        self.copies = lax.axis_size("dp") // 2
        half = half.reshape(self.copies, -1, half.shape[1])
        self.parts = lax.all_to_all(half, "dp", 0, 0, axis_index_groups=self.groups())
        return half

    def gather(self):
        part = summed(self.parts)
        half = lax.all_to_all(spread(part, self.copies), "dp", 0, 0, axis_index_groups=self.groups())
        self.half = half.reshape(-1, half.shape[2])
        return part

    def double(self):
        self.other = exchange(self.half, "dp", 0)

    def result(self):
        here, there = self.half, self.other
        return jnp.where(
            self.side == 0, jnp.concatenate([here, there]), jnp.concatenate([there, here])
        )


class Passing:
    def __init__(self, local, reverse):
        self.local = local
        near = [(0, 1), (2, 3)]
        steps = [near, [(1, 2)], [(2, 3)]]
        if reverse:
            steps = [[(3 - a, 3 - b) for a, b in step] for step in steps]
        self.steps = steps
        self.got = [lax.ppermute(local, "shard", steps[0])]

    def turn(self, decay, length):
        total = combine(decay, length, self.local, self.got[0])
        self.got.append(lax.ppermute(total, "shard", self.steps[1]))
        self.got.append(lax.ppermute(self.got[1], "shard", self.steps[2]))
        return total


def entering(decay, length, h, got):
    factor = jnp.exp(jnp.full((1, 1), decay[h] * length, WIDE))
    wide = [item[h].astype(WIDE) for item in got]
    return wide[0] + wide[1] + factor * wide[2]


def after(value, *others):
    return lax.optimization_barrier((value, *others))[0]


def combine_kernel(length, decay, local, got, out):
    for h in range(H):
        factor = jnp.exp(jnp.full((1, 1), decay[h] * length, WIDE))
        out[h] = (local[h].astype(WIDE) + factor * got[h].astype(WIDE)).astype(LOW)


def combine(decay, length, local, got):
    return pl.pallas_call(
        functools.partial(combine_kernel, length),
        out_shape=shape(local.shape, LOW),
        in_specs=[smem()] + [pl.BlockSpec(memory_space=VMEM)] * 2,
        out_specs=pl.BlockSpec(memory_space=VMEM),
        compiler_params=params(),
        cost_estimate=cost(local.size, 6 * local.size),
    )(decay, local, got)


def assemble_kernel(plan, fills, sources_of, me_ref, side_ref, *refs):
    sources, outs = refs[: len(sources_of)], refs[len(sources_of) :]
    lanes = sources[0].shape[1]
    for index, row, size in fills:
        outs[index][row : row + size, :] = jnp.zeros((size, outs[index].shape[1]), LOW)

    def place(source, lane, low, high):
        for start, index, row, size in plan:
            begin, end = max(start, low), min(start + size, high)
            if begin < end:
                to = row + begin - start
                outs[index][to : to + end - begin, pl.ds(lane, lanes)] = source[
                    begin - low : end - low, :
                ]

    for (mask, half), source in zip(sources_of, sources):
        lane = pl.multiple_of(jnp.bitwise_xor(me_ref[0], mask) * lanes, lanes)
        rows = source.shape[0]
        if half is None:
            place(source, lane, 0, rows)
            continue
        for side in range(2):

            @pl.when(side_ref[0] == side)
            def _():
                low = (side ^ half) * rows
                place(source, lane, low, low + rows)


def assemble(held, plan, fills, heights, width, me, side):
    sources_of = [(mask, half) for mask, half, part in held]
    parts = [part for mask, half, part in held]
    return pl.pallas_call(
        functools.partial(assemble_kernel, plan, fills, sources_of),
        out_shape=[shape((rows, width), LOW) for rows in heights],
        in_specs=[smem()] * 2 + [pl.BlockSpec(memory_space=VMEM)] * len(parts),
        out_specs=[pl.BlockSpec(memory_space=VMEM)] * len(heights),
        compiler_params=params(),
        cost_estimate=cost(0, 4 * sum(heights) * width),
    )(me, side, *parts)


def rotated(flat, cosine, sine):
    half = KD // 2
    parts = []
    for h in range(H):
        u = flat[:, h * KD : h * KD + half]
        w = flat[:, h * KD + half : (h + 1) * KD]
        parts += [u * cosine - w * sine, w * cosine + u * sine]
    return jnp.concatenate(parts, axis=1)


def column(size):
    return lax.broadcasted_iota(jnp.int32, (size, 1), 0).astype(WIDE)


def front_kernel(
    seq, count, decay, seg_s, tok, w, gains, cos, sin, seg, *rest
):
    hid, k, v, kv, out_state, state = rest[-6:]
    c = pl.program_id(0)
    x = tok[...].astype(WIDE)
    r = lax.rsqrt(jnp.mean(x * x, axis=1, keepdims=True) + EPS)
    h1 = (x * r * gains[0:1, :].astype(WIDE)).astype(LOW)
    hid[...] = h1
    kd = H * KD
    key = rotated(dot_nt(h1, w[:kd, :]), cos[...], sin[...]).astype(LOW)
    k[...] = key
    val = dot_nt(h1, w[kd : kd + H * VP, :]).astype(LOW)
    v[...] = val
    first = seg_s[seq, c * BLOCK]
    last = seg_s[seq, c * BLOCK + BLOCK - 1]
    before = seg_s[seq, jnp.maximum(c * BLOCK - 1, 0)]
    here = (seg[...] == last).astype(WIDE)
    joined = jnp.logical_and(jnp.logical_and(first == last, first == before), c > 0)
    for h in range(H):
        a = decay[h]
        kw = jnp.exp(a * (BLOCK - 1.0 - column(BLOCK))) * here
        kk = (key[:, h * KD : (h + 1) * KD].astype(WIDE) * kw).astype(LOW)
        add = dot_tn(kk, val[:, h * VP : (h + 1) * VP])
        kv[h] = add
        factor = jnp.exp(jnp.full((1, 1), a * BLOCK, WIDE))
        total = jnp.where(joined, factor * state[h], 0.0) + add
        state[h] = total
        out_state[h] = total.astype(LOW)


def seq_block(seqs, width, seq, count):
    return pl.BlockSpec((BLOCK, width), lambda c: (seq * count + c, 0))


def front(seq, seqs, length, tokens, seg_col, segments, decay, w, gains, cos, sin, earlier):
    count = length // BLOCK
    rows = seqs * length
    width = tokens.shape[-1]
    block = lambda n: seq_block(seqs, n, seq, count)
    outs = [(width, LOW), (H * KD, LOW), (H * VP, LOW)]
    many = len(outs)
    table = pl.BlockSpec((BLOCK, KD // 2), lambda c: (c, 0))
    inputs = [decay, segments, tokens, w, gains, cos, sin, seg_col]
    specs = [smem(), smem(), block(width), whole(w.shape), whole(gains.shape), table, table, block(1)]
    aliases = {}
    if earlier is not None:
        aliases = {len(inputs) + i: i for i in range(many)}
        inputs += list(earlier)
        specs += [pl.BlockSpec(memory_space=pl.ANY)] * many
    return pl.pallas_call(
        functools.partial(front_kernel, seq, count),
        grid=(count,),
        out_shape=[shape((rows, n), kind) for n, kind in outs]
        + [shape((count, H, KD, VP), WIDE), shape((H, KD, VP), LOW)],
        in_specs=specs,
        out_specs=[block(n) for n, kind in outs]
        + [pl.BlockSpec((None, H, KD, VP), lambda c: (c, 0, 0, 0)), whole((H, KD, VP))],
        scratch_shapes=[VMEM((H, KD, VP), WIDE)],
        input_output_aliases=aliases,
        compiler_params=params(),
        cost_estimate=cost(2 * length * width * w.shape[0], 12 * length * width),
    )(*inputs)


def decay_row(a):
    return jnp.exp(-a * lax.broadcasted_iota(jnp.int32, (1, BLOCK), 1).astype(WIDE))


def mixing(a, top, size, seg, seg_row):
    reach = top + size
    rows = jnp.exp(a * (column(size) + float(top)))
    same = seg[top:reach, :] == seg_row[:, :reach]
    n = lax.broadcasted_iota(jnp.int32, (size, reach), 0) + top
    m = lax.broadcasted_iota(jnp.int32, (size, reach), 1)
    return jnp.where(jnp.logical_and(same, n >= m), rows * decay_row(a)[:, :reach], 0.0)


TILE = 256


def inner_kernel(decay, k, v, hid, w, cos, sin, seg, seg_row, q, intra, gate):
    kd = H * KD
    query = rotated(dot_nt(hid[...], w[:kd, :]), cos[...], sin[...]).astype(LOW)
    q[...] = query
    gate[...] = dot_nt(hid[...], w[kd:, :]).astype(LOW)
    for i in range(BLOCK // TILE):
        top, reach = i * TILE, (i + 1) * TILE
        for h in range(H):
            s = dot_nt(query[top:reach, h * KD : (h + 1) * KD], k[:reach, h * KD : (h + 1) * KD])
            weights = (s * mixing(decay[h], top, TILE, seg, seg_row)).astype(LOW)
            intra[top:reach, h * VP : (h + 1) * VP] = dot(
                weights, v[:reach, h * VP : (h + 1) * VP]
            ).astype(LOW)


def inner(k, v, hid, w, cos, sin, seg_col, seg_row, decay, length):
    rows, width = hid.shape
    count = length // BLOCK
    block = lambda n: pl.BlockSpec((BLOCK, n), lambda t: (t, 0))
    table = pl.BlockSpec((BLOCK, KD // 2), lambda t: (t % count, 0))
    return pl.pallas_call(
        inner_kernel,
        grid=(rows // BLOCK,),
        out_shape=[shape((rows, n), LOW) for n in (H * KD, H * VP, H * VP)],
        in_specs=[
            smem(),
            block(H * KD),
            block(H * VP),
            block(width),
            whole(w.shape),
            table,
            table,
            block(1),
            pl.BlockSpec((None, 1, BLOCK), lambda t: (t, 0, 0)),
        ],
        out_specs=[block(n) for n in (H * KD, H * VP, H * VP)],
        compiler_params=params(),
        cost_estimate=cost(rows * (2 * width * 1536 + 2 * BLOCK * H * VP), 8 * rows * H * VP),
    )(decay, k, v, hid, w, cos, sin, seg_col, seg_row)


CHUNK = 16


def interleaved(first, second):
    steps = [((i + 0.5) / len(first), 0, step) for i, step in enumerate(first)]
    steps += [((i + 0.5) / len(second), 1, step) for i, step in enumerate(second)]
    for place, which, step in sorted(steps, key=lambda item: item[:2]):
        step()


def pieces(width, size=256):
    return [(start, min(start + size, width)) for start in range(0, width, size)]


def across(narrow, width):
    return jnp.concatenate([narrow] * (width // 128), axis=1)


def middle_kernel(seq, count, ff, decay, seg_s, in_last, *refs):
    (intra, gate, q, tok, cot, seg, w, gains, *got, kv) = refs[:12]
    outs, scratch = refs[-25:-13], refs[-13:]
    (tok_out, hid2, prod, dgate, dup, mixed, glow, ggate, gret, st_out, dst, leave) = outs
    (state, now, queries, factors, ret_s, norm_s, silu_s, slope_s, inv_s, res_s, ff_s, low_s, sums) = scratch
    c = pl.program_id(0)
    start = c * BLOCK
    vp = H * VP
    width = tok.shape[1]
    before = jnp.where(c > 0, seg_s[seq, jnp.maximum(start - 1, 0)], in_last[seq])

    @pl.when(c == 0)
    def _():
        for h in range(H):
            total = entering(decay, count * BLOCK, h, got)
            state[h] = total
            now[h] = total.astype(LOW)

    for b in range(1, count):

        @pl.when(c == b)
        def _():
            prev = seg_s[seq, (b - 1) * BLOCK - 1] if b > 1 else in_last[seq]
            joined = jnp.logical_and(
                seg_s[seq, (b - 1) * BLOCK] == seg_s[seq, b * BLOCK - 1],
                seg_s[seq, (b - 1) * BLOCK] == prev,
            )
            for h in range(H):
                factor = jnp.exp(jnp.full((1, 1), decay[h] * BLOCK, WIDE))
                total = jnp.where(joined, factor * state[h], 0.0) + kv[b - 1, h]
                state[h] = total
                now[h] = total.astype(LOW)

    st_out[...] = now[...]
    here = (seg[...] == before).astype(WIDE)
    for h in range(H):
        qw = jnp.exp(decay[h] * (column(BLOCK) + 1.0)) * here
        factors[h] = jnp.broadcast_to(qw, (BLOCK, 128))

    w_out = (0, vp)
    w_gate = (vp, vp + ff)
    w_up = (vp + ff, vp + 2 * ff)
    w_down = (vp + 2 * ff, vp + 3 * ff)
    gain = gains[1:2, :].astype(WIDE)

    def phases(top):
        rs = pl.ds(top, TILE)
        lists = []

        def add(steps):
            lists.append(steps)

        def chunks():
            return [pl.ds(row, CHUNK) for row in range(top, top + TILE, CHUNK)]

        def cross(h, lo, hi):
            ret_s[rs, h * VP + lo : h * VP + hi] = dot(
                q[rs, h * KD : (h + 1) * KD], now[h, :, lo:hi]
            )

        add([functools.partial(cross, h, *piece) for h in range(H) for piece in pieces(VP)])

        def gated(h, r):
            hv = slice(h * VP, (h + 1) * VP)
            hk = slice(h * KD, (h + 1) * KD)
            qw = factors[h, r, :]
            queries[r, hk] = (q[r, hk].astype(WIDE) * across(qw, KD)).astype(LOW)
            ret = intra[r, hv].astype(WIDE) + across(qw, VP) * ret_s[r, hv]
            mean = jnp.sum(ret, axis=1, keepdims=True) * (1.0 / VD)
            centered = ret - mean
            square = jnp.sum(centered * centered, axis=1, keepdims=True)
            var = (square - (VP - VD) * (mean * mean)) * (1.0 / VD)
            inv = lax.rsqrt(var + 1.0 * KD)
            nh = centered * inv
            g = gate[r, hv].astype(WIDE)
            sg = 0.5 * jnp.tanh(0.5 * g) + 0.5
            sl = g * sg
            mixed[r, hv] = (nh * sl).astype(LOW)
            norm_s[r, hv] = nh
            silu_s[r, hv] = sl
            slope_s[r, hv] = nh * (sg + sl * (1.0 - sg))
            inv_s[h, r, :] = jnp.broadcast_to(inv, (CHUNK, 128))

        add([functools.partial(gated, h, r) for r in chunks() for h in range(H)])

        def project(lo, hi):
            res_s[rs, lo:hi] = dot(mixed[rs, :], w[w_out[0] : w_out[1], lo:hi])

        add([functools.partial(project, *piece) for piece in pieces(width)])

        def norm(r):
            resid = tok[r, :].astype(WIDE) + res_s[r, :]
            r2 = lax.rsqrt(jnp.mean(resid * resid, axis=1, keepdims=True) + EPS)
            res_s[r, :] = resid
            hid2[r, :] = (resid * r2 * gain).astype(LOW)
            inv_s[H, r, :] = jnp.broadcast_to(r2, (CHUNK, 128))

        add([functools.partial(norm, r) for r in chunks()])

        def forward(place, source, at, lo, hi):
            ff_s[place, rs, lo:hi] = dot_nt(source[rs, :], w[at[0] + lo : at[0] + hi, :])

        add(
            [
                functools.partial(forward, place, source, at, *piece)
                for piece in pieces(ff)
                for place, source, at in ((0, hid2, w_gate), (1, hid2, w_up), (2, cot, w_down))
            ]
        )

        def gelu(r, lo, hi):
            gf, uf, gp = ff_s[0, r, lo:hi], ff_s[1, r, lo:hi], ff_s[2, r, lo:hi]
            e = jnp.exp(-0.5 * (gf * gf))
            d = 1.0 / (1.0 + (0.3275911 * math.sqrt(0.5)) * jnp.abs(gf))
            poly = d * (
                0.5 * 0.254829592
                + d
                * (
                    0.5 * -0.284496736
                    + d * (0.5 * 1.421413741 + d * (0.5 * -1.453152027 + d * (0.5 * 1.061405429)))
                )
            )
            tail = poly * e
            cdf = jnp.where(gf >= 0.0, 1.0 - tail, tail)
            ge = gf * cdf
            dge = cdf + gf * (e * (1.0 / math.sqrt(2.0 * math.pi)))
            prod[r, lo:hi] = (ge * uf).astype(LOW)
            dgate[r, lo:hi] = (gp * uf * dge).astype(LOW)
            dup[r, lo:hi] = (gp * ge).astype(LOW)

        add([functools.partial(gelu, r, *piece) for r in chunks() for piece in pieces(ff, 512)])

        def down(lo, hi):
            low_s[0, rs, lo:hi] = dot(prod[rs, :], w[w_down[0] : w_down[1], lo:hi])

        def hidden(lo, hi):
            low_s[1, rs, lo:hi] = dot(dgate[rs, :], w[w_gate[0] : w_gate[1], lo:hi]) + dot(
                dup[rs, :], w[w_up[0] : w_up[1], lo:hi]
            )

        add([functools.partial(step, *piece) for piece in pieces(width) for step in (down, hidden)])

        def residual(r):
            resid = res_s[r, :]
            r2 = across(inv_s[H, r, :], width)
            tok_out[r, :] = (resid + low_s[0, r, :]).astype(LOW)
            gh = low_s[1, r, :] * gain
            xhat = resid * r2
            inner_product = jnp.mean(gh * xhat, axis=1, keepdims=True)
            glow[r, :] = (cot[r, :].astype(WIDE) + r2 * (gh - xhat * inner_product)).astype(LOW)

        add([functools.partial(residual, r) for r in chunks()])

        def mix_back(lo, hi):
            ret_s[rs, lo:hi] = dot_nt(glow[rs, :], w[w_out[0] + lo : w_out[0] + hi, :])

        add([functools.partial(mix_back, *piece) for piece in pieces(vp)])

        def gated_back(h, r):
            hv = slice(h * VP, (h + 1) * VP)
            gm = ret_s[r, hv]
            nh = norm_s[r, hv]
            ggate[r, hv] = (gm * slope_s[r, hv]).astype(LOW)
            gn = gm * silu_s[r, hv]
            one = jnp.sum(gn, axis=1, keepdims=True) * (1.0 / VD)
            two = jnp.sum(gn * nh, axis=1, keepdims=True) * (1.0 / VD)
            gret[r, hv] = (across(inv_s[h, r, :], VP) * (gn - one - nh * two)).astype(LOW)

        add([functools.partial(gated_back, h, r) for r in chunks() for h in range(H)])
        return lists

    first, second = phases(0), phases(TILE)
    for k in range(len(first) + 1):
        interleaved(first[k] if k < len(first) else [], second[k - 1] if k else [])
    for h in range(H):
        add = dot_tn(queries[:, h * KD : (h + 1) * KD], gret[:, h * VP : (h + 1) * VP])
        dst[h] = add
        sums[c, h] = add

    @pl.when(c == count - 1)
    def _():
        for h in range(H):
            total = sums[count - 1, h]
            for b in reversed(range(count - 1)):
                prev = seg_s[seq, b * BLOCK - 1] if b > 0 else in_last[seq]
                joined = jnp.logical_and(
                    seg_s[seq, b * BLOCK] == seg_s[seq, (b + 1) * BLOCK - 1],
                    seg_s[seq, b * BLOCK] == prev,
                )
                factor = jnp.exp(jnp.full((1, 1), decay[h] * BLOCK, WIDE))
                total = jnp.where(joined, factor * total, 0.0) + sums[b, h]
            leave[h] = total.astype(LOW)


def middle(seq, seqs, length, ff, data, seg_col, segments, in_last, decay, w, gains, got, kv, earlier):
    intra, gate, q, tokens, cotangent = data
    rows, width = tokens.shape
    count = length // BLOCK
    block = lambda n: seq_block(seqs, n, seq, count)
    vp = H * VP
    outs = [width, width, ff, ff, ff, vp, width, vp, vp]
    many = len(outs)
    inputs = [decay, segments, in_last, intra, gate, q, tokens, cotangent, seg_col, w, gains, *got, kv]
    specs = [smem()] * 3 + [block(vp), block(vp), block(H * KD), block(width), block(width), block(1)]
    specs += [whole(w.shape), whole(gains.shape), *(whole(item.shape) for item in got), whole(kv.shape)]
    aliases = {}
    if earlier is not None:
        aliases = {len(inputs) + i: i for i in range(many)}
        inputs += list(earlier)
        specs += [pl.BlockSpec(memory_space=pl.ANY)] * many
    one = (H, KD, VP)
    states = (count, *one)
    each = pl.BlockSpec((None, *one), lambda c: (c, 0, 0, 0))
    return pl.pallas_call(
        functools.partial(middle_kernel, seq, count, ff),
        grid=(count,),
        out_shape=[shape((rows, n), LOW) for n in outs]
        + [shape(states, LOW), shape(states, WIDE), shape(one, LOW)],
        in_specs=specs,
        out_specs=[block(n) for n in outs] + [each, each, whole(one)],
        scratch_shapes=[
            VMEM(one, WIDE),
            VMEM(one, LOW),
            VMEM((BLOCK, H * KD), LOW),
            VMEM((H, BLOCK, 128), WIDE),
            VMEM((BLOCK, vp), WIDE),
            VMEM((BLOCK, vp), WIDE),
            VMEM((BLOCK, vp), WIDE),
            VMEM((BLOCK, vp), WIDE),
            VMEM((H + 1, BLOCK, 128), WIDE),
            VMEM((BLOCK, width), WIDE),
            VMEM((3, BLOCK, ff), WIDE),
            VMEM((2, BLOCK, width), WIDE),
            VMEM(states, WIDE),
        ],
        input_output_aliases=aliases,
        compiler_params=params(),
        cost_estimate=cost(2 * length * width * (2 * vp + 6 * ff), 30 * length * width),
    )(*inputs)


def weight_kernel(plan, me_ref, *refs):
    count = len({i for pair in plan for i in pair[:2]})
    ins, (keep, send, total) = refs[:count], refs[count:]
    t = pl.program_id(0)
    last = pl.num_programs(0) - 1
    for left, right, cuts in plan:
        a, b = ins[left], ins[right]
        for source, row, size in cuts:
            add = dot_tn(a[:, source : source + size], b[...])

            @pl.when(t == 0)
            def _():
                total[row : row + size, :] = add

            @pl.when(t > 0)
            def _():
                total[row : row + size, :] += add

    @pl.when(t == last)
    def _():
        lanes = keep.shape[2]
        used = max(row + size for left, right, cuts in plan for source, row, size in cuts)
        for part in range(2 * keep.shape[0]):
            target = (keep, send)[part & 1]
            lane = pl.multiple_of(jnp.bitwise_xor(me_ref[0], part) * lanes, lanes)
            target[part >> 1, :used, :] = total[:, pl.ds(lane, lanes)].astype(LOW)
            if used < keep.shape[1]:
                target[part >> 1, used:, :] = jnp.zeros((keep.shape[1] - used, lanes), LOW)


def weight_grads(arrays, plan, rows_out, me, shards):
    rows = arrays[0].shape[0]
    width = 512
    used = max(row + size for left, right, cuts in plan for source, row, size in cuts)
    block = lambda n: pl.BlockSpec((BLOCK, n), lambda t: (t, 0))
    lanes = arrays[plan[0][1]].shape[1] // shards
    return pl.pallas_call(
        functools.partial(weight_kernel, plan),
        grid=(rows // BLOCK,),
        out_shape=[shape((shards // 2, rows_out, lanes), LOW)] * 2,
        in_specs=[smem()] + [block(item.shape[1]) for item in arrays],
        out_specs=[whole((shards // 2, rows_out, lanes))] * 2,
        scratch_shapes=[VMEM((used, lanes * shards), WIDE)],
        compiler_params=params(),
        cost_estimate=cost(2 * rows * used * lanes * shards, 2 * rows * sum(i.shape[1] for i in arrays)),
    )(me, *arrays)


def back_kernel(seq, count, decay, seg_s, in_last, *refs):
    (q, k, v, gret, cos, sin, seg, seg_row, st, dst, *got) = refs[:13]
    (dq, dk, dv, state, weights, grads) = refs[-6:]
    t = pl.program_id(0)
    c = count - 1 - t

    @pl.when(t == 0)
    def _():
        for h in range(H):
            state[h] = entering(decay, count * BLOCK, h, got)

    for b in range(1, count):

        @pl.when(c == b - 1)
        def _():
            prev = seg_s[seq, b * BLOCK - 1]
            first = seg_s[seq, b * BLOCK]
            last = seg_s[seq, (b + 1) * BLOCK - 1]
            joined = jnp.logical_and(first == last, first == prev)
            for h in range(H):
                factor = jnp.exp(jnp.full((1, 1), decay[h] * BLOCK, WIDE))
                state[h] = jnp.where(joined, factor * state[h], 0.0) + dst[b, h]

    start = c * BLOCK
    before = jnp.where(c > 0, seg_s[seq, jnp.maximum(start - 1, 0)], in_last[seq])
    final = seg_s[seq, start + BLOCK - 1]
    here = (seg[...] == before).astype(WIDE)
    ends = (seg[...] == final).astype(WIDE)
    place = column(BLOCK)
    dqs, dks = [], []
    for h in range(H):
        a = decay[h]
        qh = q[:, h * KD : (h + 1) * KD]
        kh = k[:, h * KD : (h + 1) * KD]
        vh = v[:, h * VP : (h + 1) * VP]
        gh = gret[:, h * VP : (h + 1) * VP]
        qw = jnp.exp(a * (place + 1.0)) * here
        kw = jnp.exp(a * (BLOCK - 1.0 - place)) * ends
        parts = []
        for i in range(BLOCK // TILE):
            top, reach = i * TILE, (i + 1) * TILE
            mix = mixing(a, top, TILE, seg, seg_row)
            s = dot_nt(qh[top:reach, :], kh[:reach, :])
            weights[top:reach, :reach] = (s * mix).astype(LOW)
            gs = (dot_nt(gh[top:reach, :], vh[:reach, :]) * mix).astype(LOW)
            grads[top:reach, :reach] = gs
            parts.append(dot(gs, kh[:reach, :]))
        late = state[h].astype(LOW)
        dqs.append(jnp.concatenate(parts) + qw * dot_nt(gh, st[c, h]))
        parts, values = [], []
        for i in range(BLOCK // TILE):
            top, reach = i * TILE, (i + 1) * TILE
            parts.append(dot_tn(grads[top:, top:reach], qh[top:, :]))
            values.append(dot_tn(weights[top:, top:reach], gh[top:, :]))
        dks.append(jnp.concatenate(parts) + kw * dot_nt(vh, late))
        dv[:, h * VP : (h + 1) * VP] = (jnp.concatenate(values) + kw * dot(kh, late)).astype(LOW)
    dq[...] = rotated(jnp.concatenate(dqs, axis=1), cos[...], -sin[...]).astype(LOW)
    dk[...] = rotated(jnp.concatenate(dks, axis=1), cos[...], -sin[...]).astype(LOW)


def back(seq, length, data, cos, sin, seg_col, seg_row, segments, in_last, decay, st, dst, got, earlier):
    rows = data[0].shape[0]
    count = length // BLOCK
    block = lambda n: pl.BlockSpec((BLOCK, n), lambda t: (seq * count + count - 1 - t, 0))
    table = pl.BlockSpec((BLOCK, KD // 2), lambda t: (count - 1 - t, 0))
    outs = [H * KD, H * KD, H * VP]
    many = len(outs)
    inputs = [decay, segments, in_last, *data, cos, sin, seg_col, seg_row, st, dst, *got]
    specs = [smem()] * 3 + [block(item.shape[1]) for item in data] + [table, table, block(1)]
    specs += [pl.BlockSpec((None, 1, BLOCK), lambda t: (seq * count + count - 1 - t, 0, 0))]
    specs += [whole(st.shape), whole(dst.shape), *(whole(item.shape) for item in got)]
    aliases = {}
    if earlier is not None:
        aliases = {len(inputs) + i: i for i in range(many)}
        inputs += list(earlier)
        specs += [pl.BlockSpec(memory_space=pl.ANY)] * many
    return pl.pallas_call(
        functools.partial(back_kernel, seq, count),
        grid=(count,),
        out_shape=[shape((rows, n), LOW) for n in outs],
        in_specs=specs,
        out_specs=[block(n) for n in outs],
        scratch_shapes=[
            VMEM((H, KD, VP), WIDE),
            VMEM((BLOCK, BLOCK), LOW),
            VMEM((BLOCK, BLOCK), LOW),
        ],
        input_output_aliases=aliases,
        compiler_params=params(),
        cost_estimate=cost(length * H * 2 * BLOCK * 3 * (KD + VP), 16 * length * H * VP),
    )(*inputs)


def input_kernel(dq, dk, dv, ggate, tok, glow, w_kv, w_qg, gains, out):
    kd = H * KD
    gh = dot(dq[...], w_qg[:kd, :]) + dot(dk[...], w_kv[:kd, :])
    gh += dot(dv[...], w_kv[kd:, :]) + dot(ggate[...], w_qg[kd:, :])
    x = tok[...].astype(WIDE)
    r = lax.rsqrt(jnp.mean(x * x, axis=1, keepdims=True) + EPS)
    xhat = x * r
    gh = gh * gains[0:1, :].astype(WIDE)
    inner_product = jnp.mean(gh * xhat, axis=1, keepdims=True)
    out[...] = (glow[...].astype(WIDE) + r * (gh - xhat * inner_product)).astype(LOW)


def input_grad(dq, dk, dv, ggate, tokens, glow, w_kv, w_qg, gains):
    rows, width = tokens.shape
    block = lambda item: pl.BlockSpec((BLOCK, item.shape[1]), lambda t: (t, 0))
    return pl.pallas_call(
        input_kernel,
        grid=(rows // BLOCK,),
        out_shape=shape((rows, width), LOW),
        in_specs=[block(item) for item in (dq, dk, dv, ggate, tokens, glow)]
        + [whole(w_kv.shape), whole(w_qg.shape), whole(gains.shape)],
        out_specs=block(tokens),
        compiler_params=params(),
        cost_estimate=cost(2 * rows * width * 2 * w_kv.shape[0], 20 * rows * width),
    )(dq, dk, dv, ggate, tokens, glow, w_kv, w_qg, gains)


def adam_step(master, moment, second, grad, scale, rate, decay_weight):
    clipped = grad * scale
    moment_new = BETA_ONE * moment + (1.0 - BETA_ONE) * clipped
    second_new = BETA_TWO * second + (1.0 - BETA_TWO) * clipped * clipped
    corrected = (
        moment_new
        * (1.0 / (1.0 - BETA_ONE**STEP))
        / (jnp.sqrt(second_new * (1.0 / (1.0 - BETA_TWO**STEP))) + ADAM_EPS)
    )
    return (master - rate * (corrected + decay_weight * master), moment_new, second_new)


def squares_kernel(vd, ff, one, two, three, w_qk, w_vg, w_gu, low_gains, grad_gains, total):
    kd = H * KD

    def rows(source, start, size):
        return source[start : start + size, :].astype(WIDE)

    def product(weight, grad):
        return jnp.sum(weight.astype(LOW).astype(WIDE) * grad, axis=0, keepdims=True)

    sums = []

    def square(item):
        sums.append(jnp.sum(item * item, axis=0, keepdims=True))
        return item

    first = jnp.zeros((1, low_gains.shape[1]), WIDE)
    for i in range(2):
        grad = square(rows(three, i * kd, kd))
        first += jnp.sum(w_qk[i].astype(LOW).astype(WIDE).T * grad, axis=0, keepdims=True)
    first += product(w_vg[0], square(rows(three, 2 * kd, vd)))
    first += product(w_vg[1], square(rows(two, vd, vd)))
    square(rows(two, 0, vd))
    square(rows(one, 0, ff))
    second = product(w_gu[0], square(rows(one, ff, ff)))
    second += product(w_gu[1], square(rows(one, 2 * ff, ff)))
    gains = jnp.concatenate([first, second]) / low_gains[...].astype(LOW).astype(WIDE)
    grad_gains[...] = gains
    sums.append(jnp.sum(gains * gains, axis=0, keepdims=True))
    total[...] = jnp.broadcast_to(jnp.sum(sum(sums), axis=1, keepdims=True), total.shape)


def squares(vd, ff, grads, w_qk, w_vg, w_gu, gains):
    return pl.pallas_call(
        functools.partial(squares_kernel, vd, ff),
        out_shape=[shape(gains.shape, WIDE), shape((8, 128), WIDE)],
        in_specs=[pl.BlockSpec(memory_space=VMEM)] * 7,
        out_specs=[pl.BlockSpec(memory_space=VMEM)] * 2,
        compiler_params=params(),
    )(*grads, w_qk, w_vg, w_gu, gains)


def update_kernel(vd, ff, here, there, one, two, three, gain_grads, *refs):
    ins, outs = refs[:18], refs[18:36]
    norm_out = refs[36]
    kd = H * KD
    norm = jnp.sqrt(here[...] + there[...])
    norm_out[...] = norm
    scale = jnp.minimum(1.0, CLIP / (norm + 1e-06))[0:1, 0:1]

    def step(place, at, grad, rate, decay_weight):
        results = adam_step(
            ins[place][at], ins[6 + place][at], ins[12 + place][at], grad, scale, rate, decay_weight
        )
        for group, result in enumerate(results):
            outs[6 * group + place][at] = result

    def rows(source, start, size):
        return source[start : start + size, :].astype(WIDE)

    step(4, ..., rows(one, 0, ff), MATRIX_RATE, DECAY_WEIGHT)
    step(3, 0, rows(one, ff, ff), MATRIX_RATE, DECAY_WEIGHT)
    step(3, 1, rows(one, 2 * ff, ff), MATRIX_RATE, DECAY_WEIGHT)
    step(2, ..., rows(two, 0, vd), MATRIX_RATE, DECAY_WEIGHT)
    step(1, 1, rows(two, vd, vd), MATRIX_RATE, DECAY_WEIGHT)
    step(1, 0, rows(three, 2 * kd, vd), MATRIX_RATE, DECAY_WEIGHT)
    step(0, 0, rows(three, 0, kd).T, MATRIX_RATE, DECAY_WEIGHT)
    step(0, 1, rows(three, kd, kd).T, MATRIX_RATE, DECAY_WEIGHT)
    step(5, ..., gain_grads[...], GAIN_RATE, 0.0)


def update(vd, ff, here, there, grads, gain_grads, arrays):
    return pl.pallas_call(
        functools.partial(update_kernel, vd, ff),
        out_shape=[shape(item.shape, WIDE) for item in arrays] + [shape(here.shape, WIDE)],
        in_specs=[pl.BlockSpec(memory_space=VMEM)] * 24,
        out_specs=[pl.BlockSpec(memory_space=VMEM)] * 19,
        compiler_params=params(),
    )(here, there, *grads, gain_grads, *arrays)


def on_device(
    tokens,
    cotangent,
    segments,
    log_decay,
    w_qk,
    w_vg,
    w_out,
    w_gu,
    w_down,
    norm_gains,
    *states,
):
    turned = lambda item: jnp.swapaxes(item, 1, 2)
    shards = lax.axis_size("shard")
    me = lax.axis_index("shard").reshape(1)
    seqs, length, width = tokens.shape
    rows = seqs * length
    kd, vd, ff = H * KD, H * VD, w_down.shape[0]
    vp = H * VP
    vg_t, gu_t = turned(w_vg), turned(w_gu)

    low = lambda item: item.astype(LOW)
    first = jnp.concatenate(
        [low(w_qk[1]).T, low(vg_t[0]), jnp.pad(low(norm_gains), ((0, 14), (0, 0)))]
    )
    second = jnp.concatenate([low(w_qk[0]).T, low(vg_t[1])])
    third = jnp.concatenate([low(w_out), low(gu_t[0]), low(gu_t[1]), low(w_down)])
    side = (lax.axis_index("dp") & 1).reshape(1)
    first_held = gather_shards(first)
    second_held = gather_shards(second)
    third_held, sent = gather_halves(third, side, second_held[1][2])

    def padded(start, row):
        return [(start + h * VD, 0, row + h * VP, VD) for h in range(H)]

    def fills(row):
        return [(0, row + h * VP + VD, VP - VD) for h in range(H)]

    half_width = KD // 2
    freq_rates = jnp.exp(-math.log(10000.0) * jnp.arange(half_width).astype(WIDE) / half_width)
    positions = (lax.axis_index("shard") * length + jnp.arange(length)).astype(WIDE)
    angles = positions[:, None] * freq_rates[None, :]
    cos, sin = jnp.cos(angles), jnp.sin(angles)

    tok = tokens.reshape(rows, width)
    cot = cotangent.reshape(rows, width)
    seg_col = segments.reshape(rows, 1)
    seg_row = segments.reshape(rows // BLOCK, 1, BLOCK)
    in_last = jnp.where(lax.axis_index("shard") > 0, segments[:, 0], -1)
    decay = log_decay

    def tick(*done):
        nonlocal decay, me, gains
        decay, me, gains = lax.optimization_barrier((decay, me, gains, *done))[:3]

    plan = [(0, 0, 0, kd)] + padded(kd, kd) + [(kd + vd, 1, 0, 16)]
    w_kv, gains = assemble(first_held, plan, fills(kd), [kd + vp, 16], width, me, side)
    tick(sent)
    flat, kvs, passing = None, [], []
    for seq in range(seqs):
        *flat, kv, leaving = front(
            seq, seqs, length, tok, seg_col, segments, decay, w_kv, gains, cos, sin, flat
        )
        kvs.append(kv)
        passing.append(Passing(leaving, False))
        tick(leaving)
    hid, k, v = flat
    for item in passing[:-1]:
        tick(item.turn(decay, length))
    plan = [(0, 0, 0, kd)] + padded(kd, kd)
    (w_qg,) = assemble(second_held, plan, fills(kd), [kd + vp], width, me, side)
    tick(w_qg)
    tick(passing[-1].turn(decay, length))
    q, intra, gate = inner(k, v, hid, w_qg, cos, sin, seg_col, seg_row, decay, length)
    tick(q)
    plan = padded(0, 0) + [(vd, 0, vp, 3 * ff)]
    (w_rest,) = assemble(third_held, plan, fills(0), [vp + 3 * ff], width, me, side)
    tick(w_rest)
    data = (intra, gate, q, tok, cot)
    flat, sts, dsts, returning = None, [], [], []
    for seq in range(seqs):
        *flat, st, dst, leaving = middle(
            seq, seqs, length, ff, data, seg_col, segments, in_last, decay,
            w_rest, gains, passing[seq].got, kvs[seq], flat,
        )
        sts.append(st)
        dsts.append(dst)
        returning.append(Passing(leaving, True))
        tick(leaving)
    tokens_out, hid2, prod, dgate, dup, mixed, glow, ggate, gret = flat

    quantum = 16 * lax.axis_size("dp")
    fit = lambda used: used + -used % quantum

    def halves(row):
        return [(h * VP, row + h * VD, VD) for h in range(H)]

    for item in returning[:-1]:
        tick(item.turn(decay, length))
    plan = [(0, 1, [(0, 0, ff)]), (2, 3, [(0, ff, ff)]), (4, 3, [(0, 2 * ff, ff)])]
    made = weight_grads([prod, cot, dgate, hid2, dup], plan, fit(3 * ff), me, shards)
    one = Staged(*made)
    tick(made[0])
    tick(returning[-1].turn(decay, length))
    tick(one.cross())
    plan = [(0, 1, halves(0)), (2, 3, halves(vd))]
    made = weight_grads([mixed, glow, ggate, hid], plan, fit(2 * vd), me, shards)
    two = Staged(*made)
    tick(made[0])
    flat = None
    for seq in range(seqs):
        flat = back(
            seq, length, (q, k, v, gret), cos, sin, seg_col, seg_row, segments, in_last, decay,
            sts[seq], dsts[seq], returning[seq].got, flat,
        )
        tick(flat[0])
        if seq == 0:
            tick(two.cross(), one.halve())
    dq, dk, dv = flat
    tick(one.scatter(), two.halve())
    plan = [(0, 3, [(0, 0, kd)]), (1, 3, [(0, kd, kd)]), (2, 3, halves(2 * kd))]
    made = weight_grads([dq, dk, dv, hid], plan, fit(2 * kd + vd), me, shards)
    three = Reduction(*made)
    tick(made[0])
    tick(two.scatter(), one.gather())
    tick(three.cross())
    grad_input = input_grad(dq, dk, dv, ggate, tok, glow, w_kv, w_qg, gains)
    three.far, one.half, two.parts = lax.optimization_barrier(
        (three.far, one.half, two.parts, grad_input)
    )[:3]
    three.scatter()
    one.double()
    two.gather()
    three.gather()
    two.double()
    grads = (one.result(), two.result(), three.result())

    gain_grads, total = squares(vd, ff, grads, w_qk, vg_t, gu_t, norm_gains)
    count = bits_of("shard")
    for bit in range(count - 1):
        total = total + exchange(total, "shard", bit)
    arrays = []
    for group in ((w_qk, w_vg, w_out, w_gu, w_down, norm_gains), states[:6], states[6:]):
        arrays += [turned(item) if i in (1, 3) else item for i, item in enumerate(group)]
    *results, norm = update(
        vd, ff, total, exchange(total, "shard", count - 1), grads, gain_grads, arrays
    )
    results = [turned(item) if i % 6 in (1, 3) else item for i, item in enumerate(results)]
    return (
        tokens_out.reshape(tokens.shape),
        grad_input.reshape(tokens.shape),
        *results,
        norm[0, 0],
    )


def solution(mesh):
    split = P("dp", "shard", None)
    rows, columns = P(None, "shard", None), P(None, "shard")
    group = (rows, rows, columns, rows, columns, columns)
    in_specs = (split, split, P("dp", "shard"), P()) + group * 3
    out_specs = (split, split) + group * 3 + (P(),)
    return jax.shard_map(
        on_device, mesh=mesh, in_specs=in_specs, out_specs=out_specs, check_vma=False
    )
```

```python
import functools
import math

import jax
import jax.numpy as jnp
from jax import lax
from jax.experimental import pallas as pl
from jax.experimental.pallas import tpu as pltpu
from jax.sharding import PartitionSpec as P

H = 2
KD = 256
VD = 432
VP = 512
BLOCK = 512
STEP = 10

EPS = 1e-05
ADAM_EPS = 1e-08
BETA_ONE = 0.9
BETA_TWO = 0.95
MATRIX_RATE = 0.15
GAIN_RATE = 1.0
DECAY_WEIGHT = 0.1
CLIP = 1.0

LOW = jnp.bfloat16
WIDE = jnp.float32
VMEM = pltpu.VMEM
SMEM = pltpu.SMEM
LIMIT = 60 * 1024 * 1024


def dot(a, b):
    return jnp.dot(a, b, preferred_element_type=WIDE)


def dot_nt(a, b):
    return lax.dot_general(a, b, (((1,), (1,)), ((), ())), preferred_element_type=WIDE)


def dot_tn(a, b):
    return lax.dot_general(a, b, (((0,), (0,)), ((), ())), preferred_element_type=WIDE)


def params(**more):
    return pltpu.CompilerParams(vmem_limit_bytes=LIMIT, **more)


def cost(flops, moved):
    return pl.CostEstimate(flops=int(flops), bytes_accessed=int(moved), transcendentals=0)


def smem():
    return pl.BlockSpec(memory_space=SMEM)


def whole(shape):
    return pl.BlockSpec(shape, lambda *at: (0,) * len(shape), pipeline_mode=pl.Buffered(1))


def shape(dims, kind):
    return jax.ShapeDtypeStruct(dims, kind)


def bits_of(axis):
    return (lax.axis_size(axis) - 1).bit_length()


def exchange(value, axis, bit):
    size = lax.axis_size(axis)
    return lax.ppermute(value, axis, [(i, i ^ (1 << bit)) for i in range(size)])


def gather_shards(own):
    held = [(0, own)]
    for bit in reversed(range(bits_of("shard"))):
        held += [(mask | (1 << bit), exchange(part, "shard", bit)) for mask, part in held]
    return held


def add_low(one, two):
    return (one.astype(WIDE) + two.astype(WIDE)).astype(LOW)


def spread(part, copies):
    return jnp.broadcast_to(part[None], (copies, *part.shape))


def summed(parts):
    return jnp.sum(parts.astype(WIDE), axis=0).astype(LOW)


class Reduction:
    def __init__(self, keep, send):
        self.keep = keep
        self.near = exchange(send, "shard", 0)

    def cross(self):
        low = add_low(self.keep[1], self.near[1])
        self.far = exchange(low, "shard", 1)
        return low

    def own(self):
        total = self.keep[0].astype(WIDE) + self.near[0].astype(WIDE) + self.far.astype(WIDE)
        return total.astype(LOW)

    def scatter(self):
        own = self.own()
        copies = lax.axis_size("dp")
        self.parts = lax.all_to_all(own.reshape(copies, -1, own.shape[1]), "dp", 0, 0)
        return own

    def gather(self):
        part = summed(self.parts)
        self.full = lax.all_to_all(spread(part, lax.axis_size("dp")), "dp", 0, 0)
        return part

    def result(self):
        return self.full.reshape(-1, self.full.shape[2])


class Passing:
    def __init__(self, local, reverse):
        self.local = local
        steps = [[(0, 1), (2, 3)], [(1, 2)], [(2, 3)]]
        if reverse:
            steps = [[(3 - a, 3 - b) for a, b in step] for step in steps]
        self.steps = steps
        self.got = [lax.ppermute(local, "shard", steps[0])]

    def turn(self, decay, length):
        total = combine(decay, length, self.local, self.got[0])
        self.got.append(lax.ppermute(total, "shard", self.steps[1]))
        return total

    def finish(self, *done):
        self.got.append(lax.ppermute(after(self.got[1], *done), "shard", self.steps[2]))


def entering(decay, length, h, got):
    factor = jnp.exp(jnp.full((1, 1), decay[h] * length, WIDE))
    wide = [item[h].astype(WIDE) for item in got]
    return wide[0] + wide[1] + factor * wide[2]


def after(value, *others):
    return lax.optimization_barrier((value, *others))[0]


def combine_kernel(length, decay, local, got, out):
    h = pl.program_id(0) % H
    factor = jnp.exp(jnp.full((1, 1), decay[h] * length, WIDE))
    out[...] = (local[...].astype(WIDE) + factor * got[...].astype(WIDE)).astype(LOW)


def combine(decay, length, local, got):
    block = pl.BlockSpec((None, None, KD, VP), lambda i: (i // H, i % H, 0, 0))
    return pl.pallas_call(
        functools.partial(combine_kernel, length),
        grid=(local.shape[0] * H,),
        out_shape=shape(local.shape, LOW),
        in_specs=[smem(), block, block],
        out_specs=block,
        compiler_params=params(),
        cost_estimate=cost(local.size, 6 * local.size),
    )(decay, local, got)


def assemble_kernel(plan, fills, masks, me_ref, *refs):
    sources, outs = refs[: len(masks)], refs[len(masks) :]
    lanes = sources[0].shape[1]
    for index, row, size in fills:
        outs[index][row : row + size, :] = jnp.zeros((size, outs[index].shape[1]), LOW)
    for mask, source in zip(masks, sources):
        lane = pl.multiple_of(jnp.bitwise_xor(me_ref[0], mask) * lanes, lanes)
        for start, index, row, size in plan:
            outs[index][row : row + size, pl.ds(lane, lanes)] = source[start : start + size, :]


def assemble(held, plan, fills, heights, width, me):
    masks = [mask for mask, part in held]
    parts = [part for mask, part in held]
    return pl.pallas_call(
        functools.partial(assemble_kernel, plan, fills, masks),
        out_shape=[shape((rows, width), LOW) for rows in heights],
        in_specs=[smem()] + [pl.BlockSpec(memory_space=VMEM)] * len(parts),
        out_specs=[pl.BlockSpec(memory_space=VMEM)] * len(heights),
        compiler_params=params(),
        cost_estimate=cost(0, 4 * sum(heights) * width),
    )(me, *parts)


def rotated(flat, cosine, sine):
    half = KD // 2
    parts = []
    for h in range(H):
        u = flat[:, h * KD : h * KD + half]
        w = flat[:, h * KD + half : (h + 1) * KD]
        parts += [u * cosine - w * sine, w * cosine + u * sine]
    return jnp.concatenate(parts, axis=1)


def column(size):
    return lax.broadcasted_iota(jnp.int32, (size, 1), 0).astype(WIDE)


def front_kernel(count, decay, seg_s, tok, w, gains, cos, sin, seg, *rest):
    hid, k, v, kv, out_state, state = rest
    seq = pl.program_id(0) // count
    c = pl.program_id(0) % count
    x = tok[...].astype(WIDE)
    r = lax.rsqrt(jnp.mean(x * x, axis=1, keepdims=True) + EPS)
    h1 = (x * r * gains[0:1, :].astype(WIDE)).astype(LOW)
    hid[...] = h1
    kd = H * KD
    key = rotated(dot_nt(h1, w[:kd, :]), cos[...], sin[...]).astype(LOW)
    k[...] = key
    val = dot_nt(h1, w[kd : kd + H * VP, :]).astype(LOW)
    v[...] = val
    first = seg_s[seq, c * BLOCK]
    last = seg_s[seq, c * BLOCK + BLOCK - 1]
    before = seg_s[seq, jnp.maximum(c * BLOCK - 1, 0)]
    here = (seg[...] == last).astype(WIDE)
    joined = jnp.logical_and(jnp.logical_and(first == last, first == before), c > 0)
    for h in range(H):
        a = decay[h]
        kw = jnp.exp(a * (BLOCK - 1.0 - column(BLOCK))) * here
        kk = (key[:, h * KD : (h + 1) * KD].astype(WIDE) * kw).astype(LOW)
        add = dot_tn(kk, val[:, h * VP : (h + 1) * VP])
        kv[h] = add
        factor = jnp.exp(jnp.full((1, 1), a * BLOCK, WIDE))
        total = jnp.where(joined, factor * state[h], 0.0) + add
        state[h] = total
        out_state[h] = total.astype(LOW)


def row_block(width):
    return pl.BlockSpec((BLOCK, width), lambda t: (t, 0))


def state_block(count, at=lambda c: c):
    return pl.BlockSpec(
        (None, None, H, KD, VP), lambda t: (t // count, at(t % count), 0, 0, 0)
    )


def seq_block(count):
    return pl.BlockSpec((None, H, KD, VP), lambda t: (t // count, 0, 0, 0))


def front(seqs, length, tokens, seg_col, segments, decay, w, gains, cos, sin):
    count = length // BLOCK
    rows, width = tokens.shape
    outs = [width, H * KD, H * VP]
    table = pl.BlockSpec((BLOCK, KD // 2), lambda t: (t % count, 0))
    return pl.pallas_call(
        functools.partial(front_kernel, count),
        grid=(seqs * count,),
        out_shape=[shape((rows, n), LOW) for n in outs]
        + [shape((seqs, count, H, KD, VP), WIDE), shape((seqs, H, KD, VP), LOW)],
        in_specs=[smem(), smem(), row_block(width), whole(w.shape), whole(gains.shape)]
        + [table, table, row_block(1)],
        out_specs=[row_block(n) for n in outs]
        + [state_block(count), seq_block(count)],
        scratch_shapes=[VMEM((H, KD, VP), WIDE)],
        compiler_params=params(),
        cost_estimate=cost(2 * rows * width * w.shape[0], 12 * rows * width),
    )(decay, segments, tokens, w, gains, cos, sin, seg_col)


def decay_row(a):
    return jnp.exp(-a * lax.broadcasted_iota(jnp.int32, (1, BLOCK), 1).astype(WIDE))


def mixing(a, top, size, seg, seg_row):
    reach = top + size
    rows = jnp.exp(a * (column(size) + float(top)))
    same = seg[top:reach, :] == seg_row[:, :reach]
    n = lax.broadcasted_iota(jnp.int32, (size, reach), 0) + top
    m = lax.broadcasted_iota(jnp.int32, (size, reach), 1)
    return jnp.where(jnp.logical_and(same, n >= m), rows * decay_row(a)[:, :reach], 0.0)


TILE = 256


def inner_kernel(decay, k, v, hid, w, cos, sin, seg, seg_row, q, intra, gate):
    kd = H * KD
    query = rotated(dot_nt(hid[...], w[:kd, :]), cos[...], sin[...]).astype(LOW)
    q[...] = query
    gate[...] = dot_nt(hid[...], w[kd:, :]).astype(LOW)
    for i in range(BLOCK // TILE):
        top, reach = i * TILE, (i + 1) * TILE
        for h in range(H):
            s = dot_nt(query[top:reach, h * KD : (h + 1) * KD], k[:reach, h * KD : (h + 1) * KD])
            weights = (s * mixing(decay[h], top, TILE, seg, seg_row)).astype(LOW)
            intra[top:reach, h * VP : (h + 1) * VP] = dot(
                weights, v[:reach, h * VP : (h + 1) * VP]
            ).astype(LOW)


def inner(k, v, hid, w, cos, sin, seg_col, seg_row, decay, length):
    rows, width = hid.shape
    count = length // BLOCK
    block = lambda n: pl.BlockSpec((BLOCK, n), lambda t: (t, 0))
    table = pl.BlockSpec((BLOCK, KD // 2), lambda t: (t % count, 0))
    return pl.pallas_call(
        inner_kernel,
        grid=(rows // BLOCK,),
        out_shape=[shape((rows, n), LOW) for n in (H * KD, H * VP, H * VP)],
        in_specs=[
            smem(),
            block(H * KD),
            block(H * VP),
            block(width),
            whole(w.shape),
            table,
            table,
            block(1),
            pl.BlockSpec((None, 1, BLOCK), lambda t: (t, 0, 0)),
        ],
        out_specs=[block(n) for n in (H * KD, H * VP, H * VP)],
        compiler_params=params(),
        cost_estimate=cost(rows * (2 * width * 1536 + 2 * BLOCK * H * VP), 8 * rows * H * VP),
    )(decay, k, v, hid, w, cos, sin, seg_col, seg_row)


CHUNK = 16


def interleaved(first, second):
    steps = [((i + 0.5) / len(first), 0, step) for i, step in enumerate(first)]
    steps += [((i + 0.5) / len(second), 1, step) for i, step in enumerate(second)]
    for place, which, step in sorted(steps, key=lambda item: item[:2]):
        step()


def pieces(width, size=256):
    return [(start, min(start + size, width)) for start in range(0, width, size)]


def across(narrow, width):
    return jnp.concatenate([narrow] * (width // 128), axis=1)


def middle_kernel(count, ff, decay, seg_s, in_last, *refs):
    (intra, gate, q, tok, cot, seg, w, gains, *got, kv) = refs[:12]
    outs, scratch = refs[12:24], refs[24:]
    (tok_out, hid2, prod, dgate, dup, mixed, glow, ggate, gret, st_out, dst, leave) = outs
    (state, now, queries, factors, ret_s, norm_s, silu_s, slope_s, inv_s, res_s, ff_s, low_s, sums) = scratch
    seq = pl.program_id(0) // count
    c = pl.program_id(0) % count
    start = c * BLOCK
    vp = H * VP
    width = tok.shape[1]
    before = jnp.where(c > 0, seg_s[seq, jnp.maximum(start - 1, 0)], in_last[seq])

    @pl.when(c == 0)
    def _():
        for h in range(H):
            total = entering(decay, count * BLOCK, h, got)
            state[h] = total
            now[h] = total.astype(LOW)

    for b in range(1, count):

        @pl.when(c == b)
        def _():
            prev = seg_s[seq, (b - 1) * BLOCK - 1] if b > 1 else in_last[seq]
            joined = jnp.logical_and(
                seg_s[seq, (b - 1) * BLOCK] == seg_s[seq, b * BLOCK - 1],
                seg_s[seq, (b - 1) * BLOCK] == prev,
            )
            for h in range(H):
                factor = jnp.exp(jnp.full((1, 1), decay[h] * BLOCK, WIDE))
                total = jnp.where(joined, factor * state[h], 0.0) + kv[h]
                state[h] = total
                now[h] = total.astype(LOW)

    st_out[...] = now[...]
    here = (seg[...] == before).astype(WIDE)
    for h in range(H):
        qw = jnp.exp(decay[h] * (column(BLOCK) + 1.0)) * here
        factors[h] = jnp.broadcast_to(qw, (BLOCK, 128))

    w_out = (0, vp)
    w_gate = (vp, vp + ff)
    w_up = (vp + ff, vp + 2 * ff)
    w_down = (vp + 2 * ff, vp + 3 * ff)
    gain = gains[1:2, :].astype(WIDE)

    def phases(top):
        rs = pl.ds(top, TILE)
        lists = []

        def add(steps):
            lists.append(steps)

        def chunks():
            return [pl.ds(row, CHUNK) for row in range(top, top + TILE, CHUNK)]

        def cross(h, lo, hi):
            ret_s[rs, h * VP + lo : h * VP + hi] = dot(
                q[rs, h * KD : (h + 1) * KD], now[h, :, lo:hi]
            )

        add([functools.partial(cross, h, *piece) for h in range(H) for piece in pieces(VP)])

        def gated(h, r):
            hv = slice(h * VP, (h + 1) * VP)
            hk = slice(h * KD, (h + 1) * KD)
            qw = factors[h, r, :]
            queries[r, hk] = (q[r, hk].astype(WIDE) * across(qw, KD)).astype(LOW)
            ret = intra[r, hv].astype(WIDE) + across(qw, VP) * ret_s[r, hv]
            mean = jnp.sum(ret, axis=1, keepdims=True) * (1.0 / VD)
            centered = ret - mean
            square = jnp.sum(centered * centered, axis=1, keepdims=True)
            var = (square - (VP - VD) * (mean * mean)) * (1.0 / VD)
            inv = lax.rsqrt(var + 1.0 * KD)
            nh = centered * inv
            g = gate[r, hv].astype(WIDE)
            sg = 0.5 * jnp.tanh(0.5 * g) + 0.5
            sl = g * sg
            mixed[r, hv] = (nh * sl).astype(LOW)
            norm_s[r, hv] = nh
            silu_s[r, hv] = sl
            slope_s[r, hv] = nh * (sg + sl * (1.0 - sg))
            inv_s[h, r, :] = jnp.broadcast_to(inv, (CHUNK, 128))

        add([functools.partial(gated, h, r) for r in chunks() for h in range(H)])

        def project(lo, hi):
            res_s[rs, lo:hi] = dot(mixed[rs, :], w[w_out[0] : w_out[1], lo:hi])

        add([functools.partial(project, *piece) for piece in pieces(width)])

        def norm(r):
            resid = tok[r, :].astype(WIDE) + res_s[r, :]
            r2 = lax.rsqrt(jnp.mean(resid * resid, axis=1, keepdims=True) + EPS)
            res_s[r, :] = resid
            hid2[r, :] = (resid * r2 * gain).astype(LOW)
            inv_s[H, r, :] = jnp.broadcast_to(r2, (CHUNK, 128))

        add([functools.partial(norm, r) for r in chunks()])

        def forward(place, source, at, lo, hi):
            ff_s[place, rs, lo:hi] = dot_nt(source[rs, :], w[at[0] + lo : at[0] + hi, :])

        add(
            [
                functools.partial(forward, place, source, at, *piece)
                for piece in pieces(ff)
                for place, source, at in ((0, hid2, w_gate), (1, hid2, w_up), (2, cot, w_down))
            ]
        )

        def gelu(r, lo, hi):
            gf, uf, gp = ff_s[0, r, lo:hi], ff_s[1, r, lo:hi], ff_s[2, r, lo:hi]
            e = jnp.exp(-0.5 * (gf * gf))
            d = 1.0 / (1.0 + (0.3275911 * math.sqrt(0.5)) * jnp.abs(gf))
            poly = d * (
                0.5 * 0.254829592
                + d
                * (
                    0.5 * -0.284496736
                    + d * (0.5 * 1.421413741 + d * (0.5 * -1.453152027 + d * (0.5 * 1.061405429)))
                )
            )
            tail = poly * e
            cdf = jnp.where(gf >= 0.0, 1.0 - tail, tail)
            ge = gf * cdf
            dge = cdf + gf * (e * (1.0 / math.sqrt(2.0 * math.pi)))
            prod[r, lo:hi] = (ge * uf).astype(LOW)
            dgate[r, lo:hi] = (gp * uf * dge).astype(LOW)
            dup[r, lo:hi] = (gp * ge).astype(LOW)

        add([functools.partial(gelu, r, *piece) for r in chunks() for piece in pieces(ff, 512)])

        def down(lo, hi):
            low_s[0, rs, lo:hi] = dot(prod[rs, :], w[w_down[0] : w_down[1], lo:hi])

        def hidden(lo, hi):
            low_s[1, rs, lo:hi] = dot(dgate[rs, :], w[w_gate[0] : w_gate[1], lo:hi]) + dot(
                dup[rs, :], w[w_up[0] : w_up[1], lo:hi]
            )

        add([functools.partial(step, *piece) for piece in pieces(width) for step in (down, hidden)])

        def residual(r):
            resid = res_s[r, :]
            r2 = across(inv_s[H, r, :], width)
            tok_out[r, :] = (resid + low_s[0, r, :]).astype(LOW)
            gh = low_s[1, r, :] * gain
            xhat = resid * r2
            inner_product = jnp.mean(gh * xhat, axis=1, keepdims=True)
            glow[r, :] = (cot[r, :].astype(WIDE) + r2 * (gh - xhat * inner_product)).astype(LOW)

        add([functools.partial(residual, r) for r in chunks()])

        def mix_back(lo, hi):
            ret_s[rs, lo:hi] = dot_nt(glow[rs, :], w[w_out[0] + lo : w_out[0] + hi, :])

        add([functools.partial(mix_back, *piece) for piece in pieces(vp)])

        def gated_back(h, r):
            hv = slice(h * VP, (h + 1) * VP)
            gm = ret_s[r, hv]
            nh = norm_s[r, hv]
            ggate[r, hv] = (gm * slope_s[r, hv]).astype(LOW)
            gn = gm * silu_s[r, hv]
            one = jnp.sum(gn, axis=1, keepdims=True) * (1.0 / VD)
            two = jnp.sum(gn * nh, axis=1, keepdims=True) * (1.0 / VD)
            gret[r, hv] = (across(inv_s[h, r, :], VP) * (gn - one - nh * two)).astype(LOW)

        add([functools.partial(gated_back, h, r) for r in chunks() for h in range(H)])
        return lists

    first, second = phases(0), phases(TILE)
    for k in range(len(first) + 1):
        interleaved(first[k] if k < len(first) else [], second[k - 1] if k else [])
    for h in range(H):
        add = dot_tn(queries[:, h * KD : (h + 1) * KD], gret[:, h * VP : (h + 1) * VP])
        dst[h] = add
        sums[c, h] = add

    @pl.when(c == count - 1)
    def _():
        for h in range(H):
            total = sums[count - 1, h]
            for b in reversed(range(count - 1)):
                prev = seg_s[seq, b * BLOCK - 1] if b > 0 else in_last[seq]
                joined = jnp.logical_and(
                    seg_s[seq, b * BLOCK] == seg_s[seq, (b + 1) * BLOCK - 1],
                    seg_s[seq, b * BLOCK] == prev,
                )
                factor = jnp.exp(jnp.full((1, 1), decay[h] * BLOCK, WIDE))
                total = jnp.where(joined, factor * total, 0.0) + sums[b, h]
            leave[h] = total.astype(LOW)


def middle(seqs, length, ff, data, seg_col, segments, in_last, decay, w, gains, got, kv):
    intra, gate, q, tokens, cotangent = data
    rows, width = tokens.shape
    count = length // BLOCK
    vp = H * VP
    outs = [width, width, ff, ff, ff, vp, width, vp, vp]
    inputs = [decay, segments, in_last, intra, gate, q, tokens, cotangent, seg_col, w, gains, *got, kv]
    specs = [smem()] * 3 + [row_block(n) for n in (vp, vp, H * KD, width, width, 1)]
    specs += [whole(w.shape), whole(gains.shape), *[seq_block(count)] * 3]
    specs += [state_block(count, lambda c: jnp.maximum(c - 1, 0))]
    one = (H, KD, VP)
    states = (seqs, count, *one)
    return pl.pallas_call(
        functools.partial(middle_kernel, count, ff),
        grid=(seqs * count,),
        out_shape=[shape((rows, n), LOW) for n in outs]
        + [shape(states, LOW), shape(states, WIDE), shape((seqs, *one), LOW)],
        in_specs=specs,
        out_specs=[row_block(n) for n in outs]
        + [state_block(count)] * 2
        + [seq_block(count)],
        scratch_shapes=[
            VMEM(one, WIDE),
            VMEM(one, LOW),
            VMEM((BLOCK, H * KD), LOW),
            VMEM((H, BLOCK, 128), WIDE),
            VMEM((BLOCK, vp), WIDE),
            VMEM((BLOCK, vp), WIDE),
            VMEM((BLOCK, vp), WIDE),
            VMEM((BLOCK, vp), WIDE),
            VMEM((H + 1, BLOCK, 128), WIDE),
            VMEM((BLOCK, width), WIDE),
            VMEM((3, BLOCK, ff), WIDE),
            VMEM((2, BLOCK, width), WIDE),
            VMEM(states[1:], WIDE),
        ],
        compiler_params=params(),
        cost_estimate=cost(2 * rows * width * (2 * vp + 6 * ff), 30 * rows * width),
    )(*inputs)


def weight_kernel(plan, count, split, me_ref, *refs):
    ins, outs, total = refs[:count], refs[count:-1], refs[-1]
    t = pl.program_id(0)
    last = pl.num_programs(0) - 1
    for left, right, cuts in plan:
        a, b = ins[left], ins[right]
        for source, row, size in cuts:
            add = dot_tn(a[:, source : source + size], b[...])

            @pl.when(t == 0)
            def _():
                total[row : row + size, :] = add

            @pl.when(t > 0)
            def _():
                total[row : row + size, :] += add

    @pl.when(t == last)
    def _():
        if not split:
            shards, _, lanes = outs[0].shape
            for part in range(shards):
                outs[0][part] = total[:, part * lanes : (part + 1) * lanes].astype(LOW)
            return
        lanes = outs[0].shape[2]
        used = total.shape[0]
        for part in range(2 * outs[0].shape[0]):
            target = outs[part & 1]
            lane = pl.multiple_of(jnp.bitwise_xor(me_ref[0], part) * lanes, lanes)
            target[part >> 1, :used, :] = total[:, pl.ds(lane, lanes)].astype(LOW)
            if used < target.shape[1]:
                target[part >> 1, used:, :] = jnp.zeros((target.shape[1] - used, lanes), LOW)


def weight_grads(arrays, plan, me, shards, split=0):
    rows = arrays[0].shape[0]
    used = max(row + size for left, right, cuts in plan for source, row, size in cuts)
    width = arrays[plan[0][1]].shape[1]
    tile = 2 * BLOCK
    block = lambda n: pl.BlockSpec((tile, n), lambda t: (t, 0))
    if split:
        outs = [(shards // 2, split, width // shards)] * 2
    else:
        outs = [(shards, used, width // shards)]
    return pl.pallas_call(
        functools.partial(weight_kernel, plan, len(arrays), split),
        grid=(rows // tile,),
        out_shape=[shape(dims, LOW) for dims in outs],
        in_specs=[smem()] + [block(item.shape[1]) for item in arrays],
        out_specs=[pl.BlockSpec(dims, lambda t: (0,) * len(dims)) for dims in outs],
        scratch_shapes=[VMEM((used, width), WIDE)],
        compiler_params=params(),
        cost_estimate=cost(2 * rows * used * width, 2 * rows * sum(i.shape[1] for i in arrays)),
    )(me, *arrays)


def back_kernel(count, decay, seg_s, in_last, *refs):
    (q, k, v, gret, cos, sin, seg, seg_row, st, dst, *got) = refs[:13]
    (dq, dk, dv, state, weights, grads) = refs[13:]
    seq = pl.program_id(0) // count
    c = count - 1 - pl.program_id(0) % count

    @pl.when(c == count - 1)
    def _():
        for h in range(H):
            state[h] = entering(decay, count * BLOCK, h, got)

    for b in range(1, count):

        @pl.when(c == b - 1)
        def _():
            prev = seg_s[seq, b * BLOCK - 1]
            first = seg_s[seq, b * BLOCK]
            last = seg_s[seq, (b + 1) * BLOCK - 1]
            joined = jnp.logical_and(first == last, first == prev)
            for h in range(H):
                factor = jnp.exp(jnp.full((1, 1), decay[h] * BLOCK, WIDE))
                state[h] = jnp.where(joined, factor * state[h], 0.0) + dst[h]

    start = c * BLOCK
    before = jnp.where(c > 0, seg_s[seq, jnp.maximum(start - 1, 0)], in_last[seq])
    final = seg_s[seq, start + BLOCK - 1]
    here = (seg[...] == before).astype(WIDE)
    ends = (seg[...] == final).astype(WIDE)
    place = column(BLOCK)
    dqs, dks = [], []
    for h in range(H):
        a = decay[h]
        qh = q[:, h * KD : (h + 1) * KD]
        kh = k[:, h * KD : (h + 1) * KD]
        vh = v[:, h * VP : (h + 1) * VP]
        gh = gret[:, h * VP : (h + 1) * VP]
        qw = jnp.exp(a * (place + 1.0)) * here
        kw = jnp.exp(a * (BLOCK - 1.0 - place)) * ends
        parts = []
        for i in range(BLOCK // TILE):
            top, reach = i * TILE, (i + 1) * TILE
            mix = mixing(a, top, TILE, seg, seg_row)
            s = dot_nt(qh[top:reach, :], kh[:reach, :])
            weights[top:reach, :reach] = (s * mix).astype(LOW)
            gs = (dot_nt(gh[top:reach, :], vh[:reach, :]) * mix).astype(LOW)
            grads[top:reach, :reach] = gs
            parts.append(dot(gs, kh[:reach, :]))
        late = state[h].astype(LOW)
        dqs.append(jnp.concatenate(parts) + qw * dot_nt(gh, st[h]))
        parts, values = [], []
        for i in range(BLOCK // TILE):
            top, reach = i * TILE, (i + 1) * TILE
            parts.append(dot_tn(grads[top:, top:reach], qh[top:, :]))
            values.append(dot_tn(weights[top:, top:reach], gh[top:, :]))
        dks.append(jnp.concatenate(parts) + kw * dot_nt(vh, late))
        dv[:, h * VP : (h + 1) * VP] = (jnp.concatenate(values) + kw * dot(kh, late)).astype(LOW)
    dq[...] = rotated(jnp.concatenate(dqs, axis=1), cos[...], -sin[...]).astype(LOW)
    dk[...] = rotated(jnp.concatenate(dks, axis=1), cos[...], -sin[...]).astype(LOW)


def back(seqs, length, data, cos, sin, seg_col, seg_row, segments, in_last, decay, st, dst, got):
    rows = data[0].shape[0]
    count = length // BLOCK
    turn = lambda t: (t // count) * count + count - 1 - t % count
    block = lambda n: pl.BlockSpec((BLOCK, n), lambda t: (turn(t), 0))
    table = pl.BlockSpec((BLOCK, KD // 2), lambda t: (count - 1 - t % count, 0))
    outs = [H * KD, H * KD, H * VP]
    inputs = [decay, segments, in_last, *data, cos, sin, seg_col, seg_row, st, dst, *got]
    specs = [smem()] * 3 + [block(item.shape[1]) for item in data] + [table, table, block(1)]
    specs += [pl.BlockSpec((None, 1, BLOCK), lambda t: (turn(t), 0, 0))]
    specs += [state_block(count, lambda c: count - 1 - c)]
    specs += [state_block(count, lambda c: jnp.minimum(count - c, count - 1))]
    specs += [seq_block(count)] * 3
    return pl.pallas_call(
        functools.partial(back_kernel, count),
        grid=(seqs * count,),
        out_shape=[shape((rows, n), LOW) for n in outs],
        in_specs=specs,
        out_specs=[block(n) for n in outs],
        scratch_shapes=[
            VMEM((H, KD, VP), WIDE),
            VMEM((BLOCK, BLOCK), LOW),
            VMEM((BLOCK, BLOCK), LOW),
        ],
        compiler_params=params(),
        cost_estimate=cost(rows * H * 2 * BLOCK * 3 * (KD + VP), 16 * rows * H * VP),
    )(*inputs)


def input_kernel(dq, dk, dv, ggate, tok, glow, w_kv, w_qg, gains, out):
    kd = H * KD
    gh = dot(dq[...], w_qg[:kd, :]) + dot(dk[...], w_kv[:kd, :])
    gh += dot(dv[...], w_kv[kd:, :]) + dot(ggate[...], w_qg[kd:, :])
    x = tok[...].astype(WIDE)
    r = lax.rsqrt(jnp.mean(x * x, axis=1, keepdims=True) + EPS)
    xhat = x * r
    gh = gh * gains[0:1, :].astype(WIDE)
    inner_product = jnp.mean(gh * xhat, axis=1, keepdims=True)
    out[...] = (glow[...].astype(WIDE) + r * (gh - xhat * inner_product)).astype(LOW)


def input_grad(dq, dk, dv, ggate, tokens, glow, w_kv, w_qg, gains):
    rows, width = tokens.shape
    block = lambda item: pl.BlockSpec((BLOCK, item.shape[1]), lambda t: (t, 0))
    return pl.pallas_call(
        input_kernel,
        grid=(rows // BLOCK,),
        out_shape=shape((rows, width), LOW),
        in_specs=[block(item) for item in (dq, dk, dv, ggate, tokens, glow)]
        + [whole(w_kv.shape), whole(w_qg.shape), whole(gains.shape)],
        out_specs=block(tokens),
        compiler_params=params(),
        cost_estimate=cost(2 * rows * width * 2 * w_kv.shape[0], 20 * rows * width),
    )(dq, dk, dv, ggate, tokens, glow, w_kv, w_qg, gains)


def adam_step(master, moment, second, grad, scale, rate, decay_weight):
    clipped = grad * scale
    moment_new = BETA_ONE * moment + (1.0 - BETA_ONE) * clipped
    second_new = BETA_TWO * second + (1.0 - BETA_TWO) * clipped * clipped
    corrected = (
        moment_new
        * (1.0 / (1.0 - BETA_ONE**STEP))
        / (jnp.sqrt(second_new * (1.0 / (1.0 - BETA_TWO**STEP))) + ADAM_EPS)
    )
    return (master - rate * (corrected + decay_weight * master), moment_new, second_new)


def squares_kernel(vd, ff, one, two, three, w_qk, w_vg, w_gu, low_gains, grad_gains, total):
    kd = H * KD

    def rows(source, start, size):
        return source[start : start + size, :].astype(WIDE)

    def product(weight, grad):
        return jnp.sum(weight.astype(LOW).astype(WIDE) * grad, axis=0, keepdims=True)

    sums = []

    def square(item):
        sums.append(jnp.sum(item * item, axis=0, keepdims=True))
        return item

    first = jnp.zeros((1, low_gains.shape[1]), WIDE)
    for i in range(2):
        grad = square(rows(three, i * kd, kd))
        first += jnp.sum(w_qk[i].astype(LOW).astype(WIDE).T * grad, axis=0, keepdims=True)
    first += product(w_vg[0], square(rows(three, 2 * kd, vd)))
    first += product(w_vg[1], square(rows(two, vd, vd)))
    square(rows(two, 0, vd))
    square(rows(one, 0, ff))
    second = product(w_gu[0], square(rows(one, ff, ff)))
    second += product(w_gu[1], square(rows(one, 2 * ff, ff)))
    gains = jnp.concatenate([first, second]) / low_gains[...].astype(LOW).astype(WIDE)
    grad_gains[...] = gains
    sums.append(jnp.sum(gains * gains, axis=0, keepdims=True))
    total[...] = jnp.broadcast_to(jnp.sum(sum(sums), axis=1, keepdims=True), total.shape)


def squares(vd, ff, grads, w_qk, w_vg, w_gu, gains):
    return pl.pallas_call(
        functools.partial(squares_kernel, vd, ff),
        out_shape=[shape(gains.shape, WIDE), shape((8, 128), WIDE)],
        in_specs=[pl.BlockSpec(memory_space=VMEM)] * 7,
        out_specs=[pl.BlockSpec(memory_space=VMEM)] * 2,
        compiler_params=params(),
    )(*grads, w_qk, w_vg, w_gu, gains)


def update_kernel(vd, ff, here, there, one, two, three, gain_grads, *refs):
    ins, outs = refs[:18], refs[18:36]
    norm_out = refs[36]
    kd = H * KD
    norm = jnp.sqrt(here[...] + there[...])
    norm_out[0, 0] = jnp.max(norm)
    scale = jnp.minimum(1.0, CLIP / (norm + 1e-06))[0:1, 0:1]

    def step(place, at, grad, rate, decay_weight):
        results = adam_step(
            ins[place][at], ins[6 + place][at], ins[12 + place][at], grad, scale, rate, decay_weight
        )
        for group, result in enumerate(results):
            outs[6 * group + place][at] = result

    def rows(source, start, size):
        return source[start : start + size, :].astype(WIDE)

    step(4, ..., rows(one, 0, ff), MATRIX_RATE, DECAY_WEIGHT)
    step(3, 0, rows(one, ff, ff), MATRIX_RATE, DECAY_WEIGHT)
    step(3, 1, rows(one, 2 * ff, ff), MATRIX_RATE, DECAY_WEIGHT)
    step(2, ..., rows(two, 0, vd), MATRIX_RATE, DECAY_WEIGHT)
    step(1, 1, rows(two, vd, vd), MATRIX_RATE, DECAY_WEIGHT)
    step(1, 0, rows(three, 2 * kd, vd), MATRIX_RATE, DECAY_WEIGHT)
    step(0, 0, rows(three, 0, kd).T, MATRIX_RATE, DECAY_WEIGHT)
    step(0, 1, rows(three, kd, kd).T, MATRIX_RATE, DECAY_WEIGHT)
    step(5, ..., gain_grads[...], GAIN_RATE, 0.0)


def update(vd, ff, here, there, grads, gain_grads, arrays):
    return pl.pallas_call(
        functools.partial(update_kernel, vd, ff),
        out_shape=[shape(item.shape, WIDE) for item in arrays] + [shape((1, 1), WIDE)],
        in_specs=[pl.BlockSpec(memory_space=VMEM)] * 24,
        out_specs=[pl.BlockSpec(memory_space=VMEM)] * 18 + [smem()],
        compiler_params=params(),
    )(here, there, *grads, gain_grads, *arrays)


def on_device(
    tokens,
    cotangent,
    segments,
    log_decay,
    w_qk,
    w_vg,
    w_out,
    w_gu,
    w_down,
    norm_gains,
    *states,
):
    turned = lambda item: jnp.swapaxes(item, 1, 2)
    shards = lax.axis_size("shard")
    me = lax.axis_index("shard").reshape(1)
    seqs, length, width = tokens.shape
    rows = seqs * length
    kd, vd, ff = H * KD, H * VD, w_down.shape[0]
    vp = H * VP
    vg_t, gu_t = turned(w_vg), turned(w_gu)

    low = lambda item: item.astype(LOW)
    def heads(item):
        return [
            jnp.pad(item[h * VD : (h + 1) * VD], ((0, VP - VD), (0, 0))) for h in range(H)
        ]

    first = jnp.concatenate(
        [low(w_qk[1]).T, low(vg_t[0]), jnp.pad(low(norm_gains), ((0, 14), (0, 0)))]
    )
    second = jnp.concatenate([low(w_qk[0]).T, *heads(low(vg_t[1]))])
    third = jnp.concatenate([*heads(low(w_out)), low(gu_t[0]), low(gu_t[1]), low(w_down)])
    first_held = gather_shards(first)
    second = after(second, first_held[1][1])
    w_qg = lax.all_gather(second, "shard", axis=1, tiled=True)
    third = after(third, second)
    w_rest = lax.all_gather(third, "shard", axis=1, tiled=True)

    half_width = KD // 2
    freq_rates = jnp.exp(-math.log(10000.0) * jnp.arange(half_width).astype(WIDE) / half_width)
    positions = (lax.axis_index("shard") * length + jnp.arange(length)).astype(WIDE)
    angles = positions[:, None] * freq_rates[None, :]
    cos, sin = jnp.cos(angles), jnp.sin(angles)

    tok = tokens.reshape(rows, width)
    cot = cotangent.reshape(rows, width)
    seg_col = segments.reshape(rows, 1)
    seg_row = segments.reshape(rows // BLOCK, 1, BLOCK)
    in_last = jnp.where(lax.axis_index("shard") > 0, segments[:, 0], -1)
    decay = log_decay

    def tick(*done):
        nonlocal decay, me, gains
        decay, me, gains = lax.optimization_barrier((decay, me, gains, *done))[:3]

    plan = [(0, 0, 0, kd)] + [(kd + h * VD, 0, kd + h * VP, VD) for h in range(H)]
    plan += [(kd + vd, 1, 0, 16)]
    fills = [(0, kd + h * VP + VD, VP - VD) for h in range(H)]
    w_kv, gains = assemble(first_held, plan, fills, [kd + vp, 16], width, me)
    tick(third)
    hid, k, v, kv, leaving = front(
        seqs, length, tok, seg_col, segments, decay, w_kv, gains, cos, sin
    )
    passing = Passing(leaving, False)
    tick(leaving)
    tick(passing.turn(decay, length))
    q, intra, gate = inner(k, v, hid, w_qg, cos, sin, seg_col, seg_row, decay, length)
    tick(q)
    passing.finish(q)
    tokens_out, hid2, prod, dgate, dup, mixed, glow, ggate, gret, st, dst, leaving = middle(
        seqs, length, ff, (intra, gate, q, tok, cot), seg_col, segments, in_last, decay,
        w_rest, gains, passing.got, kv,
    )
    returning = Passing(leaving, True)
    tick(leaving)

    def halves(row):
        return [(h * VP, row + h * VD, VD) for h in range(H)]

    plan = [(0, 1, [(0, 0, ff)]), (2, 3, [(0, ff, ff)]), (4, 3, [(0, 2 * ff, ff)])]
    (one,) = weight_grads([prod, cot, dgate, hid2, dup], plan, me, shards)
    tick(one)
    one = lax.psum_scatter(one, "shard", scatter_dimension=0)
    tick(returning.turn(decay, length))
    plan = [(0, 1, halves(0)), (2, 3, halves(vd))]
    (two,) = weight_grads([mixed, glow, ggate, hid], plan, me, shards)
    tick(two)
    returning.finish(two)
    two = lax.psum_scatter(two, "shard", scatter_dimension=0)
    one, two = lax.psum((one, two), "dp")
    dq, dk, dv = back(
        seqs, length, (q, k, v, gret), cos, sin, seg_col, seg_row, segments, in_last, decay,
        st, dst, returning.got,
    )
    tick(dq)
    plan = [(0, 3, [(0, 0, kd)]), (1, 3, [(0, kd, kd)]), (2, 3, halves(2 * kd))]
    used = 2 * kd + vd
    split = used + -used % (16 * lax.axis_size("dp"))
    made = weight_grads([dq, dk, dv, hid], plan, me, shards, split)
    three = Reduction(*made)
    tick(made[0])
    tick(three.cross())
    grad_input = input_grad(dq, dk, dv, ggate, tok, glow, w_kv, w_qg, gains)
    three.far = after(three.far, grad_input)
    three.scatter()
    three.gather()
    grads = (one, two, three.result())

    gain_grads, total = squares(vd, ff, grads, w_qk, vg_t, gu_t, norm_gains)
    count = bits_of("shard")
    for bit in range(count - 1):
        total = total + exchange(total, "shard", bit)
    arrays = []
    for group in ((w_qk, w_vg, w_out, w_gu, w_down, norm_gains), states[:6], states[6:]):
        arrays += [turned(item) if i in (1, 3) else item for i, item in enumerate(group)]
    *results, norm = update(
        vd, ff, total, exchange(total, "shard", count - 1), grads, gain_grads, arrays
    )
    results = [turned(item) if i % 6 in (1, 3) else item for i, item in enumerate(results)]
    return (
        tokens_out.reshape(tokens.shape),
        grad_input.reshape(tokens.shape),
        *results,
        norm.reshape(()),
    )


def solution(mesh):
    split = P("dp", "shard", None)
    rows, columns = P(None, "shard", None), P(None, "shard")
    group = (rows, rows, columns, rows, columns, columns)
    in_specs = (split, split, P("dp", "shard"), P()) + group * 3
    out_specs = (split, split) + group * 3 + (P(),)
    return jax.shard_map(
        on_device, mesh=mesh, in_specs=in_specs, out_specs=out_specs, check_vma=False
    )
```

```python
import functools
import math

import jax
import jax.numpy as jnp
from jax import lax
from jax.experimental import pallas as pl
from jax.experimental.pallas import tpu as pltpu
from jax.sharding import PartitionSpec as P

H = 2
KD = 256
VD = 432
VP = 512
BLOCK = 512
STEP = 10

EPS = 1e-05
ADAM_EPS = 1e-08
BETA_ONE = 0.9
BETA_TWO = 0.95
MATRIX_RATE = 0.15
GAIN_RATE = 1.0
DECAY_WEIGHT = 0.1
CLIP = 1.0

LOW = jnp.bfloat16
WIDE = jnp.float32
VMEM = pltpu.VMEM
SMEM = pltpu.SMEM
LIMIT = 60 * 1024 * 1024


def dot(a, b):
    return jnp.dot(a, b, preferred_element_type=WIDE)


def dot_nt(a, b):
    return lax.dot_general(a, b, (((1,), (1,)), ((), ())), preferred_element_type=WIDE)


def dot_tn(a, b):
    return lax.dot_general(a, b, (((0,), (0,)), ((), ())), preferred_element_type=WIDE)


def params(**more):
    return pltpu.CompilerParams(vmem_limit_bytes=LIMIT, **more)


def cost(flops, moved):
    return pl.CostEstimate(flops=int(flops), bytes_accessed=int(moved), transcendentals=0)


def smem():
    return pl.BlockSpec(memory_space=SMEM)


def whole(shape):
    return pl.BlockSpec(shape, lambda *at: (0,) * len(shape), pipeline_mode=pl.Buffered(1))


def shape(dims, kind):
    return jax.ShapeDtypeStruct(dims, kind)


def bits_of(axis):
    return (lax.axis_size(axis) - 1).bit_length()


def exchange(value, axis, bit):
    size = lax.axis_size(axis)
    return lax.ppermute(value, axis, [(i, i ^ (1 << bit)) for i in range(size)])


def gather_shards(own):
    held = [(0, own)]
    for bit in reversed(range(bits_of("shard"))):
        held += [(mask | (1 << bit), exchange(part, "shard", bit)) for mask, part in held]
    return [(mask, None, part) for mask, part in held]


def gather_halves(own, side, first):
    rows = own.shape[0] // 2
    send = after(lax.dynamic_slice_in_dim(own, side[0] * rows, rows, 0), first)
    here = exchange(send, "shard", 1)
    there = exchange(here, "dp", 0)
    held = [(0, None, own), (1, None, exchange(own, "shard", 0))]
    held += [(2, 0, here), (2, 1, there)]
    held += [(3, 0, exchange(here, "shard", 0)), (3, 1, exchange(there, "shard", 0))]
    return held, send


def add_low(one, two):
    return (one.astype(WIDE) + two.astype(WIDE)).astype(LOW)


def spread(part, copies):
    return jnp.broadcast_to(part[None], (copies, *part.shape))


def summed(parts):
    return jnp.sum(parts.astype(WIDE), axis=0).astype(LOW)


class Reduction:
    def __init__(self, keep, send):
        self.keep = keep
        self.near = exchange(send, "shard", 0)

    def cross(self):
        low = add_low(self.keep[1], self.near[1])
        self.far = exchange(low, "shard", 1)
        return low

    def own(self):
        total = self.keep[0].astype(WIDE) + self.near[0].astype(WIDE) + self.far.astype(WIDE)
        return total.astype(LOW)


class Staged(Reduction):
    def groups(self):
        size = lax.axis_size("dp")
        return [list(range(0, size, 2)), list(range(1, size, 2))]

    def halve(self):
        own = self.own()
        self.side = lax.axis_index("dp") & 1
        rows = own.shape[0] // 2
        self.mine = lax.dynamic_slice_in_dim(own, self.side * rows, rows, 0)
        send = lax.dynamic_slice_in_dim(own, (1 - self.side) * rows, rows, 0)
        self.other = exchange(send, "dp", 0)
        return send

    def scatter(self):
        half = add_low(self.mine, self.other)
        self.copies = lax.axis_size("dp") // 2
        half = half.reshape(self.copies, -1, half.shape[1])
        self.parts = lax.all_to_all(half, "dp", 0, 0, axis_index_groups=self.groups())
        return half

    def gather(self):
        part = summed(self.parts)
        half = lax.all_to_all(spread(part, self.copies), "dp", 0, 0, axis_index_groups=self.groups())
        self.half = half.reshape(-1, half.shape[2])
        return part

    def double(self):
        self.other = exchange(self.half, "dp", 0)

    def result(self):
        here, there = self.half, self.other
        return jnp.where(
            self.side == 0, jnp.concatenate([here, there]), jnp.concatenate([there, here])
        )


class Passing:
    def __init__(self, local, reverse):
        self.local = local
        steps = [[(0, 1), (2, 3)], [(1, 2)], [(2, 3)]]
        if reverse:
            steps = [[(3 - a, 3 - b) for a, b in step] for step in steps]
        self.steps = steps
        self.got = [lax.ppermute(local, "shard", steps[0])]

    def turn(self, decay, length):
        total = combine(decay, length, self.local, self.got[0])
        self.got.append(lax.ppermute(total, "shard", self.steps[1]))
        return total

    def finish(self, *done):
        self.got.append(lax.ppermute(after(self.got[1], *done), "shard", self.steps[2]))


def entering(decay, length, h, got):
    factor = jnp.exp(jnp.full((1, 1), decay[h] * length, WIDE))
    wide = [item[h].astype(WIDE) for item in got]
    return wide[0] + wide[1] + factor * wide[2]


def after(value, *others):
    return lax.optimization_barrier((value, *others))[0]


def combine_kernel(length, decay, local, got, out):
    h = pl.program_id(0) % H
    factor = jnp.exp(jnp.full((1, 1), decay[h] * length, WIDE))
    out[...] = (local[...].astype(WIDE) + factor * got[...].astype(WIDE)).astype(LOW)


def combine(decay, length, local, got):
    block = pl.BlockSpec((None, None, KD, VP), lambda i: (i // H, i % H, 0, 0))
    return pl.pallas_call(
        functools.partial(combine_kernel, length),
        grid=(local.shape[0] * H,),
        out_shape=shape(local.shape, LOW),
        in_specs=[smem(), block, block],
        out_specs=block,
        compiler_params=params(),
        cost_estimate=cost(local.size, 6 * local.size),
    )(decay, local, got)


def assemble_kernel(plan, fills, sources_of, me_ref, side_ref, *refs):
    sources, outs = refs[: len(sources_of)], refs[len(sources_of) :]
    lanes = sources[0].shape[1]
    for index, row, size in fills:
        outs[index][row : row + size, :] = jnp.zeros((size, outs[index].shape[1]), LOW)

    def place(source, lane, low, high):
        for start, index, row, size in plan:
            begin, end = max(start, low), min(start + size, high)
            if begin < end:
                to = row + begin - start
                outs[index][to : to + end - begin, pl.ds(lane, lanes)] = source[
                    begin - low : end - low, :
                ]

    for (mask, half), source in zip(sources_of, sources):
        lane = pl.multiple_of(jnp.bitwise_xor(me_ref[0], mask) * lanes, lanes)
        rows = source.shape[0]
        if half is None:
            place(source, lane, 0, rows)
            continue
        for side in range(2):

            @pl.when(side_ref[0] == side)
            def _():
                low = (side ^ half) * rows
                place(source, lane, low, low + rows)


def assemble(held, plan, fills, heights, width, me, side):
    sources_of = [(mask, half) for mask, half, part in held]
    parts = [part for mask, half, part in held]
    return pl.pallas_call(
        functools.partial(assemble_kernel, plan, fills, sources_of),
        out_shape=[shape((rows, width), LOW) for rows in heights],
        in_specs=[smem()] * 2 + [pl.BlockSpec(memory_space=VMEM)] * len(parts),
        out_specs=[pl.BlockSpec(memory_space=VMEM)] * len(heights),
        compiler_params=params(),
        cost_estimate=cost(0, 4 * sum(heights) * width),
    )(me, side, *parts)


def rotated(flat, cosine, sine):
    half = KD // 2
    parts = []
    for h in range(H):
        u = flat[:, h * KD : h * KD + half]
        w = flat[:, h * KD + half : (h + 1) * KD]
        parts += [u * cosine - w * sine, w * cosine + u * sine]
    return jnp.concatenate(parts, axis=1)


def column(size):
    return lax.broadcasted_iota(jnp.int32, (size, 1), 0).astype(WIDE)


def front_kernel(count, decay, seg_s, tok, w, gains, cos, sin, seg, *rest):
    hid, k, v, kv, out_state, state = rest
    seq = pl.program_id(0) // count
    c = pl.program_id(0) % count
    x = tok[...].astype(WIDE)
    r = lax.rsqrt(jnp.mean(x * x, axis=1, keepdims=True) + EPS)
    h1 = (x * r * gains[0:1, :].astype(WIDE)).astype(LOW)
    hid[...] = h1
    kd = H * KD
    key = rotated(dot_nt(h1, w[:kd, :]), cos[...], sin[...]).astype(LOW)
    k[...] = key
    val = dot_nt(h1, w[kd : kd + H * VP, :]).astype(LOW)
    v[...] = val
    first = seg_s[seq, c * BLOCK]
    last = seg_s[seq, c * BLOCK + BLOCK - 1]
    before = seg_s[seq, jnp.maximum(c * BLOCK - 1, 0)]
    here = (seg[...] == last).astype(WIDE)
    joined = jnp.logical_and(jnp.logical_and(first == last, first == before), c > 0)
    for h in range(H):
        a = decay[h]
        kw = jnp.exp(a * (BLOCK - 1.0 - column(BLOCK))) * here
        kk = (key[:, h * KD : (h + 1) * KD].astype(WIDE) * kw).astype(LOW)
        add = dot_tn(kk, val[:, h * VP : (h + 1) * VP])
        kv[h] = add
        factor = jnp.exp(jnp.full((1, 1), a * BLOCK, WIDE))
        total = jnp.where(joined, factor * state[h], 0.0) + add
        state[h] = total
        out_state[h] = total.astype(LOW)


def row_block(width):
    return pl.BlockSpec((BLOCK, width), lambda t: (t, 0))


def state_block(count, at=lambda c: c):
    return pl.BlockSpec(
        (None, None, H, KD, VP), lambda t: (t // count, at(t % count), 0, 0, 0)
    )


def seq_block(count):
    return pl.BlockSpec((None, H, KD, VP), lambda t: (t // count, 0, 0, 0))


def front(seqs, length, tokens, seg_col, segments, decay, w, gains, cos, sin):
    count = length // BLOCK
    rows, width = tokens.shape
    outs = [width, H * KD, H * VP]
    table = pl.BlockSpec((BLOCK, KD // 2), lambda t: (t % count, 0))
    return pl.pallas_call(
        functools.partial(front_kernel, count),
        grid=(seqs * count,),
        out_shape=[shape((rows, n), LOW) for n in outs]
        + [shape((seqs, count, H, KD, VP), WIDE), shape((seqs, H, KD, VP), LOW)],
        in_specs=[smem(), smem(), row_block(width), whole(w.shape), whole(gains.shape)]
        + [table, table, row_block(1)],
        out_specs=[row_block(n) for n in outs]
        + [state_block(count), seq_block(count)],
        scratch_shapes=[VMEM((H, KD, VP), WIDE)],
        compiler_params=params(),
        cost_estimate=cost(2 * rows * width * w.shape[0], 12 * rows * width),
    )(decay, segments, tokens, w, gains, cos, sin, seg_col)


def decay_row(a):
    return jnp.exp(-a * lax.broadcasted_iota(jnp.int32, (1, BLOCK), 1).astype(WIDE))


def mixing(a, top, size, seg, seg_row):
    reach = top + size
    rows = jnp.exp(a * (column(size) + float(top)))
    same = seg[top:reach, :] == seg_row[:, :reach]
    n = lax.broadcasted_iota(jnp.int32, (size, reach), 0) + top
    m = lax.broadcasted_iota(jnp.int32, (size, reach), 1)
    return jnp.where(jnp.logical_and(same, n >= m), rows * decay_row(a)[:, :reach], 0.0)


TILE = 256


def inner_kernel(decay, k, v, hid, w, cos, sin, seg, seg_row, q, intra, gate):
    kd = H * KD
    query = rotated(dot_nt(hid[...], w[:kd, :]), cos[...], sin[...]).astype(LOW)
    q[...] = query
    gate[...] = dot_nt(hid[...], w[kd:, :]).astype(LOW)
    for i in range(BLOCK // TILE):
        top, reach = i * TILE, (i + 1) * TILE
        for h in range(H):
            s = dot_nt(query[top:reach, h * KD : (h + 1) * KD], k[:reach, h * KD : (h + 1) * KD])
            weights = (s * mixing(decay[h], top, TILE, seg, seg_row)).astype(LOW)
            intra[top:reach, h * VP : (h + 1) * VP] = dot(
                weights, v[:reach, h * VP : (h + 1) * VP]
            ).astype(LOW)


def inner(k, v, hid, w, cos, sin, seg_col, seg_row, decay, length):
    rows, width = hid.shape
    count = length // BLOCK
    block = lambda n: pl.BlockSpec((BLOCK, n), lambda t: (t, 0))
    table = pl.BlockSpec((BLOCK, KD // 2), lambda t: (t % count, 0))
    return pl.pallas_call(
        inner_kernel,
        grid=(rows // BLOCK,),
        out_shape=[shape((rows, n), LOW) for n in (H * KD, H * VP, H * VP)],
        in_specs=[
            smem(),
            block(H * KD),
            block(H * VP),
            block(width),
            whole(w.shape),
            table,
            table,
            block(1),
            pl.BlockSpec((None, 1, BLOCK), lambda t: (t, 0, 0)),
        ],
        out_specs=[block(n) for n in (H * KD, H * VP, H * VP)],
        compiler_params=params(),
        cost_estimate=cost(rows * (2 * width * 1536 + 2 * BLOCK * H * VP), 8 * rows * H * VP),
    )(decay, k, v, hid, w, cos, sin, seg_col, seg_row)


CHUNK = 16


def interleaved(first, second):
    steps = [((i + 0.5) / len(first), 0, step) for i, step in enumerate(first)]
    steps += [((i + 0.5) / len(second), 1, step) for i, step in enumerate(second)]
    for place, which, step in sorted(steps, key=lambda item: item[:2]):
        step()


def pieces(width, size=256):
    return [(start, min(start + size, width)) for start in range(0, width, size)]


def across(narrow, width):
    return jnp.concatenate([narrow] * (width // 128), axis=1)


def middle_kernel(count, ff, decay, seg_s, in_last, *refs):
    (intra, gate, q, tok, cot, seg, w, gains, *got, kv) = refs[:12]
    outs, scratch = refs[12:24], refs[24:]
    (tok_out, hid2, prod, dgate, dup, mixed, glow, ggate, gret, st_out, dst, leave) = outs
    (state, now, queries, factors, ret_s, norm_s, silu_s, slope_s, inv_s, res_s, ff_s, low_s, sums) = scratch
    seq = pl.program_id(0) // count
    c = pl.program_id(0) % count
    start = c * BLOCK
    vp = H * VP
    width = tok.shape[1]
    before = jnp.where(c > 0, seg_s[seq, jnp.maximum(start - 1, 0)], in_last[seq])

    @pl.when(c == 0)
    def _():
        for h in range(H):
            total = entering(decay, count * BLOCK, h, got)
            state[h] = total
            now[h] = total.astype(LOW)

    for b in range(1, count):

        @pl.when(c == b)
        def _():
            prev = seg_s[seq, (b - 1) * BLOCK - 1] if b > 1 else in_last[seq]
            joined = jnp.logical_and(
                seg_s[seq, (b - 1) * BLOCK] == seg_s[seq, b * BLOCK - 1],
                seg_s[seq, (b - 1) * BLOCK] == prev,
            )
            for h in range(H):
                factor = jnp.exp(jnp.full((1, 1), decay[h] * BLOCK, WIDE))
                total = jnp.where(joined, factor * state[h], 0.0) + kv[h]
                state[h] = total
                now[h] = total.astype(LOW)

    st_out[...] = now[...]
    here = (seg[...] == before).astype(WIDE)
    for h in range(H):
        qw = jnp.exp(decay[h] * (column(BLOCK) + 1.0)) * here
        factors[h] = jnp.broadcast_to(qw, (BLOCK, 128))

    w_out = (0, vp)
    w_gate = (vp, vp + ff)
    w_up = (vp + ff, vp + 2 * ff)
    w_down = (vp + 2 * ff, vp + 3 * ff)
    gain = gains[1:2, :].astype(WIDE)

    def phases(top):
        rs = pl.ds(top, TILE)
        lists = []

        def add(steps):
            lists.append(steps)

        def chunks():
            return [pl.ds(row, CHUNK) for row in range(top, top + TILE, CHUNK)]

        def cross(h, lo, hi):
            ret_s[rs, h * VP + lo : h * VP + hi] = dot(
                q[rs, h * KD : (h + 1) * KD], now[h, :, lo:hi]
            )

        add([functools.partial(cross, h, *piece) for h in range(H) for piece in pieces(VP)])

        def gated(h, r):
            hv = slice(h * VP, (h + 1) * VP)
            hk = slice(h * KD, (h + 1) * KD)
            qw = factors[h, r, :]
            queries[r, hk] = (q[r, hk].astype(WIDE) * across(qw, KD)).astype(LOW)
            ret = intra[r, hv].astype(WIDE) + across(qw, VP) * ret_s[r, hv]
            mean = jnp.sum(ret, axis=1, keepdims=True) * (1.0 / VD)
            centered = ret - mean
            square = jnp.sum(centered * centered, axis=1, keepdims=True)
            var = (square - (VP - VD) * (mean * mean)) * (1.0 / VD)
            inv = lax.rsqrt(var + 1.0 * KD)
            nh = centered * inv
            g = gate[r, hv].astype(WIDE)
            sg = 0.5 * jnp.tanh(0.5 * g) + 0.5
            sl = g * sg
            mixed[r, hv] = (nh * sl).astype(LOW)
            norm_s[r, hv] = nh
            silu_s[r, hv] = sl
            slope_s[r, hv] = nh * (sg + sl * (1.0 - sg))
            inv_s[h, r, :] = jnp.broadcast_to(inv, (CHUNK, 128))

        add([functools.partial(gated, h, r) for r in chunks() for h in range(H)])

        def project(lo, hi):
            res_s[rs, lo:hi] = dot(mixed[rs, :], w[w_out[0] : w_out[1], lo:hi])

        add([functools.partial(project, *piece) for piece in pieces(width)])

        def norm(r):
            resid = tok[r, :].astype(WIDE) + res_s[r, :]
            r2 = lax.rsqrt(jnp.mean(resid * resid, axis=1, keepdims=True) + EPS)
            res_s[r, :] = resid
            hid2[r, :] = (resid * r2 * gain).astype(LOW)
            inv_s[H, r, :] = jnp.broadcast_to(r2, (CHUNK, 128))

        add([functools.partial(norm, r) for r in chunks()])

        def forward(place, source, at, lo, hi):
            ff_s[place, rs, lo:hi] = dot_nt(source[rs, :], w[at[0] + lo : at[0] + hi, :])

        add(
            [
                functools.partial(forward, place, source, at, *piece)
                for piece in pieces(ff)
                for place, source, at in ((0, hid2, w_gate), (1, hid2, w_up), (2, cot, w_down))
            ]
        )

        def gelu(r, lo, hi):
            gf, uf, gp = ff_s[0, r, lo:hi], ff_s[1, r, lo:hi], ff_s[2, r, lo:hi]
            e = jnp.exp(-0.5 * (gf * gf))
            d = 1.0 / (1.0 + (0.3275911 * math.sqrt(0.5)) * jnp.abs(gf))
            poly = d * (
                0.5 * 0.254829592
                + d
                * (
                    0.5 * -0.284496736
                    + d * (0.5 * 1.421413741 + d * (0.5 * -1.453152027 + d * (0.5 * 1.061405429)))
                )
            )
            tail = poly * e
            cdf = jnp.where(gf >= 0.0, 1.0 - tail, tail)
            ge = gf * cdf
            dge = cdf + gf * (e * (1.0 / math.sqrt(2.0 * math.pi)))
            prod[r, lo:hi] = (ge * uf).astype(LOW)
            dgate[r, lo:hi] = (gp * uf * dge).astype(LOW)
            dup[r, lo:hi] = (gp * ge).astype(LOW)

        add([functools.partial(gelu, r, *piece) for r in chunks() for piece in pieces(ff, 512)])

        def down(lo, hi):
            low_s[0, rs, lo:hi] = dot(prod[rs, :], w[w_down[0] : w_down[1], lo:hi])

        def hidden(lo, hi):
            low_s[1, rs, lo:hi] = dot(dgate[rs, :], w[w_gate[0] : w_gate[1], lo:hi]) + dot(
                dup[rs, :], w[w_up[0] : w_up[1], lo:hi]
            )

        add([functools.partial(step, *piece) for piece in pieces(width) for step in (down, hidden)])

        def residual(r):
            resid = res_s[r, :]
            r2 = across(inv_s[H, r, :], width)
            tok_out[r, :] = (resid + low_s[0, r, :]).astype(LOW)
            gh = low_s[1, r, :] * gain
            xhat = resid * r2
            inner_product = jnp.mean(gh * xhat, axis=1, keepdims=True)
            glow[r, :] = (cot[r, :].astype(WIDE) + r2 * (gh - xhat * inner_product)).astype(LOW)

        add([functools.partial(residual, r) for r in chunks()])

        def mix_back(lo, hi):
            ret_s[rs, lo:hi] = dot_nt(glow[rs, :], w[w_out[0] + lo : w_out[0] + hi, :])

        add([functools.partial(mix_back, *piece) for piece in pieces(vp)])

        def gated_back(h, r):
            hv = slice(h * VP, (h + 1) * VP)
            gm = ret_s[r, hv]
            nh = norm_s[r, hv]
            ggate[r, hv] = (gm * slope_s[r, hv]).astype(LOW)
            gn = gm * silu_s[r, hv]
            one = jnp.sum(gn, axis=1, keepdims=True) * (1.0 / VD)
            two = jnp.sum(gn * nh, axis=1, keepdims=True) * (1.0 / VD)
            gret[r, hv] = (across(inv_s[h, r, :], VP) * (gn - one - nh * two)).astype(LOW)

        add([functools.partial(gated_back, h, r) for r in chunks() for h in range(H)])
        return lists

    first, second = phases(0), phases(TILE)
    for k in range(len(first) + 1):
        interleaved(first[k] if k < len(first) else [], second[k - 1] if k else [])
    for h in range(H):
        add = dot_tn(queries[:, h * KD : (h + 1) * KD], gret[:, h * VP : (h + 1) * VP])
        dst[h] = add
        sums[c, h] = add

    @pl.when(c == count - 1)
    def _():
        for h in range(H):
            total = sums[count - 1, h]
            for b in reversed(range(count - 1)):
                prev = seg_s[seq, b * BLOCK - 1] if b > 0 else in_last[seq]
                joined = jnp.logical_and(
                    seg_s[seq, b * BLOCK] == seg_s[seq, (b + 1) * BLOCK - 1],
                    seg_s[seq, b * BLOCK] == prev,
                )
                factor = jnp.exp(jnp.full((1, 1), decay[h] * BLOCK, WIDE))
                total = jnp.where(joined, factor * total, 0.0) + sums[b, h]
            leave[h] = total.astype(LOW)


def middle(seqs, length, ff, data, seg_col, segments, in_last, decay, w, gains, got, kv):
    intra, gate, q, tokens, cotangent = data
    rows, width = tokens.shape
    count = length // BLOCK
    vp = H * VP
    outs = [width, width, ff, ff, ff, vp, width, vp, vp]
    inputs = [decay, segments, in_last, intra, gate, q, tokens, cotangent, seg_col, w, gains, *got, kv]
    specs = [smem()] * 3 + [row_block(n) for n in (vp, vp, H * KD, width, width, 1)]
    specs += [whole(w.shape), whole(gains.shape), *[seq_block(count)] * 3]
    specs += [state_block(count, lambda c: jnp.maximum(c - 1, 0))]
    one = (H, KD, VP)
    states = (seqs, count, *one)
    return pl.pallas_call(
        functools.partial(middle_kernel, count, ff),
        grid=(seqs * count,),
        out_shape=[shape((rows, n), LOW) for n in outs]
        + [shape(states, LOW), shape(states, WIDE), shape((seqs, *one), LOW)],
        in_specs=specs,
        out_specs=[row_block(n) for n in outs]
        + [state_block(count)] * 2
        + [seq_block(count)],
        scratch_shapes=[
            VMEM(one, WIDE),
            VMEM(one, LOW),
            VMEM((BLOCK, H * KD), LOW),
            VMEM((H, BLOCK, 128), WIDE),
            VMEM((BLOCK, vp), WIDE),
            VMEM((BLOCK, vp), WIDE),
            VMEM((BLOCK, vp), WIDE),
            VMEM((BLOCK, vp), WIDE),
            VMEM((H + 1, BLOCK, 128), WIDE),
            VMEM((BLOCK, width), WIDE),
            VMEM((3, BLOCK, ff), WIDE),
            VMEM((2, BLOCK, width), WIDE),
            VMEM(states[1:], WIDE),
        ],
        compiler_params=params(),
        cost_estimate=cost(2 * rows * width * (2 * vp + 6 * ff), 30 * rows * width),
    )(*inputs)


def weight_kernel(plan, count, split, me_ref, *refs):
    ins, outs, total = refs[:count], refs[count:-1], refs[-1]
    t = pl.program_id(0)
    last = pl.num_programs(0) - 1
    for left, right, cuts in plan:
        a, b = ins[left], ins[right]
        for source, row, size in cuts:
            add = dot_tn(a[:, source : source + size], b[...])

            @pl.when(t == 0)
            def _():
                total[row : row + size, :] = add

            @pl.when(t > 0)
            def _():
                total[row : row + size, :] += add

    @pl.when(t == last)
    def _():
        if not split:
            shards, _, lanes = outs[0].shape
            for part in range(shards):
                outs[0][part] = total[:, part * lanes : (part + 1) * lanes].astype(LOW)
            return
        lanes = outs[0].shape[2]
        used = total.shape[0]
        for part in range(2 * outs[0].shape[0]):
            target = outs[part & 1]
            lane = pl.multiple_of(jnp.bitwise_xor(me_ref[0], part) * lanes, lanes)
            target[part >> 1, :used, :] = total[:, pl.ds(lane, lanes)].astype(LOW)
            if used < target.shape[1]:
                target[part >> 1, used:, :] = jnp.zeros((target.shape[1] - used, lanes), LOW)


def weight_grads(arrays, plan, me, shards, split=0):
    rows = arrays[0].shape[0]
    used = max(row + size for left, right, cuts in plan for source, row, size in cuts)
    width = arrays[plan[0][1]].shape[1]
    tile = 2 * BLOCK
    block = lambda n: pl.BlockSpec((tile, n), lambda t: (t, 0))
    if split:
        outs = [(shards // 2, split, width // shards)] * 2
    else:
        outs = [(shards, used, width // shards)]
    return pl.pallas_call(
        functools.partial(weight_kernel, plan, len(arrays), split),
        grid=(rows // tile,),
        out_shape=[shape(dims, LOW) for dims in outs],
        in_specs=[smem()] + [block(item.shape[1]) for item in arrays],
        out_specs=[pl.BlockSpec(dims, lambda t: (0,) * len(dims)) for dims in outs],
        scratch_shapes=[VMEM((used, width), WIDE)],
        compiler_params=params(),
        cost_estimate=cost(2 * rows * used * width, 2 * rows * sum(i.shape[1] for i in arrays)),
    )(me, *arrays)


def back_kernel(count, decay, seg_s, in_last, *refs):
    (q, k, v, gret, cos, sin, seg, seg_row, st, dst, *got) = refs[:13]
    (dq, dk, dv, state, weights, grads) = refs[13:]
    seq = pl.program_id(0) // count
    c = count - 1 - pl.program_id(0) % count

    @pl.when(c == count - 1)
    def _():
        for h in range(H):
            state[h] = entering(decay, count * BLOCK, h, got)

    for b in range(1, count):

        @pl.when(c == b - 1)
        def _():
            prev = seg_s[seq, b * BLOCK - 1]
            first = seg_s[seq, b * BLOCK]
            last = seg_s[seq, (b + 1) * BLOCK - 1]
            joined = jnp.logical_and(first == last, first == prev)
            for h in range(H):
                factor = jnp.exp(jnp.full((1, 1), decay[h] * BLOCK, WIDE))
                state[h] = jnp.where(joined, factor * state[h], 0.0) + dst[h]

    start = c * BLOCK
    before = jnp.where(c > 0, seg_s[seq, jnp.maximum(start - 1, 0)], in_last[seq])
    final = seg_s[seq, start + BLOCK - 1]
    here = (seg[...] == before).astype(WIDE)
    ends = (seg[...] == final).astype(WIDE)
    place = column(BLOCK)
    dqs, dks = [], []
    for h in range(H):
        a = decay[h]
        qh = q[:, h * KD : (h + 1) * KD]
        kh = k[:, h * KD : (h + 1) * KD]
        vh = v[:, h * VP : (h + 1) * VP]
        gh = gret[:, h * VP : (h + 1) * VP]
        qw = jnp.exp(a * (place + 1.0)) * here
        kw = jnp.exp(a * (BLOCK - 1.0 - place)) * ends
        parts = []
        for i in range(BLOCK // TILE):
            top, reach = i * TILE, (i + 1) * TILE
            mix = mixing(a, top, TILE, seg, seg_row)
            s = dot_nt(qh[top:reach, :], kh[:reach, :])
            weights[top:reach, :reach] = (s * mix).astype(LOW)
            gs = (dot_nt(gh[top:reach, :], vh[:reach, :]) * mix).astype(LOW)
            grads[top:reach, :reach] = gs
            parts.append(dot(gs, kh[:reach, :]))
        late = state[h].astype(LOW)
        dqs.append(jnp.concatenate(parts) + qw * dot_nt(gh, st[h]))
        parts, values = [], []
        for i in range(BLOCK // TILE):
            top, reach = i * TILE, (i + 1) * TILE
            parts.append(dot_tn(grads[top:, top:reach], qh[top:, :]))
            values.append(dot_tn(weights[top:, top:reach], gh[top:, :]))
        dks.append(jnp.concatenate(parts) + kw * dot_nt(vh, late))
        dv[:, h * VP : (h + 1) * VP] = (jnp.concatenate(values) + kw * dot(kh, late)).astype(LOW)
    dq[...] = rotated(jnp.concatenate(dqs, axis=1), cos[...], -sin[...]).astype(LOW)
    dk[...] = rotated(jnp.concatenate(dks, axis=1), cos[...], -sin[...]).astype(LOW)


def back(seqs, length, data, cos, sin, seg_col, seg_row, segments, in_last, decay, st, dst, got):
    rows = data[0].shape[0]
    count = length // BLOCK
    turn = lambda t: (t // count) * count + count - 1 - t % count
    block = lambda n: pl.BlockSpec((BLOCK, n), lambda t: (turn(t), 0))
    table = pl.BlockSpec((BLOCK, KD // 2), lambda t: (count - 1 - t % count, 0))
    outs = [H * KD, H * KD, H * VP]
    inputs = [decay, segments, in_last, *data, cos, sin, seg_col, seg_row, st, dst, *got]
    specs = [smem()] * 3 + [block(item.shape[1]) for item in data] + [table, table, block(1)]
    specs += [pl.BlockSpec((None, 1, BLOCK), lambda t: (turn(t), 0, 0))]
    specs += [state_block(count, lambda c: count - 1 - c)]
    specs += [state_block(count, lambda c: jnp.minimum(count - c, count - 1))]
    specs += [seq_block(count)] * 3
    return pl.pallas_call(
        functools.partial(back_kernel, count),
        grid=(seqs * count,),
        out_shape=[shape((rows, n), LOW) for n in outs],
        in_specs=specs,
        out_specs=[block(n) for n in outs],
        scratch_shapes=[
            VMEM((H, KD, VP), WIDE),
            VMEM((BLOCK, BLOCK), LOW),
            VMEM((BLOCK, BLOCK), LOW),
        ],
        compiler_params=params(),
        cost_estimate=cost(rows * H * 2 * BLOCK * 3 * (KD + VP), 16 * rows * H * VP),
    )(*inputs)


def input_kernel(dq, dk, dv, ggate, tok, glow, w_kv, w_qg, gains, *rest):
    out = rest[-1]
    kd = H * KD
    gh = dot(dq[...], w_qg[:kd, :]) + dot(dk[...], w_kv[:kd, :])
    gh += dot(dv[...], w_kv[kd:, :]) + dot(ggate[...], w_qg[kd:, :])
    x = tok[...].astype(WIDE)
    r = lax.rsqrt(jnp.mean(x * x, axis=1, keepdims=True) + EPS)
    xhat = x * r
    gh = gh * gains[0:1, :].astype(WIDE)
    inner_product = jnp.mean(gh * xhat, axis=1, keepdims=True)
    out[...] = (glow[...].astype(WIDE) + r * (gh - xhat * inner_product)).astype(LOW)


def input_grad(part, parts, dq, dk, dv, ggate, tokens, glow, w_kv, w_qg, gains, earlier):
    rows, width = tokens.shape
    steps = rows // BLOCK // parts
    arrays = [dq, dk, dv, ggate, tokens, glow]
    block = lambda item: pl.BlockSpec((BLOCK, item.shape[1]), lambda t: (part * steps + t, 0))
    inputs = [*arrays, w_kv, w_qg, gains]
    specs = [block(item) for item in arrays] + [whole(item.shape) for item in (w_kv, w_qg, gains)]
    aliases = {}
    if earlier is not None:
        aliases = {len(inputs): 0}
        inputs.append(earlier)
        specs.append(pl.BlockSpec(memory_space=pl.ANY))
    return pl.pallas_call(
        input_kernel,
        grid=(steps,),
        out_shape=shape((rows, width), LOW),
        in_specs=specs,
        out_specs=block(tokens),
        input_output_aliases=aliases,
        compiler_params=params(),
        cost_estimate=cost(2 * rows * width * 2 * w_kv.shape[0] // parts, 20 * rows * width // parts),
    )(*inputs)


def adam_step(master, moment, second, grad, scale, rate, decay_weight):
    clipped = grad * scale
    moment_new = BETA_ONE * moment + (1.0 - BETA_ONE) * clipped
    second_new = BETA_TWO * second + (1.0 - BETA_TWO) * clipped * clipped
    corrected = (
        moment_new
        * (1.0 / (1.0 - BETA_ONE**STEP))
        / (jnp.sqrt(second_new * (1.0 / (1.0 - BETA_TWO**STEP))) + ADAM_EPS)
    )
    return (master - rate * (corrected + decay_weight * master), moment_new, second_new)


def squares_kernel(vd, ff, one, two, three, w_qk, w_vg, w_gu, low_gains, grad_gains, total):
    kd = H * KD

    def rows(source, start, size):
        return source[start : start + size, :].astype(WIDE)

    def product(weight, grad):
        return jnp.sum(weight.astype(LOW).astype(WIDE) * grad, axis=0, keepdims=True)

    sums = []

    def square(item):
        sums.append(jnp.sum(item * item, axis=0, keepdims=True))
        return item

    first = jnp.zeros((1, low_gains.shape[1]), WIDE)
    for i in range(2):
        grad = square(rows(three, i * kd, kd))
        first += jnp.sum(w_qk[i].astype(LOW).astype(WIDE).T * grad, axis=0, keepdims=True)
    first += product(w_vg[0], square(rows(three, 2 * kd, vd)))
    first += product(w_vg[1], square(rows(two, vd, vd)))
    square(rows(two, 0, vd))
    square(rows(one, 0, ff))
    second = product(w_gu[0], square(rows(one, ff, ff)))
    second += product(w_gu[1], square(rows(one, 2 * ff, ff)))
    gains = jnp.concatenate([first, second]) / low_gains[...].astype(LOW).astype(WIDE)
    grad_gains[...] = gains
    sums.append(jnp.sum(gains * gains, axis=0, keepdims=True))
    total[...] = jnp.broadcast_to(jnp.sum(sum(sums), axis=1, keepdims=True), total.shape)


def squares(vd, ff, grads, w_qk, w_vg, w_gu, gains):
    return pl.pallas_call(
        functools.partial(squares_kernel, vd, ff),
        out_shape=[shape(gains.shape, WIDE), shape((8, 128), WIDE)],
        in_specs=[pl.BlockSpec(memory_space=VMEM)] * 7,
        out_specs=[pl.BlockSpec(memory_space=VMEM)] * 2,
        compiler_params=params(),
    )(*grads, w_qk, w_vg, w_gu, gains)


def update_kernel(vd, ff, *refs):
    totals, (one, two, three, gain_grads) = refs[:4], refs[4:8]
    sources, targets, norm_out = refs[8:26], refs[26:44], refs[44]
    ins, outs = refs[45:63], refs[63:81]
    arrived, sent = refs[81:]
    kd = H * KD
    order = [4, 3, 2, 1, 0, 5]
    places = [6 * group + place for place in order for group in range(3)]
    fetch = {i: pltpu.make_async_copy(sources[i], ins[i], arrived.at[i]) for i in places}
    send = {i: pltpu.make_async_copy(outs[i], targets[i], sent.at[i]) for i in places}
    for i in places:
        fetch[i].start()
    norm = jnp.sqrt((totals[0][...] + totals[1][...]) + (totals[2][...] + totals[3][...]))
    norm_out[0, 0] = jnp.max(norm)
    scale = jnp.minimum(1.0, CLIP / (norm + 1e-06))[0:1, 0:1]

    def step(place, at, grad, rate, decay_weight):
        results = adam_step(
            ins[place][at], ins[6 + place][at], ins[12 + place][at], grad, scale, rate, decay_weight
        )
        for group, result in enumerate(results):
            outs[6 * group + place][at] = result

    def rows(source, start, size):
        return source[start : start + size, :].astype(WIDE)

    grads = {
        4: [(..., lambda: rows(one, 0, ff))],
        3: [(0, lambda: rows(one, ff, ff)), (1, lambda: rows(one, 2 * ff, ff))],
        2: [(..., lambda: rows(two, 0, vd))],
        1: [(0, lambda: rows(three, 2 * kd, vd)), (1, lambda: rows(two, vd, vd))],
        0: [(0, lambda: rows(three, 0, kd).T), (1, lambda: rows(three, kd, kd).T)],
        5: [(..., lambda: gain_grads[...])],
    }
    for place in order:
        for group in range(3):
            fetch[6 * group + place].wait()
        rate, decay_weight = (GAIN_RATE, 0.0) if place == 5 else (MATRIX_RATE, DECAY_WEIGHT)
        for at, grad in grads[place]:
            step(place, at, grad(), rate, decay_weight)
        for group in range(3):
            send[6 * group + place].start()
    for i in places:
        send[i].wait()


def update(vd, ff, totals, grads, gain_grads, arrays):
    anywhere = pl.BlockSpec(memory_space=pl.ANY)
    return pl.pallas_call(
        functools.partial(update_kernel, vd, ff),
        out_shape=[shape(item.shape, WIDE) for item in arrays] + [shape((1, 1), WIDE)],
        in_specs=[pl.BlockSpec(memory_space=VMEM)] * 8 + [anywhere] * 18,
        out_specs=[anywhere] * 18 + [smem()],
        scratch_shapes=[VMEM(item.shape, WIDE) for item in arrays] * 2
        + [pltpu.SemaphoreType.DMA((18,))] * 2,
        compiler_params=params(),
    )(*totals, *grads, gain_grads, *arrays)


def on_device(
    tokens,
    cotangent,
    segments,
    log_decay,
    w_qk,
    w_vg,
    w_out,
    w_gu,
    w_down,
    norm_gains,
    *states,
):
    turned = lambda item: jnp.swapaxes(item, 1, 2)
    shards = lax.axis_size("shard")
    me = lax.axis_index("shard").reshape(1)
    seqs, length, width = tokens.shape
    rows = seqs * length
    kd, vd, ff = H * KD, H * VD, w_down.shape[0]
    vp = H * VP
    vg_t, gu_t = turned(w_vg), turned(w_gu)

    low = lambda item: item.astype(LOW)
    def heads(item):
        return [
            jnp.pad(item[h * VD : (h + 1) * VD], ((0, VP - VD), (0, 0))) for h in range(H)
        ]

    first = jnp.concatenate(
        [low(w_qk[1]).T, low(vg_t[0]), jnp.pad(low(norm_gains), ((0, 14), (0, 0)))]
    )
    second = jnp.concatenate([low(w_qk[0]).T, *heads(low(vg_t[1]))])
    third = jnp.concatenate([low(w_out), low(gu_t[0]), low(gu_t[1]), low(w_down)])
    first_held = gather_shards(first)
    second = after(second, first_held[1][2])
    w_qg = lax.all_gather(second, "shard", axis=1, tiled=True)
    side = (lax.axis_index("dp") & 1).reshape(1)
    third_held, sent = gather_halves(third, side, second)

    half_width = KD // 2
    freq_rates = jnp.exp(-math.log(10000.0) * jnp.arange(half_width).astype(WIDE) / half_width)
    positions = (lax.axis_index("shard") * length + jnp.arange(length)).astype(WIDE)
    angles = positions[:, None] * freq_rates[None, :]
    cos, sin = jnp.cos(angles), jnp.sin(angles)

    tok = tokens.reshape(rows, width)
    cot = cotangent.reshape(rows, width)
    seg_col = segments.reshape(rows, 1)
    seg_row = segments.reshape(rows // BLOCK, 1, BLOCK)
    in_last = jnp.where(lax.axis_index("shard") > 0, segments[:, 0], -1)
    decay = log_decay

    def tick(*done):
        nonlocal decay, me, gains
        decay, me, gains = lax.optimization_barrier((decay, me, gains, *done))[:3]

    plan = [(0, 0, 0, kd)] + [(kd + h * VD, 0, kd + h * VP, VD) for h in range(H)]
    plan += [(kd + vd, 1, 0, 16)]
    fills = [(0, kd + h * VP + VD, VP - VD) for h in range(H)]
    w_kv, gains = assemble(first_held, plan, fills, [kd + vp, 16], width, me, side)
    tick(sent)
    hid, k, v, kv, leaving = front(
        seqs, length, tok, seg_col, segments, decay, w_kv, gains, cos, sin
    )
    passing = Passing(leaving, False)
    tick(leaving)
    tick(passing.turn(decay, length))
    q, intra, gate = inner(k, v, hid, w_qg, cos, sin, seg_col, seg_row, decay, length)
    tick(q)
    passing.finish(q)
    plan = [(h * VD, 0, h * VP, VD) for h in range(H)] + [(vd, 0, vp, 3 * ff)]
    fills = [(0, h * VP + VD, VP - VD) for h in range(H)]
    (w_rest,) = assemble(third_held, plan, fills, [vp + 3 * ff], width, me, side)
    tick(w_rest)
    tokens_out, hid2, prod, dgate, dup, mixed, glow, ggate, gret, st, dst, leaving = middle(
        seqs, length, ff, (intra, gate, q, tok, cot), seg_col, segments, in_last, decay,
        w_rest, gains, passing.got, kv,
    )
    returning = Passing(leaving, True)
    tick(leaving)

    def halves(row):
        return [(h * VP, row + h * VD, VD) for h in range(H)]

    fit = lambda used: used + -used % (16 * lax.axis_size("dp"))
    plan = [(0, 1, [(0, 0, ff)]), (2, 3, [(0, ff, ff)]), (4, 3, [(0, 2 * ff, ff)])]
    made = weight_grads([prod, cot, dgate, hid2, dup], plan, me, shards, fit(3 * ff))
    one = Staged(*made)
    tick(made[0])
    tick(returning.turn(decay, length))
    plan = [(0, 1, halves(0)), (2, 3, halves(vd))]
    made = weight_grads([mixed, glow, ggate, hid], plan, me, shards, fit(2 * vd))
    two = Staged(*made)
    tick(made[0])
    returning.finish(made[0])
    tick(one.cross())
    dq, dk, dv = back(
        seqs, length, (q, k, v, gret), cos, sin, seg_col, seg_row, segments, in_last, decay,
        st, dst, returning.got,
    )
    tick(dq)
    tick(one.halve(), two.cross())
    plan = [(0, 3, [(0, 0, kd)]), (1, 3, [(0, kd, kd)]), (2, 3, halves(2 * kd))]
    made = weight_grads([dq, dk, dv, hid], plan, me, shards, fit(2 * kd + vd))
    three = Staged(*made)
    tick(made[0])
    tick(one.scatter(), two.halve())
    tick(three.cross())
    grad_input = None
    for part in range(2):
        grad_input = input_grad(
            part, 2, dq, dk, dv, ggate, tok, glow, w_kv, w_qg, gains, grad_input
        )
        if part == 0:
            one.parts, two.other = lax.optimization_barrier((one.parts, two.other, grad_input))[:2]
            tick(one.gather(), two.scatter(), grad_input)
    three.far, two.parts, one.half = lax.optimization_barrier(
        (three.far, two.parts, one.half, grad_input)
    )[:3]
    three.halve()
    one.double()
    two.gather()
    three.scatter()
    two.double()
    three.gather()
    three.double()
    grads = (one.result(), two.result(), three.result())

    gain_grads, total = squares(vd, ff, grads, w_qk, vg_t, gu_t, norm_gains)
    others = [
        lax.ppermute(total, "shard", [(i, i ^ mask) for i in range(shards)]) for mask in (1, 2, 3)
    ]
    arrays = []
    for group in ((w_qk, w_vg, w_out, w_gu, w_down, norm_gains), states[:6], states[6:]):
        arrays += [turned(item) if i in (1, 3) else item for i, item in enumerate(group)]
    *results, norm = update(vd, ff, [total, *others], grads, gain_grads, arrays)
    results = [turned(item) if i % 6 in (1, 3) else item for i, item in enumerate(results)]
    return (
        tokens_out.reshape(tokens.shape),
        grad_input.reshape(tokens.shape),
        *results,
        norm.reshape(()),
    )


def solution(mesh):
    split = P("dp", "shard", None)
    rows, columns = P(None, "shard", None), P(None, "shard")
    group = (rows, rows, columns, rows, columns, columns)
    in_specs = (split, split, P("dp", "shard"), P()) + group * 3
    out_specs = (split, split) + group * 3 + (P(),)
    return jax.shard_map(
        on_device, mesh=mesh, in_specs=in_specs, out_specs=out_specs, check_vma=False
    )
```

```python
import functools
import math

import jax
import jax.numpy as jnp
from jax import lax
from jax.experimental import pallas as pl
from jax.experimental.pallas import tpu as pltpu
from jax.sharding import PartitionSpec as P

H = 2
KD = 256
VD = 432
VP = 512
BLOCK = 512
STEP = 10

EPS = 1e-05
ADAM_EPS = 1e-08
BETA_ONE = 0.9
BETA_TWO = 0.95
MATRIX_RATE = 0.15
GAIN_RATE = 1.0
DECAY_WEIGHT = 0.1
CLIP = 1.0

LOW = jnp.bfloat16
WIDE = jnp.float32
VMEM = pltpu.VMEM
SMEM = pltpu.SMEM
LIMIT = 60 * 1024 * 1024


def dot(a, b):
    return jnp.dot(a, b, preferred_element_type=WIDE)


def dot_nt(a, b):
    return lax.dot_general(a, b, (((1,), (1,)), ((), ())), preferred_element_type=WIDE)


def dot_tn(a, b):
    return lax.dot_general(a, b, (((0,), (0,)), ((), ())), preferred_element_type=WIDE)


def params(**more):
    return pltpu.CompilerParams(vmem_limit_bytes=LIMIT, **more)


def cost(flops, moved):
    return pl.CostEstimate(flops=int(flops), bytes_accessed=int(moved), transcendentals=0)


def smem():
    return pl.BlockSpec(memory_space=SMEM)


def whole(shape):
    return pl.BlockSpec(shape, lambda *at: (0,) * len(shape), pipeline_mode=pl.Buffered(1))


def shape(dims, kind):
    return jax.ShapeDtypeStruct(dims, kind)


def bits_of(axis):
    return (lax.axis_size(axis) - 1).bit_length()


def exchange(value, axis, bit):
    size = lax.axis_size(axis)
    return lax.ppermute(value, axis, [(i, i ^ (1 << bit)) for i in range(size)])


def gather_shards(own):
    held = [(0, own)]
    for bit in reversed(range(bits_of("shard"))):
        held += [(mask | (1 << bit), exchange(part, "shard", bit)) for mask, part in held]
    return [(mask, None, part) for mask, part in held]


def gather_halves(own, side, first):
    rows = own.shape[0] // 2
    send = after(lax.dynamic_slice_in_dim(own, side[0] * rows, rows, 0), first)
    here = exchange(send, "shard", 1)
    there = exchange(here, "dp", 0)
    held = [(0, None, own), (1, None, exchange(own, "shard", 0))]
    held += [(2, 0, here), (2, 1, there)]
    held += [(3, 0, exchange(here, "shard", 0)), (3, 1, exchange(there, "shard", 0))]
    return held, send


def add_low(one, two):
    return (one.astype(WIDE) + two.astype(WIDE)).astype(LOW)


def shifted(value, shift):
    size = lax.axis_size("dp")
    return lax.ppermute(value, "dp", [(i, (i + 2 * shift) % size) for i in range(size)])


class Reduction:
    def __init__(self, keep, send):
        self.keep = keep
        self.near = exchange(send, "shard", 0)

    def cross(self, *done):
        near = after(self.near, *done)
        self.near = near
        low = add_low(self.keep[1], near[1])
        self.far = exchange(low, "shard", 1)
        return low

    def halve(self, *done):
        far = after(self.far, *done)
        rows = far.shape[0] // 2

        def total(at):
            parts = (self.keep[0, at], self.near[0, at], far[at])
            return sum(part.astype(WIDE) for part in parts).astype(LOW)

        self.mine = total(slice(0, rows))
        send = total(slice(rows, 2 * rows))
        self.other = exchange(send, "dp", 0)
        return send

    def scatter(self, *done):
        other = after(self.other, *done)
        copies = lax.axis_size("dp") // 2
        rows = other.shape[0] // copies
        at = [slice(k * rows, (k + 1) * rows) for k in range(copies)]
        pieces = [add_low(self.mine[place], other[place]) for place in at]
        self.piece = pieces[0]
        self.parts = [shifted(pieces[k], k) for k in range(1, copies)]
        return pieces[-1]

    def gather(self, *done):
        parts = lax.optimization_barrier((*self.parts, *done))[: len(self.parts)]
        self.part = sum(part.astype(WIDE) for part in (self.piece, *parts)).astype(LOW)
        self.parts = [shifted(self.part, k) for k in range(1, len(parts) + 1)]
        return self.part

    def double(self, *done):
        parts = lax.optimization_barrier((*self.parts, *done))[: len(self.parts)]
        self.here = jnp.concatenate([self.part, *parts])
        self.there = exchange(self.here, "dp", 0)
        return self.here

    def result(self):
        return self.here, self.there


class Passing:
    def __init__(self, local, reverse):
        self.local = local
        steps = [[(0, 1), (2, 3)], [(1, 2)], [(2, 3)]]
        if reverse:
            steps = [[(3 - a, 3 - b) for a, b in step] for step in steps]
        self.steps = steps
        self.got = [lax.ppermute(local, "shard", steps[0])]

    def turn(self, decay, length, *done):
        self.got[0] = after(self.got[0], *done)
        total = combine(decay, length, self.local, self.got[0])
        self.got.append(lax.ppermute(total, "shard", self.steps[1]))
        return total

    def finish(self, *done):
        self.got.append(lax.ppermute(after(self.got[1], *done), "shard", self.steps[2]))


def entering(decay, length, h, got):
    factor = jnp.exp(jnp.full((1, 1), decay[h] * length, WIDE))
    wide = [item[h].astype(WIDE) for item in got]
    return wide[0] + wide[1] + factor * wide[2]


def after(value, *others):
    return lax.optimization_barrier((value, *others))[0]


def combine_kernel(length, decay, local, got, out):
    h = pl.program_id(0) % H
    factor = jnp.exp(jnp.full((1, 1), decay[h] * length, WIDE))
    out[...] = (local[...].astype(WIDE) + factor * got[...].astype(WIDE)).astype(LOW)


def combine(decay, length, local, got):
    block = pl.BlockSpec((None, None, KD, VP), lambda i: (i // H, i % H, 0, 0))
    return pl.pallas_call(
        functools.partial(combine_kernel, length),
        grid=(local.shape[0] * H,),
        out_shape=shape(local.shape, LOW),
        in_specs=[smem(), block, block],
        out_specs=block,
        compiler_params=params(),
        cost_estimate=cost(local.size, 6 * local.size),
    )(decay, local, got)


def assemble_kernel(plan, fills, sources_of, me_ref, side_ref, *refs):
    sources, outs = refs[: len(sources_of)], refs[len(sources_of) :]
    lanes = sources[0].shape[1]
    for index, row, size in fills:
        outs[index][row : row + size, :] = jnp.zeros((size, outs[index].shape[1]), LOW)

    def place(source, lane, low, high):
        for start, index, row, size in plan:
            begin, end = max(start, low), min(start + size, high)
            if begin < end:
                to = row + begin - start
                outs[index][to : to + end - begin, pl.ds(lane, lanes)] = source[
                    begin - low : end - low, :
                ]

    for (mask, half), source in zip(sources_of, sources):
        lane = pl.multiple_of(jnp.bitwise_xor(me_ref[0], mask) * lanes, lanes)
        rows = source.shape[0]
        if half is None:
            place(source, lane, 0, rows)
            continue
        for side in range(2):

            @pl.when(side_ref[0] == side)
            def _():
                low = (side ^ half) * rows
                place(source, lane, low, low + rows)


def assemble(held, plan, fills, heights, width, me, side):
    sources_of = [(mask, half) for mask, half, part in held]
    parts = [part for mask, half, part in held]
    return pl.pallas_call(
        functools.partial(assemble_kernel, plan, fills, sources_of),
        out_shape=[shape((rows, width), LOW) for rows in heights],
        in_specs=[smem()] * 2 + [pl.BlockSpec(memory_space=VMEM)] * len(parts),
        out_specs=[pl.BlockSpec(memory_space=VMEM)] * len(heights),
        compiler_params=params(),
        cost_estimate=cost(0, 4 * sum(heights) * width),
    )(me, side, *parts)


def rotated(flat, cosine, sine):
    half = KD // 2
    parts = []
    for h in range(H):
        u = flat[:, h * KD : h * KD + half]
        w = flat[:, h * KD + half : (h + 1) * KD]
        parts += [u * cosine - w * sine, w * cosine + u * sine]
    return jnp.concatenate(parts, axis=1)


def column(size):
    return lax.broadcasted_iota(jnp.int32, (size, 1), 0).astype(WIDE)


def front_kernel(count, decay, seg_s, tok, w, gains, cos, sin, seg, *rest):
    hid, k, v, kv, out_state, state = rest
    seq = pl.program_id(0) // count
    c = pl.program_id(0) % count
    x = tok[...].astype(WIDE)
    r = lax.rsqrt(jnp.mean(x * x, axis=1, keepdims=True) + EPS)
    h1 = (x * r * gains[0:1, :].astype(WIDE)).astype(LOW)
    hid[...] = h1
    kd = H * KD
    key = rotated(dot_nt(h1, w[:kd, :]), cos[...], sin[...]).astype(LOW)
    k[...] = key
    val = dot_nt(h1, w[kd : kd + H * VP, :]).astype(LOW)
    v[...] = val
    first = seg_s[seq, c * BLOCK]
    last = seg_s[seq, c * BLOCK + BLOCK - 1]
    before = seg_s[seq, jnp.maximum(c * BLOCK - 1, 0)]
    here = (seg[...] == last).astype(WIDE)
    joined = jnp.logical_and(jnp.logical_and(first == last, first == before), c > 0)
    for h in range(H):
        a = decay[h]
        kw = jnp.exp(a * (BLOCK - 1.0 - column(BLOCK))) * here
        kk = (key[:, h * KD : (h + 1) * KD].astype(WIDE) * kw).astype(LOW)
        add = dot_tn(kk, val[:, h * VP : (h + 1) * VP])
        kv[h] = add
        factor = jnp.exp(jnp.full((1, 1), a * BLOCK, WIDE))
        total = jnp.where(joined, factor * state[h], 0.0) + add
        state[h] = total
        out_state[h] = total.astype(LOW)


def row_block(width):
    return pl.BlockSpec((BLOCK, width), lambda t: (t, 0))


def state_block(count, at=lambda c: c):
    return pl.BlockSpec(
        (None, None, H, KD, VP), lambda t: (t // count, at(t % count), 0, 0, 0)
    )


def seq_block(count):
    return pl.BlockSpec((None, H, KD, VP), lambda t: (t // count, 0, 0, 0))


def front(seqs, length, tokens, seg_col, segments, decay, w, gains, cos, sin):
    count = length // BLOCK
    rows, width = tokens.shape
    outs = [width, H * KD, H * VP]
    table = pl.BlockSpec((BLOCK, KD // 2), lambda t: (t % count, 0))
    return pl.pallas_call(
        functools.partial(front_kernel, count),
        grid=(seqs * count,),
        out_shape=[shape((rows, n), LOW) for n in outs]
        + [shape((seqs, count, H, KD, VP), WIDE), shape((seqs, H, KD, VP), LOW)],
        in_specs=[smem(), smem(), row_block(width), whole(w.shape), whole(gains.shape)]
        + [table, table, row_block(1)],
        out_specs=[row_block(n) for n in outs]
        + [state_block(count), seq_block(count)],
        scratch_shapes=[VMEM((H, KD, VP), WIDE)],
        compiler_params=params(),
        cost_estimate=cost(2 * rows * width * w.shape[0], 12 * rows * width),
    )(decay, segments, tokens, w, gains, cos, sin, seg_col)


def decay_row(a):
    return jnp.exp(-a * lax.broadcasted_iota(jnp.int32, (1, BLOCK), 1).astype(WIDE))


def mixing(a, top, size, seg, seg_row):
    reach = top + size
    rows = jnp.exp(a * (column(size) + float(top)))
    same = seg[top:reach, :] == seg_row[:, :reach]
    n = lax.broadcasted_iota(jnp.int32, (size, reach), 0) + top
    m = lax.broadcasted_iota(jnp.int32, (size, reach), 1)
    return jnp.where(jnp.logical_and(same, n >= m), rows * decay_row(a)[:, :reach], 0.0)


TILE = 256


def inner_kernel(decay, k, v, hid, w, cos, sin, seg, seg_row, q, intra, gate):
    kd = H * KD
    query = rotated(dot_nt(hid[...], w[:kd, :]), cos[...], sin[...]).astype(LOW)
    q[...] = query
    gate[...] = dot_nt(hid[...], w[kd:, :]).astype(LOW)
    for i in range(BLOCK // TILE):
        top, reach = i * TILE, (i + 1) * TILE
        for h in range(H):
            s = dot_nt(query[top:reach, h * KD : (h + 1) * KD], k[:reach, h * KD : (h + 1) * KD])
            weights = (s * mixing(decay[h], top, TILE, seg, seg_row)).astype(LOW)
            intra[top:reach, h * VP : (h + 1) * VP] = dot(
                weights, v[:reach, h * VP : (h + 1) * VP]
            ).astype(LOW)


def inner(k, v, hid, w, cos, sin, seg_col, seg_row, decay, length):
    rows, width = hid.shape
    count = length // BLOCK
    block = lambda n: pl.BlockSpec((BLOCK, n), lambda t: (t, 0))
    table = pl.BlockSpec((BLOCK, KD // 2), lambda t: (t % count, 0))
    return pl.pallas_call(
        inner_kernel,
        grid=(rows // BLOCK,),
        out_shape=[shape((rows, n), LOW) for n in (H * KD, H * VP, H * VP)],
        in_specs=[
            smem(),
            block(H * KD),
            block(H * VP),
            block(width),
            whole(w.shape),
            table,
            table,
            block(1),
            pl.BlockSpec((None, 1, BLOCK), lambda t: (t, 0, 0)),
        ],
        out_specs=[block(n) for n in (H * KD, H * VP, H * VP)],
        compiler_params=params(),
        cost_estimate=cost(rows * (2 * width * 1536 + 2 * BLOCK * H * VP), 8 * rows * H * VP),
    )(decay, k, v, hid, w, cos, sin, seg_col, seg_row)


CHUNK = 16


def interleaved(first, second):
    steps = [((i + 0.5) / len(first), 0, step) for i, step in enumerate(first)]
    steps += [((i + 0.5) / len(second), 1, step) for i, step in enumerate(second)]
    for place, which, step in sorted(steps, key=lambda item: item[:2]):
        step()


def pieces(width, size=256):
    return [(start, min(start + size, width)) for start in range(0, width, size)]


def across(narrow, width):
    return jnp.concatenate([narrow] * (width // 128), axis=1)


def middle_kernel(count, ff, decay, seg_s, in_last, *refs):
    (intra, gate, q, tok, cot, seg, w, gains, *got, kv) = refs[:12]
    outs, scratch = refs[12:24], refs[24:]
    (tok_out, hid2, prod, dgate, dup, mixed, glow, ggate, gret, st_out, dst, leave) = outs
    (state, now, queries, factors, ret_s, norm_s, silu_s, slope_s, inv_s, res_s, ff_s, low_s, sums) = scratch
    seq = pl.program_id(0) // count
    c = pl.program_id(0) % count
    start = c * BLOCK
    vp = H * VP
    width = tok.shape[1]
    before = jnp.where(c > 0, seg_s[seq, jnp.maximum(start - 1, 0)], in_last[seq])

    @pl.when(c == 0)
    def _():
        for h in range(H):
            total = entering(decay, count * BLOCK, h, got)
            state[h] = total
            now[h] = total.astype(LOW)

    for b in range(1, count):

        @pl.when(c == b)
        def _():
            prev = seg_s[seq, (b - 1) * BLOCK - 1] if b > 1 else in_last[seq]
            joined = jnp.logical_and(
                seg_s[seq, (b - 1) * BLOCK] == seg_s[seq, b * BLOCK - 1],
                seg_s[seq, (b - 1) * BLOCK] == prev,
            )
            for h in range(H):
                factor = jnp.exp(jnp.full((1, 1), decay[h] * BLOCK, WIDE))
                total = jnp.where(joined, factor * state[h], 0.0) + kv[h]
                state[h] = total
                now[h] = total.astype(LOW)

    st_out[...] = now[...]
    here = (seg[...] == before).astype(WIDE)
    for h in range(H):
        qw = jnp.exp(decay[h] * (column(BLOCK) + 1.0)) * here
        factors[h] = jnp.broadcast_to(qw, (BLOCK, 128))

    w_out = (0, vp)
    w_gate = (vp, vp + ff)
    w_up = (vp + ff, vp + 2 * ff)
    w_down = (vp + 2 * ff, vp + 3 * ff)
    gain = gains[1:2, :].astype(WIDE)

    def phases(top):
        rs = pl.ds(top, TILE)
        lists = []

        def add(steps):
            lists.append(steps)

        def chunks():
            return [pl.ds(row, CHUNK) for row in range(top, top + TILE, CHUNK)]

        def cross(h, lo, hi):
            ret_s[rs, h * VP + lo : h * VP + hi] = dot(
                q[rs, h * KD : (h + 1) * KD], now[h, :, lo:hi]
            )

        add([functools.partial(cross, h, *piece) for h in range(H) for piece in pieces(VP)])

        def gated(h, r):
            hv = slice(h * VP, (h + 1) * VP)
            hk = slice(h * KD, (h + 1) * KD)
            qw = factors[h, r, :]
            queries[r, hk] = (q[r, hk].astype(WIDE) * across(qw, KD)).astype(LOW)
            ret = intra[r, hv].astype(WIDE) + across(qw, VP) * ret_s[r, hv]
            mean = jnp.sum(ret, axis=1, keepdims=True) * (1.0 / VD)
            centered = ret - mean
            square = jnp.sum(centered * centered, axis=1, keepdims=True)
            var = (square - (VP - VD) * (mean * mean)) * (1.0 / VD)
            inv = lax.rsqrt(var + 1.0 * KD)
            nh = centered * inv
            g = gate[r, hv].astype(WIDE)
            sg = 0.5 * jnp.tanh(0.5 * g) + 0.5
            sl = g * sg
            mixed[r, hv] = (nh * sl).astype(LOW)
            norm_s[r, hv] = nh
            silu_s[r, hv] = sl
            slope_s[r, hv] = nh * (sg + sl * (1.0 - sg))
            inv_s[h, r, :] = jnp.broadcast_to(inv, (CHUNK, 128))

        add([functools.partial(gated, h, r) for r in chunks() for h in range(H)])

        def project(lo, hi):
            res_s[rs, lo:hi] = dot(mixed[rs, :], w[w_out[0] : w_out[1], lo:hi])

        add([functools.partial(project, *piece) for piece in pieces(width)])

        def norm(r):
            resid = tok[r, :].astype(WIDE) + res_s[r, :]
            r2 = lax.rsqrt(jnp.mean(resid * resid, axis=1, keepdims=True) + EPS)
            res_s[r, :] = resid
            hid2[r, :] = (resid * r2 * gain).astype(LOW)
            inv_s[H, r, :] = jnp.broadcast_to(r2, (CHUNK, 128))

        add([functools.partial(norm, r) for r in chunks()])

        def forward(place, source, at, lo, hi):
            ff_s[place, rs, lo:hi] = dot_nt(source[rs, :], w[at[0] + lo : at[0] + hi, :])

        add(
            [
                functools.partial(forward, place, source, at, *piece)
                for piece in pieces(ff)
                for place, source, at in ((0, hid2, w_gate), (1, hid2, w_up), (2, cot, w_down))
            ]
        )

        def gelu(r, lo, hi):
            gf, uf, gp = ff_s[0, r, lo:hi], ff_s[1, r, lo:hi], ff_s[2, r, lo:hi]
            e = jnp.exp(-0.5 * (gf * gf))
            d = 1.0 / (1.0 + (0.3275911 * math.sqrt(0.5)) * jnp.abs(gf))
            poly = d * (
                0.5 * 0.254829592
                + d
                * (
                    0.5 * -0.284496736
                    + d * (0.5 * 1.421413741 + d * (0.5 * -1.453152027 + d * (0.5 * 1.061405429)))
                )
            )
            tail = poly * e
            cdf = jnp.where(gf >= 0.0, 1.0 - tail, tail)
            ge = gf * cdf
            dge = cdf + gf * (e * (1.0 / math.sqrt(2.0 * math.pi)))
            prod[r, lo:hi] = (ge * uf).astype(LOW)
            dgate[r, lo:hi] = (gp * uf * dge).astype(LOW)
            dup[r, lo:hi] = (gp * ge).astype(LOW)

        add([functools.partial(gelu, r, *piece) for r in chunks() for piece in pieces(ff, 512)])

        def down(lo, hi):
            low_s[0, rs, lo:hi] = dot(prod[rs, :], w[w_down[0] : w_down[1], lo:hi])

        def hidden(lo, hi):
            low_s[1, rs, lo:hi] = dot(dgate[rs, :], w[w_gate[0] : w_gate[1], lo:hi]) + dot(
                dup[rs, :], w[w_up[0] : w_up[1], lo:hi]
            )

        add([functools.partial(step, *piece) for piece in pieces(width) for step in (down, hidden)])

        def residual(r):
            resid = res_s[r, :]
            r2 = across(inv_s[H, r, :], width)
            tok_out[r, :] = (resid + low_s[0, r, :]).astype(LOW)
            gh = low_s[1, r, :] * gain
            xhat = resid * r2
            inner_product = jnp.mean(gh * xhat, axis=1, keepdims=True)
            glow[r, :] = (cot[r, :].astype(WIDE) + r2 * (gh - xhat * inner_product)).astype(LOW)

        add([functools.partial(residual, r) for r in chunks()])

        def mix_back(lo, hi):
            ret_s[rs, lo:hi] = dot_nt(glow[rs, :], w[w_out[0] + lo : w_out[0] + hi, :])

        add([functools.partial(mix_back, *piece) for piece in pieces(vp)])

        def gated_back(h, r):
            hv = slice(h * VP, (h + 1) * VP)
            gm = ret_s[r, hv]
            nh = norm_s[r, hv]
            ggate[r, hv] = (gm * slope_s[r, hv]).astype(LOW)
            gn = gm * silu_s[r, hv]
            one = jnp.sum(gn, axis=1, keepdims=True) * (1.0 / VD)
            two = jnp.sum(gn * nh, axis=1, keepdims=True) * (1.0 / VD)
            gret[r, hv] = (across(inv_s[h, r, :], VP) * (gn - one - nh * two)).astype(LOW)

        add([functools.partial(gated_back, h, r) for r in chunks() for h in range(H)])
        return lists

    first, second = phases(0), phases(TILE)
    for k in range(len(first) + 1):
        interleaved(first[k] if k < len(first) else [], second[k - 1] if k else [])
    for h in range(H):
        add = dot_tn(queries[:, h * KD : (h + 1) * KD], gret[:, h * VP : (h + 1) * VP])
        dst[h] = add
        sums[c, h] = add

    @pl.when(c == count - 1)
    def _():
        for h in range(H):
            total = sums[count - 1, h]
            for b in reversed(range(count - 1)):
                prev = seg_s[seq, b * BLOCK - 1] if b > 0 else in_last[seq]
                joined = jnp.logical_and(
                    seg_s[seq, b * BLOCK] == seg_s[seq, (b + 1) * BLOCK - 1],
                    seg_s[seq, b * BLOCK] == prev,
                )
                factor = jnp.exp(jnp.full((1, 1), decay[h] * BLOCK, WIDE))
                total = jnp.where(joined, factor * total, 0.0) + sums[b, h]
            leave[h] = total.astype(LOW)


def middle(seqs, length, ff, data, seg_col, segments, in_last, decay, w, gains, got, kv):
    intra, gate, q, tokens, cotangent = data
    rows, width = tokens.shape
    count = length // BLOCK
    vp = H * VP
    outs = [width, width, ff, ff, ff, vp, width, vp, vp]
    inputs = [decay, segments, in_last, intra, gate, q, tokens, cotangent, seg_col, w, gains, *got, kv]
    specs = [smem()] * 3 + [row_block(n) for n in (vp, vp, H * KD, width, width, 1)]
    specs += [whole(w.shape), whole(gains.shape), *[seq_block(count)] * 3]
    specs += [state_block(count, lambda c: jnp.maximum(c - 1, 0))]
    one = (H, KD, VP)
    states = (seqs, count, *one)
    return pl.pallas_call(
        functools.partial(middle_kernel, count, ff),
        grid=(seqs * count,),
        out_shape=[shape((rows, n), LOW) for n in outs]
        + [shape(states, LOW), shape(states, WIDE), shape((seqs, *one), LOW)],
        in_specs=specs,
        out_specs=[row_block(n) for n in outs]
        + [state_block(count)] * 2
        + [seq_block(count)],
        scratch_shapes=[
            VMEM(one, WIDE),
            VMEM(one, LOW),
            VMEM((BLOCK, H * KD), LOW),
            VMEM((H, BLOCK, 128), WIDE),
            VMEM((BLOCK, vp), WIDE),
            VMEM((BLOCK, vp), WIDE),
            VMEM((BLOCK, vp), WIDE),
            VMEM((BLOCK, vp), WIDE),
            VMEM((H + 1, BLOCK, 128), WIDE),
            VMEM((BLOCK, width), WIDE),
            VMEM((3, BLOCK, ff), WIDE),
            VMEM((2, BLOCK, width), WIDE),
            VMEM(states[1:], WIDE),
        ],
        compiler_params=params(),
        cost_estimate=cost(2 * rows * width * (2 * vp + 6 * ff), 30 * rows * width),
    )(*inputs)


def weight_kernel(plan, count, me_ref, *refs):
    ins, outs, total = refs[:count], refs[count:-1], refs[-1]
    t = pl.program_id(0)
    last = pl.num_programs(0) - 1
    for left, right, cuts in plan:
        a, b = ins[left], ins[right]
        for source, row, size in cuts:
            add = dot_tn(a[:, source : source + size], b[...])

            @pl.when(t == 0)
            def _():
                total[row : row + size, :] = add

            @pl.when(t > 0)
            def _():
                total[row : row + size, :] += add

    @pl.when(t == last)
    def _():
        lanes = outs[0].shape[2]
        side, step, copies = me_ref[1], me_ref[2], me_ref.shape[0] - 3
        rows = outs[0].shape[1] // (2 * copies)
        used = sum(size for left, right, cuts in plan for source, row, size in cuts)
        if used < total.shape[0]:
            total[used:, :] = jnp.zeros((total.shape[0] - used, total.shape[1]), WIDE)
        for part in range(2 * outs[0].shape[0]):
            target = outs[part & 1]
            lane = pl.multiple_of(jnp.bitwise_xor(me_ref[0], part) * lanes, lanes)
            for half in range(2):
                for k in range(copies):
                    piece = jnp.bitwise_xor(side, half) * copies + (step + k) % copies
                    row = pl.multiple_of(piece * rows, 16)
                    to = (half * copies + k) * rows
                    target[part >> 1, to : to + rows, :] = total[
                        pl.ds(row, rows), pl.ds(lane, lanes)
                    ].astype(LOW)


def weight_grads(arrays, plan, place, shards, height):
    rows = arrays[0].shape[0]
    used = max(row + size for left, right, cuts in plan for source, row, size in cuts)
    width = arrays[plan[0][1]].shape[1]
    tile = 2 * BLOCK
    block = lambda n: pl.BlockSpec((tile, n), lambda t: (t, 0))
    dims = (shards // 2, height, width // shards)
    return pl.pallas_call(
        functools.partial(weight_kernel, plan, len(arrays)),
        grid=(rows // tile,),
        out_shape=[shape(dims, LOW)] * 2,
        in_specs=[smem()] + [block(item.shape[1]) for item in arrays],
        out_specs=[pl.BlockSpec(dims, lambda t: (0,) * len(dims))] * 2,
        scratch_shapes=[VMEM((height, width), WIDE)],
        compiler_params=params(),
        cost_estimate=cost(2 * rows * used * width, 2 * rows * sum(i.shape[1] for i in arrays)),
    )(place, *arrays)


def back_kernel(count, decay, seg_s, in_last, *refs):
    (q, k, v, gret, cos, sin, seg, seg_row, st, dst, *got) = refs[:13]
    (dq, dk, dv, state, weights, grads) = refs[13:]
    seq = pl.program_id(0) // count
    c = count - 1 - pl.program_id(0) % count

    @pl.when(c == count - 1)
    def _():
        for h in range(H):
            state[h] = entering(decay, count * BLOCK, h, got)

    for b in range(1, count):

        @pl.when(c == b - 1)
        def _():
            prev = seg_s[seq, b * BLOCK - 1]
            first = seg_s[seq, b * BLOCK]
            last = seg_s[seq, (b + 1) * BLOCK - 1]
            joined = jnp.logical_and(first == last, first == prev)
            for h in range(H):
                factor = jnp.exp(jnp.full((1, 1), decay[h] * BLOCK, WIDE))
                state[h] = jnp.where(joined, factor * state[h], 0.0) + dst[h]

    start = c * BLOCK
    before = jnp.where(c > 0, seg_s[seq, jnp.maximum(start - 1, 0)], in_last[seq])
    final = seg_s[seq, start + BLOCK - 1]
    here = (seg[...] == before).astype(WIDE)
    ends = (seg[...] == final).astype(WIDE)
    place = column(BLOCK)
    dqs, dks = [], []
    for h in range(H):
        a = decay[h]
        qh = q[:, h * KD : (h + 1) * KD]
        kh = k[:, h * KD : (h + 1) * KD]
        vh = v[:, h * VP : (h + 1) * VP]
        gh = gret[:, h * VP : (h + 1) * VP]
        qw = jnp.exp(a * (place + 1.0)) * here
        kw = jnp.exp(a * (BLOCK - 1.0 - place)) * ends
        parts = []
        for i in range(BLOCK // TILE):
            top, reach = i * TILE, (i + 1) * TILE
            mix = mixing(a, top, TILE, seg, seg_row)
            s = dot_nt(qh[top:reach, :], kh[:reach, :])
            weights[top:reach, :reach] = (s * mix).astype(LOW)
            gs = (dot_nt(gh[top:reach, :], vh[:reach, :]) * mix).astype(LOW)
            grads[top:reach, :reach] = gs
            parts.append(dot(gs, kh[:reach, :]))
        late = state[h].astype(LOW)
        dqs.append(jnp.concatenate(parts) + qw * dot_nt(gh, st[h]))
        parts, values = [], []
        for i in range(BLOCK // TILE):
            top, reach = i * TILE, (i + 1) * TILE
            parts.append(dot_tn(grads[top:, top:reach], qh[top:, :]))
            values.append(dot_tn(weights[top:, top:reach], gh[top:, :]))
        dks.append(jnp.concatenate(parts) + kw * dot_nt(vh, late))
        dv[:, h * VP : (h + 1) * VP] = (jnp.concatenate(values) + kw * dot(kh, late)).astype(LOW)
    dq[...] = rotated(jnp.concatenate(dqs, axis=1), cos[...], -sin[...]).astype(LOW)
    dk[...] = rotated(jnp.concatenate(dks, axis=1), cos[...], -sin[...]).astype(LOW)


def back(seqs, length, data, cos, sin, seg_col, seg_row, segments, in_last, decay, st, dst, got):
    rows = data[0].shape[0]
    count = length // BLOCK
    turn = lambda t: (t // count) * count + count - 1 - t % count
    block = lambda n: pl.BlockSpec((BLOCK, n), lambda t: (turn(t), 0))
    table = pl.BlockSpec((BLOCK, KD // 2), lambda t: (count - 1 - t % count, 0))
    outs = [H * KD, H * KD, H * VP]
    inputs = [decay, segments, in_last, *data, cos, sin, seg_col, seg_row, st, dst, *got]
    specs = [smem()] * 3 + [block(item.shape[1]) for item in data] + [table, table, block(1)]
    specs += [pl.BlockSpec((None, 1, BLOCK), lambda t: (turn(t), 0, 0))]
    specs += [state_block(count, lambda c: count - 1 - c)]
    specs += [state_block(count, lambda c: jnp.minimum(count - c, count - 1))]
    specs += [seq_block(count)] * 3
    return pl.pallas_call(
        functools.partial(back_kernel, count),
        grid=(seqs * count,),
        out_shape=[shape((rows, n), LOW) for n in outs],
        in_specs=specs,
        out_specs=[block(n) for n in outs],
        scratch_shapes=[
            VMEM((H, KD, VP), WIDE),
            VMEM((BLOCK, BLOCK), LOW),
            VMEM((BLOCK, BLOCK), LOW),
        ],
        compiler_params=params(),
        cost_estimate=cost(rows * H * 2 * BLOCK * 3 * (KD + VP), 16 * rows * H * VP),
    )(*inputs)


def input_kernel(dq, dk, dv, ggate, tok, glow, w_kv, w_qg, gains, *rest):
    out = rest[-1]
    kd = H * KD
    gh = dot(dq[...], w_qg[:kd, :]) + dot(dk[...], w_kv[:kd, :])
    gh += dot(dv[...], w_kv[kd:, :]) + dot(ggate[...], w_qg[kd:, :])
    x = tok[...].astype(WIDE)
    r = lax.rsqrt(jnp.mean(x * x, axis=1, keepdims=True) + EPS)
    xhat = x * r
    gh = gh * gains[0:1, :].astype(WIDE)
    inner_product = jnp.mean(gh * xhat, axis=1, keepdims=True)
    out[...] = (glow[...].astype(WIDE) + r * (gh - xhat * inner_product)).astype(LOW)


def input_grad(first, steps, dq, dk, dv, ggate, tokens, glow, w_kv, w_qg, gains, earlier):
    rows, width = tokens.shape
    parts = rows // BLOCK // steps
    arrays = [dq, dk, dv, ggate, tokens, glow]
    block = lambda item: pl.BlockSpec((BLOCK, item.shape[1]), lambda t: (first + t, 0))
    inputs = [*arrays, w_kv, w_qg, gains]
    specs = [block(item) for item in arrays] + [whole(item.shape) for item in (w_kv, w_qg, gains)]
    aliases = {}
    if earlier is not None:
        aliases = {len(inputs): 0}
        inputs.append(earlier)
        specs.append(pl.BlockSpec(memory_space=pl.ANY))
    return pl.pallas_call(
        input_kernel,
        grid=(steps,),
        out_shape=shape((rows, width), LOW),
        in_specs=specs,
        out_specs=block(tokens),
        input_output_aliases=aliases,
        compiler_params=params(),
        cost_estimate=cost(2 * rows * width * 2 * w_kv.shape[0] // parts, 20 * rows * width // parts),
    )(*inputs)


def adam_step(master, moment, second, grad, scale, rate, decay_weight):
    clipped = grad * scale
    moment_new = BETA_ONE * moment + (1.0 - BETA_ONE) * clipped
    second_new = BETA_TWO * second + (1.0 - BETA_TWO) * clipped * clipped
    corrected = (
        moment_new
        * (1.0 / (1.0 - BETA_ONE**STEP))
        / (jnp.sqrt(second_new * (1.0 / (1.0 - BETA_TWO**STEP))) + ADAM_EPS)
    )
    return (master - rate * (corrected + decay_weight * master), moment_new, second_new)


def squares_kernel(vd, ff, place, *refs):
    halves, (w_qk, w_vg, w_gu, low_gains) = refs[:6], refs[6:10]
    grad_gains, total, one, two, three = refs[10:]
    kd = H * KD
    side, step, copies = place[1], place[2], place.shape[0] - 3
    for index, target in enumerate((one, two, three)):
        rows = target.shape[0] // (2 * copies)
        for half in range(2):
            for k in range(copies):
                piece = jnp.bitwise_xor(side, half) * copies + (step + copies - k) % copies
                row = pl.multiple_of(piece * rows, 16)
                target[pl.ds(row, rows), :] = halves[2 * index + half][k * rows : (k + 1) * rows, :]

    def rows(source, start, size):
        return source[start : start + size, :].astype(WIDE)

    def product(weight, grad):
        return jnp.sum(weight.astype(LOW).astype(WIDE) * grad, axis=0, keepdims=True)

    sums = []

    def square(item):
        sums.append(jnp.sum(item * item, axis=0, keepdims=True))
        return item

    first = jnp.zeros((1, low_gains.shape[1]), WIDE)
    for i in range(2):
        grad = square(rows(three, i * kd, kd))
        first += jnp.sum(w_qk[i].astype(LOW).astype(WIDE).T * grad, axis=0, keepdims=True)
    first += product(w_vg[0], square(rows(three, 2 * kd, vd)))
    first += product(w_vg[1], square(rows(two, vd, vd)))
    square(rows(two, 0, vd))
    square(rows(one, 0, ff))
    second = product(w_gu[0], square(rows(one, ff, ff)))
    second += product(w_gu[1], square(rows(one, 2 * ff, ff)))
    gains = jnp.concatenate([first, second]) / low_gains[...].astype(LOW).astype(WIDE)
    grad_gains[...] = gains
    sums.append(jnp.sum(gains * gains, axis=0, keepdims=True))
    total[...] = jnp.broadcast_to(jnp.sum(sum(sums), axis=1, keepdims=True), total.shape)


def squares(vd, ff, place, grads, w_qk, w_vg, w_gu, gains):
    halves = [half for pair in grads for half in pair]
    vmem = pl.BlockSpec(memory_space=VMEM)
    return pl.pallas_call(
        functools.partial(squares_kernel, vd, ff),
        out_shape=[shape(gains.shape, WIDE), shape((8, 128), WIDE)]
        + [shape((2 * pair[0].shape[0], pair[0].shape[1]), LOW) for pair in grads],
        in_specs=[smem()] + [vmem] * 10,
        out_specs=[vmem] * 5,
        compiler_params=params(),
    )(place, *halves, w_qk, w_vg, w_gu, gains)


def update_kernel(vd, ff, *refs):
    totals, (one, two, three, gain_grads) = refs[:4], refs[4:8]
    sources, targets, norm_out = refs[8:26], refs[26:44], refs[44]
    ins, outs = refs[45:63], refs[63:81]
    arrived, sent = refs[81:]
    kd = H * KD
    order = [4, 3, 2, 1, 0, 5]
    places = [6 * group + place for place in order for group in range(3)]
    fetch = {i: pltpu.make_async_copy(sources[i], ins[i], arrived.at[i]) for i in places}
    send = {i: pltpu.make_async_copy(outs[i], targets[i], sent.at[i]) for i in places}
    for i in places:
        fetch[i].start()
    norm = jnp.sqrt((totals[0][...] + totals[1][...]) + (totals[2][...] + totals[3][...]))
    norm_out[0, 0] = jnp.max(norm)
    scale = jnp.minimum(1.0, CLIP / (norm + 1e-06))[0:1, 0:1]

    def step(place, at, grad, rate, decay_weight):
        results = adam_step(
            ins[place][at], ins[6 + place][at], ins[12 + place][at], grad, scale, rate, decay_weight
        )
        for group, result in enumerate(results):
            outs[6 * group + place][at] = result

    def rows(source, start, size):
        return source[start : start + size, :].astype(WIDE)

    grads = {
        4: [(..., lambda: rows(one, 0, ff))],
        3: [(0, lambda: rows(one, ff, ff)), (1, lambda: rows(one, 2 * ff, ff))],
        2: [(..., lambda: rows(two, 0, vd))],
        1: [(0, lambda: rows(three, 2 * kd, vd)), (1, lambda: rows(two, vd, vd))],
        0: [(0, lambda: rows(three, 0, kd).T), (1, lambda: rows(three, kd, kd).T)],
        5: [(..., lambda: gain_grads[...])],
    }
    for place in order:
        for group in range(3):
            fetch[6 * group + place].wait()
        rate, decay_weight = (GAIN_RATE, 0.0) if place == 5 else (MATRIX_RATE, DECAY_WEIGHT)
        for at, grad in grads[place]:
            step(place, at, grad(), rate, decay_weight)
        for group in range(3):
            send[6 * group + place].start()
    for i in places:
        send[i].wait()


def update(vd, ff, totals, grads, gain_grads, arrays):
    anywhere = pl.BlockSpec(memory_space=pl.ANY)
    return pl.pallas_call(
        functools.partial(update_kernel, vd, ff),
        out_shape=[shape(item.shape, WIDE) for item in arrays] + [shape((1, 1), WIDE)],
        in_specs=[pl.BlockSpec(memory_space=VMEM)] * 8 + [anywhere] * 18,
        out_specs=[anywhere] * 18 + [smem()],
        scratch_shapes=[VMEM(item.shape, WIDE) for item in arrays] * 2
        + [pltpu.SemaphoreType.DMA((18,))] * 2,
        compiler_params=params(),
    )(*totals, *grads, gain_grads, *arrays)


def on_device(
    tokens,
    cotangent,
    segments,
    log_decay,
    w_qk,
    w_vg,
    w_out,
    w_gu,
    w_down,
    norm_gains,
    *states,
):
    turned = lambda item: jnp.swapaxes(item, 1, 2)
    shards = lax.axis_size("shard")
    me = lax.axis_index("shard").reshape(1)
    replica = lax.axis_index("dp")
    copies = lax.axis_size("dp") // 2
    place = jnp.concatenate(
        [me, jnp.stack([replica & 1, replica >> 1]), jnp.zeros((copies,), me.dtype)]
    )
    seqs, length, width = tokens.shape
    rows = seqs * length
    kd, vd, ff = H * KD, H * VD, w_down.shape[0]
    vp = H * VP
    vg_t, gu_t = turned(w_vg), turned(w_gu)

    low = lambda item: item.astype(LOW)
    def heads(item):
        return [
            jnp.pad(item[h * VD : (h + 1) * VD], ((0, VP - VD), (0, 0))) for h in range(H)
        ]

    first = jnp.concatenate(
        [low(w_qk[1]).T, low(vg_t[0]), jnp.pad(low(norm_gains), ((0, 14), (0, 0)))]
    )
    second = jnp.concatenate([low(w_qk[0]).T, *heads(low(vg_t[1]))])
    third = jnp.concatenate([low(w_out), low(gu_t[0]), low(gu_t[1]), low(w_down)])
    first_held = gather_shards(first)
    second = after(second, first_held[1][2])
    w_qg = lax.all_gather(second, "shard", axis=1, tiled=True)
    side = (lax.axis_index("dp") & 1).reshape(1)
    third_held, sent = gather_halves(third, side, second)

    half_width = KD // 2
    freq_rates = jnp.exp(-math.log(10000.0) * jnp.arange(half_width).astype(WIDE) / half_width)
    positions = (lax.axis_index("shard") * length + jnp.arange(length)).astype(WIDE)
    angles = positions[:, None] * freq_rates[None, :]
    cos, sin = jnp.cos(angles), jnp.sin(angles)

    tok = tokens.reshape(rows, width)
    cot = cotangent.reshape(rows, width)
    seg_col = segments.reshape(rows, 1)
    seg_row = segments.reshape(rows // BLOCK, 1, BLOCK)
    in_last = jnp.where(lax.axis_index("shard") > 0, segments[:, 0], -1)
    decay = log_decay

    def tick(*done):
        nonlocal decay, place, gains
        decay, place, gains = lax.optimization_barrier((decay, place, gains, *done))[:3]

    plan = [(0, 0, 0, kd)] + [(kd + h * VD, 0, kd + h * VP, VD) for h in range(H)]
    plan += [(kd + vd, 1, 0, 16)]
    fills = [(0, kd + h * VP + VD, VP - VD) for h in range(H)]
    w_kv, gains = assemble(first_held, plan, fills, [kd + vp, 16], width, me, side)
    tick(sent, third_held[1][2])
    hid, k, v, kv, leaving = front(
        seqs, length, tok, seg_col, segments, decay, w_kv, gains, cos, sin
    )
    passing = Passing(leaving, False)
    tick(leaving, third_held[4][2])
    tick(passing.turn(decay, length, leaving))
    q, intra, gate = inner(k, v, hid, w_qg, cos, sin, seg_col, seg_row, decay, length)
    tick(q)
    passing.finish(q)
    plan = [(h * VD, 0, h * VP, VD) for h in range(H)] + [(vd, 0, vp, 3 * ff)]
    fills = [(0, h * VP + VD, VP - VD) for h in range(H)]
    (w_rest,) = assemble(third_held, plan, fills, [vp + 3 * ff], width, me, side)
    tick(w_rest)
    tokens_out, hid2, prod, dgate, dup, mixed, glow, ggate, gret, st, dst, leaving = middle(
        seqs, length, ff, (intra, gate, q, tok, cot), seg_col, segments, in_last, decay,
        w_rest, gains, passing.got, kv,
    )
    returning = Passing(leaving, True)
    tick(leaving)

    def halves(row):
        return [(h * VP, row + h * VD, VD) for h in range(H)]

    fit = lambda used: used + -used % (16 * lax.axis_size("dp"))
    plan = [(0, 1, [(0, 0, ff)]), (2, 3, [(0, ff, ff)]), (4, 3, [(0, 2 * ff, ff)])]
    made = weight_grads([prod, cot, dgate, hid2, dup], plan, place, shards, fit(3 * ff))
    one = Reduction(*made)
    tick(made[0])
    tick(returning.turn(decay, length, made[0]))
    plan = [(0, 1, halves(0)), (2, 3, halves(vd))]
    made = weight_grads([mixed, glow, ggate, hid], plan, place, shards, fit(2 * vd))
    two = Reduction(*made)
    tick(made[0])
    returning.finish(made[0])
    tick(one.cross(made[0]))
    dq, dk, dv = back(
        seqs, length, (q, k, v, gret), cos, sin, seg_col, seg_row, segments, in_last, decay,
        st, dst, returning.got,
    )
    tick(dq)
    tick(one.halve(dq), two.cross(dq))
    plan = [(0, 3, [(0, 0, kd)]), (1, 3, [(0, kd, kd)]), (2, 3, halves(2 * kd))]
    made = weight_grads([dq, dk, dv, hid], plan, place, shards, fit(2 * kd + vd))
    three = Reduction(*made)
    tick(made[0])
    tick(one.scatter(made[0]), two.halve(made[0]))
    tick(three.cross(made[0]))
    blocks = rows // BLOCK
    data = (dq, dk, dv, ggate, tok, glow, w_kv, w_qg)
    grad_input = input_grad(0, blocks // 2, *data, gains, None)
    tick(grad_input)
    tick(one.gather(grad_input), two.scatter(grad_input))
    for block in range(blocks // 2, blocks):
        grad_input = input_grad(block, 1, *data, gains, grad_input)
        tick(grad_input)
        if block == blocks // 2:
            tick(three.halve(grad_input), one.double(grad_input), two.gather(grad_input))
    three.scatter(grad_input)
    two.double(grad_input)
    three.gather()
    three.double()

    gain_grads, total, *grads = squares(
        vd, ff, place, [item.result() for item in (one, two, three)], w_qk, vg_t, gu_t, norm_gains
    )
    others = [
        lax.ppermute(total, "shard", [(i, i ^ mask) for i in range(shards)]) for mask in (1, 2, 3)
    ]
    arrays = []
    for group in ((w_qk, w_vg, w_out, w_gu, w_down, norm_gains), states[:6], states[6:]):
        arrays += [turned(item) if i in (1, 3) else item for i, item in enumerate(group)]
    *results, norm = update(vd, ff, [total, *others], grads, gain_grads, arrays)
    results = [turned(item) if i % 6 in (1, 3) else item for i, item in enumerate(results)]
    return (
        tokens_out.reshape(tokens.shape),
        grad_input.reshape(tokens.shape),
        *results,
        norm.reshape(()),
    )


def solution(mesh):
    split = P("dp", "shard", None)
    rows, columns = P(None, "shard", None), P(None, "shard")
    group = (rows, rows, columns, rows, columns, columns)
    in_specs = (split, split, P("dp", "shard"), P()) + group * 3
    out_specs = (split, split) + group * 3 + (P(),)
    return jax.shard_map(
        on_device, mesh=mesh, in_specs=in_specs, out_specs=out_specs, check_vma=False
    )
```

```python
import functools
import math

import jax
import jax.numpy as jnp
from jax import lax
from jax.experimental import pallas as pl
from jax.experimental.pallas import tpu as pltpu
from jax.sharding import PartitionSpec as P

H = 2
KD = 256
VD = 432
VP = 512
BLOCK = 512
STEP = 10

EPS = 1e-05
ADAM_EPS = 1e-08
BETA_ONE = 0.9
BETA_TWO = 0.95
MATRIX_RATE = 0.15
GAIN_RATE = 1.0
DECAY_WEIGHT = 0.1
CLIP = 1.0

LOW = jnp.bfloat16
WIDE = jnp.float32
VMEM = pltpu.VMEM
SMEM = pltpu.SMEM
LIMIT = 60 * 1024 * 1024


def dot(a, b):
    return jnp.dot(a, b, preferred_element_type=WIDE)


def dot_nt(a, b):
    return lax.dot_general(a, b, (((1,), (1,)), ((), ())), preferred_element_type=WIDE)


def dot_tn(a, b):
    return lax.dot_general(a, b, (((0,), (0,)), ((), ())), preferred_element_type=WIDE)


def params(**more):
    return pltpu.CompilerParams(vmem_limit_bytes=LIMIT, **more)


def cost(flops, moved):
    return pl.CostEstimate(flops=int(flops), bytes_accessed=int(moved), transcendentals=0)


def smem():
    return pl.BlockSpec(memory_space=SMEM)


def whole(shape):
    return pl.BlockSpec(shape, lambda *at: (0,) * len(shape), pipeline_mode=pl.Buffered(1))


def shape(dims, kind):
    return jax.ShapeDtypeStruct(dims, kind)


def bits_of(axis):
    return (lax.axis_size(axis) - 1).bit_length()


def exchange(value, axis, bit):
    size = lax.axis_size(axis)
    return lax.ppermute(value, axis, [(i, i ^ (1 << bit)) for i in range(size)])


def gather_shards(own):
    held = [(0, own)]
    for bit in reversed(range(bits_of("shard"))):
        held += [(mask | (1 << bit), exchange(part, "shard", bit)) for mask, part in held]
    return [(mask, None, part) for mask, part in held]


def add_low(one, two):
    return (one.astype(WIDE) + two.astype(WIDE)).astype(LOW)


class Reduction:
    def __init__(self, keep, send, levels):
        self.keep = keep
        self.near = exchange(send, "shard", 0)
        self.levels = levels
        self.bit = 0

    def cross(self, *done):
        self.near = after(self.near, *done)
        low = add_low(self.keep[1], self.near[1])
        self.got = exchange(low, "shard", 1)
        self.terms = [self.keep[0], self.near[0]]
        return low

    def next(self, *done):
        got = after(self.got, *done)
        count = bits_of("dp")
        if self.bit <= count:
            terms = [*self.terms, got]

            def total(at):
                return sum(term[at].astype(WIDE) for term in terms).astype(LOW)

            rows = got.shape[0]
            if self.bit == count:
                self.held = total(slice(0, rows))
            elif self.bit < self.levels:
                self.terms = [total(slice(0, rows // 2))]
                sent = total(slice(rows // 2, rows))
            else:
                sent = total(slice(0, rows))
                self.terms = [sent]
        else:
            self.held = jnp.concatenate([self.held, got])
        if self.bit >= count:
            bit = self.levels - 1 - (self.bit - count)
            sent = self.held
        else:
            bit = self.bit
        self.bit += 1
        self.got = exchange(sent, "dp", bit)
        return sent

    def stages(self):
        return bits_of("dp") + self.levels

    def result(self):
        return self.held, self.got


class Passing:
    def __init__(self, local, reverse):
        self.local = local
        steps = [[(0, 1), (2, 3)], [(1, 2)], [(2, 3)]]
        if reverse:
            steps = [[(3 - a, 3 - b) for a, b in step] for step in steps]
        self.steps = steps
        self.got = [lax.ppermute(local, "shard", steps[0])]

    def turn(self, decay, length, *done):
        self.got[0] = after(self.got[0], *done)
        total = combine(decay, length, self.local, self.got[0])
        self.got.append(lax.ppermute(total, "shard", self.steps[1]))
        return total

    def finish(self, *done):
        self.got.append(lax.ppermute(after(self.got[1], *done), "shard", self.steps[2]))


def entering(decay, length, h, got):
    factor = jnp.exp(jnp.full((1, 1), decay[h] * length, WIDE))
    wide = [item[h].astype(WIDE) for item in got]
    return wide[0] + wide[1] + factor * wide[2]


def after(value, *others):
    return lax.optimization_barrier((value, *others))[0]


def combine_kernel(length, decay, local, got, out):
    h = pl.program_id(0) % H
    factor = jnp.exp(jnp.full((1, 1), decay[h] * length, WIDE))
    out[...] = (local[...].astype(WIDE) + factor * got[...].astype(WIDE)).astype(LOW)


def combine(decay, length, local, got):
    block = pl.BlockSpec((None, None, KD, VP), lambda i: (i // H, i % H, 0, 0))
    return pl.pallas_call(
        functools.partial(combine_kernel, length),
        grid=(local.shape[0] * H,),
        out_shape=shape(local.shape, LOW),
        in_specs=[smem(), block, block],
        out_specs=block,
        compiler_params=params(),
        cost_estimate=cost(local.size, 6 * local.size),
    )(decay, local, got)


def assemble_kernel(plan, fills, sources_of, me_ref, side_ref, *refs):
    sources, outs = refs[: len(sources_of)], refs[len(sources_of) :]
    lanes = sources[0].shape[1]
    for index, row, size in fills:
        outs[index][row : row + size, :] = jnp.zeros((size, outs[index].shape[1]), LOW)

    def place(source, lane, low, high):
        for start, index, row, size in plan:
            begin, end = max(start, low), min(start + size, high)
            if begin < end:
                to = row + begin - start
                outs[index][to : to + end - begin, pl.ds(lane, lanes)] = source[
                    begin - low : end - low, :
                ]

    for (mask, half), source in zip(sources_of, sources):
        lane = pl.multiple_of(jnp.bitwise_xor(me_ref[0], mask) * lanes, lanes)
        rows = source.shape[0]
        if half is None:
            place(source, lane, 0, rows)
            continue
        for side in range(2):

            @pl.when(side_ref[0] == side)
            def _():
                low = (side ^ half) * rows
                place(source, lane, low, low + rows)


def assemble(held, plan, fills, heights, width, me, side):
    sources_of = [(mask, half) for mask, half, part in held]
    parts = [part for mask, half, part in held]
    return pl.pallas_call(
        functools.partial(assemble_kernel, plan, fills, sources_of),
        out_shape=[shape((rows, width), LOW) for rows in heights],
        in_specs=[smem()] * 2 + [pl.BlockSpec(memory_space=VMEM)] * len(parts),
        out_specs=[pl.BlockSpec(memory_space=VMEM)] * len(heights),
        compiler_params=params(),
        cost_estimate=cost(0, 4 * sum(heights) * width),
    )(me, side, *parts)


def rotated(flat, cosine, sine):
    half = KD // 2
    parts = []
    for h in range(H):
        u = flat[:, h * KD : h * KD + half]
        w = flat[:, h * KD + half : (h + 1) * KD]
        parts += [u * cosine - w * sine, w * cosine + u * sine]
    return jnp.concatenate(parts, axis=1)


def column(size):
    return lax.broadcasted_iota(jnp.int32, (size, 1), 0).astype(WIDE)


def front_kernel(count, decay, seg_s, tok, w, gains, cos, sin, seg, *rest):
    hid, k, v, kv, out_state, state = rest
    seq = pl.program_id(0) // count
    c = pl.program_id(0) % count
    x = tok[...].astype(WIDE)
    r = lax.rsqrt(jnp.mean(x * x, axis=1, keepdims=True) + EPS)
    h1 = (x * r * gains[0:1, :].astype(WIDE)).astype(LOW)
    hid[...] = h1
    kd = H * KD
    key = rotated(dot_nt(h1, w[:kd, :]), cos[...], sin[...]).astype(LOW)
    k[...] = key
    val = dot_nt(h1, w[kd : kd + H * VP, :]).astype(LOW)
    v[...] = val
    first = seg_s[seq, c * BLOCK]
    last = seg_s[seq, c * BLOCK + BLOCK - 1]
    before = seg_s[seq, jnp.maximum(c * BLOCK - 1, 0)]
    here = (seg[...] == last).astype(WIDE)
    joined = jnp.logical_and(jnp.logical_and(first == last, first == before), c > 0)
    for h in range(H):
        a = decay[h]
        kw = jnp.exp(a * (BLOCK - 1.0 - column(BLOCK))) * here
        kk = (key[:, h * KD : (h + 1) * KD].astype(WIDE) * kw).astype(LOW)
        add = dot_tn(kk, val[:, h * VP : (h + 1) * VP])
        kv[h] = add
        factor = jnp.exp(jnp.full((1, 1), a * BLOCK, WIDE))
        total = jnp.where(joined, factor * state[h], 0.0) + add
        state[h] = total
        out_state[h] = total.astype(LOW)


def row_block(width):
    return pl.BlockSpec((BLOCK, width), lambda t: (t, 0))


def state_block(count, at=lambda c: c):
    return pl.BlockSpec(
        (None, None, H, KD, VP), lambda t: (t // count, at(t % count), 0, 0, 0)
    )


def seq_block(count):
    return pl.BlockSpec((None, H, KD, VP), lambda t: (t // count, 0, 0, 0))


def front(seqs, length, tokens, seg_col, segments, decay, w, gains, cos, sin):
    count = length // BLOCK
    rows, width = tokens.shape
    outs = [width, H * KD, H * VP]
    table = pl.BlockSpec((BLOCK, KD // 2), lambda t: (t % count, 0))
    return pl.pallas_call(
        functools.partial(front_kernel, count),
        grid=(seqs * count,),
        out_shape=[shape((rows, n), LOW) for n in outs]
        + [shape((seqs, count, H, KD, VP), WIDE), shape((seqs, H, KD, VP), LOW)],
        in_specs=[smem(), smem(), row_block(width), whole(w.shape), whole(gains.shape)]
        + [table, table, row_block(1)],
        out_specs=[row_block(n) for n in outs]
        + [state_block(count), seq_block(count)],
        scratch_shapes=[VMEM((H, KD, VP), WIDE)],
        compiler_params=params(),
        cost_estimate=cost(2 * rows * width * w.shape[0], 12 * rows * width),
    )(decay, segments, tokens, w, gains, cos, sin, seg_col)


def decay_row(a):
    return jnp.exp(-a * lax.broadcasted_iota(jnp.int32, (1, BLOCK), 1).astype(WIDE))


def mixing(a, top, size, seg, seg_row):
    reach = top + size
    rows = jnp.exp(a * (column(size) + float(top)))
    same = seg[top:reach, :] == seg_row[:, :reach]
    n = lax.broadcasted_iota(jnp.int32, (size, reach), 0) + top
    m = lax.broadcasted_iota(jnp.int32, (size, reach), 1)
    return jnp.where(jnp.logical_and(same, n >= m), rows * decay_row(a)[:, :reach], 0.0)


TILE = 256


def inner_kernel(decay, k, v, hid, w, cos, sin, seg, seg_row, q, intra, gate):
    kd = H * KD
    query = rotated(dot_nt(hid[...], w[:kd, :]), cos[...], sin[...]).astype(LOW)
    q[...] = query
    gate[...] = dot_nt(hid[...], w[kd:, :]).astype(LOW)
    for i in range(BLOCK // TILE):
        top, reach = i * TILE, (i + 1) * TILE
        for h in range(H):
            s = dot_nt(query[top:reach, h * KD : (h + 1) * KD], k[:reach, h * KD : (h + 1) * KD])
            weights = (s * mixing(decay[h], top, TILE, seg, seg_row)).astype(LOW)
            intra[top:reach, h * VP : (h + 1) * VP] = dot(
                weights, v[:reach, h * VP : (h + 1) * VP]
            ).astype(LOW)


def inner(k, v, hid, w, cos, sin, seg_col, seg_row, decay, length):
    rows, width = hid.shape
    count = length // BLOCK
    block = lambda n: pl.BlockSpec((BLOCK, n), lambda t: (t, 0))
    table = pl.BlockSpec((BLOCK, KD // 2), lambda t: (t % count, 0))
    return pl.pallas_call(
        inner_kernel,
        grid=(rows // BLOCK,),
        out_shape=[shape((rows, n), LOW) for n in (H * KD, H * VP, H * VP)],
        in_specs=[
            smem(),
            block(H * KD),
            block(H * VP),
            block(width),
            whole(w.shape),
            table,
            table,
            block(1),
            pl.BlockSpec((None, 1, BLOCK), lambda t: (t, 0, 0)),
        ],
        out_specs=[block(n) for n in (H * KD, H * VP, H * VP)],
        compiler_params=params(),
        cost_estimate=cost(rows * (2 * width * 1536 + 2 * BLOCK * H * VP), 8 * rows * H * VP),
    )(decay, k, v, hid, w, cos, sin, seg_col, seg_row)


CHUNK = 16


def interleaved(first, second):
    steps = [((i + 0.5) / len(first), 0, step) for i, step in enumerate(first)]
    steps += [((i + 0.5) / len(second), 1, step) for i, step in enumerate(second)]
    for place, which, step in sorted(steps, key=lambda item: item[:2]):
        step()


def pieces(width, size=256):
    return [(start, min(start + size, width)) for start in range(0, width, size)]


def across(narrow, width):
    return jnp.concatenate([narrow] * (width // 128), axis=1)


def middle_kernel(count, ff, decay, seg_s, in_last, *refs):
    (intra, gate, q, tok, cot, seg, w, gains, *got, kv) = refs[:12]
    outs, scratch = refs[12:24], refs[24:]
    (tok_out, hid2, prod, dgate, dup, mixed, glow, ggate, gret, st_out, dst, leave) = outs
    (state, now, queries, factors, ret_s, norm_s, silu_s, slope_s, inv_s, res_s, ff_s, low_s, sums) = scratch
    seq = pl.program_id(0) // count
    c = pl.program_id(0) % count
    start = c * BLOCK
    vp = H * VP
    width = tok.shape[1]
    before = jnp.where(c > 0, seg_s[seq, jnp.maximum(start - 1, 0)], in_last[seq])

    @pl.when(c == 0)
    def _():
        for h in range(H):
            total = entering(decay, count * BLOCK, h, got)
            state[h] = total
            now[h] = total.astype(LOW)

    for b in range(1, count):

        @pl.when(c == b)
        def _():
            prev = seg_s[seq, (b - 1) * BLOCK - 1] if b > 1 else in_last[seq]
            joined = jnp.logical_and(
                seg_s[seq, (b - 1) * BLOCK] == seg_s[seq, b * BLOCK - 1],
                seg_s[seq, (b - 1) * BLOCK] == prev,
            )
            for h in range(H):
                factor = jnp.exp(jnp.full((1, 1), decay[h] * BLOCK, WIDE))
                total = jnp.where(joined, factor * state[h], 0.0) + kv[h]
                state[h] = total
                now[h] = total.astype(LOW)

    st_out[...] = now[...]
    here = (seg[...] == before).astype(WIDE)
    for h in range(H):
        qw = jnp.exp(decay[h] * (column(BLOCK) + 1.0)) * here
        factors[h] = jnp.broadcast_to(qw, (BLOCK, 128))

    w_out = (0, vp)
    w_gate = (vp, vp + ff)
    w_up = (vp + ff, vp + 2 * ff)
    w_down = (vp + 2 * ff, vp + 3 * ff)
    gain = gains[1:2, :].astype(WIDE)

    def phases(top):
        rs = pl.ds(top, TILE)
        lists = []

        def add(steps):
            lists.append(steps)

        def chunks():
            return [pl.ds(row, CHUNK) for row in range(top, top + TILE, CHUNK)]

        def cross(h, lo, hi):
            ret_s[rs, h * VP + lo : h * VP + hi] = dot(
                q[rs, h * KD : (h + 1) * KD], now[h, :, lo:hi]
            )

        add([functools.partial(cross, h, *piece) for h in range(H) for piece in pieces(VP)])

        def gated(h, r):
            hv = slice(h * VP, (h + 1) * VP)
            hk = slice(h * KD, (h + 1) * KD)
            qw = factors[h, r, :]
            queries[r, hk] = (q[r, hk].astype(WIDE) * across(qw, KD)).astype(LOW)
            ret = intra[r, hv].astype(WIDE) + across(qw, VP) * ret_s[r, hv]
            mean = jnp.sum(ret, axis=1, keepdims=True) * (1.0 / VD)
            centered = ret - mean
            square = jnp.sum(centered * centered, axis=1, keepdims=True)
            var = (square - (VP - VD) * (mean * mean)) * (1.0 / VD)
            inv = lax.rsqrt(var + 1.0 * KD)
            nh = centered * inv
            g = gate[r, hv].astype(WIDE)
            sg = 0.5 * jnp.tanh(0.5 * g) + 0.5
            sl = g * sg
            mixed[r, hv] = (nh * sl).astype(LOW)
            norm_s[r, hv] = nh
            silu_s[r, hv] = sl
            slope_s[r, hv] = nh * (sg + sl * (1.0 - sg))
            inv_s[h, r, :] = jnp.broadcast_to(inv, (CHUNK, 128))

        add([functools.partial(gated, h, r) for r in chunks() for h in range(H)])

        def project(lo, hi):
            res_s[rs, lo:hi] = dot(mixed[rs, :], w[w_out[0] : w_out[1], lo:hi])

        add([functools.partial(project, *piece) for piece in pieces(width)])

        def norm(r):
            resid = tok[r, :].astype(WIDE) + res_s[r, :]
            r2 = lax.rsqrt(jnp.mean(resid * resid, axis=1, keepdims=True) + EPS)
            res_s[r, :] = resid
            hid2[r, :] = (resid * r2 * gain).astype(LOW)
            inv_s[H, r, :] = jnp.broadcast_to(r2, (CHUNK, 128))

        add([functools.partial(norm, r) for r in chunks()])

        def forward(place, source, at, lo, hi):
            ff_s[place, rs, lo:hi] = dot_nt(source[rs, :], w[at[0] + lo : at[0] + hi, :])

        add(
            [
                functools.partial(forward, place, source, at, *piece)
                for piece in pieces(ff)
                for place, source, at in ((0, hid2, w_gate), (1, hid2, w_up), (2, cot, w_down))
            ]
        )

        def gelu(r, lo, hi):
            gf, uf, gp = ff_s[0, r, lo:hi], ff_s[1, r, lo:hi], ff_s[2, r, lo:hi]
            e = jnp.exp(-0.5 * (gf * gf))
            d = 1.0 / (1.0 + (0.3275911 * math.sqrt(0.5)) * jnp.abs(gf))
            poly = d * (
                0.5 * 0.254829592
                + d
                * (
                    0.5 * -0.284496736
                    + d * (0.5 * 1.421413741 + d * (0.5 * -1.453152027 + d * (0.5 * 1.061405429)))
                )
            )
            tail = poly * e
            cdf = jnp.where(gf >= 0.0, 1.0 - tail, tail)
            ge = gf * cdf
            dge = cdf + gf * (e * (1.0 / math.sqrt(2.0 * math.pi)))
            prod[r, lo:hi] = (ge * uf).astype(LOW)
            dgate[r, lo:hi] = (gp * uf * dge).astype(LOW)
            dup[r, lo:hi] = (gp * ge).astype(LOW)

        add([functools.partial(gelu, r, *piece) for r in chunks() for piece in pieces(ff, 512)])

        def down(lo, hi):
            low_s[0, rs, lo:hi] = dot(prod[rs, :], w[w_down[0] : w_down[1], lo:hi])

        def hidden(lo, hi):
            low_s[1, rs, lo:hi] = dot(dgate[rs, :], w[w_gate[0] : w_gate[1], lo:hi]) + dot(
                dup[rs, :], w[w_up[0] : w_up[1], lo:hi]
            )

        add([functools.partial(step, *piece) for piece in pieces(width) for step in (down, hidden)])

        def residual(r):
            resid = res_s[r, :]
            r2 = across(inv_s[H, r, :], width)
            tok_out[r, :] = (resid + low_s[0, r, :]).astype(LOW)
            gh = low_s[1, r, :] * gain
            xhat = resid * r2
            inner_product = jnp.mean(gh * xhat, axis=1, keepdims=True)
            glow[r, :] = (cot[r, :].astype(WIDE) + r2 * (gh - xhat * inner_product)).astype(LOW)

        add([functools.partial(residual, r) for r in chunks()])

        def mix_back(lo, hi):
            ret_s[rs, lo:hi] = dot_nt(glow[rs, :], w[w_out[0] + lo : w_out[0] + hi, :])

        add([functools.partial(mix_back, *piece) for piece in pieces(vp)])

        def gated_back(h, r):
            hv = slice(h * VP, (h + 1) * VP)
            gm = ret_s[r, hv]
            nh = norm_s[r, hv]
            ggate[r, hv] = (gm * slope_s[r, hv]).astype(LOW)
            gn = gm * silu_s[r, hv]
            one = jnp.sum(gn, axis=1, keepdims=True) * (1.0 / VD)
            two = jnp.sum(gn * nh, axis=1, keepdims=True) * (1.0 / VD)
            gret[r, hv] = (across(inv_s[h, r, :], VP) * (gn - one - nh * two)).astype(LOW)

        add([functools.partial(gated_back, h, r) for r in chunks() for h in range(H)])
        return lists

    first, second = phases(0), phases(TILE)
    for k in range(len(first) + 1):
        interleaved(first[k] if k < len(first) else [], second[k - 1] if k else [])
    for h in range(H):
        add = dot_tn(queries[:, h * KD : (h + 1) * KD], gret[:, h * VP : (h + 1) * VP])
        dst[h] = add
        sums[c, h] = add

    @pl.when(c == count - 1)
    def _():
        for h in range(H):
            total = sums[count - 1, h]
            for b in reversed(range(count - 1)):
                prev = seg_s[seq, b * BLOCK - 1] if b > 0 else in_last[seq]
                joined = jnp.logical_and(
                    seg_s[seq, b * BLOCK] == seg_s[seq, (b + 1) * BLOCK - 1],
                    seg_s[seq, b * BLOCK] == prev,
                )
                factor = jnp.exp(jnp.full((1, 1), decay[h] * BLOCK, WIDE))
                total = jnp.where(joined, factor * total, 0.0) + sums[b, h]
            leave[h] = total.astype(LOW)


def middle(seqs, length, ff, data, seg_col, segments, in_last, decay, w, gains, got, kv):
    intra, gate, q, tokens, cotangent = data
    rows, width = tokens.shape
    count = length // BLOCK
    vp = H * VP
    outs = [width, width, ff, ff, ff, vp, width, vp, vp]
    inputs = [decay, segments, in_last, intra, gate, q, tokens, cotangent, seg_col, w, gains, *got, kv]
    specs = [smem()] * 3 + [row_block(n) for n in (vp, vp, H * KD, width, width, 1)]
    specs += [whole(w.shape), whole(gains.shape), *[seq_block(count)] * 3]
    specs += [state_block(count, lambda c: jnp.maximum(c - 1, 0))]
    one = (H, KD, VP)
    states = (seqs, count, *one)
    return pl.pallas_call(
        functools.partial(middle_kernel, count, ff),
        grid=(seqs * count,),
        out_shape=[shape((rows, n), LOW) for n in outs]
        + [shape(states, LOW), shape(states, WIDE), shape((seqs, *one), LOW)],
        in_specs=specs,
        out_specs=[row_block(n) for n in outs]
        + [state_block(count)] * 2
        + [seq_block(count)],
        scratch_shapes=[
            VMEM(one, WIDE),
            VMEM(one, LOW),
            VMEM((BLOCK, H * KD), LOW),
            VMEM((H, BLOCK, 128), WIDE),
            VMEM((BLOCK, vp), WIDE),
            VMEM((BLOCK, vp), WIDE),
            VMEM((BLOCK, vp), WIDE),
            VMEM((BLOCK, vp), WIDE),
            VMEM((H + 1, BLOCK, 128), WIDE),
            VMEM((BLOCK, width), WIDE),
            VMEM((3, BLOCK, ff), WIDE),
            VMEM((2, BLOCK, width), WIDE),
            VMEM(states[1:], WIDE),
        ],
        compiler_params=params(),
        cost_estimate=cost(2 * rows * width * (2 * vp + 6 * ff), 30 * rows * width),
    )(*inputs)


def weight_kernel(plan, count, levels, me_ref, *refs):
    ins, ready, outs, total = refs[:count], refs[count:-3], refs[-3:-1], refs[-1]
    if levels is None:
        outs = refs[-2:-1]
    t = pl.program_id(0)
    last = pl.num_programs(0) - 1
    for left, right, cuts in plan:
        a, b = ins[left], ins[right]
        for source, row, size in cuts:
            add = dot_tn(a[:, source : source + size], b[...])

            @pl.when(t == 0)
            def _():
                total[row : row + size, :] = add

            @pl.when(t > 0)
            def _():
                total[row : row + size, :] += add

    @pl.when(t == last)
    def _():
        used = max(row + size for left, right, cuts in plan for source, row, size in cuts)
        if levels is None:
            outs[0][...] = total[...].astype(LOW)
            return
        for item in ready:
            total[used : used + item.shape[0], :] = item[...].astype(WIDE)
            used += item.shape[0]
        if used < total.shape[0]:
            total[used:, :] = jnp.zeros((total.shape[0] - used, total.shape[1]), WIDE)
        lanes = outs[0].shape[2]
        pieces = 2**levels
        rows = outs[0].shape[1] // pieces
        for part in range(2 * outs[0].shape[0]):
            target = outs[part & 1]
            lane = pl.multiple_of(jnp.bitwise_xor(me_ref[0], part) * lanes, lanes)
            for q in range(pieces):
                row = pl.multiple_of(jnp.bitwise_xor(me_ref[levels], q) * rows, 16)
                target[part >> 1, q * rows : (q + 1) * rows, :] = total[
                    pl.ds(row, rows), pl.ds(lane, lanes)
                ].astype(LOW)


def weight_grads(arrays, plan, place, shards=2, height=0, levels=None, ready=()):
    rows = arrays[0].shape[0]
    used = max(row + size for left, right, cuts in plan for source, row, size in cuts)
    width = arrays[plan[0][1]].shape[1]
    tile = 2 * BLOCK
    block = lambda n: pl.BlockSpec((tile, n), lambda t: (t, 0))
    dims = [(shards // 2, height, width // shards)] * 2
    if levels is None:
        height, dims = used, [(used, width)]
    full = lambda item: pl.BlockSpec(item, lambda t: (0,) * len(item))
    return pl.pallas_call(
        functools.partial(weight_kernel, plan, len(arrays), levels),
        grid=(rows // tile,),
        out_shape=[shape(item, LOW) for item in dims],
        in_specs=[smem()] + [block(item.shape[1]) for item in arrays]
        + [full(item.shape) for item in ready],
        out_specs=[full(item) for item in dims],
        scratch_shapes=[VMEM((height, width), WIDE)],
        compiler_params=params(),
        cost_estimate=cost(2 * rows * used * width, 2 * rows * sum(i.shape[1] for i in arrays)),
    )(place, *arrays, *ready)


def back_kernel(count, decay, seg_s, in_last, *refs):
    (q, k, v, gret, cos, sin, seg, seg_row, st, dst, *got) = refs[:13]
    (dq, dk, dv, state, weights, grads) = refs[13:]
    seq = pl.program_id(0) // count
    c = count - 1 - pl.program_id(0) % count

    @pl.when(c == count - 1)
    def _():
        for h in range(H):
            state[h] = entering(decay, count * BLOCK, h, got)

    for b in range(1, count):

        @pl.when(c == b - 1)
        def _():
            prev = seg_s[seq, b * BLOCK - 1]
            first = seg_s[seq, b * BLOCK]
            last = seg_s[seq, (b + 1) * BLOCK - 1]
            joined = jnp.logical_and(first == last, first == prev)
            for h in range(H):
                factor = jnp.exp(jnp.full((1, 1), decay[h] * BLOCK, WIDE))
                state[h] = jnp.where(joined, factor * state[h], 0.0) + dst[h]

    start = c * BLOCK
    before = jnp.where(c > 0, seg_s[seq, jnp.maximum(start - 1, 0)], in_last[seq])
    final = seg_s[seq, start + BLOCK - 1]
    here = (seg[...] == before).astype(WIDE)
    ends = (seg[...] == final).astype(WIDE)
    place = column(BLOCK)
    dqs, dks = [], []
    for h in range(H):
        a = decay[h]
        qh = q[:, h * KD : (h + 1) * KD]
        kh = k[:, h * KD : (h + 1) * KD]
        vh = v[:, h * VP : (h + 1) * VP]
        gh = gret[:, h * VP : (h + 1) * VP]
        qw = jnp.exp(a * (place + 1.0)) * here
        kw = jnp.exp(a * (BLOCK - 1.0 - place)) * ends
        parts = []
        for i in range(BLOCK // TILE):
            top, reach = i * TILE, (i + 1) * TILE
            mix = mixing(a, top, TILE, seg, seg_row)
            s = dot_nt(qh[top:reach, :], kh[:reach, :])
            weights[top:reach, :reach] = (s * mix).astype(LOW)
            gs = (dot_nt(gh[top:reach, :], vh[:reach, :]) * mix).astype(LOW)
            grads[top:reach, :reach] = gs
            parts.append(dot(gs, kh[:reach, :]))
        late = state[h].astype(LOW)
        dqs.append(jnp.concatenate(parts) + qw * dot_nt(gh, st[h]))
        parts, values = [], []
        for i in range(BLOCK // TILE):
            top, reach = i * TILE, (i + 1) * TILE
            parts.append(dot_tn(grads[top:, top:reach], qh[top:, :]))
            values.append(dot_tn(weights[top:, top:reach], gh[top:, :]))
        dks.append(jnp.concatenate(parts) + kw * dot_nt(vh, late))
        dv[:, h * VP : (h + 1) * VP] = (jnp.concatenate(values) + kw * dot(kh, late)).astype(LOW)
    dq[...] = rotated(jnp.concatenate(dqs, axis=1), cos[...], -sin[...]).astype(LOW)
    dk[...] = rotated(jnp.concatenate(dks, axis=1), cos[...], -sin[...]).astype(LOW)


def back(seqs, length, data, cos, sin, seg_col, seg_row, segments, in_last, decay, st, dst, got):
    rows = data[0].shape[0]
    count = length // BLOCK
    turn = lambda t: (t // count) * count + count - 1 - t % count
    block = lambda n: pl.BlockSpec((BLOCK, n), lambda t: (turn(t), 0))
    table = pl.BlockSpec((BLOCK, KD // 2), lambda t: (count - 1 - t % count, 0))
    outs = [H * KD, H * KD, H * VP]
    inputs = [decay, segments, in_last, *data, cos, sin, seg_col, seg_row, st, dst, *got]
    specs = [smem()] * 3 + [block(item.shape[1]) for item in data] + [table, table, block(1)]
    specs += [pl.BlockSpec((None, 1, BLOCK), lambda t: (turn(t), 0, 0))]
    specs += [state_block(count, lambda c: count - 1 - c)]
    specs += [state_block(count, lambda c: jnp.minimum(count - c, count - 1))]
    specs += [seq_block(count)] * 3
    return pl.pallas_call(
        functools.partial(back_kernel, count),
        grid=(seqs * count,),
        out_shape=[shape((rows, n), LOW) for n in outs],
        in_specs=specs,
        out_specs=[block(n) for n in outs],
        scratch_shapes=[
            VMEM((H, KD, VP), WIDE),
            VMEM((BLOCK, BLOCK), LOW),
            VMEM((BLOCK, BLOCK), LOW),
        ],
        compiler_params=params(),
        cost_estimate=cost(rows * H * 2 * BLOCK * 3 * (KD + VP), 16 * rows * H * VP),
    )(*inputs)


def input_kernel(dq, dk, dv, ggate, tok, glow, w_kv, w_qg, gains, *rest):
    out = rest[-1]
    kd = H * KD
    gh = dot(dq[...], w_qg[:kd, :]) + dot(dk[...], w_kv[:kd, :])
    gh += dot(dv[...], w_kv[kd:, :]) + dot(ggate[...], w_qg[kd:, :])
    x = tok[...].astype(WIDE)
    r = lax.rsqrt(jnp.mean(x * x, axis=1, keepdims=True) + EPS)
    xhat = x * r
    gh = gh * gains[0:1, :].astype(WIDE)
    inner_product = jnp.mean(gh * xhat, axis=1, keepdims=True)
    out[...] = (glow[...].astype(WIDE) + r * (gh - xhat * inner_product)).astype(LOW)


def input_grad(first, steps, dq, dk, dv, ggate, tokens, glow, w_kv, w_qg, gains, earlier):
    rows, width = tokens.shape
    parts = rows // BLOCK // steps
    arrays = [dq, dk, dv, ggate, tokens, glow]
    block = lambda item: pl.BlockSpec((BLOCK, item.shape[1]), lambda t: (first + t, 0))
    inputs = [*arrays, w_kv, w_qg, gains]
    specs = [block(item) for item in arrays] + [whole(item.shape) for item in (w_kv, w_qg, gains)]
    aliases = {}
    if earlier is not None:
        aliases = {len(inputs): 0}
        inputs.append(earlier)
        specs.append(pl.BlockSpec(memory_space=pl.ANY))
    return pl.pallas_call(
        input_kernel,
        grid=(steps,),
        out_shape=shape((rows, width), LOW),
        in_specs=specs,
        out_specs=block(tokens),
        input_output_aliases=aliases,
        compiler_params=params(),
        cost_estimate=cost(2 * rows * width * 2 * w_kv.shape[0] // parts, 20 * rows * width // parts),
    )(*inputs)


def adam_step(master, moment, second, grad, scale, rate, decay_weight):
    clipped = grad * scale
    moment_new = BETA_ONE * moment + (1.0 - BETA_ONE) * clipped
    second_new = BETA_TWO * second + (1.0 - BETA_TWO) * clipped * clipped
    corrected = (
        moment_new
        * (1.0 / (1.0 - BETA_ONE**STEP))
        / (jnp.sqrt(second_new * (1.0 / (1.0 - BETA_TWO**STEP))) + ADAM_EPS)
    )
    return (master - rate * (corrected + decay_weight * master), moment_new, second_new)


def squares_kernel(vd, ff, levels, place, *refs):
    halves, (w_qk, w_vg, w_gu, low_gains) = refs[:4], refs[4:8]
    grad_gains, total, early, late = refs[8:]
    kd = H * KD
    for index, target in enumerate((early, late)):
        pieces = 2 ** levels[index]
        rows = target.shape[0] // pieces
        for q in range(pieces):
            row = pl.multiple_of(jnp.bitwise_xor(place[levels[index]], q) * rows, 16)
            source = halves[2 * index + q // (pieces // 2)]
            start = q % (pieces // 2) * rows
            target[pl.ds(row, rows), :] = source[start : start + rows, :]

    def rows(source, start, size):
        return source[start : start + size, :].astype(WIDE)

    def product(weight, grad):
        return jnp.sum(weight.astype(LOW).astype(WIDE) * grad, axis=0, keepdims=True)

    sums = []

    def square(item):
        sums.append(jnp.sum(item * item, axis=0, keepdims=True))
        return item

    first = jnp.zeros((1, low_gains.shape[1]), WIDE)
    for i in range(2):
        grad = square(rows(late, i * kd, kd))
        first += jnp.sum(w_qk[i].astype(LOW).astype(WIDE).T * grad, axis=0, keepdims=True)
    first += product(w_vg[0], square(rows(late, 2 * kd, vd)))
    first += product(w_vg[1], square(rows(early, vd, vd)))
    square(rows(early, 0, vd))
    square(rows(early, 2 * vd, ff))
    second = product(w_gu[0], square(rows(early, 2 * vd + ff, ff)))
    second += product(w_gu[1], square(rows(early, 2 * vd + 2 * ff, ff)))
    gains = jnp.concatenate([first, second]) / low_gains[...].astype(LOW).astype(WIDE)
    grad_gains[...] = gains
    sums.append(jnp.sum(gains * gains, axis=0, keepdims=True))
    total[...] = jnp.broadcast_to(jnp.sum(sum(sums), axis=1, keepdims=True), total.shape)


def squares(vd, ff, levels, place, grads, w_qk, w_vg, w_gu, gains):
    halves = [half for pair in grads for half in pair]
    vmem = pl.BlockSpec(memory_space=VMEM)
    return pl.pallas_call(
        functools.partial(squares_kernel, vd, ff, levels),
        out_shape=[shape(gains.shape, WIDE), shape((8, 128), WIDE)]
        + [shape((2 * pair[0].shape[0], pair[0].shape[1]), LOW) for pair in grads],
        in_specs=[smem()] + [vmem] * 8,
        out_specs=[vmem] * 4,
        compiler_params=params(),
    )(place, *halves, w_qk, w_vg, w_gu, gains)


def update_kernel(vd, ff, *refs):
    totals, (early, late, gain_grads) = refs[:4], refs[4:7]
    sources, targets, norm_out = refs[7:25], refs[25:43], refs[43]
    ins, outs = refs[44:62], refs[62:80]
    arrived, sent = refs[80:]
    kd = H * KD
    order = [4, 3, 2, 1, 0, 5]
    places = [6 * group + place for place in order for group in range(3)]
    fetch = {i: pltpu.make_async_copy(sources[i], ins[i], arrived.at[i]) for i in places}
    send = {i: pltpu.make_async_copy(outs[i], targets[i], sent.at[i]) for i in places}
    for i in places:
        fetch[i].start()
    norm = jnp.sqrt((totals[0][...] + totals[1][...]) + (totals[2][...] + totals[3][...]))
    norm_out[0, 0] = jnp.max(norm)
    scale = jnp.minimum(1.0, CLIP / (norm + 1e-06))[0:1, 0:1]

    def step(place, at, grad, rate, decay_weight):
        results = adam_step(
            ins[place][at], ins[6 + place][at], ins[12 + place][at], grad, scale, rate, decay_weight
        )
        for group, result in enumerate(results):
            outs[6 * group + place][at] = result

    def rows(source, start, size):
        return source[start : start + size, :].astype(WIDE)

    grads = {
        4: [(..., lambda: rows(early, 2 * vd, ff))],
        3: [(i, lambda i=i: rows(early, 2 * vd + (1 + i) * ff, ff)) for i in range(2)],
        2: [(..., lambda: rows(early, 0, vd))],
        1: [(0, lambda: rows(late, 2 * kd, vd)), (1, lambda: rows(early, vd, vd))],
        0: [(i, lambda i=i: rows(late, i * kd, kd).T) for i in range(2)],
        5: [(..., lambda: gain_grads[...])],
    }
    for place in order:
        for group in range(3):
            fetch[6 * group + place].wait()
        rate, decay_weight = (GAIN_RATE, 0.0) if place == 5 else (MATRIX_RATE, DECAY_WEIGHT)
        for at, grad in grads[place]:
            step(place, at, grad(), rate, decay_weight)
        for group in range(3):
            send[6 * group + place].start()
    for i in places:
        send[i].wait()


def update(vd, ff, totals, grads, gain_grads, arrays):
    anywhere = pl.BlockSpec(memory_space=pl.ANY)
    return pl.pallas_call(
        functools.partial(update_kernel, vd, ff),
        out_shape=[shape(item.shape, WIDE) for item in arrays] + [shape((1, 1), WIDE)],
        in_specs=[pl.BlockSpec(memory_space=VMEM)] * 7 + [anywhere] * 18,
        out_specs=[anywhere] * 18 + [smem()],
        scratch_shapes=[VMEM(item.shape, WIDE) for item in arrays] * 2
        + [pltpu.SemaphoreType.DMA((18,))] * 2,
        compiler_params=params(),
    )(*totals, *grads, gain_grads, *arrays)


def on_device(
    tokens,
    cotangent,
    segments,
    log_decay,
    w_qk,
    w_vg,
    w_out,
    w_gu,
    w_down,
    norm_gains,
    *states,
):
    turned = lambda item: jnp.swapaxes(item, 1, 2)
    shards = lax.axis_size("shard")
    me = lax.axis_index("shard").reshape(1)
    replica = lax.axis_index("dp")
    count = bits_of("dp")
    levels = (count, 1)
    numbers = [
        sum(((replica >> bit) & 1) << (level - 1 - bit) for bit in range(level))
        for level in range(1, count + 1)
    ]
    place = jnp.concatenate([me, jnp.stack(numbers)])
    seqs, length, width = tokens.shape
    rows = seqs * length
    kd, vd, ff = H * KD, H * VD, w_down.shape[0]
    vp = H * VP
    vg_t, gu_t = turned(w_vg), turned(w_gu)

    low = lambda item: item.astype(LOW)
    def heads(item):
        return [
            jnp.pad(item[h * VD : (h + 1) * VD], ((0, VP - VD), (0, 0))) for h in range(H)
        ]

    first = jnp.concatenate(
        [low(w_qk[1]).T, low(vg_t[0]), jnp.pad(low(norm_gains), ((0, 14), (0, 0)))]
    )
    second = jnp.concatenate([low(w_qk[0]).T, low(vg_t[1])])
    third = jnp.concatenate([*heads(low(w_out)), low(gu_t[0]), low(gu_t[1]), low(w_down)])
    first_held = gather_shards(first)
    second = after(second, first_held[1][2])
    second_held = gather_shards(second)
    third = after(third, second_held[1][2])
    w_rest = lax.all_gather(third, "shard", axis=1, tiled=True)
    side = (lax.axis_index("dp") & 1).reshape(1)

    half_width = KD // 2
    freq_rates = jnp.exp(-math.log(10000.0) * jnp.arange(half_width).astype(WIDE) / half_width)
    positions = (lax.axis_index("shard") * length + jnp.arange(length)).astype(WIDE)
    angles = positions[:, None] * freq_rates[None, :]
    cos, sin = jnp.cos(angles), jnp.sin(angles)

    tok = tokens.reshape(rows, width)
    cot = cotangent.reshape(rows, width)
    seg_col = segments.reshape(rows, 1)
    seg_row = segments.reshape(rows // BLOCK, 1, BLOCK)
    in_last = jnp.where(lax.axis_index("shard") > 0, segments[:, 0], -1)
    decay = log_decay

    def tick(*done):
        nonlocal decay, place, gains
        decay, place, gains = lax.optimization_barrier((decay, place, gains, *done))[:3]

    plan = [(0, 0, 0, kd)] + [(kd + h * VD, 0, kd + h * VP, VD) for h in range(H)]
    plan += [(kd + vd, 1, 0, 16)]
    fills = [(0, kd + h * VP + VD, VP - VD) for h in range(H)]
    w_kv, gains = assemble(first_held, plan, fills, [kd + vp, 16], width, me, side)
    tick(third, second_held[2][2])
    hid, k, v, kv, leaving = front(
        seqs, length, tok, seg_col, segments, decay, w_kv, gains, cos, sin
    )
    passing = Passing(leaving, False)
    tick(leaving)
    plan = [(0, 0, 0, kd)] + [(kd + h * VD, 0, kd + h * VP, VD) for h in range(H)]
    (w_qg,) = assemble(second_held, plan, fills, [kd + vp], width, after(me, leaving), side)
    tick(w_qg)
    tick(passing.turn(decay, length, leaving))
    q, intra, gate = inner(k, v, hid, w_qg, cos, sin, seg_col, seg_row, decay, length)
    tick(q)
    passing.finish(q)
    tokens_out, hid2, prod, dgate, dup, mixed, glow, ggate, gret, st, dst, leaving = middle(
        seqs, length, ff, (intra, gate, q, tok, cot), seg_col, segments, in_last, decay,
        w_rest, gains, passing.got, kv,
    )
    returning = Passing(leaving, True)
    tick(leaving)

    def halves(row):
        return [(h * VP, row + h * VD, VD) for h in range(H)]

    fit = lambda used, level: used + -used % (16 << level)
    plan = [(0, 1, [(0, 0, ff)]), (2, 3, [(0, ff, ff)]), (4, 3, [(0, 2 * ff, ff)])]
    (made,) = weight_grads([prod, cot, dgate, hid2, dup], plan, place)
    tick(made)
    tick(returning.turn(decay, length, made))
    plan = [(0, 1, halves(0)), (2, 3, halves(vd))]
    made = weight_grads(
        [mixed, glow, ggate, hid], plan, place, shards,
        fit(2 * vd + 3 * ff, levels[0]), levels[0], (made,),
    )
    early = Reduction(*made, levels[0])
    tick(made[0])
    returning.finish(made[0])
    tick(early.cross(made[0]))
    dq, dk, dv = back(
        seqs, length, (q, k, v, gret), cos, sin, seg_col, seg_row, segments, in_last, decay,
        st, dst, returning.got,
    )
    tick(dq)
    plan = [(0, 3, [(0, 0, kd)]), (1, 3, [(0, kd, kd)]), (2, 3, halves(2 * kd))]
    made = weight_grads(
        [dq, dk, dv, hid], plan, place, shards, fit(2 * kd + vd, levels[1]), levels[1]
    )
    late = Reduction(*made, levels[1])
    tick(made[0])
    tick(early.next(made[0]))
    tick(late.cross(made[0]))
    blocks = rows // BLOCK
    data = (dq, dk, dv, ggate, tok, glow, w_kv, w_qg)
    grad_input = input_grad(0, blocks // 2, *data, gains, None)
    tick(grad_input)
    tick(early.next(grad_input))
    for block in range(blocks // 2, blocks):
        grad_input = input_grad(block, 1, *data, gains, grad_input)
        tick(grad_input)
        sent = late.next(grad_input)
        if block < blocks - 1:
            tick(sent, early.next(grad_input))
    while early.bit < early.stages() or late.bit < late.stages():
        for item in (late, early):
            if item.bit < item.stages():
                item.next()

    gain_grads, total, *grads = squares(
        vd, ff, levels, place, [early.result(), late.result()], w_qk, vg_t, gu_t, norm_gains
    )
    others = [
        lax.ppermute(total, "shard", [(i, i ^ mask) for i in range(shards)]) for mask in (1, 2, 3)
    ]
    arrays = []
    for group in ((w_qk, w_vg, w_out, w_gu, w_down, norm_gains), states[:6], states[6:]):
        arrays += [turned(item) if i in (1, 3) else item for i, item in enumerate(group)]
    *results, norm = update(vd, ff, [total, *others], grads, gain_grads, arrays)
    results = [turned(item) if i % 6 in (1, 3) else item for i, item in enumerate(results)]
    return (
        tokens_out.reshape(tokens.shape),
        grad_input.reshape(tokens.shape),
        *results,
        norm.reshape(()),
    )


def solution(mesh):
    split = P("dp", "shard", None)
    rows, columns = P(None, "shard", None), P(None, "shard")
    group = (rows, rows, columns, rows, columns, columns)
    in_specs = (split, split, P("dp", "shard"), P()) + group * 3
    out_specs = (split, split) + group * 3 + (P(),)
    return jax.shard_map(
        on_device, mesh=mesh, in_specs=in_specs, out_specs=out_specs, check_vma=False
    )
```

```python
import functools
import math

import jax
import jax.numpy as jnp
from jax import lax
from jax.experimental import pallas as pl
from jax.experimental.pallas import tpu as pltpu
from jax.sharding import PartitionSpec as P

H = 2
KD = 256
VD = 432
VP = 512
BLOCK = 512
STEP = 10

EPS = 1e-05
ADAM_EPS = 1e-08
BETA_ONE = 0.9
BETA_TWO = 0.95
MATRIX_RATE = 0.15
GAIN_RATE = 1.0
DECAY_WEIGHT = 0.1
CLIP = 1.0

LOW = jnp.bfloat16
WIDE = jnp.float32
VMEM = pltpu.VMEM
SMEM = pltpu.SMEM
LIMIT = 60 * 1024 * 1024


def dot(a, b):
    return jnp.dot(a, b, preferred_element_type=WIDE)


def dot_nt(a, b):
    return lax.dot_general(a, b, (((1,), (1,)), ((), ())), preferred_element_type=WIDE)


def dot_tn(a, b):
    return lax.dot_general(a, b, (((0,), (0,)), ((), ())), preferred_element_type=WIDE)


def params(**more):
    return pltpu.CompilerParams(vmem_limit_bytes=LIMIT, **more)


def cost(flops, moved):
    return pl.CostEstimate(flops=int(flops), bytes_accessed=int(moved), transcendentals=0)


def smem():
    return pl.BlockSpec(memory_space=SMEM)


def whole(shape):
    return pl.BlockSpec(shape, lambda *at: (0,) * len(shape), pipeline_mode=pl.Buffered(1))


def shape(dims, kind):
    return jax.ShapeDtypeStruct(dims, kind)


def bits_of(axis):
    return (lax.axis_size(axis) - 1).bit_length()


def exchange(value, axis, bit):
    size = lax.axis_size(axis)
    return lax.ppermute(value, axis, [(i, i ^ (1 << bit)) for i in range(size)])


def gather_shards(own):
    held = [(0, own)]
    for bit in reversed(range(bits_of("shard"))):
        held += [(mask | (1 << bit), exchange(part, "shard", bit)) for mask, part in held]
    return [(mask, None, part) for mask, part in held]


def add_low(one, two):
    return (one.astype(WIDE) + two.astype(WIDE)).astype(LOW)


class Reduction:
    def __init__(self, keep, send, levels):
        self.keep = keep
        self.near = exchange(send, "shard", 0)
        self.levels = levels
        self.bit = 0

    def cross(self, *done):
        self.near = after(self.near, *done)
        low = add_low(self.keep[1], self.near[1])
        self.got = exchange(low, "shard", 1)
        self.terms = [self.keep[0], self.near[0]]
        return low

    def next(self, *done):
        got = after(self.got, *done)
        count = bits_of("dp")
        if self.bit <= count:
            terms = [*self.terms, got]

            def total(at):
                return sum(term[at].astype(WIDE) for term in terms).astype(LOW)

            rows = got.shape[0]
            if self.bit == count:
                self.held = total(slice(0, rows))
            elif self.bit < self.levels:
                self.terms = [total(slice(0, rows // 2))]
                sent = total(slice(rows // 2, rows))
            else:
                sent = total(slice(0, rows))
                self.terms = [sent]
        else:
            self.held = jnp.concatenate([self.held, got])
        if self.bit >= count:
            bit = self.levels - 1 - (self.bit - count)
            sent = self.held
        else:
            bit = self.bit
        self.bit += 1
        self.got = exchange(sent, "dp", bit)
        return sent

    def stages(self):
        return bits_of("dp") + self.levels

    def result(self):
        return self.held, self.got


class Passing:
    def __init__(self, local, reverse):
        self.local = local
        steps = [[(0, 1), (2, 3)], [(1, 2)], [(2, 3)]]
        if reverse:
            steps = [[(3 - a, 3 - b) for a, b in step] for step in steps]
        self.steps = steps
        self.got = [lax.ppermute(local, "shard", steps[0])]

    def turn(self, decay, length, *done):
        self.got[0] = after(self.got[0], *done)
        total = combine(decay, length, self.local, self.got[0])
        self.got.append(lax.ppermute(total, "shard", self.steps[1]))
        return total

    def finish(self, *done):
        self.got.append(lax.ppermute(after(self.got[1], *done), "shard", self.steps[2]))


def entering(decay, length, h, got):
    factor = jnp.exp(jnp.full((1, 1), decay[h] * length, WIDE))
    wide = [item[h].astype(WIDE) for item in got]
    return wide[0] + wide[1] + factor * wide[2]


def after(value, *others):
    return lax.optimization_barrier((value, *others))[0]


def combine_kernel(length, decay, local, got, out):
    h = pl.program_id(0) % H
    factor = jnp.exp(jnp.full((1, 1), decay[h] * length, WIDE))
    out[...] = (local[...].astype(WIDE) + factor * got[...].astype(WIDE)).astype(LOW)


def combine(decay, length, local, got):
    block = pl.BlockSpec((None, None, KD, VP), lambda i: (i // H, i % H, 0, 0))
    return pl.pallas_call(
        functools.partial(combine_kernel, length),
        grid=(local.shape[0] * H,),
        out_shape=shape(local.shape, LOW),
        in_specs=[smem(), block, block],
        out_specs=block,
        compiler_params=params(),
        cost_estimate=cost(local.size, 6 * local.size),
    )(decay, local, got)


def assemble_kernel(plan, fills, sources_of, me_ref, side_ref, *refs):
    sources, outs = refs[: len(sources_of)], refs[len(sources_of) :]
    lanes = sources[0].shape[1]
    for index, row, size in fills:
        outs[index][row : row + size, :] = jnp.zeros((size, outs[index].shape[1]), LOW)

    def place(source, lane, low, high):
        for start, index, row, size in plan:
            begin, end = max(start, low), min(start + size, high)
            if begin < end:
                to = row + begin - start
                outs[index][to : to + end - begin, pl.ds(lane, lanes)] = source[
                    begin - low : end - low, :
                ]

    for (mask, half), source in zip(sources_of, sources):
        lane = pl.multiple_of(jnp.bitwise_xor(me_ref[0], mask) * lanes, lanes)
        rows = source.shape[0]
        if half is None:
            place(source, lane, 0, rows)
            continue
        for side in range(2):

            @pl.when(side_ref[0] == side)
            def _():
                low = (side ^ half) * rows
                place(source, lane, low, low + rows)


def assemble(held, plan, fills, heights, width, me, side):
    sources_of = [(mask, half) for mask, half, part in held]
    parts = [part for mask, half, part in held]
    return pl.pallas_call(
        functools.partial(assemble_kernel, plan, fills, sources_of),
        out_shape=[shape((rows, width), LOW) for rows in heights],
        in_specs=[smem()] * 2 + [pl.BlockSpec(memory_space=VMEM)] * len(parts),
        out_specs=[pl.BlockSpec(memory_space=VMEM)] * len(heights),
        compiler_params=params(),
        cost_estimate=cost(0, 4 * sum(heights) * width),
    )(me, side, *parts)


def rotated(flat, cosine, sine):
    half = KD // 2
    parts = []
    for h in range(H):
        u = flat[:, h * KD : h * KD + half]
        w = flat[:, h * KD + half : (h + 1) * KD]
        parts += [u * cosine - w * sine, w * cosine + u * sine]
    return jnp.concatenate(parts, axis=1)


def column(size):
    return lax.broadcasted_iota(jnp.int32, (size, 1), 0).astype(WIDE)


def front_kernel(count, decay, seg_s, tok, w, gains, cos, sin, seg, *rest):
    hid, k, v, kv, out_state, state = rest
    seq = pl.program_id(0) // count
    c = pl.program_id(0) % count
    x = tok[...].astype(WIDE)
    r = lax.rsqrt(jnp.mean(x * x, axis=1, keepdims=True) + EPS)
    h1 = (x * r * gains[0:1, :].astype(WIDE)).astype(LOW)
    hid[...] = h1
    kd = H * KD
    key = rotated(dot_nt(h1, w[:kd, :]), cos[...], sin[...]).astype(LOW)
    k[...] = key
    val = dot_nt(h1, w[kd : kd + H * VP, :]).astype(LOW)
    v[...] = val
    first = seg_s[seq, c * BLOCK]
    last = seg_s[seq, c * BLOCK + BLOCK - 1]
    before = seg_s[seq, jnp.maximum(c * BLOCK - 1, 0)]
    here = (seg[...] == last).astype(WIDE)
    joined = jnp.logical_and(jnp.logical_and(first == last, first == before), c > 0)
    for h in range(H):
        a = decay[h]
        kw = jnp.exp(a * (BLOCK - 1.0 - column(BLOCK))) * here
        kk = (key[:, h * KD : (h + 1) * KD].astype(WIDE) * kw).astype(LOW)
        add = dot_tn(kk, val[:, h * VP : (h + 1) * VP])
        kv[h] = add
        factor = jnp.exp(jnp.full((1, 1), a * BLOCK, WIDE))
        total = jnp.where(joined, factor * state[h], 0.0) + add
        state[h] = total
        out_state[h] = total.astype(LOW)


def row_block(width):
    return pl.BlockSpec((BLOCK, width), lambda t: (t, 0))


def state_block(count, at=lambda c: c):
    return pl.BlockSpec(
        (None, None, H, KD, VP), lambda t: (t // count, at(t % count), 0, 0, 0)
    )


def seq_block(count):
    return pl.BlockSpec((None, H, KD, VP), lambda t: (t // count, 0, 0, 0))


def front(seqs, length, tokens, seg_col, segments, decay, w, gains, cos, sin):
    count = length // BLOCK
    rows, width = tokens.shape
    outs = [width, H * KD, H * VP]
    table = pl.BlockSpec((BLOCK, KD // 2), lambda t: (t % count, 0))
    return pl.pallas_call(
        functools.partial(front_kernel, count),
        grid=(seqs * count,),
        out_shape=[shape((rows, n), LOW) for n in outs]
        + [shape((seqs, count, H, KD, VP), WIDE), shape((seqs, H, KD, VP), LOW)],
        in_specs=[smem(), smem(), row_block(width), whole(w.shape), whole(gains.shape)]
        + [table, table, row_block(1)],
        out_specs=[row_block(n) for n in outs]
        + [state_block(count), seq_block(count)],
        scratch_shapes=[VMEM((H, KD, VP), WIDE)],
        compiler_params=params(),
        cost_estimate=cost(2 * rows * width * w.shape[0], 12 * rows * width),
    )(decay, segments, tokens, w, gains, cos, sin, seg_col)


def decay_row(a):
    return jnp.exp(-a * lax.broadcasted_iota(jnp.int32, (1, BLOCK), 1).astype(WIDE))


def mixing(a, top, size, seg, seg_row):
    reach = top + size
    rows = jnp.exp(a * (column(size) + float(top)))
    same = seg[top:reach, :] == seg_row[:, :reach]
    n = lax.broadcasted_iota(jnp.int32, (size, reach), 0) + top
    m = lax.broadcasted_iota(jnp.int32, (size, reach), 1)
    return jnp.where(jnp.logical_and(same, n >= m), rows * decay_row(a)[:, :reach], 0.0)


TILE = 256


def inner_kernel(decay, k, v, hid, w, cos, sin, seg, seg_row, q, intra, gate):
    kd = H * KD
    query = rotated(dot_nt(hid[...], w[:kd, :]), cos[...], sin[...]).astype(LOW)
    q[...] = query
    gate[...] = dot_nt(hid[...], w[kd:, :]).astype(LOW)
    for i in range(BLOCK // TILE):
        top, reach = i * TILE, (i + 1) * TILE
        for h in range(H):
            s = dot_nt(query[top:reach, h * KD : (h + 1) * KD], k[:reach, h * KD : (h + 1) * KD])
            weights = (s * mixing(decay[h], top, TILE, seg, seg_row)).astype(LOW)
            intra[top:reach, h * VP : (h + 1) * VP] = dot(
                weights, v[:reach, h * VP : (h + 1) * VP]
            ).astype(LOW)


def inner(k, v, hid, w, cos, sin, seg_col, seg_row, decay, length):
    rows, width = hid.shape
    count = length // BLOCK
    block = lambda n: pl.BlockSpec((BLOCK, n), lambda t: (t, 0))
    table = pl.BlockSpec((BLOCK, KD // 2), lambda t: (t % count, 0))
    return pl.pallas_call(
        inner_kernel,
        grid=(rows // BLOCK,),
        out_shape=[shape((rows, n), LOW) for n in (H * KD, H * VP, H * VP)],
        in_specs=[
            smem(),
            block(H * KD),
            block(H * VP),
            block(width),
            whole(w.shape),
            table,
            table,
            block(1),
            pl.BlockSpec((None, 1, BLOCK), lambda t: (t, 0, 0)),
        ],
        out_specs=[block(n) for n in (H * KD, H * VP, H * VP)],
        compiler_params=params(),
        cost_estimate=cost(rows * (2 * width * 1536 + 2 * BLOCK * H * VP), 8 * rows * H * VP),
    )(decay, k, v, hid, w, cos, sin, seg_col, seg_row)


CHUNK = 16


def interleaved(first, second):
    steps = [((i + 0.5) / len(first), 0, step) for i, step in enumerate(first)]
    steps += [((i + 0.5) / len(second), 1, step) for i, step in enumerate(second)]
    for place, which, step in sorted(steps, key=lambda item: item[:2]):
        step()


def pieces(width, size=256):
    return [(start, min(start + size, width)) for start in range(0, width, size)]


def across(narrow, width):
    return jnp.concatenate([narrow] * (width // 128), axis=1)


def middle_kernel(count, ff, decay, seg_s, in_last, *refs):
    (intra, gate, q, tok, cot, seg, w, gains, *got, kv) = refs[:12]
    outs, scratch = refs[12:24], refs[24:]
    (tok_out, hid2, prod, dgate, dup, mixed, glow, ggate, gret, st_out, dst, leave) = outs
    (state, now, queries, factors, ret_s, norm_s, silu_s, slope_s, inv_s, res_s, ff_s, low_s, sums) = scratch
    seq = pl.program_id(0) // count
    c = pl.program_id(0) % count
    start = c * BLOCK
    vp = H * VP
    width = tok.shape[1]
    before = jnp.where(c > 0, seg_s[seq, jnp.maximum(start - 1, 0)], in_last[seq])

    @pl.when(c == 0)
    def _():
        for h in range(H):
            total = entering(decay, count * BLOCK, h, got)
            state[h] = total
            now[h] = total.astype(LOW)

    for b in range(1, count):

        @pl.when(c == b)
        def _():
            prev = seg_s[seq, (b - 1) * BLOCK - 1] if b > 1 else in_last[seq]
            joined = jnp.logical_and(
                seg_s[seq, (b - 1) * BLOCK] == seg_s[seq, b * BLOCK - 1],
                seg_s[seq, (b - 1) * BLOCK] == prev,
            )
            for h in range(H):
                factor = jnp.exp(jnp.full((1, 1), decay[h] * BLOCK, WIDE))
                total = jnp.where(joined, factor * state[h], 0.0) + kv[h]
                state[h] = total
                now[h] = total.astype(LOW)

    st_out[...] = now[...]
    here = (seg[...] == before).astype(WIDE)
    for h in range(H):
        qw = jnp.exp(decay[h] * (column(BLOCK) + 1.0)) * here
        factors[h] = jnp.broadcast_to(qw, (BLOCK, 128))

    w_out = (0, vp)
    w_gate = (vp, vp + ff)
    w_up = (vp + ff, vp + 2 * ff)
    w_down = (vp + 2 * ff, vp + 3 * ff)
    gain = gains[1:2, :].astype(WIDE)

    def phases(top):
        rs = pl.ds(top, TILE)
        lists = []

        def add(steps):
            lists.append(steps)

        def chunks():
            return [pl.ds(row, CHUNK) for row in range(top, top + TILE, CHUNK)]

        def cross(h, lo, hi):
            ret_s[rs, h * VP + lo : h * VP + hi] = dot(
                q[rs, h * KD : (h + 1) * KD], now[h, :, lo:hi]
            )

        add([functools.partial(cross, h, *piece) for h in range(H) for piece in pieces(VP)])

        def gated(h, r):
            hv = slice(h * VP, (h + 1) * VP)
            hk = slice(h * KD, (h + 1) * KD)
            qw = factors[h, r, :]
            queries[r, hk] = (q[r, hk].astype(WIDE) * across(qw, KD)).astype(LOW)
            ret = intra[r, hv].astype(WIDE) + across(qw, VP) * ret_s[r, hv]
            mean = jnp.sum(ret, axis=1, keepdims=True) * (1.0 / VD)
            centered = ret - mean
            square = jnp.sum(centered * centered, axis=1, keepdims=True)
            var = (square - (VP - VD) * (mean * mean)) * (1.0 / VD)
            inv = lax.rsqrt(var + 1.0 * KD)
            nh = centered * inv
            g = gate[r, hv].astype(WIDE)
            sg = 0.5 * jnp.tanh(0.5 * g) + 0.5
            sl = g * sg
            mixed[r, hv] = (nh * sl).astype(LOW)
            norm_s[r, hv] = nh
            silu_s[r, hv] = sl
            slope_s[r, hv] = nh * (sg + sl * (1.0 - sg))
            inv_s[h, r, :] = jnp.broadcast_to(inv, (CHUNK, 128))

        add([functools.partial(gated, h, r) for r in chunks() for h in range(H)])

        def project(lo, hi):
            res_s[rs, lo:hi] = dot(mixed[rs, :], w[w_out[0] : w_out[1], lo:hi])

        add([functools.partial(project, *piece) for piece in pieces(width)])

        def norm(r):
            resid = tok[r, :].astype(WIDE) + res_s[r, :]
            r2 = lax.rsqrt(jnp.mean(resid * resid, axis=1, keepdims=True) + EPS)
            res_s[r, :] = resid
            hid2[r, :] = (resid * r2 * gain).astype(LOW)
            inv_s[H, r, :] = jnp.broadcast_to(r2, (CHUNK, 128))

        add([functools.partial(norm, r) for r in chunks()])

        def forward(place, source, at, lo, hi):
            ff_s[place, rs, lo:hi] = dot_nt(source[rs, :], w[at[0] + lo : at[0] + hi, :])

        add(
            [
                functools.partial(forward, place, source, at, *piece)
                for piece in pieces(ff)
                for place, source, at in ((0, hid2, w_gate), (1, hid2, w_up), (2, cot, w_down))
            ]
        )

        def gelu(r, lo, hi):
            gf, uf, gp = ff_s[0, r, lo:hi], ff_s[1, r, lo:hi], ff_s[2, r, lo:hi]
            e = jnp.exp(-0.5 * (gf * gf))
            d = 1.0 / (1.0 + (0.3275911 * math.sqrt(0.5)) * jnp.abs(gf))
            poly = d * (
                0.5 * 0.254829592
                + d
                * (
                    0.5 * -0.284496736
                    + d * (0.5 * 1.421413741 + d * (0.5 * -1.453152027 + d * (0.5 * 1.061405429)))
                )
            )
            tail = poly * e
            cdf = jnp.where(gf >= 0.0, 1.0 - tail, tail)
            ge = gf * cdf
            dge = cdf + gf * (e * (1.0 / math.sqrt(2.0 * math.pi)))
            prod[r, lo:hi] = (ge * uf).astype(LOW)
            dgate[r, lo:hi] = (gp * uf * dge).astype(LOW)
            dup[r, lo:hi] = (gp * ge).astype(LOW)

        add([functools.partial(gelu, r, *piece) for r in chunks() for piece in pieces(ff, 512)])

        def down(lo, hi):
            low_s[0, rs, lo:hi] = dot(prod[rs, :], w[w_down[0] : w_down[1], lo:hi])

        def hidden(lo, hi):
            low_s[1, rs, lo:hi] = dot(dgate[rs, :], w[w_gate[0] : w_gate[1], lo:hi]) + dot(
                dup[rs, :], w[w_up[0] : w_up[1], lo:hi]
            )

        add([functools.partial(step, *piece) for piece in pieces(width) for step in (down, hidden)])

        def residual(r):
            resid = res_s[r, :]
            r2 = across(inv_s[H, r, :], width)
            tok_out[r, :] = (resid + low_s[0, r, :]).astype(LOW)
            gh = low_s[1, r, :] * gain
            xhat = resid * r2
            inner_product = jnp.mean(gh * xhat, axis=1, keepdims=True)
            glow[r, :] = (cot[r, :].astype(WIDE) + r2 * (gh - xhat * inner_product)).astype(LOW)

        add([functools.partial(residual, r) for r in chunks()])

        def mix_back(lo, hi):
            ret_s[rs, lo:hi] = dot_nt(glow[rs, :], w[w_out[0] + lo : w_out[0] + hi, :])

        add([functools.partial(mix_back, *piece) for piece in pieces(vp)])

        def gated_back(h, r):
            hv = slice(h * VP, (h + 1) * VP)
            gm = ret_s[r, hv]
            nh = norm_s[r, hv]
            ggate[r, hv] = (gm * slope_s[r, hv]).astype(LOW)
            gn = gm * silu_s[r, hv]
            one = jnp.sum(gn, axis=1, keepdims=True) * (1.0 / VD)
            two = jnp.sum(gn * nh, axis=1, keepdims=True) * (1.0 / VD)
            gret[r, hv] = (across(inv_s[h, r, :], VP) * (gn - one - nh * two)).astype(LOW)

        add([functools.partial(gated_back, h, r) for r in chunks() for h in range(H)])
        return lists

    first, second = phases(0), phases(TILE)
    for k in range(len(first) + 1):
        interleaved(first[k] if k < len(first) else [], second[k - 1] if k else [])
    for h in range(H):
        add = dot_tn(queries[:, h * KD : (h + 1) * KD], gret[:, h * VP : (h + 1) * VP])
        dst[h] = add
        sums[c, h] = add

    @pl.when(c == count - 1)
    def _():
        for h in range(H):
            total = sums[count - 1, h]
            for b in reversed(range(count - 1)):
                prev = seg_s[seq, b * BLOCK - 1] if b > 0 else in_last[seq]
                joined = jnp.logical_and(
                    seg_s[seq, b * BLOCK] == seg_s[seq, (b + 1) * BLOCK - 1],
                    seg_s[seq, b * BLOCK] == prev,
                )
                factor = jnp.exp(jnp.full((1, 1), decay[h] * BLOCK, WIDE))
                total = jnp.where(joined, factor * total, 0.0) + sums[b, h]
            leave[h] = total.astype(LOW)


def middle(seqs, length, ff, data, seg_col, segments, in_last, decay, w, gains, got, kv):
    intra, gate, q, tokens, cotangent = data
    rows, width = tokens.shape
    count = length // BLOCK
    vp = H * VP
    outs = [width, width, ff, ff, ff, vp, width, vp, vp]
    inputs = [decay, segments, in_last, intra, gate, q, tokens, cotangent, seg_col, w, gains, *got, kv]
    specs = [smem()] * 3 + [row_block(n) for n in (vp, vp, H * KD, width, width, 1)]
    specs += [whole(w.shape), whole(gains.shape), *[seq_block(count)] * 3]
    specs += [state_block(count, lambda c: jnp.maximum(c - 1, 0))]
    one = (H, KD, VP)
    states = (seqs, count, *one)
    return pl.pallas_call(
        functools.partial(middle_kernel, count, ff),
        grid=(seqs * count,),
        out_shape=[shape((rows, n), LOW) for n in outs]
        + [shape(states, LOW), shape(states, WIDE), shape((seqs, *one), LOW)],
        in_specs=specs,
        out_specs=[row_block(n) for n in outs]
        + [state_block(count)] * 2
        + [seq_block(count)],
        scratch_shapes=[
            VMEM(one, WIDE),
            VMEM(one, LOW),
            VMEM((BLOCK, H * KD), LOW),
            VMEM((H, BLOCK, 128), WIDE),
            VMEM((BLOCK, vp), WIDE),
            VMEM((BLOCK, vp), WIDE),
            VMEM((BLOCK, vp), WIDE),
            VMEM((BLOCK, vp), WIDE),
            VMEM((H + 1, BLOCK, 128), WIDE),
            VMEM((BLOCK, width), WIDE),
            VMEM((3, BLOCK, ff), WIDE),
            VMEM((2, BLOCK, width), WIDE),
            VMEM(states[1:], WIDE),
        ],
        compiler_params=params(),
        cost_estimate=cost(2 * rows * width * (2 * vp + 6 * ff), 30 * rows * width),
    )(*inputs)


def weight_kernel(plan, count, levels, me_ref, *refs):
    ins, ready, outs, total = refs[:count], refs[count:-3], refs[-3:-1], refs[-1]
    if levels is None:
        outs = refs[-2:-1]
    t = pl.program_id(0)
    last = pl.num_programs(0) - 1
    for left, right, cuts in plan:
        a, b = ins[left], ins[right]
        for source, row, size in cuts:
            add = dot_tn(a[:, source : source + size], b[...])

            @pl.when(t == 0)
            def _():
                total[row : row + size, :] = add

            @pl.when(t > 0)
            def _():
                total[row : row + size, :] += add

    @pl.when(t == last)
    def _():
        used = max(row + size for left, right, cuts in plan for source, row, size in cuts)
        if levels is None:
            outs[0][...] = total[...].astype(LOW)
            return
        for item in ready:
            total[used : used + item.shape[0], :] = item[...].astype(WIDE)
            used += item.shape[0]
        if used < total.shape[0]:
            total[used:, :] = jnp.zeros((total.shape[0] - used, total.shape[1]), WIDE)
        lanes = outs[0].shape[2]
        pieces = 2**levels
        rows = outs[0].shape[1] // pieces
        for part in range(2 * outs[0].shape[0]):
            target = outs[part & 1]
            lane = pl.multiple_of(jnp.bitwise_xor(me_ref[0], part) * lanes, lanes)
            for q in range(pieces):
                row = pl.multiple_of(jnp.bitwise_xor(me_ref[levels], q) * rows, 16)
                target[part >> 1, q * rows : (q + 1) * rows, :] = total[
                    pl.ds(row, rows), pl.ds(lane, lanes)
                ].astype(LOW)


def weight_grads(arrays, plan, place, shards=2, height=0, levels=None, ready=()):
    rows = arrays[0].shape[0]
    used = max(row + size for left, right, cuts in plan for source, row, size in cuts)
    width = arrays[plan[0][1]].shape[1]
    tile = 2 * BLOCK
    block = lambda n: pl.BlockSpec((tile, n), lambda t: (t, 0))
    dims = [(shards // 2, height, width // shards)] * 2
    if levels is None:
        height, dims = used, [(used, width)]
    full = lambda item: pl.BlockSpec(item, lambda t: (0,) * len(item))
    return pl.pallas_call(
        functools.partial(weight_kernel, plan, len(arrays), levels),
        grid=(rows // tile,),
        out_shape=[shape(item, LOW) for item in dims],
        in_specs=[smem()] + [block(item.shape[1]) for item in arrays]
        + [full(item.shape) for item in ready],
        out_specs=[full(item) for item in dims],
        scratch_shapes=[VMEM((height, width), WIDE)],
        compiler_params=params(),
        cost_estimate=cost(2 * rows * used * width, 2 * rows * sum(i.shape[1] for i in arrays)),
    )(place, *arrays, *ready)


def back_kernel(count, decay, seg_s, in_last, *refs):
    (q, k, v, gret, cos, sin, seg, seg_row, st, dst, *got) = refs[:13]
    (dq, dk, dv, state, weights, grads) = refs[13:]
    seq = pl.program_id(0) // count
    c = count - 1 - pl.program_id(0) % count

    @pl.when(c == count - 1)
    def _():
        for h in range(H):
            state[h] = entering(decay, count * BLOCK, h, got)

    for b in range(1, count):

        @pl.when(c == b - 1)
        def _():
            prev = seg_s[seq, b * BLOCK - 1]
            first = seg_s[seq, b * BLOCK]
            last = seg_s[seq, (b + 1) * BLOCK - 1]
            joined = jnp.logical_and(first == last, first == prev)
            for h in range(H):
                factor = jnp.exp(jnp.full((1, 1), decay[h] * BLOCK, WIDE))
                state[h] = jnp.where(joined, factor * state[h], 0.0) + dst[h]

    start = c * BLOCK
    before = jnp.where(c > 0, seg_s[seq, jnp.maximum(start - 1, 0)], in_last[seq])
    final = seg_s[seq, start + BLOCK - 1]
    here = (seg[...] == before).astype(WIDE)
    ends = (seg[...] == final).astype(WIDE)
    place = column(BLOCK)
    dqs, dks = [], []
    for h in range(H):
        a = decay[h]
        qh = q[:, h * KD : (h + 1) * KD]
        kh = k[:, h * KD : (h + 1) * KD]
        vh = v[:, h * VP : (h + 1) * VP]
        gh = gret[:, h * VP : (h + 1) * VP]
        qw = jnp.exp(a * (place + 1.0)) * here
        kw = jnp.exp(a * (BLOCK - 1.0 - place)) * ends
        parts = []
        for i in range(BLOCK // TILE):
            top, reach = i * TILE, (i + 1) * TILE
            mix = mixing(a, top, TILE, seg, seg_row)
            s = dot_nt(qh[top:reach, :], kh[:reach, :])
            weights[top:reach, :reach] = (s * mix).astype(LOW)
            gs = (dot_nt(gh[top:reach, :], vh[:reach, :]) * mix).astype(LOW)
            grads[top:reach, :reach] = gs
            parts.append(dot(gs, kh[:reach, :]))
        late = state[h].astype(LOW)
        dqs.append(jnp.concatenate(parts) + qw * dot_nt(gh, st[h]))
        parts, values = [], []
        for i in range(BLOCK // TILE):
            top, reach = i * TILE, (i + 1) * TILE
            parts.append(dot_tn(grads[top:, top:reach], qh[top:, :]))
            values.append(dot_tn(weights[top:, top:reach], gh[top:, :]))
        dks.append(jnp.concatenate(parts) + kw * dot_nt(vh, late))
        dv[:, h * VP : (h + 1) * VP] = (jnp.concatenate(values) + kw * dot(kh, late)).astype(LOW)
    dq[...] = rotated(jnp.concatenate(dqs, axis=1), cos[...], -sin[...]).astype(LOW)
    dk[...] = rotated(jnp.concatenate(dks, axis=1), cos[...], -sin[...]).astype(LOW)


def back(seqs, length, data, cos, sin, seg_col, seg_row, segments, in_last, decay, st, dst, got):
    rows = data[0].shape[0]
    count = length // BLOCK
    turn = lambda t: (t // count) * count + count - 1 - t % count
    block = lambda n: pl.BlockSpec((BLOCK, n), lambda t: (turn(t), 0))
    table = pl.BlockSpec((BLOCK, KD // 2), lambda t: (count - 1 - t % count, 0))
    outs = [H * KD, H * KD, H * VP]
    inputs = [decay, segments, in_last, *data, cos, sin, seg_col, seg_row, st, dst, *got]
    specs = [smem()] * 3 + [block(item.shape[1]) for item in data] + [table, table, block(1)]
    specs += [pl.BlockSpec((None, 1, BLOCK), lambda t: (turn(t), 0, 0))]
    specs += [state_block(count, lambda c: count - 1 - c)]
    specs += [state_block(count, lambda c: jnp.minimum(count - c, count - 1))]
    specs += [seq_block(count)] * 3
    return pl.pallas_call(
        functools.partial(back_kernel, count),
        grid=(seqs * count,),
        out_shape=[shape((rows, n), LOW) for n in outs],
        in_specs=specs,
        out_specs=[block(n) for n in outs],
        scratch_shapes=[
            VMEM((H, KD, VP), WIDE),
            VMEM((BLOCK, BLOCK), LOW),
            VMEM((BLOCK, BLOCK), LOW),
        ],
        compiler_params=params(),
        cost_estimate=cost(rows * H * 2 * BLOCK * 3 * (KD + VP), 16 * rows * H * VP),
    )(*inputs)


def input_kernel(dq, dk, dv, ggate, tok, glow, w_kv, w_qg, gains, *rest):
    out = rest[-1]
    kd = H * KD
    gh = dot(dq[...], w_qg[:kd, :]) + dot(dk[...], w_kv[:kd, :])
    gh += dot(dv[...], w_kv[kd:, :]) + dot(ggate[...], w_qg[kd:, :])
    x = tok[...].astype(WIDE)
    r = lax.rsqrt(jnp.mean(x * x, axis=1, keepdims=True) + EPS)
    xhat = x * r
    gh = gh * gains[0:1, :].astype(WIDE)
    inner_product = jnp.mean(gh * xhat, axis=1, keepdims=True)
    out[...] = (glow[...].astype(WIDE) + r * (gh - xhat * inner_product)).astype(LOW)


def input_grad(first, steps, dq, dk, dv, ggate, tokens, glow, w_kv, w_qg, gains, earlier):
    rows, width = tokens.shape
    parts = rows // BLOCK // steps
    arrays = [dq, dk, dv, ggate, tokens, glow]
    block = lambda item: pl.BlockSpec((BLOCK, item.shape[1]), lambda t: (first + t, 0))
    inputs = [*arrays, w_kv, w_qg, gains]
    specs = [block(item) for item in arrays] + [whole(item.shape) for item in (w_kv, w_qg, gains)]
    aliases = {}
    if earlier is not None:
        aliases = {len(inputs): 0}
        inputs.append(earlier)
        specs.append(pl.BlockSpec(memory_space=pl.ANY))
    return pl.pallas_call(
        input_kernel,
        grid=(steps,),
        out_shape=shape((rows, width), LOW),
        in_specs=specs,
        out_specs=block(tokens),
        input_output_aliases=aliases,
        compiler_params=params(),
        cost_estimate=cost(2 * rows * width * 2 * w_kv.shape[0] // parts, 20 * rows * width // parts),
    )(*inputs)


def adam_step(master, moment, second, grad, scale, rate, decay_weight):
    clipped = grad * scale
    moment_new = BETA_ONE * moment + (1.0 - BETA_ONE) * clipped
    second_new = BETA_TWO * second + (1.0 - BETA_TWO) * clipped * clipped
    corrected = (
        moment_new
        * (1.0 / (1.0 - BETA_ONE**STEP))
        / (jnp.sqrt(second_new * (1.0 / (1.0 - BETA_TWO**STEP))) + ADAM_EPS)
    )
    return (master - rate * (corrected + decay_weight * master), moment_new, second_new)


def squares_kernel(vd, ff, levels, place, *refs):
    halves, (w_qk, w_vg, w_gu, low_gains) = refs[:4], refs[4:8]
    grad_gains, total, early, late = refs[8:]
    kd = H * KD
    for index, target in enumerate((early, late)):
        pieces = 2 ** levels[index]
        rows = target.shape[0] // pieces
        for q in range(pieces):
            row = pl.multiple_of(jnp.bitwise_xor(place[levels[index]], q) * rows, 16)
            source = halves[2 * index + q // (pieces // 2)]
            start = q % (pieces // 2) * rows
            target[pl.ds(row, rows), :] = source[start : start + rows, :]

    def rows(source, start, size):
        return source[start : start + size, :].astype(WIDE)

    def product(weight, grad):
        return jnp.sum(weight.astype(LOW).astype(WIDE) * grad, axis=0, keepdims=True)

    sums = []

    def square(item):
        sums.append(jnp.sum(item * item, axis=0, keepdims=True))
        return item

    first = jnp.zeros((1, low_gains.shape[1]), WIDE)
    for i in range(2):
        grad = square(rows(late, i * kd, kd))
        first += jnp.sum(w_qk[i].astype(LOW).astype(WIDE).T * grad, axis=0, keepdims=True)
    first += product(w_vg[0], square(rows(late, 2 * kd, vd)))
    first += product(w_vg[1], square(rows(early, vd, vd)))
    square(rows(early, 0, vd))
    square(rows(early, 2 * vd, ff))
    second = product(w_gu[0], square(rows(early, 2 * vd + ff, ff)))
    second += product(w_gu[1], square(rows(early, 2 * vd + 2 * ff, ff)))
    gains = jnp.concatenate([first, second]) / low_gains[...].astype(LOW).astype(WIDE)
    grad_gains[...] = gains
    sums.append(jnp.sum(gains * gains, axis=0, keepdims=True))
    total[...] = jnp.broadcast_to(jnp.sum(sum(sums), axis=1, keepdims=True), total.shape)


def squares(vd, ff, levels, place, grads, w_qk, w_vg, w_gu, gains):
    halves = [half for pair in grads for half in pair]
    vmem = pl.BlockSpec(memory_space=VMEM)
    return pl.pallas_call(
        functools.partial(squares_kernel, vd, ff, levels),
        out_shape=[shape(gains.shape, WIDE), shape((8, 128), WIDE)]
        + [shape((2 * pair[0].shape[0], pair[0].shape[1]), LOW) for pair in grads],
        in_specs=[smem()] + [vmem] * 8,
        out_specs=[vmem] * 4,
        compiler_params=params(),
    )(place, *halves, w_qk, w_vg, w_gu, gains)


def update_kernel(vd, ff, *refs):
    totals, (early, late, gain_grads) = refs[:4], refs[4:7]
    sources, targets, norm_out = refs[7:25], refs[25:43], refs[43]
    ins, outs = refs[44:62], refs[62:80]
    arrived, sent = refs[80:]
    kd = H * KD
    order = [4, 3, 2, 1, 0, 5]
    places = [6 * group + place for place in order for group in range(3)]
    fetch = {i: pltpu.make_async_copy(sources[i], ins[i], arrived.at[i]) for i in places}
    send = {i: pltpu.make_async_copy(outs[i], targets[i], sent.at[i]) for i in places}
    for i in places:
        fetch[i].start()
    norm = jnp.sqrt((totals[0][...] + totals[1][...]) + (totals[2][...] + totals[3][...]))
    norm_out[0, 0] = jnp.max(norm)
    scale = jnp.minimum(1.0, CLIP / (norm + 1e-06))[0:1, 0:1]

    def step(place, at, grad, rate, decay_weight):
        results = adam_step(
            ins[place][at], ins[6 + place][at], ins[12 + place][at], grad, scale, rate, decay_weight
        )
        for group, result in enumerate(results):
            outs[6 * group + place][at] = result

    def rows(source, start, size):
        return source[start : start + size, :].astype(WIDE)

    grads = {
        4: [(..., lambda: rows(early, 2 * vd, ff))],
        3: [(i, lambda i=i: rows(early, 2 * vd + (1 + i) * ff, ff)) for i in range(2)],
        2: [(..., lambda: rows(early, 0, vd))],
        1: [(0, lambda: rows(late, 2 * kd, vd)), (1, lambda: rows(early, vd, vd))],
        0: [(i, lambda i=i: rows(late, i * kd, kd).T) for i in range(2)],
        5: [(..., lambda: gain_grads[...])],
    }
    for place in order:
        for group in range(3):
            fetch[6 * group + place].wait()
        rate, decay_weight = (GAIN_RATE, 0.0) if place == 5 else (MATRIX_RATE, DECAY_WEIGHT)
        for at, grad in grads[place]:
            step(place, at, grad(), rate, decay_weight)
        for group in range(3):
            send[6 * group + place].start()
    for i in places:
        send[i].wait()


def update(vd, ff, totals, grads, gain_grads, arrays):
    anywhere = pl.BlockSpec(memory_space=pl.ANY)
    return pl.pallas_call(
        functools.partial(update_kernel, vd, ff),
        out_shape=[shape(item.shape, WIDE) for item in arrays] + [shape((1, 1), WIDE)],
        in_specs=[pl.BlockSpec(memory_space=VMEM)] * 7 + [anywhere] * 18,
        out_specs=[anywhere] * 18 + [smem()],
        scratch_shapes=[VMEM(item.shape, WIDE) for item in arrays] * 2
        + [pltpu.SemaphoreType.DMA((18,))] * 2,
        compiler_params=params(),
    )(*totals, *grads, gain_grads, *arrays)


def on_device(
    tokens,
    cotangent,
    segments,
    log_decay,
    w_qk,
    w_vg,
    w_out,
    w_gu,
    w_down,
    norm_gains,
    *states,
):
    turned = lambda item: jnp.swapaxes(item, 1, 2)
    shards = lax.axis_size("shard")
    me = lax.axis_index("shard").reshape(1)
    replica = lax.axis_index("dp")
    count = bits_of("dp")
    levels = (count, 1)
    numbers = [
        sum(((replica >> bit) & 1) << (level - 1 - bit) for bit in range(level))
        for level in range(1, count + 1)
    ]
    place = jnp.concatenate([me, jnp.stack(numbers)])
    seqs, length, width = tokens.shape
    rows = seqs * length
    kd, vd, ff = H * KD, H * VD, w_down.shape[0]
    vp = H * VP
    vg_t, gu_t = turned(w_vg), turned(w_gu)

    low = lambda item: item.astype(LOW)
    def heads(item):
        return [
            jnp.pad(item[h * VD : (h + 1) * VD], ((0, VP - VD), (0, 0))) for h in range(H)
        ]

    first = jnp.concatenate(
        [low(w_qk[1]).T, low(vg_t[0]), jnp.pad(low(norm_gains), ((0, 14), (0, 0)))]
    )
    second = jnp.concatenate([low(w_qk[0]).T, low(vg_t[1])])
    third = jnp.concatenate([*heads(low(w_out)), low(gu_t[0]), low(gu_t[1]), low(w_down)])
    first_held = gather_shards(first)
    second_held = gather_shards(second)
    third = after(third, first_held[1][2])
    w_rest = lax.all_gather(third, "shard", axis=1, tiled=True)
    side = (lax.axis_index("dp") & 1).reshape(1)

    half_width = KD // 2
    freq_rates = jnp.exp(-math.log(10000.0) * jnp.arange(half_width).astype(WIDE) / half_width)
    positions = (lax.axis_index("shard") * length + jnp.arange(length)).astype(WIDE)
    angles = positions[:, None] * freq_rates[None, :]
    cos, sin = jnp.cos(angles), jnp.sin(angles)

    tok = tokens.reshape(rows, width)
    cot = cotangent.reshape(rows, width)
    seg_col = segments.reshape(rows, 1)
    seg_row = segments.reshape(rows // BLOCK, 1, BLOCK)
    in_last = jnp.where(lax.axis_index("shard") > 0, segments[:, 0], -1)
    decay = log_decay

    def tick(*done):
        nonlocal decay, place, gains
        decay, place, gains = lax.optimization_barrier((decay, place, gains, *done))[:3]

    plan = [(0, 0, 0, kd)] + [(kd + h * VD, 0, kd + h * VP, VD) for h in range(H)]
    plan += [(kd + vd, 1, 0, 16)]
    fills = [(0, kd + h * VP + VD, VP - VD) for h in range(H)]
    w_kv, gains = assemble(first_held, plan, fills, [kd + vp, 16], width, me, side)
    tick(third)
    hid, k, v, kv, leaving = front(
        seqs, length, tok, seg_col, segments, decay, w_kv, gains, cos, sin
    )
    passing = Passing(leaving, False)
    tick(leaving)
    plan = [(0, 0, 0, kd)] + [(kd + h * VD, 0, kd + h * VP, VD) for h in range(H)]
    (w_qg,) = assemble(second_held, plan, fills, [kd + vp], width, after(me, leaving), side)
    tick(w_qg)
    tick(passing.turn(decay, length, leaving))
    q, intra, gate = inner(k, v, hid, w_qg, cos, sin, seg_col, seg_row, decay, length)
    tick(q)
    passing.finish(q)
    tokens_out, hid2, prod, dgate, dup, mixed, glow, ggate, gret, st, dst, leaving = middle(
        seqs, length, ff, (intra, gate, q, tok, cot), seg_col, segments, in_last, decay,
        w_rest, gains, passing.got, kv,
    )
    returning = Passing(leaving, True)
    tick(leaving)

    def halves(row):
        return [(h * VP, row + h * VD, VD) for h in range(H)]

    fit = lambda used, level: used + -used % (16 << level)
    plan = [(0, 1, [(0, 0, ff)]), (2, 3, [(0, ff, ff)]), (4, 3, [(0, 2 * ff, ff)])]
    (made,) = weight_grads([prod, cot, dgate, hid2, dup], plan, place)
    tick(made)
    tick(returning.turn(decay, length, made))
    plan = [(0, 1, halves(0)), (2, 3, halves(vd))]
    made = weight_grads(
        [mixed, glow, ggate, hid], plan, place, shards,
        fit(2 * vd + 3 * ff, levels[0]), levels[0], (made,),
    )
    tick(made[0])
    returning.finish(made[0])
    early = Reduction(made[0], after(made[1], returning.got[1]), levels[0])
    tick(early.cross(made[0]))
    dq, dk, dv = back(
        seqs, length, (q, k, v, gret), cos, sin, seg_col, seg_row, segments, in_last, decay,
        st, dst, returning.got,
    )
    tick(dq)
    tick(early.next(dq))
    plan = [(0, 3, [(0, 0, kd)]), (1, 3, [(0, kd, kd)]), (2, 3, halves(2 * kd))]
    made = weight_grads(
        [dq, dk, dv, hid], plan, place, shards, fit(2 * kd + vd, levels[1]), levels[1]
    )
    late = Reduction(*made, levels[1])
    tick(made[0])
    tick(early.next(made[0]))
    tick(late.cross(made[0]))
    blocks = rows // BLOCK
    data = (dq, dk, dv, ggate, tok, glow, w_kv, w_qg)
    grad_input = input_grad(0, blocks // 2, *data, gains, None)
    tick(grad_input)
    tick(late.next(grad_input), early.next(grad_input))
    for block in range(blocks // 2, blocks):
        grad_input = input_grad(block, 1, *data, gains, grad_input)
        tick(grad_input)
        tick(late.next(grad_input), early.next(grad_input))
    while early.bit < early.stages() or late.bit < late.stages():
        for item in (late, early):
            if item.bit < item.stages():
                item.next()

    gain_grads, total, *grads = squares(
        vd, ff, levels, place, [early.result(), late.result()], w_qk, vg_t, gu_t, norm_gains
    )
    others = [
        lax.ppermute(total, "shard", [(i, i ^ mask) for i in range(shards)]) for mask in (1, 2, 3)
    ]
    arrays = []
    for group in ((w_qk, w_vg, w_out, w_gu, w_down, norm_gains), states[:6], states[6:]):
        arrays += [turned(item) if i in (1, 3) else item for i, item in enumerate(group)]
    *results, norm = update(vd, ff, [total, *others], grads, gain_grads, arrays)
    results = [turned(item) if i % 6 in (1, 3) else item for i, item in enumerate(results)]
    return (
        tokens_out.reshape(tokens.shape),
        grad_input.reshape(tokens.shape),
        *results,
        norm.reshape(()),
    )


def solution(mesh):
    split = P("dp", "shard", None)
    rows, columns = P(None, "shard", None), P(None, "shard")
    group = (rows, rows, columns, rows, columns, columns)
    in_specs = (split, split, P("dp", "shard"), P()) + group * 3
    out_specs = (split, split) + group * 3 + (P(),)
    return jax.shard_map(
        on_device, mesh=mesh, in_specs=in_specs, out_specs=out_specs, check_vma=False
    )
```

```python
import functools
import math

import jax
import jax.numpy as jnp
from jax import lax
from jax.experimental import pallas as pl
from jax.experimental.pallas import tpu as pltpu
from jax.sharding import PartitionSpec as P

H = 2
KD = 256
VD = 432
VP = 512
BLOCK = 512
STEP = 10

EPS = 1e-05
ADAM_EPS = 1e-08
BETA_ONE = 0.9
BETA_TWO = 0.95
MATRIX_RATE = 0.15
GAIN_RATE = 1.0
DECAY_WEIGHT = 0.1
CLIP = 1.0

LOW = jnp.bfloat16
WIDE = jnp.float32
VMEM = pltpu.VMEM
SMEM = pltpu.SMEM
MIB = 1024 * 1024


def dot(a, b):
    return jnp.dot(a, b, preferred_element_type=WIDE)


def dot_nt(a, b):
    return lax.dot_general(a, b, (((1,), (1,)), ((), ())), preferred_element_type=WIDE)


def dot_tn(a, b):
    return lax.dot_general(a, b, (((0,), (0,)), ((), ())), preferred_element_type=WIDE)


def params(size):
    return pltpu.CompilerParams(vmem_limit_bytes=size * MIB)


def cost(flops, moved):
    return pl.CostEstimate(flops=int(flops), bytes_accessed=int(moved), transcendentals=0)


def smem():
    return pl.BlockSpec(memory_space=SMEM)


def whole(shape):
    return pl.BlockSpec(shape, lambda *at: (0,) * len(shape), pipeline_mode=pl.Buffered(1))


def shape(dims, kind):
    return jax.ShapeDtypeStruct(dims, kind)


def bits_of(axis):
    return (lax.axis_size(axis) - 1).bit_length()


def exchange(value, axis, bit):
    size = lax.axis_size(axis)
    return lax.ppermute(value, axis, [(i, i ^ (1 << bit)) for i in range(size)])


def gather_shards(own):
    held = [(0, own)]
    for bit in reversed(range(bits_of("shard"))):
        held += [(mask | (1 << bit), exchange(part, "shard", bit)) for mask, part in held]
    return [(mask, None, part) for mask, part in held]


def add_low(one, two):
    return (one.astype(WIDE) + two.astype(WIDE)).astype(LOW)


class Reduction:
    def __init__(self, keep, send, halved):
        self.keep = keep
        self.near = exchange(send, "shard", 0)
        self.halved = halved
        self.stage = 0

    def cross(self, *done):
        self.near = after(self.near, *done)
        low = add_low(self.keep[1], self.near[1])
        self.got = exchange(low, "shard", 1)
        self.terms = [self.keep[0], self.near[0]]
        return low

    def next(self, *done):
        got = after(self.got, *done)
        count = bits_of("dp")
        rows = got.shape[0]

        def total(at):
            return sum(term[at].astype(WIDE) for term in (*self.terms, got)).astype(LOW)

        bit = self.stage
        if self.stage < count:
            if bit in self.halved:
                sent = total(slice(rows // 2, rows))
                self.terms = [total(slice(0, rows // 2))]
            else:
                sent = total(slice(0, rows))
                self.terms = [sent]
        else:
            bit = self.halved[count - 1 - self.stage]
            if self.stage == count:
                sent = total(slice(0, rows))
            else:
                sent = jnp.concatenate([self.held, got])
            self.held = sent
        self.stage += 1
        self.got = exchange(sent, "dp", bit)
        return sent

    def left(self):
        return bits_of("dp") + len(self.halved) - self.stage

    def result(self):
        return self.held, self.got


class Passing:
    def __init__(self, local, reverse):
        self.local = local
        steps = [[(0, 1), (2, 3)], [(1, 2)], [(2, 3)]]
        if reverse:
            steps = [[(3 - a, 3 - b) for a, b in step] for step in steps]
        self.steps = steps
        self.got = [lax.ppermute(local, "shard", steps[0])]

    def turn(self, decay, length, *done):
        self.got[0] = after(self.got[0], *done)
        total = combine(decay, length, self.local, self.got[0])
        self.got.append(lax.ppermute(total, "shard", self.steps[1]))
        return total

    def finish(self, *done):
        self.got.append(lax.ppermute(after(self.got[1], *done), "shard", self.steps[2]))


def entering(decay, length, h, got):
    factor = jnp.exp(jnp.full((1, 1), decay[h] * length, WIDE))
    wide = [item[h].astype(WIDE) for item in got]
    return wide[0] + wide[1] + factor * wide[2]


def after(value, *others):
    return lax.optimization_barrier((value, *others))[0]


def combine_kernel(length, decay, local, got, out):
    h = pl.program_id(0) % H
    factor = jnp.exp(jnp.full((1, 1), decay[h] * length, WIDE))
    out[...] = (local[...].astype(WIDE) + factor * got[...].astype(WIDE)).astype(LOW)


def combine(decay, length, local, got):
    block = pl.BlockSpec((None, None, KD, VP), lambda i: (i // H, i % H, 0, 0))
    return pl.pallas_call(
        functools.partial(combine_kernel, length),
        grid=(local.shape[0] * H,),
        out_shape=shape(local.shape, LOW),
        in_specs=[smem(), block, block],
        out_specs=block,
        compiler_params=params(12),
        cost_estimate=cost(local.size, 6 * local.size),
    )(decay, local, got)


def assemble_kernel(plan, fills, sources_of, me_ref, side_ref, *refs):
    sources, outs = refs[: len(sources_of)], refs[len(sources_of) :]
    lanes = sources[0].shape[1]
    for index, row, size in fills:
        outs[index][row : row + size, :] = jnp.zeros((size, outs[index].shape[1]), LOW)

    def place(source, lane, low, high):
        for start, index, row, size in plan:
            begin, end = max(start, low), min(start + size, high)
            if begin < end:
                to = row + begin - start
                outs[index][to : to + end - begin, pl.ds(lane, lanes)] = source[
                    begin - low : end - low, :
                ]

    for (mask, half), source in zip(sources_of, sources):
        lane = pl.multiple_of(jnp.bitwise_xor(me_ref[0], mask) * lanes, lanes)
        rows = source.shape[0]
        if half is None:
            place(source, lane, 0, rows)
            continue
        for side in range(2):

            @pl.when(side_ref[0] == side)
            def _():
                low = (side ^ half) * rows
                place(source, lane, low, low + rows)


def assemble(held, plan, fills, heights, width, me, side):
    sources_of = [(mask, half) for mask, half, part in held]
    parts = [part for mask, half, part in held]
    return pl.pallas_call(
        functools.partial(assemble_kernel, plan, fills, sources_of),
        out_shape=[shape((rows, width), LOW) for rows in heights],
        in_specs=[smem()] * 2 + [pl.BlockSpec(memory_space=VMEM)] * len(parts),
        out_specs=[pl.BlockSpec(memory_space=VMEM)] * len(heights),
        compiler_params=params(20),
        cost_estimate=cost(0, 4 * sum(heights) * width),
    )(me, side, *parts)


def rotated(flat, cosine, sine):
    half = KD // 2
    parts = []
    for h in range(H):
        u = flat[:, h * KD : h * KD + half]
        w = flat[:, h * KD + half : (h + 1) * KD]
        parts += [u * cosine - w * sine, w * cosine + u * sine]
    return jnp.concatenate(parts, axis=1)


def column(size):
    return lax.broadcasted_iota(jnp.int32, (size, 1), 0).astype(WIDE)


def front_kernel(count, decay, seg_s, tok, w, gains, cos, sin, seg, *rest):
    hid, k, v, kv, out_state, state = rest
    seq = pl.program_id(0) // count
    c = pl.program_id(0) % count
    x = tok[...].astype(WIDE)
    r = lax.rsqrt(jnp.mean(x * x, axis=1, keepdims=True) + EPS)
    h1 = (x * r * gains[0:1, :].astype(WIDE)).astype(LOW)
    hid[...] = h1
    kd = H * KD
    key = rotated(dot_nt(h1, w[:kd, :]), cos[...], sin[...]).astype(LOW)
    k[...] = key
    val = dot_nt(h1, w[kd : kd + H * VP, :]).astype(LOW)
    v[...] = val
    first = seg_s[seq, c * BLOCK]
    last = seg_s[seq, c * BLOCK + BLOCK - 1]
    before = seg_s[seq, jnp.maximum(c * BLOCK - 1, 0)]
    here = (seg[...] == last).astype(WIDE)
    joined = jnp.logical_and(jnp.logical_and(first == last, first == before), c > 0)
    for h in range(H):
        a = decay[h]
        kw = jnp.exp(a * (BLOCK - 1.0 - column(BLOCK))) * here
        kk = (key[:, h * KD : (h + 1) * KD].astype(WIDE) * kw).astype(LOW)
        add = dot_tn(kk, val[:, h * VP : (h + 1) * VP])
        kv[h] = add
        factor = jnp.exp(jnp.full((1, 1), a * BLOCK, WIDE))
        total = jnp.where(joined, factor * state[h], 0.0) + add
        state[h] = total
        out_state[h] = total.astype(LOW)


def row_block(width):
    return pl.BlockSpec((BLOCK, width), lambda t: (t, 0))


def state_block(count, at=lambda c: c):
    return pl.BlockSpec(
        (None, None, H, KD, VP), lambda t: (t // count, at(t % count), 0, 0, 0)
    )


def seq_block(count):
    return pl.BlockSpec((None, H, KD, VP), lambda t: (t // count, 0, 0, 0))


def front(seqs, length, tokens, seg_col, segments, decay, w, gains, cos, sin):
    count = length // BLOCK
    rows, width = tokens.shape
    outs = [width, H * KD, H * VP]
    table = pl.BlockSpec((BLOCK, KD // 2), lambda t: (t % count, 0))
    return pl.pallas_call(
        functools.partial(front_kernel, count),
        grid=(seqs * count,),
        out_shape=[shape((rows, n), LOW) for n in outs]
        + [shape((seqs, count, H, KD, VP), WIDE), shape((seqs, H, KD, VP), LOW)],
        in_specs=[smem(), smem(), row_block(width), whole(w.shape), whole(gains.shape)]
        + [table, table, row_block(1)],
        out_specs=[row_block(n) for n in outs]
        + [state_block(count), seq_block(count)],
        scratch_shapes=[VMEM((H, KD, VP), WIDE)],
        compiler_params=params(28),
        cost_estimate=cost(2 * rows * width * w.shape[0], 12 * rows * width),
    )(decay, segments, tokens, w, gains, cos, sin, seg_col)


def decay_row(a):
    return jnp.exp(-a * lax.broadcasted_iota(jnp.int32, (1, BLOCK), 1).astype(WIDE))


def mixing(a, top, size, seg, seg_row):
    reach = top + size
    rows = jnp.exp(a * (column(size) + float(top)))
    same = seg[top:reach, :] == seg_row[:, :reach]
    n = lax.broadcasted_iota(jnp.int32, (size, reach), 0) + top
    m = lax.broadcasted_iota(jnp.int32, (size, reach), 1)
    return jnp.where(jnp.logical_and(same, n >= m), rows * decay_row(a)[:, :reach], 0.0)


TILE = 256


def inner_kernel(decay, k, v, hid, w, cos, sin, seg, seg_row, q, intra, gate):
    kd = H * KD
    query = rotated(dot_nt(hid[...], w[:kd, :]), cos[...], sin[...]).astype(LOW)
    q[...] = query
    gate[...] = dot_nt(hid[...], w[kd:, :]).astype(LOW)
    for i in range(BLOCK // TILE):
        top, reach = i * TILE, (i + 1) * TILE
        for h in range(H):
            s = dot_nt(query[top:reach, h * KD : (h + 1) * KD], k[:reach, h * KD : (h + 1) * KD])
            weights = (s * mixing(decay[h], top, TILE, seg, seg_row)).astype(LOW)
            intra[top:reach, h * VP : (h + 1) * VP] = dot(
                weights, v[:reach, h * VP : (h + 1) * VP]
            ).astype(LOW)


def inner(k, v, hid, w, cos, sin, seg_col, seg_row, decay, length):
    rows, width = hid.shape
    count = length // BLOCK
    block = lambda n: pl.BlockSpec((BLOCK, n), lambda t: (t, 0))
    table = pl.BlockSpec((BLOCK, KD // 2), lambda t: (t % count, 0))
    return pl.pallas_call(
        inner_kernel,
        grid=(rows // BLOCK,),
        out_shape=[shape((rows, n), LOW) for n in (H * KD, H * VP, H * VP)],
        in_specs=[
            smem(),
            block(H * KD),
            block(H * VP),
            block(width),
            whole(w.shape),
            table,
            table,
            block(1),
            pl.BlockSpec((None, 1, BLOCK), lambda t: (t, 0, 0)),
        ],
        out_specs=[block(n) for n in (H * KD, H * VP, H * VP)],
        compiler_params=params(36),
        cost_estimate=cost(rows * (2 * width * 1536 + 2 * BLOCK * H * VP), 8 * rows * H * VP),
    )(decay, k, v, hid, w, cos, sin, seg_col, seg_row)


CHUNK = 16


def interleaved(first, second):
    steps = [((i + 0.5) / len(first), 0, step) for i, step in enumerate(first)]
    steps += [((i + 0.5) / len(second), 1, step) for i, step in enumerate(second)]
    for place, which, step in sorted(steps, key=lambda item: item[:2]):
        step()


def pieces(width, size=256):
    return [(start, min(start + size, width)) for start in range(0, width, size)]


def across(narrow, width):
    return jnp.concatenate([narrow] * (width // 128), axis=1)


def middle_kernel(count, ff, decay, seg_s, in_last, *refs):
    (intra, gate, q, tok, cot, seg, w, gains, *got, kv) = refs[:12]
    outs, scratch = refs[12:24], refs[24:]
    (tok_out, hid2, prod, dgate, dup, mixed, glow, ggate, gret, st_out, dst, leave) = outs
    (state, now, queries, factors, ret_s, norm_s, silu_s, slope_s, inv_s, res_s, ff_s, low_s, sums) = scratch
    seq = pl.program_id(0) // count
    c = pl.program_id(0) % count
    start = c * BLOCK
    vp = H * VP
    width = tok.shape[1]
    before = jnp.where(c > 0, seg_s[seq, jnp.maximum(start - 1, 0)], in_last[seq])

    @pl.when(c == 0)
    def _():
        for h in range(H):
            total = entering(decay, count * BLOCK, h, got)
            state[h] = total
            now[h] = total.astype(LOW)

    for b in range(1, count):

        @pl.when(c == b)
        def _():
            prev = seg_s[seq, (b - 1) * BLOCK - 1] if b > 1 else in_last[seq]
            joined = jnp.logical_and(
                seg_s[seq, (b - 1) * BLOCK] == seg_s[seq, b * BLOCK - 1],
                seg_s[seq, (b - 1) * BLOCK] == prev,
            )
            for h in range(H):
                factor = jnp.exp(jnp.full((1, 1), decay[h] * BLOCK, WIDE))
                total = jnp.where(joined, factor * state[h], 0.0) + kv[h]
                state[h] = total
                now[h] = total.astype(LOW)

    st_out[...] = now[...]
    here = (seg[...] == before).astype(WIDE)
    for h in range(H):
        qw = jnp.exp(decay[h] * (column(BLOCK) + 1.0)) * here
        factors[h] = jnp.broadcast_to(qw, (BLOCK, 128))

    w_out = (0, vp)
    w_gate = (vp, vp + ff)
    w_up = (vp + ff, vp + 2 * ff)
    w_down = (vp + 2 * ff, vp + 3 * ff)
    gain = gains[1:2, :].astype(WIDE)

    def phases(top):
        rs = pl.ds(top, TILE)
        lists = []

        def add(steps):
            lists.append(steps)

        def chunks():
            return [pl.ds(row, CHUNK) for row in range(top, top + TILE, CHUNK)]

        def cross(h, lo, hi):
            ret_s[rs, h * VP + lo : h * VP + hi] = dot(
                q[rs, h * KD : (h + 1) * KD], now[h, :, lo:hi]
            )

        add([functools.partial(cross, h, *piece) for h in range(H) for piece in pieces(VP)])

        def gated(h, r):
            hv = slice(h * VP, (h + 1) * VP)
            hk = slice(h * KD, (h + 1) * KD)
            qw = factors[h, r, :]
            queries[r, hk] = (q[r, hk].astype(WIDE) * across(qw, KD)).astype(LOW)
            ret = intra[r, hv].astype(WIDE) + across(qw, VP) * ret_s[r, hv]
            mean = jnp.sum(ret, axis=1, keepdims=True) * (1.0 / VD)
            centered = ret - mean
            square = jnp.sum(centered * centered, axis=1, keepdims=True)
            var = (square - (VP - VD) * (mean * mean)) * (1.0 / VD)
            inv = lax.rsqrt(var + 1.0 * KD)
            nh = centered * inv
            g = gate[r, hv].astype(WIDE)
            sg = 0.5 * jnp.tanh(0.5 * g) + 0.5
            sl = g * sg
            mixed[r, hv] = (nh * sl).astype(LOW)
            norm_s[r, hv] = nh
            silu_s[r, hv] = sl
            slope_s[r, hv] = nh * (sg + sl * (1.0 - sg))
            inv_s[h, r, :] = jnp.broadcast_to(inv, (CHUNK, 128))

        add([functools.partial(gated, h, r) for r in chunks() for h in range(H)])

        def project(lo, hi):
            res_s[rs, lo:hi] = dot(mixed[rs, :], w[w_out[0] : w_out[1], lo:hi])

        add([functools.partial(project, *piece) for piece in pieces(width)])

        def norm(r):
            resid = tok[r, :].astype(WIDE) + res_s[r, :]
            r2 = lax.rsqrt(jnp.mean(resid * resid, axis=1, keepdims=True) + EPS)
            res_s[r, :] = resid
            hid2[r, :] = (resid * r2 * gain).astype(LOW)
            inv_s[H, r, :] = jnp.broadcast_to(r2, (CHUNK, 128))

        add([functools.partial(norm, r) for r in chunks()])

        def forward(place, source, at, lo, hi):
            ff_s[place, rs, lo:hi] = dot_nt(source[rs, :], w[at[0] + lo : at[0] + hi, :])

        add(
            [
                functools.partial(forward, place, source, at, *piece)
                for piece in pieces(ff)
                for place, source, at in ((0, hid2, w_gate), (1, hid2, w_up), (2, cot, w_down))
            ]
        )

        def gelu(r, lo, hi):
            gf, uf, gp = ff_s[0, r, lo:hi], ff_s[1, r, lo:hi], ff_s[2, r, lo:hi]
            e = jnp.exp(-0.5 * (gf * gf))
            d = 1.0 / (1.0 + (0.3275911 * math.sqrt(0.5)) * jnp.abs(gf))
            poly = d * (
                0.5 * 0.254829592
                + d
                * (
                    0.5 * -0.284496736
                    + d * (0.5 * 1.421413741 + d * (0.5 * -1.453152027 + d * (0.5 * 1.061405429)))
                )
            )
            tail = poly * e
            cdf = jnp.where(gf >= 0.0, 1.0 - tail, tail)
            ge = gf * cdf
            dge = cdf + gf * (e * (1.0 / math.sqrt(2.0 * math.pi)))
            prod[r, lo:hi] = (ge * uf).astype(LOW)
            dgate[r, lo:hi] = (gp * uf * dge).astype(LOW)
            dup[r, lo:hi] = (gp * ge).astype(LOW)

        add([functools.partial(gelu, r, *piece) for r in chunks() for piece in pieces(ff, 512)])

        def down(lo, hi):
            low_s[0, rs, lo:hi] = dot(prod[rs, :], w[w_down[0] : w_down[1], lo:hi])

        def hidden(lo, hi):
            low_s[1, rs, lo:hi] = dot(dgate[rs, :], w[w_gate[0] : w_gate[1], lo:hi]) + dot(
                dup[rs, :], w[w_up[0] : w_up[1], lo:hi]
            )

        add([functools.partial(step, *piece) for piece in pieces(width) for step in (down, hidden)])

        def residual(r):
            resid = res_s[r, :]
            r2 = across(inv_s[H, r, :], width)
            tok_out[r, :] = (resid + low_s[0, r, :]).astype(LOW)
            gh = low_s[1, r, :] * gain
            xhat = resid * r2
            inner_product = jnp.mean(gh * xhat, axis=1, keepdims=True)
            glow[r, :] = (cot[r, :].astype(WIDE) + r2 * (gh - xhat * inner_product)).astype(LOW)

        add([functools.partial(residual, r) for r in chunks()])

        def mix_back(lo, hi):
            ret_s[rs, lo:hi] = dot_nt(glow[rs, :], w[w_out[0] + lo : w_out[0] + hi, :])

        add([functools.partial(mix_back, *piece) for piece in pieces(vp)])

        def gated_back(h, r):
            hv = slice(h * VP, (h + 1) * VP)
            gm = ret_s[r, hv]
            nh = norm_s[r, hv]
            ggate[r, hv] = (gm * slope_s[r, hv]).astype(LOW)
            gn = gm * silu_s[r, hv]
            one = jnp.sum(gn, axis=1, keepdims=True) * (1.0 / VD)
            two = jnp.sum(gn * nh, axis=1, keepdims=True) * (1.0 / VD)
            gret[r, hv] = (across(inv_s[h, r, :], VP) * (gn - one - nh * two)).astype(LOW)

        add([functools.partial(gated_back, h, r) for r in chunks() for h in range(H)])
        return lists

    first, second = phases(0), phases(TILE)
    for k in range(len(first) + 1):
        interleaved(first[k] if k < len(first) else [], second[k - 1] if k else [])
    for h in range(H):
        add = dot_tn(queries[:, h * KD : (h + 1) * KD], gret[:, h * VP : (h + 1) * VP])
        dst[h] = add
        sums[c, h] = add

    @pl.when(c == count - 1)
    def _():
        for h in range(H):
            total = sums[count - 1, h]
            for b in reversed(range(count - 1)):
                prev = seg_s[seq, b * BLOCK - 1] if b > 0 else in_last[seq]
                joined = jnp.logical_and(
                    seg_s[seq, b * BLOCK] == seg_s[seq, (b + 1) * BLOCK - 1],
                    seg_s[seq, b * BLOCK] == prev,
                )
                factor = jnp.exp(jnp.full((1, 1), decay[h] * BLOCK, WIDE))
                total = jnp.where(joined, factor * total, 0.0) + sums[b, h]
            leave[h] = total.astype(LOW)


def middle(seqs, length, ff, data, seg_col, segments, in_last, decay, w, gains, got, kv):
    intra, gate, q, tokens, cotangent = data
    rows, width = tokens.shape
    count = length // BLOCK
    vp = H * VP
    outs = [width, width, ff, ff, ff, vp, width, vp, vp]
    inputs = [decay, segments, in_last, intra, gate, q, tokens, cotangent, seg_col, w, gains, *got, kv]
    specs = [smem()] * 3 + [row_block(n) for n in (vp, vp, H * KD, width, width, 1)]
    specs += [whole(w.shape), whole(gains.shape), *[seq_block(count)] * 3]
    specs += [state_block(count, lambda c: jnp.maximum(c - 1, 0))]
    one = (H, KD, VP)
    states = (seqs, count, *one)
    return pl.pallas_call(
        functools.partial(middle_kernel, count, ff),
        grid=(seqs * count,),
        out_shape=[shape((rows, n), LOW) for n in outs]
        + [shape(states, LOW), shape(states, WIDE), shape((seqs, *one), LOW)],
        in_specs=specs,
        out_specs=[row_block(n) for n in outs]
        + [state_block(count)] * 2
        + [seq_block(count)],
        scratch_shapes=[
            VMEM(one, WIDE),
            VMEM(one, LOW),
            VMEM((BLOCK, H * KD), LOW),
            VMEM((H, BLOCK, 128), WIDE),
            VMEM((BLOCK, vp), WIDE),
            VMEM((BLOCK, vp), WIDE),
            VMEM((BLOCK, vp), WIDE),
            VMEM((BLOCK, vp), WIDE),
            VMEM((H + 1, BLOCK, 128), WIDE),
            VMEM((BLOCK, width), WIDE),
            VMEM((3, BLOCK, ff), WIDE),
            VMEM((2, BLOCK, width), WIDE),
            VMEM(states[1:], WIDE),
        ],
        compiler_params=params(60),
        cost_estimate=cost(2 * rows * width * (2 * vp + 6 * ff), 30 * rows * width),
    )(*inputs)


def weight_kernel(plan, count, layout, me_ref, *refs):
    ins, ready, outs, total = refs[:count], refs[count:-3], refs[-3:-1], refs[-1]
    if layout is None:
        outs = refs[-2:-1]
    t = pl.program_id(0)
    last = pl.num_programs(0) - 1
    for left, right, cuts in plan:
        a, b = ins[left], ins[right]
        for source, row, size in cuts:
            add = dot_tn(a[:, source : source + size], b[...])

            @pl.when(t == 0)
            def _():
                total[row : row + size, :] = add

            @pl.when(t > 0)
            def _():
                total[row : row + size, :] += add

    @pl.when(t == last)
    def _():
        used = max(row + size for left, right, cuts in plan for source, row, size in cuts)
        if layout is None:
            outs[0][...] = total[...].astype(LOW)
            return
        for item in ready:
            total[used : used + item.shape[0], :] = item[...].astype(WIDE)
            used += item.shape[0]
        if used < total.shape[0]:
            total[used:, :] = jnp.zeros((total.shape[0] - used, total.shape[1]), WIDE)
        lanes = outs[0].shape[2]
        which, pieces = layout
        rows = outs[0].shape[1] // pieces
        for part in range(2 * outs[0].shape[0]):
            target = outs[part & 1]
            lane = pl.multiple_of(jnp.bitwise_xor(me_ref[0], part) * lanes, lanes)
            for q in range(pieces):
                row = pl.multiple_of(jnp.bitwise_xor(me_ref[which], q) * rows, 16)
                target[part >> 1, q * rows : (q + 1) * rows, :] = total[
                    pl.ds(row, rows), pl.ds(lane, lanes)
                ].astype(LOW)


def weight_grads(arrays, plan, place, shards=2, height=0, layout=None, ready=()):
    rows = arrays[0].shape[0]
    used = max(row + size for left, right, cuts in plan for source, row, size in cuts)
    width = arrays[plan[0][1]].shape[1]
    tile = 2 * BLOCK
    block = lambda n: pl.BlockSpec((tile, n), lambda t: (t, 0))
    dims = [(shards // 2, height, width // shards)] * 2
    if layout is None:
        height, dims = used, [(used, width)]
    full = lambda item: pl.BlockSpec(item, lambda t: (0,) * len(item))
    return pl.pallas_call(
        functools.partial(weight_kernel, plan, len(arrays), layout),
        grid=(rows // tile,),
        out_shape=[shape(item, LOW) for item in dims],
        in_specs=[smem()] + [block(item.shape[1]) for item in arrays]
        + [full(item.shape) for item in ready],
        out_specs=[full(item) for item in dims],
        scratch_shapes=[VMEM((height, width), WIDE)],
        compiler_params=params(48),
        cost_estimate=cost(2 * rows * used * width, 2 * rows * sum(i.shape[1] for i in arrays)),
    )(place, *arrays, *ready)


def back_kernel(count, decay, seg_s, in_last, *refs):
    (q, k, v, gret, cos, sin, seg, seg_row, st, dst, *got) = refs[:13]
    (dq, dk, dv, state, weights, grads) = refs[13:]
    seq = pl.program_id(0) // count
    c = count - 1 - pl.program_id(0) % count

    @pl.when(c == count - 1)
    def _():
        for h in range(H):
            state[h] = entering(decay, count * BLOCK, h, got)

    for b in range(1, count):

        @pl.when(c == b - 1)
        def _():
            prev = seg_s[seq, b * BLOCK - 1]
            first = seg_s[seq, b * BLOCK]
            last = seg_s[seq, (b + 1) * BLOCK - 1]
            joined = jnp.logical_and(first == last, first == prev)
            for h in range(H):
                factor = jnp.exp(jnp.full((1, 1), decay[h] * BLOCK, WIDE))
                state[h] = jnp.where(joined, factor * state[h], 0.0) + dst[h]

    start = c * BLOCK
    before = jnp.where(c > 0, seg_s[seq, jnp.maximum(start - 1, 0)], in_last[seq])
    final = seg_s[seq, start + BLOCK - 1]
    here = (seg[...] == before).astype(WIDE)
    ends = (seg[...] == final).astype(WIDE)
    place = column(BLOCK)
    dqs, dks = [], []
    for h in range(H):
        a = decay[h]
        qh = q[:, h * KD : (h + 1) * KD]
        kh = k[:, h * KD : (h + 1) * KD]
        vh = v[:, h * VP : (h + 1) * VP]
        gh = gret[:, h * VP : (h + 1) * VP]
        qw = jnp.exp(a * (place + 1.0)) * here
        kw = jnp.exp(a * (BLOCK - 1.0 - place)) * ends
        parts = []
        for i in range(BLOCK // TILE):
            top, reach = i * TILE, (i + 1) * TILE
            mix = mixing(a, top, TILE, seg, seg_row)
            s = dot_nt(qh[top:reach, :], kh[:reach, :])
            weights[top:reach, :reach] = (s * mix).astype(LOW)
            gs = (dot_nt(gh[top:reach, :], vh[:reach, :]) * mix).astype(LOW)
            grads[top:reach, :reach] = gs
            parts.append(dot(gs, kh[:reach, :]))
        late = state[h].astype(LOW)
        dqs.append(jnp.concatenate(parts) + qw * dot_nt(gh, st[h]))
        parts, values = [], []
        for i in range(BLOCK // TILE):
            top, reach = i * TILE, (i + 1) * TILE
            parts.append(dot_tn(grads[top:, top:reach], qh[top:, :]))
            values.append(dot_tn(weights[top:, top:reach], gh[top:, :]))
        dks.append(jnp.concatenate(parts) + kw * dot_nt(vh, late))
        dv[:, h * VP : (h + 1) * VP] = (jnp.concatenate(values) + kw * dot(kh, late)).astype(LOW)
    dq[...] = rotated(jnp.concatenate(dqs, axis=1), cos[...], -sin[...]).astype(LOW)
    dk[...] = rotated(jnp.concatenate(dks, axis=1), cos[...], -sin[...]).astype(LOW)


def back(seqs, length, data, cos, sin, seg_col, seg_row, segments, in_last, decay, st, dst, got):
    rows = data[0].shape[0]
    count = length // BLOCK
    turn = lambda t: (t // count) * count + count - 1 - t % count
    block = lambda n: pl.BlockSpec((BLOCK, n), lambda t: (turn(t), 0))
    table = pl.BlockSpec((BLOCK, KD // 2), lambda t: (count - 1 - t % count, 0))
    outs = [H * KD, H * KD, H * VP]
    inputs = [decay, segments, in_last, *data, cos, sin, seg_col, seg_row, st, dst, *got]
    specs = [smem()] * 3 + [block(item.shape[1]) for item in data] + [table, table, block(1)]
    specs += [pl.BlockSpec((None, 1, BLOCK), lambda t: (turn(t), 0, 0))]
    specs += [state_block(count, lambda c: count - 1 - c)]
    specs += [state_block(count, lambda c: jnp.minimum(count - c, count - 1))]
    specs += [seq_block(count)] * 3
    return pl.pallas_call(
        functools.partial(back_kernel, count),
        grid=(seqs * count,),
        out_shape=[shape((rows, n), LOW) for n in outs],
        in_specs=specs,
        out_specs=[block(n) for n in outs],
        scratch_shapes=[
            VMEM((H, KD, VP), WIDE),
            VMEM((BLOCK, BLOCK), LOW),
            VMEM((BLOCK, BLOCK), LOW),
        ],
        compiler_params=params(40),
        cost_estimate=cost(rows * H * 2 * BLOCK * 3 * (KD + VP), 16 * rows * H * VP),
    )(*inputs)


def input_kernel(dq, dk, dv, ggate, tok, glow, w_kv, w_qg, gains, *rest):
    out = rest[-1]
    kd = H * KD
    gh = dot(dq[...], w_qg[:kd, :]) + dot(dk[...], w_kv[:kd, :])
    gh += dot(dv[...], w_kv[kd:, :]) + dot(ggate[...], w_qg[kd:, :])
    x = tok[...].astype(WIDE)
    r = lax.rsqrt(jnp.mean(x * x, axis=1, keepdims=True) + EPS)
    xhat = x * r
    gh = gh * gains[0:1, :].astype(WIDE)
    inner_product = jnp.mean(gh * xhat, axis=1, keepdims=True)
    out[...] = (glow[...].astype(WIDE) + r * (gh - xhat * inner_product)).astype(LOW)


def input_grad(first, steps, dq, dk, dv, ggate, tokens, glow, w_kv, w_qg, gains, earlier):
    rows, width = tokens.shape
    parts = rows // BLOCK // steps
    arrays = [dq, dk, dv, ggate, tokens, glow]
    block = lambda item: pl.BlockSpec((BLOCK, item.shape[1]), lambda t: (first + t, 0))
    inputs = [*arrays, w_kv, w_qg, gains]
    specs = [block(item) for item in arrays] + [whole(item.shape) for item in (w_kv, w_qg, gains)]
    aliases = {}
    if earlier is not None:
        aliases = {len(inputs): 0}
        inputs.append(earlier)
        specs.append(pl.BlockSpec(memory_space=pl.ANY))
    return pl.pallas_call(
        input_kernel,
        grid=(steps,),
        out_shape=shape((rows, width), LOW),
        in_specs=specs,
        out_specs=block(tokens),
        input_output_aliases=aliases,
        compiler_params=params(32),
        cost_estimate=cost(2 * rows * width * 2 * w_kv.shape[0] // parts, 20 * rows * width // parts),
    )(*inputs)


def adam_step(master, moment, second, grad, scale, rate, decay_weight):
    clipped = grad * scale
    moment_new = BETA_ONE * moment + (1.0 - BETA_ONE) * clipped
    second_new = BETA_TWO * second + (1.0 - BETA_TWO) * clipped * clipped
    corrected = (
        moment_new
        * (1.0 / (1.0 - BETA_ONE**STEP))
        / (jnp.sqrt(second_new * (1.0 / (1.0 - BETA_TWO**STEP))) + ADAM_EPS)
    )
    return (master - rate * (corrected + decay_weight * master), moment_new, second_new)


def squares_kernel(vd, ff, layouts, place, *refs):
    halves, (w_qk, w_vg, w_gu, low_gains) = refs[:4], refs[4:8]
    grad_gains, total, early, late = refs[8:]
    kd = H * KD
    for index, target in enumerate((early, late)):
        which, pieces = layouts[index]
        rows = target.shape[0] // pieces
        for q in range(pieces):
            row = pl.multiple_of(jnp.bitwise_xor(place[which], q) * rows, 16)
            source = halves[2 * index + q // (pieces // 2)]
            start = q % (pieces // 2) * rows
            target[pl.ds(row, rows), :] = source[start : start + rows, :]

    def rows(source, start, size):
        return source[start : start + size, :].astype(WIDE)

    def product(weight, grad):
        return jnp.sum(weight.astype(LOW).astype(WIDE) * grad, axis=0, keepdims=True)

    sums = []

    def square(item):
        sums.append(jnp.sum(item * item, axis=0, keepdims=True))
        return item

    first = jnp.zeros((1, low_gains.shape[1]), WIDE)
    for i in range(2):
        grad = square(rows(late, i * kd, kd))
        first += jnp.sum(w_qk[i].astype(LOW).astype(WIDE).T * grad, axis=0, keepdims=True)
    first += product(w_vg[0], square(rows(late, 2 * kd, vd)))
    first += product(w_vg[1], square(rows(early, vd, vd)))
    square(rows(early, 0, vd))
    square(rows(early, 2 * vd, ff))
    second = product(w_gu[0], square(rows(early, 2 * vd + ff, ff)))
    second += product(w_gu[1], square(rows(early, 2 * vd + 2 * ff, ff)))
    gains = jnp.concatenate([first, second]) / low_gains[...].astype(LOW).astype(WIDE)
    grad_gains[...] = gains
    sums.append(jnp.sum(gains * gains, axis=0, keepdims=True))
    total[...] = jnp.broadcast_to(jnp.sum(sum(sums), axis=1, keepdims=True), total.shape)


def squares(vd, ff, layouts, place, grads, w_qk, w_vg, w_gu, gains):
    halves = [half for pair in grads for half in pair]
    vmem = pl.BlockSpec(memory_space=VMEM)
    return pl.pallas_call(
        functools.partial(squares_kernel, vd, ff, layouts),
        out_shape=[shape(gains.shape, WIDE), shape((8, 128), WIDE)]
        + [shape((2 * pair[0].shape[0], pair[0].shape[1]), LOW) for pair in grads],
        in_specs=[smem()] + [vmem] * 8,
        out_specs=[vmem] * 4,
        compiler_params=params(20),
    )(place, *halves, w_qk, w_vg, w_gu, gains)


def update_kernel(vd, ff, *refs):
    totals, (early, late, gain_grads) = refs[:4], refs[4:7]
    sources, targets, norm_out = refs[7:25], refs[25:43], refs[43]
    ins, outs = refs[44:62], refs[62:80]
    arrived, sent = refs[80:]
    kd = H * KD
    order = [4, 3, 2, 1, 0, 5]
    places = [6 * group + place for place in order for group in range(3)]
    fetch = {i: pltpu.make_async_copy(sources[i], ins[i], arrived.at[i]) for i in places}
    send = {i: pltpu.make_async_copy(outs[i], targets[i], sent.at[i]) for i in places}
    for i in places:
        fetch[i].start()
    norm = jnp.sqrt((totals[0][...] + totals[1][...]) + (totals[2][...] + totals[3][...]))
    norm_out[0, 0] = jnp.max(norm)
    scale = jnp.minimum(1.0, CLIP / (norm + 1e-06))[0:1, 0:1]

    def step(place, at, grad, rate, decay_weight):
        results = adam_step(
            ins[place][at], ins[6 + place][at], ins[12 + place][at], grad, scale, rate, decay_weight
        )
        for group, result in enumerate(results):
            outs[6 * group + place][at] = result

    def rows(source, start, size):
        return source[start : start + size, :].astype(WIDE)

    grads = {
        4: [(..., lambda: rows(early, 2 * vd, ff))],
        3: [(i, lambda i=i: rows(early, 2 * vd + (1 + i) * ff, ff)) for i in range(2)],
        2: [(..., lambda: rows(early, 0, vd))],
        1: [(0, lambda: rows(late, 2 * kd, vd)), (1, lambda: rows(early, vd, vd))],
        0: [(i, lambda i=i: rows(late, i * kd, kd).T) for i in range(2)],
        5: [(..., lambda: gain_grads[...])],
    }
    for place in order:
        for group in range(3):
            fetch[6 * group + place].wait()
        rate, decay_weight = (GAIN_RATE, 0.0) if place == 5 else (MATRIX_RATE, DECAY_WEIGHT)
        for at, grad in grads[place]:
            step(place, at, grad(), rate, decay_weight)
        for group in range(3):
            send[6 * group + place].start()
    for i in places:
        send[i].wait()


def update(vd, ff, totals, grads, gain_grads, arrays):
    anywhere = pl.BlockSpec(memory_space=pl.ANY)
    return pl.pallas_call(
        functools.partial(update_kernel, vd, ff),
        out_shape=[shape(item.shape, WIDE) for item in arrays] + [shape((1, 1), WIDE)],
        in_specs=[pl.BlockSpec(memory_space=VMEM)] * 7 + [anywhere] * 18,
        out_specs=[anywhere] * 18 + [smem()],
        scratch_shapes=[VMEM(item.shape, WIDE) for item in arrays] * 2
        + [pltpu.SemaphoreType.DMA((18,))] * 2,
        compiler_params=params(40),
    )(*totals, *grads, gain_grads, *arrays)


def on_device(
    tokens,
    cotangent,
    segments,
    log_decay,
    w_qk,
    w_vg,
    w_out,
    w_gu,
    w_down,
    norm_gains,
    *states,
):
    turned = lambda item: jnp.swapaxes(item, 1, 2)
    shards = lax.axis_size("shard")
    me = lax.axis_index("shard").reshape(1)
    replica = lax.axis_index("dp")
    count = bits_of("dp")
    halved = (tuple(range(count)), (1,))
    numbers = [
        sum(((replica >> bit) & 1) << (len(bits) - 1 - i) for i, bit in enumerate(bits))
        for bits in halved
    ]
    layouts = [(1 + i, 2 ** len(bits)) for i, bits in enumerate(halved)]
    place = jnp.concatenate([me, jnp.stack(numbers)])
    seqs, length, width = tokens.shape
    rows = seqs * length
    kd, vd, ff = H * KD, H * VD, w_down.shape[0]
    vp = H * VP
    vg_t, gu_t = turned(w_vg), turned(w_gu)

    low = lambda item: item.astype(LOW)
    def heads(item):
        return [
            jnp.pad(item[h * VD : (h + 1) * VD], ((0, VP - VD), (0, 0))) for h in range(H)
        ]

    first = jnp.concatenate(
        [low(w_qk[1]).T, low(vg_t[0]), jnp.pad(low(norm_gains), ((0, 14), (0, 0)))]
    )
    second = jnp.concatenate([low(w_qk[0]).T, low(vg_t[1])])
    third = jnp.concatenate([*heads(low(w_out)), low(gu_t[0]), low(gu_t[1]), low(w_down)])
    first_held = gather_shards(first)
    second_held = gather_shards(after(second, first_held[1][2]))
    side = (lax.axis_index("dp") & 1).reshape(1)

    half_width = KD // 2
    freq_rates = jnp.exp(-math.log(10000.0) * jnp.arange(half_width).astype(WIDE) / half_width)
    positions = (lax.axis_index("shard") * length + jnp.arange(length)).astype(WIDE)
    angles = positions[:, None] * freq_rates[None, :]
    cos, sin = jnp.cos(angles), jnp.sin(angles)

    tok = tokens.reshape(rows, width)
    cot = cotangent.reshape(rows, width)
    seg_col = segments.reshape(rows, 1)
    seg_row = segments.reshape(rows // BLOCK, 1, BLOCK)
    in_last = jnp.where(lax.axis_index("shard") > 0, segments[:, 0], -1)
    decay = log_decay

    def tick(*done):
        nonlocal decay, place, gains
        decay, place, gains = lax.optimization_barrier((decay, place, gains, *done))[:3]

    plan = [(0, 0, 0, kd)] + [(kd + h * VD, 0, kd + h * VP, VD) for h in range(H)]
    plan += [(kd + vd, 1, 0, 16)]
    fills = [(0, kd + h * VP + VD, VP - VD) for h in range(H)]
    w_kv, gains = assemble(first_held, plan, fills, [kd + vp, 16], width, me, side)
    third = after(third, w_kv)
    w_rest = lax.all_gather(third, "shard", axis=1, tiled=True)
    tick(third, second_held[1][2])
    hid, k, v, kv, leaving = front(
        seqs, length, tok, seg_col, segments, decay, w_kv, gains, cos, sin
    )
    passing = Passing(leaving, False)
    tick(leaving)
    plan = [(0, 0, 0, kd)] + [(kd + h * VD, 0, kd + h * VP, VD) for h in range(H)]
    (w_qg,) = assemble(second_held, plan, fills, [kd + vp], width, after(me, leaving), side)
    tick(w_qg)
    tick(passing.turn(decay, length, leaving))
    q, intra, gate = inner(k, v, hid, w_qg, cos, sin, seg_col, seg_row, decay, length)
    tick(q)
    passing.finish(q)
    tokens_out, hid2, prod, dgate, dup, mixed, glow, ggate, gret, st, dst, leaving = middle(
        seqs, length, ff, (intra, gate, q, tok, cot), seg_col, segments, in_last, decay,
        w_rest, gains, passing.got, kv,
    )
    returning = Passing(leaving, True)
    tick(leaving)

    def halves(row):
        return [(h * VP, row + h * VD, VD) for h in range(H)]

    fit = lambda used, layout: used + -used % (16 * layout[1])
    plan = [(0, 1, [(0, 0, ff)]), (2, 3, [(0, ff, ff)]), (4, 3, [(0, 2 * ff, ff)])]
    (made,) = weight_grads([prod, cot, dgate, hid2, dup], plan, place)
    tick(made)
    tick(returning.turn(decay, length, made))
    plan = [(0, 1, halves(0)), (2, 3, halves(vd))]
    made = weight_grads(
        [mixed, glow, ggate, hid], plan, place, shards,
        fit(2 * vd + 3 * ff, layouts[0]), layouts[0], (made,),
    )
    tick(made[0])
    returning.finish(made[0])
    early = Reduction(made[0], after(made[1], returning.got[1]), halved[0])
    tick(early.cross(made[0]))
    dq, dk, dv = back(
        seqs, length, (q, k, v, gret), cos, sin, seg_col, seg_row, segments, in_last, decay,
        st, dst, returning.got,
    )
    tick(dq)
    tick(early.next(dq))
    plan = [(0, 3, [(0, 0, kd)]), (1, 3, [(0, kd, kd)]), (2, 3, halves(2 * kd))]
    made = weight_grads(
        [dq, dk, dv, hid], plan, place, shards, fit(2 * kd + vd, layouts[1]), layouts[1]
    )
    late = Reduction(*made, halved[1])
    tick(made[0])
    tick(early.next(made[0]))
    tick(late.cross(made[0]))
    blocks = rows // BLOCK
    data = (dq, dk, dv, ggate, tok, glow, w_kv, w_qg)
    grad_input = None
    for part in range(2):
        grad_input = input_grad(part * blocks // 2, blocks // 2, *data, gains, grad_input)
        tick(grad_input)
        tick(late.next(grad_input), early.next(grad_input))
    while early.left() or late.left():
        for item in (early, late):
            if item.left():
                item.next()

    gain_grads, total, *grads = squares(
        vd, ff, layouts, place, [early.result(), late.result()], w_qk, vg_t, gu_t, norm_gains
    )
    others = [
        lax.ppermute(total, "shard", [(i, i ^ mask) for i in range(shards)]) for mask in (1, 2, 3)
    ]
    arrays = []
    for group in ((w_qk, w_vg, w_out, w_gu, w_down, norm_gains), states[:6], states[6:]):
        arrays += [turned(item) if i in (1, 3) else item for i, item in enumerate(group)]
    *results, norm = update(vd, ff, [total, *others], grads, gain_grads, arrays)
    results = [turned(item) if i % 6 in (1, 3) else item for i, item in enumerate(results)]
    return (
        tokens_out.reshape(tokens.shape),
        grad_input.reshape(tokens.shape),
        *results,
        norm.reshape(()),
    )


def solution(mesh):
    split = P("dp", "shard", None)
    rows, columns = P(None, "shard", None), P(None, "shard")
    group = (rows, rows, columns, rows, columns, columns)
    in_specs = (split, split, P("dp", "shard"), P()) + group * 3
    out_specs = (split, split) + group * 3 + (P(),)
    return jax.shard_map(
        on_device, mesh=mesh, in_specs=in_specs, out_specs=out_specs, check_vma=False
    )
```

```python
import functools
import math

import jax
import jax.numpy as jnp
from jax import lax
from jax.experimental import pallas as pl
from jax.experimental.pallas import tpu as pltpu
from jax.sharding import PartitionSpec as P

H = 2
KD = 256
VD = 432
VP = 512
BLOCK = 512
STEP = 10

EPS = 1e-05
ADAM_EPS = 1e-08
BETA_ONE = 0.9
BETA_TWO = 0.95
MATRIX_RATE = 0.15
GAIN_RATE = 1.0
DECAY_WEIGHT = 0.1
CLIP = 1.0

LOW = jnp.bfloat16
WIDE = jnp.float32
VMEM = pltpu.VMEM
SMEM = pltpu.SMEM
MIB = 1024 * 1024


def dot(a, b):
    return jnp.dot(a, b, preferred_element_type=WIDE)


def dot_nt(a, b):
    return lax.dot_general(a, b, (((1,), (1,)), ((), ())), preferred_element_type=WIDE)


def dot_tn(a, b):
    return lax.dot_general(a, b, (((0,), (0,)), ((), ())), preferred_element_type=WIDE)


def params(size):
    return pltpu.CompilerParams(vmem_limit_bytes=size * MIB)


def cost(flops, moved):
    return pl.CostEstimate(flops=int(flops), bytes_accessed=int(moved), transcendentals=0)


def smem():
    return pl.BlockSpec(memory_space=SMEM)


def whole(shape):
    return pl.BlockSpec(shape, lambda *at: (0,) * len(shape), pipeline_mode=pl.Buffered(1))


def shape(dims, kind):
    return jax.ShapeDtypeStruct(dims, kind)


def bits_of(axis):
    return (lax.axis_size(axis) - 1).bit_length()


def exchange(value, axis, bit):
    size = lax.axis_size(axis)
    return lax.ppermute(value, axis, [(i, i ^ (1 << bit)) for i in range(size)])


def gather_shards(own):
    held = [(0, own)]
    for bit in reversed(range(bits_of("shard"))):
        held += [(mask | (1 << bit), exchange(part, "shard", bit)) for mask, part in held]
    return [(mask, None, part) for mask, part in held]


def add_low(one, two):
    return (one.astype(WIDE) + two.astype(WIDE)).astype(LOW)


class Reduction:
    def __init__(self, keep, send, halved):
        self.keep = keep
        self.near = exchange(send, "shard", 0)
        self.halved = halved
        self.stage = 0

    def cross(self, *done):
        self.near = after(self.near, *done)
        low = add_low(self.keep[1], self.near[1])
        self.got = exchange(low, "shard", 1)
        self.terms = [self.keep[0], self.near[0]]
        return low

    def next(self, *done):
        got = after(self.got, *done)
        count = bits_of("dp")
        rows = got.shape[0]

        def total(at):
            return sum(term[at].astype(WIDE) for term in (*self.terms, got)).astype(LOW)

        bit = self.stage
        if self.stage < count:
            if bit in self.halved:
                sent = total(slice(rows // 2, rows))
                self.terms = [total(slice(0, rows // 2))]
            else:
                sent = total(slice(0, rows))
                self.terms = [sent]
        else:
            bit = self.halved[count - 1 - self.stage]
            if self.stage == count:
                sent = total(slice(0, rows))
            else:
                sent = jnp.concatenate([self.held, got])
            self.held = sent
        self.stage += 1
        self.got = exchange(sent, "dp", bit)
        return sent

    def left(self):
        return bits_of("dp") + len(self.halved) - self.stage

    def result(self):
        return self.held, self.got


class Passing:
    def __init__(self, local, reverse):
        self.local = local
        steps = [[(0, 1), (2, 3)], [(1, 2)], [(2, 3)]]
        if reverse:
            steps = [[(3 - a, 3 - b) for a, b in step] for step in steps]
        self.steps = steps
        self.got = [lax.ppermute(local, "shard", steps[0])]

    def turn(self, decay, length, *done):
        self.got[0] = after(self.got[0], *done)
        total = combine(decay, length, self.local, self.got[0])
        self.got.append(lax.ppermute(total, "shard", self.steps[1]))
        return total

    def finish(self, *done):
        self.got.append(lax.ppermute(after(self.got[1], *done), "shard", self.steps[2]))


def entering(decay, length, h, got):
    factor = jnp.exp(jnp.full((1, 1), decay[h] * length, WIDE))
    wide = [item[h].astype(WIDE) for item in got]
    return wide[0] + wide[1] + factor * wide[2]


def after(value, *others):
    return lax.optimization_barrier((value, *others))[0]


def combine_kernel(length, decay, local, got, out):
    h = pl.program_id(0) % H
    factor = jnp.exp(jnp.full((1, 1), decay[h] * length, WIDE))
    out[...] = (local[...].astype(WIDE) + factor * got[...].astype(WIDE)).astype(LOW)


def combine(decay, length, local, got):
    block = pl.BlockSpec((None, None, KD, VP), lambda i: (i // H, i % H, 0, 0))
    return pl.pallas_call(
        functools.partial(combine_kernel, length),
        grid=(local.shape[0] * H,),
        out_shape=shape(local.shape, LOW),
        in_specs=[smem(), block, block],
        out_specs=block,
        compiler_params=params(60),
        cost_estimate=cost(local.size, 6 * local.size),
    )(decay, local, got)


def assemble_kernel(plan, fills, sources_of, me_ref, side_ref, *refs):
    sources, outs = refs[: len(sources_of)], refs[len(sources_of) :]
    lanes = sources[0].shape[1]
    for index, row, size in fills:
        outs[index][row : row + size, :] = jnp.zeros((size, outs[index].shape[1]), LOW)

    def place(source, lane, low, high):
        for start, index, row, size in plan:
            begin, end = max(start, low), min(start + size, high)
            if begin < end:
                to = row + begin - start
                outs[index][to : to + end - begin, pl.ds(lane, lanes)] = source[
                    begin - low : end - low, :
                ]

    for (mask, half), source in zip(sources_of, sources):
        lane = pl.multiple_of(jnp.bitwise_xor(me_ref[0], mask) * lanes, lanes)
        rows = source.shape[0]
        if half is None:
            place(source, lane, 0, rows)
            continue
        for side in range(2):

            @pl.when(side_ref[0] == side)
            def _():
                low = (side ^ half) * rows
                place(source, lane, low, low + rows)


def assemble(held, plan, fills, heights, width, me, side):
    sources_of = [(mask, half) for mask, half, part in held]
    parts = [part for mask, half, part in held]
    return pl.pallas_call(
        functools.partial(assemble_kernel, plan, fills, sources_of),
        out_shape=[shape((rows, width), LOW) for rows in heights],
        in_specs=[smem()] * 2 + [pl.BlockSpec(memory_space=VMEM)] * len(parts),
        out_specs=[pl.BlockSpec(memory_space=VMEM)] * len(heights),
        compiler_params=params(20),
        cost_estimate=cost(0, 4 * sum(heights) * width),
    )(me, side, *parts)


def rotated(flat, cosine, sine):
    half = KD // 2
    parts = []
    for h in range(H):
        u = flat[:, h * KD : h * KD + half]
        w = flat[:, h * KD + half : (h + 1) * KD]
        parts += [u * cosine - w * sine, w * cosine + u * sine]
    return jnp.concatenate(parts, axis=1)


def column(size):
    return lax.broadcasted_iota(jnp.int32, (size, 1), 0).astype(WIDE)


def front_kernel(count, decay, seg_s, tok, w, gains, cos, sin, seg, *rest):
    hid, k, v, kv, out_state, state = rest
    seq = pl.program_id(0) // count
    c = pl.program_id(0) % count
    x = tok[...].astype(WIDE)
    r = lax.rsqrt(jnp.mean(x * x, axis=1, keepdims=True) + EPS)
    h1 = (x * r * gains[0:1, :].astype(WIDE)).astype(LOW)
    hid[...] = h1
    kd = H * KD
    key = rotated(dot_nt(h1, w[kd : 2 * kd, :]), cos[...], sin[...]).astype(LOW)
    k[...] = key
    val = dot_nt(h1, w[2 * kd :, :]).astype(LOW)
    v[...] = val
    first = seg_s[seq, c * BLOCK]
    last = seg_s[seq, c * BLOCK + BLOCK - 1]
    before = seg_s[seq, jnp.maximum(c * BLOCK - 1, 0)]
    here = (seg[...] == last).astype(WIDE)
    joined = jnp.logical_and(jnp.logical_and(first == last, first == before), c > 0)
    for h in range(H):
        a = decay[h]
        kw = jnp.exp(a * (BLOCK - 1.0 - column(BLOCK))) * here
        kk = (key[:, h * KD : (h + 1) * KD].astype(WIDE) * kw).astype(LOW)
        add = dot_tn(kk, val[:, h * VP : (h + 1) * VP])
        kv[h] = add
        factor = jnp.exp(jnp.full((1, 1), a * BLOCK, WIDE))
        total = jnp.where(joined, factor * state[h], 0.0) + add
        state[h] = total
        out_state[h] = total.astype(LOW)


def row_block(width):
    return pl.BlockSpec((BLOCK, width), lambda t: (t, 0))


def state_block(count, at=lambda c: c):
    return pl.BlockSpec(
        (None, None, H, KD, VP), lambda t: (t // count, at(t % count), 0, 0, 0)
    )


def seq_block(count):
    return pl.BlockSpec((None, H, KD, VP), lambda t: (t // count, 0, 0, 0))


def front(seqs, length, tokens, seg_col, segments, decay, w, gains, cos, sin):
    count = length // BLOCK
    rows, width = tokens.shape
    outs = [width, H * KD, H * VP]
    table = pl.BlockSpec((BLOCK, KD // 2), lambda t: (t % count, 0))
    return pl.pallas_call(
        functools.partial(front_kernel, count),
        grid=(seqs * count,),
        out_shape=[shape((rows, n), LOW) for n in outs]
        + [shape((seqs, count, H, KD, VP), WIDE), shape((seqs, H, KD, VP), LOW)],
        in_specs=[smem(), smem(), row_block(width), whole(w.shape), whole(gains.shape)]
        + [table, table, row_block(1)],
        out_specs=[row_block(n) for n in outs]
        + [state_block(count), seq_block(count)],
        scratch_shapes=[VMEM((H, KD, VP), WIDE)],
        compiler_params=params(60),
        cost_estimate=cost(2 * rows * width * w.shape[0], 12 * rows * width),
    )(decay, segments, tokens, w, gains, cos, sin, seg_col)


def decay_row(a):
    return jnp.exp(-a * lax.broadcasted_iota(jnp.int32, (1, BLOCK), 1).astype(WIDE))


def mixing(a, top, size, seg, seg_row):
    reach = top + size
    rows = jnp.exp(a * (column(size) + float(top)))
    same = seg[top:reach, :] == seg_row[:, :reach]
    n = lax.broadcasted_iota(jnp.int32, (size, reach), 0) + top
    m = lax.broadcasted_iota(jnp.int32, (size, reach), 1)
    return jnp.where(jnp.logical_and(same, n >= m), rows * decay_row(a)[:, :reach], 0.0)


TILE = 256


def inner_kernel(decay, k, v, hid, w, cos, sin, seg, seg_row, q, intra):
    query = rotated(dot_nt(hid[...], w[...]), cos[...], sin[...]).astype(LOW)
    q[...] = query
    for i in range(BLOCK // TILE):
        top, reach = i * TILE, (i + 1) * TILE
        for h in range(H):
            s = dot_nt(query[top:reach, h * KD : (h + 1) * KD], k[:reach, h * KD : (h + 1) * KD])
            weights = (s * mixing(decay[h], top, TILE, seg, seg_row)).astype(LOW)
            intra[top:reach, h * VP : (h + 1) * VP] = dot(
                weights, v[:reach, h * VP : (h + 1) * VP]
            ).astype(LOW)


def inner(k, v, hid, w, cos, sin, seg_col, seg_row, decay, length):
    rows, width = hid.shape
    count = length // BLOCK
    block = lambda n: pl.BlockSpec((BLOCK, n), lambda t: (t, 0))
    table = pl.BlockSpec((BLOCK, KD // 2), lambda t: (t % count, 0))
    return pl.pallas_call(
        inner_kernel,
        grid=(rows // BLOCK,),
        out_shape=[shape((rows, n), LOW) for n in (H * KD, H * VP)],
        in_specs=[
            smem(),
            block(H * KD),
            block(H * VP),
            block(width),
            pl.BlockSpec((H * KD, width), lambda t: (0, 0)),
            table,
            table,
            block(1),
            pl.BlockSpec((None, 1, BLOCK), lambda t: (t, 0, 0)),
        ],
        out_specs=[block(n) for n in (H * KD, H * VP)],
        compiler_params=params(60),
        cost_estimate=cost(rows * (2 * width * 512 + 2 * BLOCK * H * VP), 8 * rows * H * VP),
    )(decay, k, v, hid, w, cos, sin, seg_col, seg_row)


def gate_kernel(hid, w, gate):
    gate[...] = dot_nt(hid[...], w[...]).astype(LOW)


def gates(hid, w):
    rows, width = hid.shape
    vp = H * VP
    return pl.pallas_call(
        gate_kernel,
        grid=(rows // BLOCK,),
        out_shape=shape((rows, vp), LOW),
        in_specs=[row_block(width), pl.BlockSpec((vp, width), lambda t: (0, 0))],
        out_specs=row_block(vp),
        compiler_params=params(60),
        cost_estimate=cost(2 * rows * width * vp, 4 * rows * vp),
    )(hid, w)


CHUNK = 16


def interleaved(first, second):
    steps = [((i + 0.5) / len(first), 0, step) for i, step in enumerate(first)]
    steps += [((i + 0.5) / len(second), 1, step) for i, step in enumerate(second)]
    for place, which, step in sorted(steps, key=lambda item: item[:2]):
        step()


def pieces(width, size=256):
    return [(start, min(start + size, width)) for start in range(0, width, size)]


def across(narrow, width):
    return jnp.concatenate([narrow] * (width // 128), axis=1)


def middle_kernel(count, ff, decay, seg_s, in_last, *refs):
    (intra, gate, q, tok, cot, seg, w, gains, *got, kv) = refs[:12]
    outs, scratch = refs[12:24], refs[24:]
    (tok_out, hid2, prod, dgate, dup, mixed, glow, ggate, gret, st_out, dst, leave) = outs
    (state, now, queries, factors, ret_s, norm_s, silu_s, slope_s, inv_s, res_s, ff_s, low_s, sums) = scratch
    seq = pl.program_id(0) // count
    c = pl.program_id(0) % count
    start = c * BLOCK
    vp = H * VP
    width = tok.shape[1]
    before = jnp.where(c > 0, seg_s[seq, jnp.maximum(start - 1, 0)], in_last[seq])

    @pl.when(c == 0)
    def _():
        for h in range(H):
            total = entering(decay, count * BLOCK, h, got)
            state[h] = total
            now[h] = total.astype(LOW)

    for b in range(1, count):

        @pl.when(c == b)
        def _():
            prev = seg_s[seq, (b - 1) * BLOCK - 1] if b > 1 else in_last[seq]
            joined = jnp.logical_and(
                seg_s[seq, (b - 1) * BLOCK] == seg_s[seq, b * BLOCK - 1],
                seg_s[seq, (b - 1) * BLOCK] == prev,
            )
            for h in range(H):
                factor = jnp.exp(jnp.full((1, 1), decay[h] * BLOCK, WIDE))
                total = jnp.where(joined, factor * state[h], 0.0) + kv[h]
                state[h] = total
                now[h] = total.astype(LOW)

    st_out[...] = now[...]
    here = (seg[...] == before).astype(WIDE)
    for h in range(H):
        qw = jnp.exp(decay[h] * (column(BLOCK) + 1.0)) * here
        factors[h] = jnp.broadcast_to(qw, (BLOCK, 128))

    w_out = (vp, 2 * vp)
    w_gate = (2 * vp, 2 * vp + ff)
    w_up = (2 * vp + ff, 2 * vp + 2 * ff)
    w_down = (2 * vp + 2 * ff, 2 * vp + 3 * ff)
    gain = gains[1:2, :].astype(WIDE)

    def phases(top):
        rs = pl.ds(top, TILE)
        lists = []

        def add(steps):
            lists.append(steps)

        def chunks():
            return [pl.ds(row, CHUNK) for row in range(top, top + TILE, CHUNK)]

        def cross(h, lo, hi):
            ret_s[rs, h * VP + lo : h * VP + hi] = dot(
                q[rs, h * KD : (h + 1) * KD], now[h, :, lo:hi]
            )

        add([functools.partial(cross, h, *piece) for h in range(H) for piece in pieces(VP)])

        def gated(h, r):
            hv = slice(h * VP, (h + 1) * VP)
            hk = slice(h * KD, (h + 1) * KD)
            qw = factors[h, r, :]
            queries[r, hk] = (q[r, hk].astype(WIDE) * across(qw, KD)).astype(LOW)
            ret = intra[r, hv].astype(WIDE) + across(qw, VP) * ret_s[r, hv]
            mean = jnp.sum(ret, axis=1, keepdims=True) * (1.0 / VD)
            centered = ret - mean
            square = jnp.sum(centered * centered, axis=1, keepdims=True)
            var = (square - (VP - VD) * (mean * mean)) * (1.0 / VD)
            inv = lax.rsqrt(var + 1.0 * KD)
            nh = centered * inv
            g = gate[r, hv].astype(WIDE)
            sg = 0.5 * jnp.tanh(0.5 * g) + 0.5
            sl = g * sg
            mixed[r, hv] = (nh * sl).astype(LOW)
            norm_s[r, hv] = nh
            silu_s[r, hv] = sl
            slope_s[r, hv] = nh * (sg + sl * (1.0 - sg))
            inv_s[h, r, :] = jnp.broadcast_to(inv, (CHUNK, 128))

        add([functools.partial(gated, h, r) for r in chunks() for h in range(H)])

        def project(lo, hi):
            res_s[rs, lo:hi] = dot(mixed[rs, :], w[w_out[0] : w_out[1], lo:hi])

        add([functools.partial(project, *piece) for piece in pieces(width)])

        def norm(r):
            resid = tok[r, :].astype(WIDE) + res_s[r, :]
            r2 = lax.rsqrt(jnp.mean(resid * resid, axis=1, keepdims=True) + EPS)
            res_s[r, :] = resid
            hid2[r, :] = (resid * r2 * gain).astype(LOW)
            inv_s[H, r, :] = jnp.broadcast_to(r2, (CHUNK, 128))

        add([functools.partial(norm, r) for r in chunks()])

        def forward(place, source, at, lo, hi):
            ff_s[place, rs, lo:hi] = dot_nt(source[rs, :], w[at[0] + lo : at[0] + hi, :])

        add(
            [
                functools.partial(forward, place, source, at, *piece)
                for piece in pieces(ff)
                for place, source, at in ((0, hid2, w_gate), (1, hid2, w_up), (2, cot, w_down))
            ]
        )

        def gelu(r, lo, hi):
            gf, uf, gp = ff_s[0, r, lo:hi], ff_s[1, r, lo:hi], ff_s[2, r, lo:hi]
            e = jnp.exp(-0.5 * (gf * gf))
            d = 1.0 / (1.0 + (0.3275911 * math.sqrt(0.5)) * jnp.abs(gf))
            poly = d * (
                0.5 * 0.254829592
                + d
                * (
                    0.5 * -0.284496736
                    + d * (0.5 * 1.421413741 + d * (0.5 * -1.453152027 + d * (0.5 * 1.061405429)))
                )
            )
            tail = poly * e
            cdf = jnp.where(gf >= 0.0, 1.0 - tail, tail)
            ge = gf * cdf
            dge = cdf + gf * (e * (1.0 / math.sqrt(2.0 * math.pi)))
            prod[r, lo:hi] = (ge * uf).astype(LOW)
            dgate[r, lo:hi] = (gp * uf * dge).astype(LOW)
            dup[r, lo:hi] = (gp * ge).astype(LOW)

        add([functools.partial(gelu, r, *piece) for r in chunks() for piece in pieces(ff, 512)])

        def down(lo, hi):
            low_s[0, rs, lo:hi] = dot(prod[rs, :], w[w_down[0] : w_down[1], lo:hi])

        def hidden(lo, hi):
            low_s[1, rs, lo:hi] = dot(dgate[rs, :], w[w_gate[0] : w_gate[1], lo:hi]) + dot(
                dup[rs, :], w[w_up[0] : w_up[1], lo:hi]
            )

        add([functools.partial(step, *piece) for piece in pieces(width) for step in (down, hidden)])

        def residual(r):
            resid = res_s[r, :]
            r2 = across(inv_s[H, r, :], width)
            tok_out[r, :] = (resid + low_s[0, r, :]).astype(LOW)
            gh = low_s[1, r, :] * gain
            xhat = resid * r2
            inner_product = jnp.mean(gh * xhat, axis=1, keepdims=True)
            glow[r, :] = (cot[r, :].astype(WIDE) + r2 * (gh - xhat * inner_product)).astype(LOW)

        add([functools.partial(residual, r) for r in chunks()])

        def mix_back(lo, hi):
            ret_s[rs, lo:hi] = dot_nt(glow[rs, :], w[w_out[0] + lo : w_out[0] + hi, :])

        add([functools.partial(mix_back, *piece) for piece in pieces(vp)])

        def gated_back(h, r):
            hv = slice(h * VP, (h + 1) * VP)
            gm = ret_s[r, hv]
            nh = norm_s[r, hv]
            ggate[r, hv] = (gm * slope_s[r, hv]).astype(LOW)
            gn = gm * silu_s[r, hv]
            one = jnp.sum(gn, axis=1, keepdims=True) * (1.0 / VD)
            two = jnp.sum(gn * nh, axis=1, keepdims=True) * (1.0 / VD)
            gret[r, hv] = (across(inv_s[h, r, :], VP) * (gn - one - nh * two)).astype(LOW)

        add([functools.partial(gated_back, h, r) for r in chunks() for h in range(H)])
        return lists

    first, second = phases(0), phases(TILE)
    for k in range(len(first) + 1):
        interleaved(first[k] if k < len(first) else [], second[k - 1] if k else [])
    for h in range(H):
        add = dot_tn(queries[:, h * KD : (h + 1) * KD], gret[:, h * VP : (h + 1) * VP])
        dst[h] = add
        sums[c, h] = add

    @pl.when(c == count - 1)
    def _():
        for h in range(H):
            total = sums[count - 1, h]
            for b in reversed(range(count - 1)):
                prev = seg_s[seq, b * BLOCK - 1] if b > 0 else in_last[seq]
                joined = jnp.logical_and(
                    seg_s[seq, b * BLOCK] == seg_s[seq, (b + 1) * BLOCK - 1],
                    seg_s[seq, b * BLOCK] == prev,
                )
                factor = jnp.exp(jnp.full((1, 1), decay[h] * BLOCK, WIDE))
                total = jnp.where(joined, factor * total, 0.0) + sums[b, h]
            leave[h] = total.astype(LOW)


def middle(seqs, length, ff, data, seg_col, segments, in_last, decay, w, gains, got, kv):
    intra, gate, q, tokens, cotangent = data
    rows, width = tokens.shape
    count = length // BLOCK
    vp = H * VP
    outs = [width, width, ff, ff, ff, vp, width, vp, vp]
    inputs = [decay, segments, in_last, intra, gate, q, tokens, cotangent, seg_col, w, gains, *got, kv]
    specs = [smem()] * 3 + [row_block(n) for n in (vp, vp, H * KD, width, width, 1)]
    specs += [whole(w.shape), whole(gains.shape), *[seq_block(count)] * 3]
    specs += [state_block(count, lambda c: jnp.maximum(c - 1, 0))]
    one = (H, KD, VP)
    states = (seqs, count, *one)
    return pl.pallas_call(
        functools.partial(middle_kernel, count, ff),
        grid=(seqs * count,),
        out_shape=[shape((rows, n), LOW) for n in outs]
        + [shape(states, LOW), shape(states, WIDE), shape((seqs, *one), LOW)],
        in_specs=specs,
        out_specs=[row_block(n) for n in outs]
        + [state_block(count)] * 2
        + [seq_block(count)],
        scratch_shapes=[
            VMEM(one, WIDE),
            VMEM(one, LOW),
            VMEM((BLOCK, H * KD), LOW),
            VMEM((H, BLOCK, 128), WIDE),
            VMEM((BLOCK, vp), WIDE),
            VMEM((BLOCK, vp), WIDE),
            VMEM((BLOCK, vp), WIDE),
            VMEM((BLOCK, vp), WIDE),
            VMEM((H + 1, BLOCK, 128), WIDE),
            VMEM((BLOCK, width), WIDE),
            VMEM((3, BLOCK, ff), WIDE),
            VMEM((2, BLOCK, width), WIDE),
            VMEM(states[1:], WIDE),
        ],
        compiler_params=params(60),
        cost_estimate=cost(2 * rows * width * (2 * vp + 6 * ff), 30 * rows * width),
    )(*inputs)


def weight_kernel(plan, count, layout, me_ref, *refs):
    ins, ready, outs, total = refs[:count], refs[count:-3], refs[-3:-1], refs[-1]
    if layout is None:
        outs = refs[-2:-1]
    t = pl.program_id(0)
    last = pl.num_programs(0) - 1
    for left, right, cuts in plan:
        a, b = ins[left], ins[right]
        for source, row, size in cuts:
            add = dot_tn(a[:, source : source + size], b[...])

            @pl.when(t == 0)
            def _():
                total[row : row + size, :] = add

            @pl.when(t > 0)
            def _():
                total[row : row + size, :] += add

    @pl.when(t == last)
    def _():
        used = max(row + size for left, right, cuts in plan for source, row, size in cuts)
        if layout is None:
            outs[0][...] = total[...].astype(LOW)
            return
        for item in ready:
            total[used : used + item.shape[0], :] = item[...].astype(WIDE)
            used += item.shape[0]
        if used < total.shape[0]:
            total[used:, :] = jnp.zeros((total.shape[0] - used, total.shape[1]), WIDE)
        lanes = outs[0].shape[2]
        which, pieces = layout
        rows = outs[0].shape[1] // pieces
        for part in range(2 * outs[0].shape[0]):
            target = outs[part & 1]
            lane = pl.multiple_of(jnp.bitwise_xor(me_ref[0], part) * lanes, lanes)
            for q in range(pieces):
                row = pl.multiple_of(jnp.bitwise_xor(me_ref[which], q) * rows, 16)
                target[part >> 1, q * rows : (q + 1) * rows, :] = total[
                    pl.ds(row, rows), pl.ds(lane, lanes)
                ].astype(LOW)


def weight_grads(arrays, plan, place, shards=2, height=0, layout=None, ready=()):
    rows = arrays[0].shape[0]
    used = max(row + size for left, right, cuts in plan for source, row, size in cuts)
    width = arrays[plan[0][1]].shape[1]
    tile = 2 * BLOCK
    block = lambda n: pl.BlockSpec((tile, n), lambda t: (t, 0))
    dims = [(shards // 2, height, width // shards)] * 2
    if layout is None:
        height, dims = used, [(used, width)]
    full = lambda item: pl.BlockSpec(item, lambda t: (0,) * len(item))
    return pl.pallas_call(
        functools.partial(weight_kernel, plan, len(arrays), layout),
        grid=(rows // tile,),
        out_shape=[shape(item, LOW) for item in dims],
        in_specs=[smem()] + [block(item.shape[1]) for item in arrays]
        + [full(item.shape) for item in ready],
        out_specs=[full(item) for item in dims],
        scratch_shapes=[VMEM((height, width), WIDE)],
        compiler_params=params(60),
        cost_estimate=cost(2 * rows * used * width, 2 * rows * sum(i.shape[1] for i in arrays)),
    )(place, *arrays, *ready)


def back_kernel(count, decay, seg_s, in_last, *refs):
    (q, k, v, gret, cos, sin, seg, seg_row, st, dst, *got) = refs[:13]
    (dq, dk, dv, state, weights, grads) = refs[13:]
    seq = pl.program_id(0) // count
    c = count - 1 - pl.program_id(0) % count

    @pl.when(c == count - 1)
    def _():
        for h in range(H):
            state[h] = entering(decay, count * BLOCK, h, got)

    for b in range(1, count):

        @pl.when(c == b - 1)
        def _():
            prev = seg_s[seq, b * BLOCK - 1]
            first = seg_s[seq, b * BLOCK]
            last = seg_s[seq, (b + 1) * BLOCK - 1]
            joined = jnp.logical_and(first == last, first == prev)
            for h in range(H):
                factor = jnp.exp(jnp.full((1, 1), decay[h] * BLOCK, WIDE))
                state[h] = jnp.where(joined, factor * state[h], 0.0) + dst[h]

    start = c * BLOCK
    before = jnp.where(c > 0, seg_s[seq, jnp.maximum(start - 1, 0)], in_last[seq])
    final = seg_s[seq, start + BLOCK - 1]
    here = (seg[...] == before).astype(WIDE)
    ends = (seg[...] == final).astype(WIDE)
    place = column(BLOCK)
    dqs, dks = [], []
    for h in range(H):
        a = decay[h]
        qh = q[:, h * KD : (h + 1) * KD]
        kh = k[:, h * KD : (h + 1) * KD]
        vh = v[:, h * VP : (h + 1) * VP]
        gh = gret[:, h * VP : (h + 1) * VP]
        qw = jnp.exp(a * (place + 1.0)) * here
        kw = jnp.exp(a * (BLOCK - 1.0 - place)) * ends
        parts = []
        for i in range(BLOCK // TILE):
            top, reach = i * TILE, (i + 1) * TILE
            mix = mixing(a, top, TILE, seg, seg_row)
            s = dot_nt(qh[top:reach, :], kh[:reach, :])
            weights[top:reach, :reach] = (s * mix).astype(LOW)
            gs = (dot_nt(gh[top:reach, :], vh[:reach, :]) * mix).astype(LOW)
            grads[top:reach, :reach] = gs
            parts.append(dot(gs, kh[:reach, :]))
        late = state[h].astype(LOW)
        dqs.append(jnp.concatenate(parts) + qw * dot_nt(gh, st[h]))
        parts, values = [], []
        for i in range(BLOCK // TILE):
            top, reach = i * TILE, (i + 1) * TILE
            parts.append(dot_tn(grads[top:, top:reach], qh[top:, :]))
            values.append(dot_tn(weights[top:, top:reach], gh[top:, :]))
        dks.append(jnp.concatenate(parts) + kw * dot_nt(vh, late))
        dv[:, h * VP : (h + 1) * VP] = (jnp.concatenate(values) + kw * dot(kh, late)).astype(LOW)
    dq[...] = rotated(jnp.concatenate(dqs, axis=1), cos[...], -sin[...]).astype(LOW)
    dk[...] = rotated(jnp.concatenate(dks, axis=1), cos[...], -sin[...]).astype(LOW)


def back(seqs, length, data, cos, sin, seg_col, seg_row, segments, in_last, decay, st, dst, got):
    rows = data[0].shape[0]
    count = length // BLOCK
    turn = lambda t: (t // count) * count + count - 1 - t % count
    block = lambda n: pl.BlockSpec((BLOCK, n), lambda t: (turn(t), 0))
    table = pl.BlockSpec((BLOCK, KD // 2), lambda t: (count - 1 - t % count, 0))
    outs = [H * KD, H * KD, H * VP]
    inputs = [decay, segments, in_last, *data, cos, sin, seg_col, seg_row, st, dst, *got]
    specs = [smem()] * 3 + [block(item.shape[1]) for item in data] + [table, table, block(1)]
    specs += [pl.BlockSpec((None, 1, BLOCK), lambda t: (turn(t), 0, 0))]
    specs += [state_block(count, lambda c: count - 1 - c)]
    specs += [state_block(count, lambda c: jnp.minimum(count - c, count - 1))]
    specs += [seq_block(count)] * 3
    return pl.pallas_call(
        functools.partial(back_kernel, count),
        grid=(seqs * count,),
        out_shape=[shape((rows, n), LOW) for n in outs],
        in_specs=specs,
        out_specs=[block(n) for n in outs],
        scratch_shapes=[
            VMEM((H, KD, VP), WIDE),
            VMEM((BLOCK, BLOCK), LOW),
            VMEM((BLOCK, BLOCK), LOW),
        ],
        compiler_params=params(60),
        cost_estimate=cost(rows * H * 2 * BLOCK * 3 * (KD + VP), 16 * rows * H * VP),
    )(*inputs)


def input_kernel(dq, dk, dv, ggate, tok, glow, w, w_gate, gains, *rest):
    out = rest[-1]
    kd = H * KD
    gh = dot(dq[...], w[:kd, :]) + dot(dk[...], w[kd : 2 * kd, :])
    gh += dot(dv[...], w[2 * kd :, :]) + dot(ggate[...], w_gate[...])
    x = tok[...].astype(WIDE)
    r = lax.rsqrt(jnp.mean(x * x, axis=1, keepdims=True) + EPS)
    xhat = x * r
    gh = gh * gains[0:1, :].astype(WIDE)
    inner_product = jnp.mean(gh * xhat, axis=1, keepdims=True)
    out[...] = (glow[...].astype(WIDE) + r * (gh - xhat * inner_product)).astype(LOW)


def input_grad(first, steps, dq, dk, dv, ggate, tokens, glow, w, w_rest, gains, earlier):
    rows, width = tokens.shape
    parts = rows // BLOCK // steps
    arrays = [dq, dk, dv, ggate, tokens, glow]
    block = lambda item: pl.BlockSpec((BLOCK, item.shape[1]), lambda t: (first + t, 0))
    inputs = [*arrays, w, w_rest, gains]
    specs = [block(item) for item in arrays] + [whole(w.shape)]
    specs += [pl.BlockSpec((H * VP, width), lambda t: (0, 0)), whole(gains.shape)]
    aliases = {}
    if earlier is not None:
        aliases = {len(inputs): 0}
        inputs.append(earlier)
        specs.append(pl.BlockSpec(memory_space=pl.ANY))
    return pl.pallas_call(
        input_kernel,
        grid=(steps,),
        out_shape=shape((rows, width), LOW),
        in_specs=specs,
        out_specs=block(tokens),
        input_output_aliases=aliases,
        compiler_params=params(32),
        cost_estimate=cost(2 * rows * width * (w.shape[0] + H * VP) // parts, 20 * rows * width // parts),
    )(*inputs)


def adam_step(master, moment, second, grad, scale, rate, decay_weight):
    clipped = grad * scale
    moment_new = BETA_ONE * moment + (1.0 - BETA_ONE) * clipped
    second_new = BETA_TWO * second + (1.0 - BETA_TWO) * clipped * clipped
    corrected = (
        moment_new
        * (1.0 / (1.0 - BETA_ONE**STEP))
        / (jnp.sqrt(second_new * (1.0 / (1.0 - BETA_TWO**STEP))) + ADAM_EPS)
    )
    return (master - rate * (corrected + decay_weight * master), moment_new, second_new)


def squares_kernel(vd, ff, layouts, place, *refs):
    halves, (w_qk, w_vg, w_gu, low_gains) = refs[:4], refs[4:8]
    grad_gains, total, early, late = refs[8:]
    kd = H * KD
    for index, target in enumerate((early, late)):
        which, pieces = layouts[index]
        rows = target.shape[0] // pieces
        for q in range(pieces):
            row = pl.multiple_of(jnp.bitwise_xor(place[which], q) * rows, 16)
            source = halves[2 * index + q // (pieces // 2)]
            start = q % (pieces // 2) * rows
            target[pl.ds(row, rows), :] = source[start : start + rows, :]

    def rows(source, start, size):
        return source[start : start + size, :].astype(WIDE)

    def product(weight, grad):
        return jnp.sum(weight.astype(LOW).astype(WIDE) * grad, axis=0, keepdims=True)

    sums = []

    def square(item):
        sums.append(jnp.sum(item * item, axis=0, keepdims=True))
        return item

    first = jnp.zeros((1, low_gains.shape[1]), WIDE)
    for i in range(2):
        grad = square(rows(late, i * kd, kd))
        first += jnp.sum(w_qk[i].astype(LOW).astype(WIDE).T * grad, axis=0, keepdims=True)
    first += product(w_vg[0], square(rows(late, 2 * kd, vd)))
    first += product(w_vg[1], square(rows(early, vd, vd)))
    square(rows(early, 0, vd))
    square(rows(early, 2 * vd, ff))
    second = product(w_gu[0], square(rows(early, 2 * vd + ff, ff)))
    second += product(w_gu[1], square(rows(early, 2 * vd + 2 * ff, ff)))
    gains = jnp.concatenate([first, second]) / low_gains[...].astype(LOW).astype(WIDE)
    grad_gains[...] = gains
    sums.append(jnp.sum(gains * gains, axis=0, keepdims=True))
    total[...] = jnp.broadcast_to(jnp.sum(sum(sums), axis=1, keepdims=True), total.shape)


def squares(vd, ff, layouts, place, grads, w_qk, w_vg, w_gu, gains):
    halves = [half for pair in grads for half in pair]
    vmem = pl.BlockSpec(memory_space=VMEM)
    return pl.pallas_call(
        functools.partial(squares_kernel, vd, ff, layouts),
        out_shape=[shape(gains.shape, WIDE), shape((8, 128), WIDE)]
        + [shape((2 * pair[0].shape[0], pair[0].shape[1]), LOW) for pair in grads],
        in_specs=[smem()] + [vmem] * 8,
        out_specs=[vmem] * 4,
        compiler_params=params(20),
    )(place, *halves, w_qk, w_vg, w_gu, gains)


def update_kernel(vd, ff, *refs):
    totals, (early, late, gain_grads) = refs[:4], refs[4:7]
    sources, targets, norm_out = refs[7:25], refs[25:43], refs[43]
    ins, outs = refs[44:62], refs[62:80]
    arrived, sent = refs[80:]
    kd = H * KD
    order = [4, 3, 2, 1, 0, 5]
    places = [6 * group + place for place in order for group in range(3)]
    fetch = {i: pltpu.make_async_copy(sources[i], ins[i], arrived.at[i]) for i in places}
    send = {i: pltpu.make_async_copy(outs[i], targets[i], sent.at[i]) for i in places}
    for i in places:
        fetch[i].start()
    norm = jnp.sqrt((totals[0][...] + totals[1][...]) + (totals[2][...] + totals[3][...]))
    norm_out[0, 0] = jnp.max(norm)
    scale = jnp.minimum(1.0, CLIP / (norm + 1e-06))[0:1, 0:1]

    def step(place, at, grad, rate, decay_weight):
        results = adam_step(
            ins[place][at], ins[6 + place][at], ins[12 + place][at], grad, scale, rate, decay_weight
        )
        for group, result in enumerate(results):
            outs[6 * group + place][at] = result

    def rows(source, start, size):
        return source[start : start + size, :].astype(WIDE)

    grads = {
        4: [(..., lambda: rows(early, 2 * vd, ff))],
        3: [(i, lambda i=i: rows(early, 2 * vd + (1 + i) * ff, ff)) for i in range(2)],
        2: [(..., lambda: rows(early, 0, vd))],
        1: [(0, lambda: rows(late, 2 * kd, vd)), (1, lambda: rows(early, vd, vd))],
        0: [(i, lambda i=i: rows(late, i * kd, kd).T) for i in range(2)],
        5: [(..., lambda: gain_grads[...])],
    }
    for place in order:
        for group in range(3):
            fetch[6 * group + place].wait()
        rate, decay_weight = (GAIN_RATE, 0.0) if place == 5 else (MATRIX_RATE, DECAY_WEIGHT)
        for at, grad in grads[place]:
            step(place, at, grad(), rate, decay_weight)
        for group in range(3):
            send[6 * group + place].start()
    for i in places:
        send[i].wait()


def update(vd, ff, totals, grads, gain_grads, arrays):
    anywhere = pl.BlockSpec(memory_space=pl.ANY)
    return pl.pallas_call(
        functools.partial(update_kernel, vd, ff),
        out_shape=[shape(item.shape, WIDE) for item in arrays] + [shape((1, 1), WIDE)],
        in_specs=[pl.BlockSpec(memory_space=VMEM)] * 7 + [anywhere] * 18,
        out_specs=[anywhere] * 18 + [smem()],
        scratch_shapes=[VMEM(item.shape, WIDE) for item in arrays] * 2
        + [pltpu.SemaphoreType.DMA((18,))] * 2,
        compiler_params=params(40),
    )(*totals, *grads, gain_grads, *arrays)


def on_device(
    tokens,
    cotangent,
    segments,
    log_decay,
    w_qk,
    w_vg,
    w_out,
    w_gu,
    w_down,
    norm_gains,
    *states,
):
    turned = lambda item: jnp.swapaxes(item, 1, 2)
    shards = lax.axis_size("shard")
    me = lax.axis_index("shard").reshape(1)
    replica = lax.axis_index("dp")
    count = bits_of("dp")
    halved = (tuple(range(count)), (1,))
    numbers = [
        sum(((replica >> bit) & 1) << (len(bits) - 1 - i) for i, bit in enumerate(bits))
        for bits in halved
    ]
    layouts = [(1 + i, 2 ** len(bits)) for i, bits in enumerate(halved)]
    place = jnp.concatenate([me, jnp.stack(numbers)])
    seqs, length, width = tokens.shape
    rows = seqs * length
    kd, vd, ff = H * KD, H * VD, w_down.shape[0]
    vp = H * VP
    vg_t, gu_t = turned(w_vg), turned(w_gu)

    low = lambda item: item.astype(LOW)
    def heads(item):
        return [
            jnp.pad(item[h * VD : (h + 1) * VD], ((0, VP - VD), (0, 0))) for h in range(H)
        ]

    first = jnp.concatenate(
        [
            low(w_qk[0]).T,
            low(w_qk[1]).T,
            low(vg_t[0]),
            jnp.pad(low(norm_gains), ((0, 14), (0, 0))),
        ]
    )
    rest = jnp.concatenate(
        [*heads(low(vg_t[1])), *heads(low(w_out)), low(gu_t[0]), low(gu_t[1]), low(w_down)]
    )
    first_held = gather_shards(first)
    rest = after(rest, first_held[1][2])
    w_rest = lax.all_gather(rest, "shard", axis=1, tiled=True)
    side = (lax.axis_index("dp") & 1).reshape(1)

    half_width = KD // 2
    freq_rates = jnp.exp(-math.log(10000.0) * jnp.arange(half_width).astype(WIDE) / half_width)
    positions = (lax.axis_index("shard") * length + jnp.arange(length)).astype(WIDE)
    angles = positions[:, None] * freq_rates[None, :]
    cos, sin = jnp.cos(angles), jnp.sin(angles)

    tok = tokens.reshape(rows, width)
    cot = cotangent.reshape(rows, width)
    seg_col = segments.reshape(rows, 1)
    seg_row = segments.reshape(rows // BLOCK, 1, BLOCK)
    in_last = jnp.where(lax.axis_index("shard") > 0, segments[:, 0], -1)
    decay = log_decay

    def tick(*done):
        nonlocal decay, place, gains
        decay, place, gains = lax.optimization_barrier((decay, place, gains, *done))[:3]

    plan = [(0, 0, 0, 2 * kd)] + [(2 * kd + h * VD, 0, 2 * kd + h * VP, VD) for h in range(H)]
    plan += [(2 * kd + vd, 1, 0, 16)]
    fills = [(0, 2 * kd + h * VP + VD, VP - VD) for h in range(H)]
    w_qkv, gains = assemble(first_held, plan, fills, [2 * kd + vp, 16], width, me, side)
    tick(rest)
    hid, k, v, kv, leaving = front(
        seqs, length, tok, seg_col, segments, decay, w_qkv, gains, cos, sin
    )
    passing = Passing(leaving, False)
    tick(leaving)
    tick(passing.turn(decay, length, leaving))
    q, intra = inner(k, v, hid, w_qkv, cos, sin, seg_col, seg_row, decay, length)
    tick(q)
    passing.finish(q)
    gate = gates(after(hid, passing.got[1], q), w_rest)
    tick(gate)
    tokens_out, hid2, prod, dgate, dup, mixed, glow, ggate, gret, st, dst, leaving = middle(
        seqs, length, ff, (intra, gate, q, tok, cot), seg_col, segments, in_last, decay,
        w_rest, gains, passing.got, kv,
    )
    returning = Passing(leaving, True)
    tick(leaving)

    def halves(row):
        return [(h * VP, row + h * VD, VD) for h in range(H)]

    fit = lambda used, layout: used + -used % (16 * layout[1])
    plan = [(0, 1, [(0, 0, ff)]), (2, 3, [(0, ff, ff)]), (4, 3, [(0, 2 * ff, ff)])]
    (made,) = weight_grads([prod, cot, dgate, hid2, dup], plan, place)
    tick(made)
    tick(returning.turn(decay, length, made))
    plan = [(0, 1, halves(0)), (2, 3, halves(vd))]
    made = weight_grads(
        [mixed, glow, ggate, hid], plan, place, shards,
        fit(2 * vd + 3 * ff, layouts[0]), layouts[0], (made,),
    )
    tick(made[0])
    returning.finish(made[0])
    early = Reduction(made[0], after(made[1], returning.got[1]), halved[0])
    tick(early.cross(made[0]))
    dq, dk, dv = back(
        seqs, length, (q, k, v, gret), cos, sin, seg_col, seg_row, segments, in_last, decay,
        st, dst, returning.got,
    )
    tick(dq)
    tick(early.next(dq))
    plan = [(0, 3, [(0, 0, kd)]), (1, 3, [(0, kd, kd)]), (2, 3, halves(2 * kd))]
    made = weight_grads(
        [dq, dk, dv, hid], plan, place, shards, fit(2 * kd + vd, layouts[1]), layouts[1]
    )
    late = Reduction(*made, halved[1])
    tick(made[0])
    tick(early.next(made[0]))
    tick(late.cross(made[0]))
    blocks = rows // BLOCK
    data = (dq, dk, dv, ggate, tok, glow, w_qkv, w_rest)
    grad_input = None
    for part in range(2):
        grad_input = input_grad(part * blocks // 2, blocks // 2, *data, gains, grad_input)
        tick(grad_input)
        tick(late.next(grad_input), early.next(grad_input))
    while early.left() or late.left():
        for item in (early, late):
            if item.left():
                item.next()

    gain_grads, total, *grads = squares(
        vd, ff, layouts, place, [early.result(), late.result()], w_qk, vg_t, gu_t, norm_gains
    )
    others = [
        lax.ppermute(total, "shard", [(i, i ^ mask) for i in range(shards)]) for mask in (1, 2, 3)
    ]
    arrays = []
    for group in ((w_qk, w_vg, w_out, w_gu, w_down, norm_gains), states[:6], states[6:]):
        arrays += [turned(item) if i in (1, 3) else item for i, item in enumerate(group)]
    *results, norm = update(vd, ff, [total, *others], grads, gain_grads, arrays)
    results = [turned(item) if i % 6 in (1, 3) else item for i, item in enumerate(results)]
    return (
        tokens_out.reshape(tokens.shape),
        grad_input.reshape(tokens.shape),
        *results,
        norm.reshape(()),
    )


def solution(mesh):
    split = P("dp", "shard", None)
    rows, columns = P(None, "shard", None), P(None, "shard")
    group = (rows, rows, columns, rows, columns, columns)
    in_specs = (split, split, P("dp", "shard"), P()) + group * 3
    out_specs = (split, split) + group * 3 + (P(),)
    return jax.shard_map(
        on_device, mesh=mesh, in_specs=in_specs, out_specs=out_specs, check_vma=False
    )
```

```python
import functools
import math

import jax
import jax.numpy as jnp
from jax import lax
from jax.experimental import pallas as pl
from jax.experimental.pallas import tpu as pltpu
from jax.sharding import PartitionSpec as P

H = 2
KD = 256
VD = 432
VP = 512
BLOCK = 512
STEP = 10

EPS = 1e-05
ADAM_EPS = 1e-08
BETA_ONE = 0.9
BETA_TWO = 0.95
MATRIX_RATE = 0.15
GAIN_RATE = 1.0
DECAY_WEIGHT = 0.1
CLIP = 1.0

LOW = jnp.bfloat16
WIDE = jnp.float32
VMEM = pltpu.VMEM
SMEM = pltpu.SMEM
MIB = 1024 * 1024


def dot(a, b):
    return jnp.dot(a, b, preferred_element_type=WIDE)


def dot_nt(a, b):
    return lax.dot_general(a, b, (((1,), (1,)), ((), ())), preferred_element_type=WIDE)


def dot_tn(a, b):
    return lax.dot_general(a, b, (((0,), (0,)), ((), ())), preferred_element_type=WIDE)


def params(size):
    return pltpu.CompilerParams(vmem_limit_bytes=size * MIB)


def cost(flops, moved):
    return pl.CostEstimate(flops=int(flops), bytes_accessed=int(moved), transcendentals=0)


def smem():
    return pl.BlockSpec(memory_space=SMEM)


def whole(shape):
    return pl.BlockSpec(shape, lambda *at: (0,) * len(shape), pipeline_mode=pl.Buffered(1))


def shape(dims, kind):
    return jax.ShapeDtypeStruct(dims, kind)


def bits_of(axis):
    return (lax.axis_size(axis) - 1).bit_length()


def exchange(value, axis, bit):
    size = lax.axis_size(axis)
    return lax.ppermute(value, axis, [(i, i ^ (1 << bit)) for i in range(size)])


def gather_shards(own, *others):
    held = [(0, own)]
    for bit in reversed(range(bits_of("shard"))):
        held += [
            (mask | (1 << bit), after(exchange(part, "shard", bit), *others)) for mask, part in held
        ]
    return [(mask, None, part) for mask, part in held]


def add_low(one, two):
    return (one.astype(WIDE) + two.astype(WIDE)).astype(LOW)


class Reduction:
    def __init__(self, keep, send, halved):
        self.keep = keep
        self.near = exchange(send, "shard", 0)
        self.halved = halved
        self.stage = 0

    def cross(self, *done):
        self.near = after(self.near, *done)
        low = add_low(self.keep[1], self.near[1])
        self.got = exchange(low, "shard", 1)
        self.terms = [self.keep[0], self.near[0]]
        return low

    def next(self, *done):
        got = after(self.got, *done)
        count = bits_of("dp")
        rows = got.shape[0]

        def total(at):
            return sum(term[at].astype(WIDE) for term in (*self.terms, got)).astype(LOW)

        bit = self.stage
        if self.stage < count:
            if bit in self.halved:
                sent = total(slice(rows // 2, rows))
                self.terms = [total(slice(0, rows // 2))]
            else:
                sent = total(slice(0, rows))
                self.terms = [sent]
        else:
            bit = self.halved[count - 1 - self.stage]
            if self.stage == count:
                sent = total(slice(0, rows))
            else:
                sent = jnp.concatenate([self.held, got])
            self.held = sent
        self.stage += 1
        self.got = exchange(sent, "dp", bit)
        return sent

    def left(self):
        return bits_of("dp") + len(self.halved) - self.stage

    def result(self):
        return self.held, self.got


class Passing:
    def __init__(self, local, reverse):
        self.local = local
        steps = [[(0, 1), (2, 3)], [(1, 2)], [(2, 3)]]
        if reverse:
            steps = [[(3 - a, 3 - b) for a, b in step] for step in steps]
        self.steps = steps
        self.got = [lax.ppermute(local, "shard", steps[0])]

    def turn(self, decay, length, *done):
        self.got[0] = after(self.got[0], *done)
        total = combine(decay, length, self.local, self.got[0])
        self.got.append(lax.ppermute(total, "shard", self.steps[1]))
        return total

    def finish(self, *done):
        self.got.append(lax.ppermute(after(self.got[1], *done), "shard", self.steps[2]))


def entering(decay, length, h, got):
    factor = jnp.exp(jnp.full((1, 1), decay[h] * length, WIDE))
    wide = [item[h].astype(WIDE) for item in got]
    return wide[0] + wide[1] + factor * wide[2]


def after(value, *others):
    return lax.optimization_barrier((value, *others))[0]


def combine_kernel(length, decay, local, got, out):
    h = pl.program_id(0) % H
    factor = jnp.exp(jnp.full((1, 1), decay[h] * length, WIDE))
    out[...] = (local[...].astype(WIDE) + factor * got[...].astype(WIDE)).astype(LOW)


def combine(decay, length, local, got):
    block = pl.BlockSpec((None, None, KD, VP), lambda i: (i // H, i % H, 0, 0))
    return pl.pallas_call(
        functools.partial(combine_kernel, length),
        grid=(local.shape[0] * H,),
        out_shape=shape(local.shape, LOW),
        in_specs=[smem(), block, block],
        out_specs=block,
        compiler_params=params(60),
        cost_estimate=cost(local.size, 6 * local.size),
    )(decay, local, got)


def assemble_kernel(plan, fills, sources_of, me_ref, side_ref, *refs):
    sources, outs = refs[: len(sources_of)], refs[len(sources_of) :]
    lanes = sources[0].shape[1]
    for index, row, size in fills:
        outs[index][row : row + size, :] = jnp.zeros((size, outs[index].shape[1]), LOW)

    def place(source, lane, low, high):
        for start, index, row, size in plan:
            begin, end = max(start, low), min(start + size, high)
            if begin < end:
                to = row + begin - start
                outs[index][to : to + end - begin, pl.ds(lane, lanes)] = source[
                    begin - low : end - low, :
                ]

    for (mask, half), source in zip(sources_of, sources):
        lane = pl.multiple_of(jnp.bitwise_xor(me_ref[0], mask) * lanes, lanes)
        rows = source.shape[0]
        if half is None:
            place(source, lane, 0, rows)
            continue
        for side in range(2):

            @pl.when(side_ref[0] == side)
            def _():
                low = (side ^ half) * rows
                place(source, lane, low, low + rows)


def assemble(held, plan, fills, heights, width, me, side):
    sources_of = [(mask, half) for mask, half, part in held]
    parts = [part for mask, half, part in held]
    return pl.pallas_call(
        functools.partial(assemble_kernel, plan, fills, sources_of),
        out_shape=[shape((rows, width), LOW) for rows in heights],
        in_specs=[smem()] * 2 + [pl.BlockSpec(memory_space=VMEM)] * len(parts),
        out_specs=[pl.BlockSpec(memory_space=VMEM)] * len(heights),
        compiler_params=params(20),
        cost_estimate=cost(0, 4 * sum(heights) * width),
    )(me, side, *parts)


def rotated(flat, cosine, sine):
    half = KD // 2
    parts = []
    for h in range(H):
        u = flat[:, h * KD : h * KD + half]
        w = flat[:, h * KD + half : (h + 1) * KD]
        parts += [u * cosine - w * sine, w * cosine + u * sine]
    return jnp.concatenate(parts, axis=1)


def column(size):
    return lax.broadcasted_iota(jnp.int32, (size, 1), 0).astype(WIDE)


def front_kernel(count, decay, seg_s, tok, w, gains, cos, sin, seg, *rest):
    hid, k, v, kv, out_state, state = rest
    seq = pl.program_id(0) // count
    c = pl.program_id(0) % count
    x = tok[...].astype(WIDE)
    r = lax.rsqrt(jnp.mean(x * x, axis=1, keepdims=True) + EPS)
    h1 = (x * r * gains[0:1, :].astype(WIDE)).astype(LOW)
    hid[...] = h1
    kd = H * KD
    key = rotated(dot_nt(h1, w[kd : 2 * kd, :]), cos[...], sin[...]).astype(LOW)
    k[...] = key
    val = dot_nt(h1, w[2 * kd :, :]).astype(LOW)
    v[...] = val
    first = seg_s[seq, c * BLOCK]
    last = seg_s[seq, c * BLOCK + BLOCK - 1]
    before = seg_s[seq, jnp.maximum(c * BLOCK - 1, 0)]
    here = (seg[...] == last).astype(WIDE)
    joined = jnp.logical_and(jnp.logical_and(first == last, first == before), c > 0)
    for h in range(H):
        a = decay[h]
        kw = jnp.exp(a * (BLOCK - 1.0 - column(BLOCK))) * here
        kk = (key[:, h * KD : (h + 1) * KD].astype(WIDE) * kw).astype(LOW)
        add = dot_tn(kk, val[:, h * VP : (h + 1) * VP])
        kv[h] = add
        factor = jnp.exp(jnp.full((1, 1), a * BLOCK, WIDE))
        total = jnp.where(joined, factor * state[h], 0.0) + add
        state[h] = total
        out_state[h] = total.astype(LOW)


def row_block(width):
    return pl.BlockSpec((BLOCK, width), lambda t: (t, 0))


def state_block(count, at=lambda c: c):
    return pl.BlockSpec(
        (None, None, H, KD, VP), lambda t: (t // count, at(t % count), 0, 0, 0)
    )


def seq_block(count):
    return pl.BlockSpec((None, H, KD, VP), lambda t: (t // count, 0, 0, 0))


def front(seqs, length, tokens, seg_col, segments, decay, w, gains, cos, sin):
    count = length // BLOCK
    rows, width = tokens.shape
    outs = [width, H * KD, H * VP]
    table = pl.BlockSpec((BLOCK, KD // 2), lambda t: (t % count, 0))
    return pl.pallas_call(
        functools.partial(front_kernel, count),
        grid=(seqs * count,),
        out_shape=[shape((rows, n), LOW) for n in outs]
        + [shape((seqs, count, H, KD, VP), WIDE), shape((seqs, H, KD, VP), LOW)],
        in_specs=[smem(), smem(), row_block(width), whole(w.shape), whole(gains.shape)]
        + [table, table, row_block(1)],
        out_specs=[row_block(n) for n in outs]
        + [state_block(count), seq_block(count)],
        scratch_shapes=[VMEM((H, KD, VP), WIDE)],
        compiler_params=params(60),
        cost_estimate=cost(2 * rows * width * w.shape[0], 12 * rows * width),
    )(decay, segments, tokens, w, gains, cos, sin, seg_col)


def decay_row(a):
    return jnp.exp(-a * lax.broadcasted_iota(jnp.int32, (1, BLOCK), 1).astype(WIDE))


def mixing(a, top, size, seg, seg_row):
    reach = top + size
    rows = jnp.exp(a * (column(size) + float(top)))
    same = seg[top:reach, :] == seg_row[:, :reach]
    n = lax.broadcasted_iota(jnp.int32, (size, reach), 0) + top
    m = lax.broadcasted_iota(jnp.int32, (size, reach), 1)
    return jnp.where(jnp.logical_and(same, n >= m), rows * decay_row(a)[:, :reach], 0.0)


TILE = 256


def inner_kernel(decay, k, v, hid, w, cos, sin, seg, seg_row, q, intra):
    query = rotated(dot_nt(hid[...], w[...]), cos[...], sin[...]).astype(LOW)
    q[...] = query
    for i in range(BLOCK // TILE):
        top, reach = i * TILE, (i + 1) * TILE
        for h in range(H):
            s = dot_nt(query[top:reach, h * KD : (h + 1) * KD], k[:reach, h * KD : (h + 1) * KD])
            weights = (s * mixing(decay[h], top, TILE, seg, seg_row)).astype(LOW)
            intra[top:reach, h * VP : (h + 1) * VP] = dot(
                weights, v[:reach, h * VP : (h + 1) * VP]
            ).astype(LOW)


def inner(k, v, hid, w, cos, sin, seg_col, seg_row, decay, length):
    rows, width = hid.shape
    count = length // BLOCK
    block = lambda n: pl.BlockSpec((BLOCK, n), lambda t: (t, 0))
    table = pl.BlockSpec((BLOCK, KD // 2), lambda t: (t % count, 0))
    return pl.pallas_call(
        inner_kernel,
        grid=(rows // BLOCK,),
        out_shape=[shape((rows, n), LOW) for n in (H * KD, H * VP)],
        in_specs=[
            smem(),
            block(H * KD),
            block(H * VP),
            block(width),
            pl.BlockSpec((H * KD, width), lambda t: (0, 0)),
            table,
            table,
            block(1),
            pl.BlockSpec((None, 1, BLOCK), lambda t: (t, 0, 0)),
        ],
        out_specs=[block(n) for n in (H * KD, H * VP)],
        compiler_params=params(60),
        cost_estimate=cost(rows * (2 * width * 512 + 2 * BLOCK * H * VP), 8 * rows * H * VP),
    )(decay, k, v, hid, w, cos, sin, seg_col, seg_row)


def gate_kernel(hid, w, gate):
    gate[...] = dot_nt(hid[...], w[...]).astype(LOW)


def gates(hid, w):
    rows, width = hid.shape
    vp = H * VP
    return pl.pallas_call(
        gate_kernel,
        grid=(rows // BLOCK,),
        out_shape=shape((rows, vp), LOW),
        in_specs=[row_block(width), pl.BlockSpec((vp, width), lambda t: (0, 0))],
        out_specs=row_block(vp),
        compiler_params=params(60),
        cost_estimate=cost(2 * rows * width * vp, 4 * rows * vp),
    )(hid, w)


CHUNK = 16


def interleaved(first, second):
    steps = [((i + 0.5) / len(first), 0, step) for i, step in enumerate(first)]
    steps += [((i + 0.5) / len(second), 1, step) for i, step in enumerate(second)]
    for place, which, step in sorted(steps, key=lambda item: item[:2]):
        step()


def pieces(width, size=256):
    return [(start, min(start + size, width)) for start in range(0, width, size)]


def across(narrow, width):
    return jnp.concatenate([narrow] * (width // 128), axis=1)


def middle_kernel(count, ff, decay, seg_s, in_last, *refs):
    (intra, gate, q, tok, cot, seg, w, gains, *got, kv) = refs[:12]
    outs, scratch = refs[12:24], refs[24:]
    (tok_out, hid2, prod, dgate, dup, mixed, glow, ggate, gret, st_out, dst, leave) = outs
    (state, now, queries, factors, ret_s, norm_s, silu_s, slope_s, inv_s, res_s, ff_s, low_s, sums) = scratch
    seq = pl.program_id(0) // count
    c = pl.program_id(0) % count
    start = c * BLOCK
    vp = H * VP
    width = tok.shape[1]
    before = jnp.where(c > 0, seg_s[seq, jnp.maximum(start - 1, 0)], in_last[seq])

    @pl.when(c == 0)
    def _():
        for h in range(H):
            total = entering(decay, count * BLOCK, h, got)
            state[h] = total
            now[h] = total.astype(LOW)

    for b in range(1, count):

        @pl.when(c == b)
        def _():
            prev = seg_s[seq, (b - 1) * BLOCK - 1] if b > 1 else in_last[seq]
            joined = jnp.logical_and(
                seg_s[seq, (b - 1) * BLOCK] == seg_s[seq, b * BLOCK - 1],
                seg_s[seq, (b - 1) * BLOCK] == prev,
            )
            for h in range(H):
                factor = jnp.exp(jnp.full((1, 1), decay[h] * BLOCK, WIDE))
                total = jnp.where(joined, factor * state[h], 0.0) + kv[h]
                state[h] = total
                now[h] = total.astype(LOW)

    st_out[...] = now[...]
    here = (seg[...] == before).astype(WIDE)
    for h in range(H):
        qw = jnp.exp(decay[h] * (column(BLOCK) + 1.0)) * here
        factors[h] = jnp.broadcast_to(qw, (BLOCK, 128))

    w_out = (vp, 2 * vp)
    w_gate = (2 * vp, 2 * vp + ff)
    w_up = (2 * vp + ff, 2 * vp + 2 * ff)
    w_down = (2 * vp + 2 * ff, 2 * vp + 3 * ff)
    gain = gains[1:2, :].astype(WIDE)

    def phases(top):
        rs = pl.ds(top, TILE)
        lists = []

        def add(steps):
            lists.append(steps)

        def chunks():
            return [pl.ds(row, CHUNK) for row in range(top, top + TILE, CHUNK)]

        def cross(h, lo, hi):
            ret_s[rs, h * VP + lo : h * VP + hi] = dot(
                q[rs, h * KD : (h + 1) * KD], now[h, :, lo:hi]
            )

        add([functools.partial(cross, h, *piece) for h in range(H) for piece in pieces(VP)])

        def gated(h, r):
            hv = slice(h * VP, (h + 1) * VP)
            hk = slice(h * KD, (h + 1) * KD)
            qw = factors[h, r, :]
            queries[r, hk] = (q[r, hk].astype(WIDE) * across(qw, KD)).astype(LOW)
            ret = intra[r, hv].astype(WIDE) + across(qw, VP) * ret_s[r, hv]
            mean = jnp.sum(ret, axis=1, keepdims=True) * (1.0 / VD)
            centered = ret - mean
            square = jnp.sum(centered * centered, axis=1, keepdims=True)
            var = (square - (VP - VD) * (mean * mean)) * (1.0 / VD)
            inv = lax.rsqrt(var + 1.0 * KD)
            nh = centered * inv
            g = gate[r, hv].astype(WIDE)
            sg = 0.5 * jnp.tanh(0.5 * g) + 0.5
            sl = g * sg
            mixed[r, hv] = (nh * sl).astype(LOW)
            norm_s[r, hv] = nh
            silu_s[r, hv] = sl
            slope_s[r, hv] = nh * (sg + sl * (1.0 - sg))
            inv_s[h, r, :] = jnp.broadcast_to(inv, (CHUNK, 128))

        add([functools.partial(gated, h, r) for r in chunks() for h in range(H)])

        def project(lo, hi):
            res_s[rs, lo:hi] = dot(mixed[rs, :], w[w_out[0] : w_out[1], lo:hi])

        add([functools.partial(project, *piece) for piece in pieces(width)])

        def norm(r):
            resid = tok[r, :].astype(WIDE) + res_s[r, :]
            r2 = lax.rsqrt(jnp.mean(resid * resid, axis=1, keepdims=True) + EPS)
            res_s[r, :] = resid
            hid2[r, :] = (resid * r2 * gain).astype(LOW)
            inv_s[H, r, :] = jnp.broadcast_to(r2, (CHUNK, 128))

        add([functools.partial(norm, r) for r in chunks()])

        def forward(place, source, at, lo, hi):
            ff_s[place, rs, lo:hi] = dot_nt(source[rs, :], w[at[0] + lo : at[0] + hi, :])

        add(
            [
                functools.partial(forward, place, source, at, *piece)
                for piece in pieces(ff)
                for place, source, at in ((0, hid2, w_gate), (1, hid2, w_up), (2, cot, w_down))
            ]
        )

        def gelu(r, lo, hi):
            gf, uf, gp = ff_s[0, r, lo:hi], ff_s[1, r, lo:hi], ff_s[2, r, lo:hi]
            e = jnp.exp(-0.5 * (gf * gf))
            d = 1.0 / (1.0 + (0.3275911 * math.sqrt(0.5)) * jnp.abs(gf))
            poly = d * (
                0.5 * 0.254829592
                + d
                * (
                    0.5 * -0.284496736
                    + d * (0.5 * 1.421413741 + d * (0.5 * -1.453152027 + d * (0.5 * 1.061405429)))
                )
            )
            tail = poly * e
            cdf = jnp.where(gf >= 0.0, 1.0 - tail, tail)
            ge = gf * cdf
            dge = cdf + gf * (e * (1.0 / math.sqrt(2.0 * math.pi)))
            prod[r, lo:hi] = (ge * uf).astype(LOW)
            dgate[r, lo:hi] = (gp * uf * dge).astype(LOW)
            dup[r, lo:hi] = (gp * ge).astype(LOW)

        add([functools.partial(gelu, r, *piece) for r in chunks() for piece in pieces(ff, 512)])

        def down(lo, hi):
            low_s[0, rs, lo:hi] = dot(prod[rs, :], w[w_down[0] : w_down[1], lo:hi])

        def hidden(lo, hi):
            low_s[1, rs, lo:hi] = dot(dgate[rs, :], w[w_gate[0] : w_gate[1], lo:hi]) + dot(
                dup[rs, :], w[w_up[0] : w_up[1], lo:hi]
            )

        add([functools.partial(step, *piece) for piece in pieces(width) for step in (down, hidden)])

        def residual(r):
            resid = res_s[r, :]
            r2 = across(inv_s[H, r, :], width)
            tok_out[r, :] = (resid + low_s[0, r, :]).astype(LOW)
            gh = low_s[1, r, :] * gain
            xhat = resid * r2
            inner_product = jnp.mean(gh * xhat, axis=1, keepdims=True)
            glow[r, :] = (cot[r, :].astype(WIDE) + r2 * (gh - xhat * inner_product)).astype(LOW)

        add([functools.partial(residual, r) for r in chunks()])

        def mix_back(lo, hi):
            ret_s[rs, lo:hi] = dot_nt(glow[rs, :], w[w_out[0] + lo : w_out[0] + hi, :])

        add([functools.partial(mix_back, *piece) for piece in pieces(vp)])

        def gated_back(h, r):
            hv = slice(h * VP, (h + 1) * VP)
            gm = ret_s[r, hv]
            nh = norm_s[r, hv]
            ggate[r, hv] = (gm * slope_s[r, hv]).astype(LOW)
            gn = gm * silu_s[r, hv]
            one = jnp.sum(gn, axis=1, keepdims=True) * (1.0 / VD)
            two = jnp.sum(gn * nh, axis=1, keepdims=True) * (1.0 / VD)
            gret[r, hv] = (across(inv_s[h, r, :], VP) * (gn - one - nh * two)).astype(LOW)

        add([functools.partial(gated_back, h, r) for r in chunks() for h in range(H)])
        return lists

    first, second = phases(0), phases(TILE)
    for k in range(len(first) + 1):
        interleaved(first[k] if k < len(first) else [], second[k - 1] if k else [])
    for h in range(H):
        add = dot_tn(queries[:, h * KD : (h + 1) * KD], gret[:, h * VP : (h + 1) * VP])
        dst[h] = add
        sums[c, h] = add

    @pl.when(c == count - 1)
    def _():
        for h in range(H):
            total = sums[count - 1, h]
            for b in reversed(range(count - 1)):
                prev = seg_s[seq, b * BLOCK - 1] if b > 0 else in_last[seq]
                joined = jnp.logical_and(
                    seg_s[seq, b * BLOCK] == seg_s[seq, (b + 1) * BLOCK - 1],
                    seg_s[seq, b * BLOCK] == prev,
                )
                factor = jnp.exp(jnp.full((1, 1), decay[h] * BLOCK, WIDE))
                total = jnp.where(joined, factor * total, 0.0) + sums[b, h]
            leave[h] = total.astype(LOW)


def middle(seqs, length, ff, data, seg_col, segments, in_last, decay, w, gains, got, kv):
    intra, gate, q, tokens, cotangent = data
    rows, width = tokens.shape
    count = length // BLOCK
    vp = H * VP
    outs = [width, width, ff, ff, ff, vp, width, vp, vp]
    inputs = [decay, segments, in_last, intra, gate, q, tokens, cotangent, seg_col, w, gains, *got, kv]
    specs = [smem()] * 3 + [row_block(n) for n in (vp, vp, H * KD, width, width, 1)]
    specs += [whole(w.shape), whole(gains.shape), *[seq_block(count)] * 3]
    specs += [state_block(count, lambda c: jnp.maximum(c - 1, 0))]
    one = (H, KD, VP)
    states = (seqs, count, *one)
    return pl.pallas_call(
        functools.partial(middle_kernel, count, ff),
        grid=(seqs * count,),
        out_shape=[shape((rows, n), LOW) for n in outs]
        + [shape(states, LOW), shape(states, WIDE), shape((seqs, *one), LOW)],
        in_specs=specs,
        out_specs=[row_block(n) for n in outs]
        + [state_block(count)] * 2
        + [seq_block(count)],
        scratch_shapes=[
            VMEM(one, WIDE),
            VMEM(one, LOW),
            VMEM((BLOCK, H * KD), LOW),
            VMEM((H, BLOCK, 128), WIDE),
            VMEM((BLOCK, vp), WIDE),
            VMEM((BLOCK, vp), WIDE),
            VMEM((BLOCK, vp), WIDE),
            VMEM((BLOCK, vp), WIDE),
            VMEM((H + 1, BLOCK, 128), WIDE),
            VMEM((BLOCK, width), WIDE),
            VMEM((3, BLOCK, ff), WIDE),
            VMEM((2, BLOCK, width), WIDE),
            VMEM(states[1:], WIDE),
        ],
        compiler_params=params(60),
        cost_estimate=cost(2 * rows * width * (2 * vp + 6 * ff), 30 * rows * width),
    )(*inputs)


def weight_kernel(plan, count, layout, me_ref, *refs):
    ins, ready, outs, total = refs[:count], refs[count:-3], refs[-3:-1], refs[-1]
    if layout is None:
        outs = refs[-2:-1]
    t = pl.program_id(0)
    last = pl.num_programs(0) - 1
    for left, right, cuts in plan:
        a, b = ins[left], ins[right]
        for source, row, size in cuts:
            add = dot_tn(a[:, source : source + size], b[...])

            @pl.when(t == 0)
            def _():
                total[row : row + size, :] = add

            @pl.when(t > 0)
            def _():
                total[row : row + size, :] += add

    @pl.when(t == last)
    def _():
        used = max(row + size for left, right, cuts in plan for source, row, size in cuts)
        if layout is None:
            outs[0][...] = total[...].astype(LOW)
            return
        for item in ready:
            total[used : used + item.shape[0], :] = item[...].astype(WIDE)
            used += item.shape[0]
        if used < total.shape[0]:
            total[used:, :] = jnp.zeros((total.shape[0] - used, total.shape[1]), WIDE)
        lanes = outs[0].shape[2]
        which, pieces = layout
        rows = outs[0].shape[1] // pieces
        for part in range(2 * outs[0].shape[0]):
            target = outs[part & 1]
            lane = pl.multiple_of(jnp.bitwise_xor(me_ref[0], part) * lanes, lanes)
            for q in range(pieces):
                row = pl.multiple_of(jnp.bitwise_xor(me_ref[which], q) * rows, 16)
                target[part >> 1, q * rows : (q + 1) * rows, :] = total[
                    pl.ds(row, rows), pl.ds(lane, lanes)
                ].astype(LOW)


def weight_grads(arrays, plan, place, shards=2, height=0, layout=None, ready=()):
    rows = arrays[0].shape[0]
    used = max(row + size for left, right, cuts in plan for source, row, size in cuts)
    width = arrays[plan[0][1]].shape[1]
    tile = 2 * BLOCK
    block = lambda n: pl.BlockSpec((tile, n), lambda t: (t, 0))
    dims = [(shards // 2, height, width // shards)] * 2
    if layout is None:
        height, dims = used, [(used, width)]
    full = lambda item: pl.BlockSpec(item, lambda t: (0,) * len(item))
    return pl.pallas_call(
        functools.partial(weight_kernel, plan, len(arrays), layout),
        grid=(rows // tile,),
        out_shape=[shape(item, LOW) for item in dims],
        in_specs=[smem()] + [block(item.shape[1]) for item in arrays]
        + [full(item.shape) for item in ready],
        out_specs=[full(item) for item in dims],
        scratch_shapes=[VMEM((height, width), WIDE)],
        compiler_params=params(48),
        cost_estimate=cost(2 * rows * used * width, 2 * rows * sum(i.shape[1] for i in arrays)),
    )(place, *arrays, *ready)


def back_kernel(count, decay, seg_s, in_last, *refs):
    (q, k, v, gret, cos, sin, seg, seg_row, st, dst, *got) = refs[:13]
    (dq, dk, dv, state, weights, grads) = refs[13:]
    seq = pl.program_id(0) // count
    c = count - 1 - pl.program_id(0) % count

    @pl.when(c == count - 1)
    def _():
        for h in range(H):
            state[h] = entering(decay, count * BLOCK, h, got)

    for b in range(1, count):

        @pl.when(c == b - 1)
        def _():
            prev = seg_s[seq, b * BLOCK - 1]
            first = seg_s[seq, b * BLOCK]
            last = seg_s[seq, (b + 1) * BLOCK - 1]
            joined = jnp.logical_and(first == last, first == prev)
            for h in range(H):
                factor = jnp.exp(jnp.full((1, 1), decay[h] * BLOCK, WIDE))
                state[h] = jnp.where(joined, factor * state[h], 0.0) + dst[h]

    start = c * BLOCK
    before = jnp.where(c > 0, seg_s[seq, jnp.maximum(start - 1, 0)], in_last[seq])
    final = seg_s[seq, start + BLOCK - 1]
    here = (seg[...] == before).astype(WIDE)
    ends = (seg[...] == final).astype(WIDE)
    place = column(BLOCK)
    dqs, dks = [], []
    for h in range(H):
        a = decay[h]
        qh = q[:, h * KD : (h + 1) * KD]
        kh = k[:, h * KD : (h + 1) * KD]
        vh = v[:, h * VP : (h + 1) * VP]
        gh = gret[:, h * VP : (h + 1) * VP]
        qw = jnp.exp(a * (place + 1.0)) * here
        kw = jnp.exp(a * (BLOCK - 1.0 - place)) * ends
        parts = []
        for i in range(BLOCK // TILE):
            top, reach = i * TILE, (i + 1) * TILE
            mix = mixing(a, top, TILE, seg, seg_row)
            s = dot_nt(qh[top:reach, :], kh[:reach, :])
            weights[top:reach, :reach] = (s * mix).astype(LOW)
            gs = (dot_nt(gh[top:reach, :], vh[:reach, :]) * mix).astype(LOW)
            grads[top:reach, :reach] = gs
            parts.append(dot(gs, kh[:reach, :]))
        late = state[h].astype(LOW)
        dqs.append(jnp.concatenate(parts) + qw * dot_nt(gh, st[h]))
        parts, values = [], []
        for i in range(BLOCK // TILE):
            top, reach = i * TILE, (i + 1) * TILE
            parts.append(dot_tn(grads[top:, top:reach], qh[top:, :]))
            values.append(dot_tn(weights[top:, top:reach], gh[top:, :]))
        dks.append(jnp.concatenate(parts) + kw * dot_nt(vh, late))
        dv[:, h * VP : (h + 1) * VP] = (jnp.concatenate(values) + kw * dot(kh, late)).astype(LOW)
    dq[...] = rotated(jnp.concatenate(dqs, axis=1), cos[...], -sin[...]).astype(LOW)
    dk[...] = rotated(jnp.concatenate(dks, axis=1), cos[...], -sin[...]).astype(LOW)


def back(seqs, length, data, cos, sin, seg_col, seg_row, segments, in_last, decay, st, dst, got):
    rows = data[0].shape[0]
    count = length // BLOCK
    turn = lambda t: (t // count) * count + count - 1 - t % count
    block = lambda n: pl.BlockSpec((BLOCK, n), lambda t: (turn(t), 0))
    table = pl.BlockSpec((BLOCK, KD // 2), lambda t: (count - 1 - t % count, 0))
    outs = [H * KD, H * KD, H * VP]
    inputs = [decay, segments, in_last, *data, cos, sin, seg_col, seg_row, st, dst, *got]
    specs = [smem()] * 3 + [block(item.shape[1]) for item in data] + [table, table, block(1)]
    specs += [pl.BlockSpec((None, 1, BLOCK), lambda t: (turn(t), 0, 0))]
    specs += [state_block(count, lambda c: count - 1 - c)]
    specs += [state_block(count, lambda c: jnp.minimum(count - c, count - 1))]
    specs += [seq_block(count)] * 3
    return pl.pallas_call(
        functools.partial(back_kernel, count),
        grid=(seqs * count,),
        out_shape=[shape((rows, n), LOW) for n in outs],
        in_specs=specs,
        out_specs=[block(n) for n in outs],
        scratch_shapes=[
            VMEM((H, KD, VP), WIDE),
            VMEM((BLOCK, BLOCK), LOW),
            VMEM((BLOCK, BLOCK), LOW),
        ],
        compiler_params=params(60),
        cost_estimate=cost(rows * H * 2 * BLOCK * 3 * (KD + VP), 16 * rows * H * VP),
    )(*inputs)


def input_kernel(dq, dk, dv, ggate, tok, glow, w, w_gate, gains, *rest):
    out = rest[-1]
    kd = H * KD
    gh = dot(dq[...], w[:kd, :]) + dot(dk[...], w[kd : 2 * kd, :])
    gh += dot(dv[...], w[2 * kd :, :]) + dot(ggate[...], w_gate[...])
    x = tok[...].astype(WIDE)
    r = lax.rsqrt(jnp.mean(x * x, axis=1, keepdims=True) + EPS)
    xhat = x * r
    gh = gh * gains[0:1, :].astype(WIDE)
    inner_product = jnp.mean(gh * xhat, axis=1, keepdims=True)
    out[...] = (glow[...].astype(WIDE) + r * (gh - xhat * inner_product)).astype(LOW)


def input_grad(first, steps, dq, dk, dv, ggate, tokens, glow, w, w_rest, gains, earlier):
    rows, width = tokens.shape
    parts = rows // BLOCK // steps
    arrays = [dq, dk, dv, ggate, tokens, glow]
    block = lambda item: pl.BlockSpec((BLOCK, item.shape[1]), lambda t: (first + t, 0))
    inputs = [*arrays, w, w_rest, gains]
    specs = [block(item) for item in arrays] + [whole(w.shape)]
    specs += [pl.BlockSpec((H * VP, width), lambda t: (0, 0)), whole(gains.shape)]
    aliases = {}
    if earlier is not None:
        aliases = {len(inputs): 0}
        inputs.append(earlier)
        specs.append(pl.BlockSpec(memory_space=pl.ANY))
    return pl.pallas_call(
        input_kernel,
        grid=(steps,),
        out_shape=shape((rows, width), LOW),
        in_specs=specs,
        out_specs=block(tokens),
        input_output_aliases=aliases,
        compiler_params=params(32),
        cost_estimate=cost(2 * rows * width * (w.shape[0] + H * VP) // parts, 20 * rows * width // parts),
    )(*inputs)


def adam_step(master, moment, second, grad, scale, rate, decay_weight):
    clipped = grad * scale
    moment_new = BETA_ONE * moment + (1.0 - BETA_ONE) * clipped
    second_new = BETA_TWO * second + (1.0 - BETA_TWO) * clipped * clipped
    corrected = (
        moment_new
        * (1.0 / (1.0 - BETA_ONE**STEP))
        / (jnp.sqrt(second_new * (1.0 / (1.0 - BETA_TWO**STEP))) + ADAM_EPS)
    )
    return (master - rate * (corrected + decay_weight * master), moment_new, second_new)


def squares_kernel(vd, ff, layouts, place, *refs):
    halves, (w_qk, w_vg, w_gu, low_gains) = refs[:4], refs[4:8]
    grad_gains, total, early, late = refs[8:]
    kd = H * KD
    for index, target in enumerate((early, late)):
        which, pieces = layouts[index]
        rows = target.shape[0] // pieces
        for q in range(pieces):
            row = pl.multiple_of(jnp.bitwise_xor(place[which], q) * rows, 16)
            source = halves[2 * index + q // (pieces // 2)]
            start = q % (pieces // 2) * rows
            target[pl.ds(row, rows), :] = source[start : start + rows, :]

    def rows(source, start, size):
        return source[start : start + size, :].astype(WIDE)

    def product(weight, grad):
        return jnp.sum(weight.astype(LOW).astype(WIDE) * grad, axis=0, keepdims=True)

    sums = []

    def square(item):
        sums.append(jnp.sum(item * item, axis=0, keepdims=True))
        return item

    first = jnp.zeros((1, low_gains.shape[1]), WIDE)
    for i in range(2):
        grad = square(rows(late, i * kd, kd))
        first += jnp.sum(w_qk[i].astype(LOW).astype(WIDE).T * grad, axis=0, keepdims=True)
    first += product(w_vg[0], square(rows(late, 2 * kd, vd)))
    first += product(w_vg[1], square(rows(early, vd, vd)))
    square(rows(early, 0, vd))
    square(rows(early, 2 * vd, ff))
    second = product(w_gu[0], square(rows(early, 2 * vd + ff, ff)))
    second += product(w_gu[1], square(rows(early, 2 * vd + 2 * ff, ff)))
    gains = jnp.concatenate([first, second]) / low_gains[...].astype(LOW).astype(WIDE)
    grad_gains[...] = gains
    sums.append(jnp.sum(gains * gains, axis=0, keepdims=True))
    total[...] = jnp.broadcast_to(jnp.sum(sum(sums), axis=1, keepdims=True), total.shape)


def squares(vd, ff, layouts, place, grads, w_qk, w_vg, w_gu, gains):
    halves = [half for pair in grads for half in pair]
    vmem = pl.BlockSpec(memory_space=VMEM)
    return pl.pallas_call(
        functools.partial(squares_kernel, vd, ff, layouts),
        out_shape=[shape(gains.shape, WIDE), shape((8, 128), WIDE)]
        + [shape((2 * pair[0].shape[0], pair[0].shape[1]), LOW) for pair in grads],
        in_specs=[smem()] + [vmem] * 8,
        out_specs=[vmem] * 4,
        compiler_params=params(20),
    )(place, *halves, w_qk, w_vg, w_gu, gains)


def update_kernel(vd, ff, *refs):
    totals, (early, late, gain_grads) = refs[:4], refs[4:7]
    sources, targets, norm_out = refs[7:25], refs[25:43], refs[43]
    ins, outs = refs[44:62], refs[62:80]
    arrived, sent = refs[80:]
    kd = H * KD
    order = [4, 3, 2, 1, 0, 5]
    places = [6 * group + place for place in order for group in range(3)]
    fetch = {i: pltpu.make_async_copy(sources[i], ins[i], arrived.at[i]) for i in places}
    send = {i: pltpu.make_async_copy(outs[i], targets[i], sent.at[i]) for i in places}
    for i in places:
        fetch[i].start()
    norm = jnp.sqrt((totals[0][...] + totals[1][...]) + (totals[2][...] + totals[3][...]))
    norm_out[0, 0] = jnp.max(norm)
    scale = jnp.minimum(1.0, CLIP / (norm + 1e-06))[0:1, 0:1]

    def step(place, at, grad, rate, decay_weight):
        results = adam_step(
            ins[place][at], ins[6 + place][at], ins[12 + place][at], grad, scale, rate, decay_weight
        )
        for group, result in enumerate(results):
            outs[6 * group + place][at] = result

    def rows(source, start, size):
        return source[start : start + size, :].astype(WIDE)

    grads = {
        4: [(..., lambda: rows(early, 2 * vd, ff))],
        3: [(i, lambda i=i: rows(early, 2 * vd + (1 + i) * ff, ff)) for i in range(2)],
        2: [(..., lambda: rows(early, 0, vd))],
        1: [(0, lambda: rows(late, 2 * kd, vd)), (1, lambda: rows(early, vd, vd))],
        0: [(i, lambda i=i: rows(late, i * kd, kd).T) for i in range(2)],
        5: [(..., lambda: gain_grads[...])],
    }
    for place in order:
        for group in range(3):
            fetch[6 * group + place].wait()
        rate, decay_weight = (GAIN_RATE, 0.0) if place == 5 else (MATRIX_RATE, DECAY_WEIGHT)
        for at, grad in grads[place]:
            step(place, at, grad(), rate, decay_weight)
        for group in range(3):
            send[6 * group + place].start()
    for i in places:
        send[i].wait()


def update(vd, ff, totals, grads, gain_grads, arrays):
    anywhere = pl.BlockSpec(memory_space=pl.ANY)
    return pl.pallas_call(
        functools.partial(update_kernel, vd, ff),
        out_shape=[shape(item.shape, WIDE) for item in arrays] + [shape((1, 1), WIDE)],
        in_specs=[pl.BlockSpec(memory_space=VMEM)] * 7 + [anywhere] * 18,
        out_specs=[anywhere] * 18 + [smem()],
        scratch_shapes=[VMEM(item.shape, WIDE) for item in arrays] * 2
        + [pltpu.SemaphoreType.DMA((18,))] * 2,
        compiler_params=params(40),
    )(*totals, *grads, gain_grads, *arrays)


def on_device(
    tokens,
    cotangent,
    segments,
    log_decay,
    w_qk,
    w_vg,
    w_out,
    w_gu,
    w_down,
    norm_gains,
    *states,
):
    turned = lambda item: jnp.swapaxes(item, 1, 2)
    shards = lax.axis_size("shard")
    me = lax.axis_index("shard").reshape(1)
    replica = lax.axis_index("dp")
    count = bits_of("dp")
    halved = (tuple(range(count - 1)),) * 2
    numbers = [
        sum(((replica >> bit) & 1) << (len(bits) - 1 - i) for i, bit in enumerate(bits))
        for bits in halved
    ]
    layouts = [(1 + i, 2 ** len(bits)) for i, bits in enumerate(halved)]
    place = jnp.concatenate([me, jnp.stack(numbers)])
    seqs, length, width = tokens.shape
    rows = seqs * length
    kd, vd, ff = H * KD, H * VD, w_down.shape[0]
    vp = H * VP
    vg_t, gu_t = turned(w_vg), turned(w_gu)

    low = lambda item: item.astype(LOW)
    def heads(item):
        return [
            jnp.pad(item[h * VD : (h + 1) * VD], ((0, VP - VD), (0, 0))) for h in range(H)
        ]

    first = jnp.concatenate(
        [
            low(w_qk[0]).T,
            low(w_qk[1]).T,
            low(vg_t[0]),
            jnp.pad(low(norm_gains), ((0, 14), (0, 0))),
        ]
    )
    rest = jnp.concatenate(
        [*heads(low(vg_t[1])), *heads(low(w_out)), low(gu_t[0]), low(gu_t[1]), low(w_down)]
    )
    side = (lax.axis_index("dp") & 1).reshape(1)

    half_width = KD // 2
    freq_rates = jnp.exp(-math.log(10000.0) * jnp.arange(half_width).astype(WIDE) / half_width)
    positions = (lax.axis_index("shard") * length + jnp.arange(length)).astype(WIDE)
    angles = positions[:, None] * freq_rates[None, :]
    cos, sin = jnp.cos(angles), jnp.sin(angles)

    tok = tokens.reshape(rows, width)
    cot = cotangent.reshape(rows, width)
    seg_col = segments.reshape(rows, 1)
    seg_row = segments.reshape(rows // BLOCK, 1, BLOCK)
    in_last = jnp.where(lax.axis_index("shard") > 0, segments[:, 0], -1)
    first_held = gather_shards(first, cos, sin, seg_col, seg_row, in_last, place)
    rest = after(rest, first_held[1][2])
    w_rest = lax.all_gather(rest, "shard", axis=1, tiled=True)
    decay = log_decay

    def tick(*done):
        nonlocal decay, place, gains
        decay, place, gains = lax.optimization_barrier((decay, place, gains, *done))[:3]

    plan = [(0, 0, 0, 2 * kd)] + [(2 * kd + h * VD, 0, 2 * kd + h * VP, VD) for h in range(H)]
    plan += [(2 * kd + vd, 1, 0, 16)]
    fills = [(0, 2 * kd + h * VP + VD, VP - VD) for h in range(H)]
    w_qkv, gains = assemble(first_held, plan, fills, [2 * kd + vp, 16], width, me, side)
    tick(rest)
    hid, k, v, kv, leaving = front(
        seqs, length, tok, seg_col, segments, decay, w_qkv, gains, cos, sin
    )
    passing = Passing(leaving, False)
    tick(leaving)
    tick(passing.turn(decay, length, leaving))
    q, intra = inner(k, v, hid, w_qkv, cos, sin, seg_col, seg_row, decay, length)
    tick(q)
    passing.finish(q)
    gate = gates(after(hid, passing.got[1], q), w_rest)
    tick(gate)
    tokens_out, hid2, prod, dgate, dup, mixed, glow, ggate, gret, st, dst, leaving = middle(
        seqs, length, ff, (intra, gate, q, tok, cot), seg_col, segments, in_last, decay,
        w_rest, gains, passing.got, kv,
    )
    returning = Passing(leaving, True)
    tick(leaving)

    def halves(row):
        return [(h * VP, row + h * VD, VD) for h in range(H)]

    fit = lambda used, layout: used + -used % (16 * layout[1])
    plan = [(0, 1, [(0, 0, ff)]), (2, 3, [(0, ff, ff)]), (4, 3, [(0, 2 * ff, ff)])]
    (made,) = weight_grads([prod, cot, dgate, hid2, dup], plan, place)
    tick(made)
    tick(returning.turn(decay, length, made))
    plan = [(0, 1, halves(0)), (2, 3, halves(vd))]
    made = weight_grads(
        [mixed, glow, ggate, hid], plan, place, shards,
        fit(2 * vd + 3 * ff, layouts[0]), layouts[0], (made,),
    )
    tick(made[0])
    returning.finish(made[0])
    early = Reduction(made[0], after(made[1], returning.got[1]), halved[0])
    tick(early.cross(made[0]))
    dq, dk, dv = back(
        seqs, length, (q, k, v, gret), cos, sin, seg_col, seg_row, segments, in_last, decay,
        st, dst, returning.got,
    )
    tick(dq)
    tick(early.next(dq))
    plan = [(0, 3, [(0, 0, kd)]), (1, 3, [(0, kd, kd)]), (2, 3, halves(2 * kd))]
    made = weight_grads(
        [dq, dk, dv, hid], plan, place, shards, fit(2 * kd + vd, layouts[1]), layouts[1]
    )
    late = Reduction(*made, halved[1])
    tick(made[0])
    tick(early.next(made[0]))
    tick(late.cross(made[0]))
    blocks = rows // BLOCK
    data = (dq, dk, dv, ggate, tok, glow, w_qkv, w_rest)
    grad_input = None
    for part in range(2):
        grad_input = input_grad(part * blocks // 2, blocks // 2, *data, gains, grad_input)
        tick(grad_input)
        tick((early, late)[part].next(grad_input))
    while early.left() or late.left():
        for item in (early, late):
            if item.left():
                item.next()

    gain_grads, total, *grads = squares(
        vd, ff, layouts, place, [early.result(), late.result()], w_qk, vg_t, gu_t, norm_gains
    )
    others = [
        lax.ppermute(total, "shard", [(i, i ^ mask) for i in range(shards)]) for mask in (1, 2, 3)
    ]
    arrays = []
    for group in ((w_qk, w_vg, w_out, w_gu, w_down, norm_gains), states[:6], states[6:]):
        arrays += [turned(item) if i in (1, 3) else item for i, item in enumerate(group)]
    *results, norm = update(vd, ff, [total, *others], grads, gain_grads, arrays)
    results = [turned(item) if i % 6 in (1, 3) else item for i, item in enumerate(results)]
    return (
        tokens_out.reshape(tokens.shape),
        grad_input.reshape(tokens.shape),
        *results,
        norm.reshape(()),
    )


def solution(mesh):
    split = P("dp", "shard", None)
    rows, columns = P(None, "shard", None), P(None, "shard")
    group = (rows, rows, columns, rows, columns, columns)
    in_specs = (split, split, P("dp", "shard"), P()) + group * 3
    out_specs = (split, split) + group * 3 + (P(),)
    return jax.shard_map(
        on_device, mesh=mesh, in_specs=in_specs, out_specs=out_specs, check_vma=False
    )
```

```python
import functools
import math

import jax
import jax.numpy as jnp
from jax import lax
from jax.experimental import pallas as pl
from jax.experimental.pallas import tpu as pltpu
from jax.sharding import PartitionSpec as P

H = 2
KD = 256
VD = 432
VP = 512
BLOCK = 512
STEP = 10

EPS = 1e-05
ADAM_EPS = 1e-08
BETA_ONE = 0.9
BETA_TWO = 0.95
MATRIX_RATE = 0.15
GAIN_RATE = 1.0
DECAY_WEIGHT = 0.1
CLIP = 1.0

LOW = jnp.bfloat16
WIDE = jnp.float32
VMEM = pltpu.VMEM
SMEM = pltpu.SMEM
MIB = 1024 * 1024


def dot(a, b):
    return jnp.dot(a, b, preferred_element_type=WIDE)


def dot_nt(a, b):
    return lax.dot_general(a, b, (((1,), (1,)), ((), ())), preferred_element_type=WIDE)


def dot_tn(a, b):
    return lax.dot_general(a, b, (((0,), (0,)), ((), ())), preferred_element_type=WIDE)


def params(size):
    return pltpu.CompilerParams(vmem_limit_bytes=size * MIB)


def cost(flops, moved):
    return pl.CostEstimate(flops=int(flops), bytes_accessed=int(moved), transcendentals=0)


def smem():
    return pl.BlockSpec(memory_space=SMEM)


def whole(shape):
    return pl.BlockSpec(shape, lambda *at: (0,) * len(shape), pipeline_mode=pl.Buffered(1))


def shape(dims, kind):
    return jax.ShapeDtypeStruct(dims, kind)


def bits_of(axis):
    return (lax.axis_size(axis) - 1).bit_length()


def exchange(value, axis, bit):
    size = lax.axis_size(axis)
    return lax.ppermute(value, axis, [(i, i ^ (1 << bit)) for i in range(size)])


def gather_shards(own, *others):
    held = [(0, own)]
    for bit in reversed(range(bits_of("shard"))):
        held += [
            (mask | (1 << bit), after(exchange(part, "shard", bit), *others)) for mask, part in held
        ]
    return [(mask, None, part) for mask, part in held]


def add_low(one, two):
    return (one.astype(WIDE) + two.astype(WIDE)).astype(LOW)


class Reduction:
    def __init__(self, keep, send, halved):
        self.keep = keep
        self.near = exchange(send, "shard", 0)
        self.halved = halved
        self.stage = 0

    def cross(self, *done):
        self.near = after(self.near, *done)
        low = add_low(self.keep[1], self.near[1])
        self.got = exchange(low, "shard", 1)
        self.terms = [self.keep[0], self.near[0]]
        return low

    def next(self, *done):
        got = after(self.got, *done)
        count = bits_of("dp")
        rows = got.shape[0]

        def total(at):
            return sum(term[at].astype(WIDE) for term in (*self.terms, got)).astype(LOW)

        bit = self.stage
        if self.stage < count:
            if bit in self.halved:
                sent = total(slice(rows // 2, rows))
                self.terms = [total(slice(0, rows // 2))]
            else:
                sent = total(slice(0, rows))
                self.terms = [sent]
        else:
            bit = self.halved[count - 1 - self.stage]
            if self.stage == count:
                sent = total(slice(0, rows))
            else:
                sent = jnp.concatenate([self.held, got])
            self.held = sent
        self.stage += 1
        self.got = exchange(sent, "dp", bit)
        return sent

    def left(self):
        return bits_of("dp") + len(self.halved) - self.stage

    def result(self):
        return self.held, self.got


class Passing:
    def __init__(self, local, reverse):
        self.local = local
        steps = [[(0, 1), (2, 3)], [(1, 2)], [(2, 3)]]
        if reverse:
            steps = [[(3 - a, 3 - b) for a, b in step] for step in steps]
        self.steps = steps
        self.got = [lax.ppermute(local, "shard", steps[0])]

    def turn(self, decay, length, *done):
        self.got[0] = after(self.got[0], *done)
        total = combine(decay, length, self.local, self.got[0])
        self.got.append(lax.ppermute(total, "shard", self.steps[1]))
        return total

    def finish(self, *done):
        self.got.append(lax.ppermute(after(self.got[1], *done), "shard", self.steps[2]))


def entering(decay, length, h, got):
    factor = jnp.exp(jnp.full((1, 1), decay[h] * length, WIDE))
    wide = [item[h].astype(WIDE) for item in got]
    return wide[0] + wide[1] + factor * wide[2]


def after(value, *others):
    return lax.optimization_barrier((value, *others))[0]


def combine_kernel(length, decay, local, got, out):
    h = pl.program_id(0) % H
    factor = jnp.exp(jnp.full((1, 1), decay[h] * length, WIDE))
    out[...] = (local[...].astype(WIDE) + factor * got[...].astype(WIDE)).astype(LOW)


def combine(decay, length, local, got):
    block = pl.BlockSpec((None, None, KD, VP), lambda i: (i // H, i % H, 0, 0))
    return pl.pallas_call(
        functools.partial(combine_kernel, length),
        grid=(local.shape[0] * H,),
        out_shape=shape(local.shape, LOW),
        in_specs=[smem(), block, block],
        out_specs=block,
        compiler_params=params(60),
        cost_estimate=cost(local.size, 6 * local.size),
    )(decay, local, got)


def assemble_kernel(plan, fills, sources_of, me_ref, side_ref, *refs):
    sources, outs = refs[: len(sources_of)], refs[len(sources_of) :]
    lanes = sources[0].shape[1]
    for index, row, size in fills:
        outs[index][row : row + size, :] = jnp.zeros((size, outs[index].shape[1]), LOW)

    def place(source, lane, low, high):
        for start, index, row, size in plan:
            begin, end = max(start, low), min(start + size, high)
            if begin < end:
                to = row + begin - start
                outs[index][to : to + end - begin, pl.ds(lane, lanes)] = source[
                    begin - low : end - low, :
                ]

    for (mask, half), source in zip(sources_of, sources):
        lane = pl.multiple_of(jnp.bitwise_xor(me_ref[0], mask) * lanes, lanes)
        rows = source.shape[0]
        if half is None:
            place(source, lane, 0, rows)
            continue
        for side in range(2):

            @pl.when(side_ref[0] == side)
            def _():
                low = (side ^ half) * rows
                place(source, lane, low, low + rows)


def assemble(held, plan, fills, heights, width, me, side):
    sources_of = [(mask, half) for mask, half, part in held]
    parts = [part for mask, half, part in held]
    return pl.pallas_call(
        functools.partial(assemble_kernel, plan, fills, sources_of),
        out_shape=[shape((rows, width), LOW) for rows in heights],
        in_specs=[smem()] * 2 + [pl.BlockSpec(memory_space=VMEM)] * len(parts),
        out_specs=[pl.BlockSpec(memory_space=VMEM)] * len(heights),
        compiler_params=params(20),
        cost_estimate=cost(0, 4 * sum(heights) * width),
    )(me, side, *parts)


def rotated(flat, cosine, sine):
    half = KD // 2
    parts = []
    for h in range(H):
        u = flat[:, h * KD : h * KD + half]
        w = flat[:, h * KD + half : (h + 1) * KD]
        parts += [u * cosine - w * sine, w * cosine + u * sine]
    return jnp.concatenate(parts, axis=1)


def column(size):
    return lax.broadcasted_iota(jnp.int32, (size, 1), 0).astype(WIDE)


def front_kernel(count, decay, seg_s, tok, w, gains, cos, sin, seg, *rest):
    hid, k, v, kv, out_state, state = rest
    seq = pl.program_id(0) // count
    c = pl.program_id(0) % count
    x = tok[...].astype(WIDE)
    r = lax.rsqrt(jnp.mean(x * x, axis=1, keepdims=True) + EPS)
    h1 = (x * r * gains[0:1, :].astype(WIDE)).astype(LOW)
    hid[...] = h1
    kd = H * KD
    key = rotated(dot_nt(h1, w[kd : 2 * kd, :]), cos[...], sin[...]).astype(LOW)
    k[...] = key
    val = dot_nt(h1, w[2 * kd :, :]).astype(LOW)
    v[...] = val
    first = seg_s[seq, c * BLOCK]
    last = seg_s[seq, c * BLOCK + BLOCK - 1]
    before = seg_s[seq, jnp.maximum(c * BLOCK - 1, 0)]
    here = (seg[...] == last).astype(WIDE)
    joined = jnp.logical_and(jnp.logical_and(first == last, first == before), c > 0)
    for h in range(H):
        a = decay[h]
        kw = jnp.exp(a * (BLOCK - 1.0 - column(BLOCK))) * here
        kk = (key[:, h * KD : (h + 1) * KD].astype(WIDE) * kw).astype(LOW)
        add = dot_tn(kk, val[:, h * VP : (h + 1) * VP])
        kv[h] = add
        factor = jnp.exp(jnp.full((1, 1), a * BLOCK, WIDE))
        total = jnp.where(joined, factor * state[h], 0.0) + add
        state[h] = total
        out_state[h] = total.astype(LOW)


def row_block(width):
    return pl.BlockSpec((BLOCK, width), lambda t: (t, 0))


def state_block(count, at=lambda c: c):
    return pl.BlockSpec(
        (None, None, H, KD, VP), lambda t: (t // count, at(t % count), 0, 0, 0)
    )


def seq_block(count):
    return pl.BlockSpec((None, H, KD, VP), lambda t: (t // count, 0, 0, 0))


def front(seqs, length, tokens, seg_col, segments, decay, w, gains, cos, sin):
    count = length // BLOCK
    rows, width = tokens.shape
    outs = [width, H * KD, H * VP]
    table = pl.BlockSpec((BLOCK, KD // 2), lambda t: (t % count, 0))
    return pl.pallas_call(
        functools.partial(front_kernel, count),
        grid=(seqs * count,),
        out_shape=[shape((rows, n), LOW) for n in outs]
        + [shape((seqs, count, H, KD, VP), WIDE), shape((seqs, H, KD, VP), LOW)],
        in_specs=[smem(), smem(), row_block(width), whole(w.shape), whole(gains.shape)]
        + [table, table, row_block(1)],
        out_specs=[row_block(n) for n in outs]
        + [state_block(count), seq_block(count)],
        scratch_shapes=[VMEM((H, KD, VP), WIDE)],
        compiler_params=params(60),
        cost_estimate=cost(2 * rows * width * w.shape[0], 12 * rows * width),
    )(decay, segments, tokens, w, gains, cos, sin, seg_col)


def decay_row(a):
    return jnp.exp(-a * lax.broadcasted_iota(jnp.int32, (1, BLOCK), 1).astype(WIDE))


def mixing(a, top, size, seg, seg_row):
    reach = top + size
    rows = jnp.exp(a * (column(size) + float(top)))
    same = seg[top:reach, :] == seg_row[:, :reach]
    n = lax.broadcasted_iota(jnp.int32, (size, reach), 0) + top
    m = lax.broadcasted_iota(jnp.int32, (size, reach), 1)
    return jnp.where(jnp.logical_and(same, n >= m), rows * decay_row(a)[:, :reach], 0.0)


TILE = 256


def inner_kernel(decay, k, v, hid, w, cos, sin, seg, seg_row, q, intra):
    query = rotated(dot_nt(hid[...], w[...]), cos[...], sin[...]).astype(LOW)
    q[...] = query
    for i in range(BLOCK // TILE):
        top, reach = i * TILE, (i + 1) * TILE
        for h in range(H):
            s = dot_nt(query[top:reach, h * KD : (h + 1) * KD], k[:reach, h * KD : (h + 1) * KD])
            weights = (s * mixing(decay[h], top, TILE, seg, seg_row)).astype(LOW)
            intra[top:reach, h * VP : (h + 1) * VP] = dot(
                weights, v[:reach, h * VP : (h + 1) * VP]
            ).astype(LOW)


def inner(k, v, hid, w, cos, sin, seg_col, seg_row, decay, length):
    rows, width = hid.shape
    count = length // BLOCK
    block = lambda n: pl.BlockSpec((BLOCK, n), lambda t: (t, 0))
    table = pl.BlockSpec((BLOCK, KD // 2), lambda t: (t % count, 0))
    return pl.pallas_call(
        inner_kernel,
        grid=(rows // BLOCK,),
        out_shape=[shape((rows, n), LOW) for n in (H * KD, H * VP)],
        in_specs=[
            smem(),
            block(H * KD),
            block(H * VP),
            block(width),
            pl.BlockSpec((H * KD, width), lambda t: (0, 0)),
            table,
            table,
            block(1),
            pl.BlockSpec((None, 1, BLOCK), lambda t: (t, 0, 0)),
        ],
        out_specs=[block(n) for n in (H * KD, H * VP)],
        compiler_params=params(60),
        cost_estimate=cost(rows * (2 * width * 512 + 2 * BLOCK * H * VP), 8 * rows * H * VP),
    )(decay, k, v, hid, w, cos, sin, seg_col, seg_row)


def gate_kernel(hid, w, gate):
    gate[...] = dot_nt(hid[...], w[...]).astype(LOW)


def gates(hid, w):
    rows, width = hid.shape
    vp = H * VP
    return pl.pallas_call(
        gate_kernel,
        grid=(rows // BLOCK,),
        out_shape=shape((rows, vp), LOW),
        in_specs=[row_block(width), pl.BlockSpec((vp, width), lambda t: (0, 0))],
        out_specs=row_block(vp),
        compiler_params=params(60),
        cost_estimate=cost(2 * rows * width * vp, 4 * rows * vp),
    )(hid, w)


CHUNK = 16


def interleaved(first, second):
    steps = [((i + 0.5) / len(first), 0, step) for i, step in enumerate(first)]
    steps += [((i + 0.5) / len(second), 1, step) for i, step in enumerate(second)]
    for place, which, step in sorted(steps, key=lambda item: item[:2]):
        step()


def pieces(width, size=256):
    return [(start, min(start + size, width)) for start in range(0, width, size)]


def across(narrow, width):
    return jnp.concatenate([narrow] * (width // 128), axis=1)


def middle_kernel(count, ff, decay, seg_s, in_last, *refs):
    (intra, gate, q, tok, cot, seg, w, gains, *got, kv) = refs[:12]
    outs, scratch = refs[12:24], refs[24:]
    (tok_out, hid2, prod, dgate, dup, mixed, glow, ggate, gret, st_out, dst, leave) = outs
    (state, now, queries, factors, ret_s, norm_s, silu_s, slope_s, inv_s, res_s, ff_s, low_s, sums) = scratch
    seq = pl.program_id(0) // count
    c = pl.program_id(0) % count
    start = c * BLOCK
    vp = H * VP
    width = tok.shape[1]
    before = jnp.where(c > 0, seg_s[seq, jnp.maximum(start - 1, 0)], in_last[seq])

    @pl.when(c == 0)
    def _():
        for h in range(H):
            total = entering(decay, count * BLOCK, h, got)
            state[h] = total
            now[h] = total.astype(LOW)

    for b in range(1, count):

        @pl.when(c == b)
        def _():
            prev = seg_s[seq, (b - 1) * BLOCK - 1] if b > 1 else in_last[seq]
            joined = jnp.logical_and(
                seg_s[seq, (b - 1) * BLOCK] == seg_s[seq, b * BLOCK - 1],
                seg_s[seq, (b - 1) * BLOCK] == prev,
            )
            for h in range(H):
                factor = jnp.exp(jnp.full((1, 1), decay[h] * BLOCK, WIDE))
                total = jnp.where(joined, factor * state[h], 0.0) + kv[h]
                state[h] = total
                now[h] = total.astype(LOW)

    st_out[...] = now[...]
    here = (seg[...] == before).astype(WIDE)
    for h in range(H):
        qw = jnp.exp(decay[h] * (column(BLOCK) + 1.0)) * here
        factors[h] = jnp.broadcast_to(qw, (BLOCK, 128))

    w_out = (vp, 2 * vp)
    w_gate = (2 * vp, 2 * vp + ff)
    w_up = (2 * vp + ff, 2 * vp + 2 * ff)
    w_down = (2 * vp + 2 * ff, 2 * vp + 3 * ff)
    gain = gains[1:2, :].astype(WIDE)

    def phases(top):
        rs = pl.ds(top, TILE)
        lists = []

        def add(steps):
            lists.append(steps)

        def chunks():
            return [pl.ds(row, CHUNK) for row in range(top, top + TILE, CHUNK)]

        def cross(h, lo, hi):
            ret_s[rs, h * VP + lo : h * VP + hi] = dot(
                q[rs, h * KD : (h + 1) * KD], now[h, :, lo:hi]
            )

        add([functools.partial(cross, h, *piece) for h in range(H) for piece in pieces(VP)])

        def gated(h, r):
            hv = slice(h * VP, (h + 1) * VP)
            hk = slice(h * KD, (h + 1) * KD)
            qw = factors[h, r, :]
            queries[r, hk] = (q[r, hk].astype(WIDE) * across(qw, KD)).astype(LOW)
            ret = intra[r, hv].astype(WIDE) + across(qw, VP) * ret_s[r, hv]
            mean = jnp.sum(ret, axis=1, keepdims=True) * (1.0 / VD)
            centered = ret - mean
            square = jnp.sum(centered * centered, axis=1, keepdims=True)
            var = (square - (VP - VD) * (mean * mean)) * (1.0 / VD)
            inv = lax.rsqrt(var + 1.0 * KD)
            nh = centered * inv
            g = gate[r, hv].astype(WIDE)
            sg = 0.5 * jnp.tanh(0.5 * g) + 0.5
            sl = g * sg
            mixed[r, hv] = (nh * sl).astype(LOW)
            norm_s[r, hv] = nh
            silu_s[r, hv] = sl
            slope_s[r, hv] = nh * (sg + sl * (1.0 - sg))
            inv_s[h, r, :] = jnp.broadcast_to(inv, (CHUNK, 128))

        add([functools.partial(gated, h, r) for r in chunks() for h in range(H)])

        def project(lo, hi):
            res_s[rs, lo:hi] = dot(mixed[rs, :], w[w_out[0] : w_out[1], lo:hi])

        add([functools.partial(project, *piece) for piece in pieces(width)])

        def norm(r):
            resid = tok[r, :].astype(WIDE) + res_s[r, :]
            r2 = lax.rsqrt(jnp.mean(resid * resid, axis=1, keepdims=True) + EPS)
            res_s[r, :] = resid
            hid2[r, :] = (resid * r2 * gain).astype(LOW)
            inv_s[H, r, :] = jnp.broadcast_to(r2, (CHUNK, 128))

        add([functools.partial(norm, r) for r in chunks()])

        def forward(place, source, at, lo, hi):
            ff_s[place, rs, lo:hi] = dot_nt(source[rs, :], w[at[0] + lo : at[0] + hi, :])

        add(
            [
                functools.partial(forward, place, source, at, *piece)
                for piece in pieces(ff)
                for place, source, at in ((0, hid2, w_gate), (1, hid2, w_up), (2, cot, w_down))
            ]
        )

        def gelu(r, lo, hi):
            gf, uf, gp = ff_s[0, r, lo:hi], ff_s[1, r, lo:hi], ff_s[2, r, lo:hi]
            e = jnp.exp(-0.5 * (gf * gf))
            d = 1.0 / (1.0 + (0.3275911 * math.sqrt(0.5)) * jnp.abs(gf))
            poly = d * (
                0.5 * 0.254829592
                + d
                * (
                    0.5 * -0.284496736
                    + d * (0.5 * 1.421413741 + d * (0.5 * -1.453152027 + d * (0.5 * 1.061405429)))
                )
            )
            tail = poly * e
            cdf = jnp.where(gf >= 0.0, 1.0 - tail, tail)
            ge = gf * cdf
            dge = cdf + gf * (e * (1.0 / math.sqrt(2.0 * math.pi)))
            prod[r, lo:hi] = (ge * uf).astype(LOW)
            dgate[r, lo:hi] = (gp * uf * dge).astype(LOW)
            dup[r, lo:hi] = (gp * ge).astype(LOW)

        add([functools.partial(gelu, r, *piece) for r in chunks() for piece in pieces(ff, 512)])

        def down(lo, hi):
            low_s[0, rs, lo:hi] = dot(prod[rs, :], w[w_down[0] : w_down[1], lo:hi])

        def hidden(lo, hi):
            low_s[1, rs, lo:hi] = dot(dgate[rs, :], w[w_gate[0] : w_gate[1], lo:hi]) + dot(
                dup[rs, :], w[w_up[0] : w_up[1], lo:hi]
            )

        add([functools.partial(step, *piece) for piece in pieces(width) for step in (down, hidden)])

        def residual(r):
            resid = res_s[r, :]
            r2 = across(inv_s[H, r, :], width)
            tok_out[r, :] = (resid + low_s[0, r, :]).astype(LOW)
            gh = low_s[1, r, :] * gain
            xhat = resid * r2
            inner_product = jnp.mean(gh * xhat, axis=1, keepdims=True)
            glow[r, :] = (cot[r, :].astype(WIDE) + r2 * (gh - xhat * inner_product)).astype(LOW)

        add([functools.partial(residual, r) for r in chunks()])

        def mix_back(lo, hi):
            ret_s[rs, lo:hi] = dot_nt(glow[rs, :], w[w_out[0] + lo : w_out[0] + hi, :])

        add([functools.partial(mix_back, *piece) for piece in pieces(vp)])

        def gated_back(h, r):
            hv = slice(h * VP, (h + 1) * VP)
            gm = ret_s[r, hv]
            nh = norm_s[r, hv]
            ggate[r, hv] = (gm * slope_s[r, hv]).astype(LOW)
            gn = gm * silu_s[r, hv]
            one = jnp.sum(gn, axis=1, keepdims=True) * (1.0 / VD)
            two = jnp.sum(gn * nh, axis=1, keepdims=True) * (1.0 / VD)
            gret[r, hv] = (across(inv_s[h, r, :], VP) * (gn - one - nh * two)).astype(LOW)

        add([functools.partial(gated_back, h, r) for r in chunks() for h in range(H)])
        return lists

    first, second = phases(0), phases(TILE)
    for k in range(len(first) + 1):
        interleaved(first[k] if k < len(first) else [], second[k - 1] if k else [])
    for h in range(H):
        add = dot_tn(queries[:, h * KD : (h + 1) * KD], gret[:, h * VP : (h + 1) * VP])
        dst[h] = add
        sums[c, h] = add

    @pl.when(c == count - 1)
    def _():
        for h in range(H):
            total = sums[count - 1, h]
            for b in reversed(range(count - 1)):
                prev = seg_s[seq, b * BLOCK - 1] if b > 0 else in_last[seq]
                joined = jnp.logical_and(
                    seg_s[seq, b * BLOCK] == seg_s[seq, (b + 1) * BLOCK - 1],
                    seg_s[seq, b * BLOCK] == prev,
                )
                factor = jnp.exp(jnp.full((1, 1), decay[h] * BLOCK, WIDE))
                total = jnp.where(joined, factor * total, 0.0) + sums[b, h]
            leave[h] = total.astype(LOW)


def middle(seqs, length, ff, data, seg_col, segments, in_last, decay, w, gains, got, kv):
    intra, gate, q, tokens, cotangent = data
    rows, width = tokens.shape
    count = length // BLOCK
    vp = H * VP
    outs = [width, width, ff, ff, ff, vp, width, vp, vp]
    inputs = [decay, segments, in_last, intra, gate, q, tokens, cotangent, seg_col, w, gains, *got, kv]
    specs = [smem()] * 3 + [row_block(n) for n in (vp, vp, H * KD, width, width, 1)]
    specs += [whole(w.shape), whole(gains.shape), *[seq_block(count)] * 3]
    specs += [state_block(count, lambda c: jnp.maximum(c - 1, 0))]
    one = (H, KD, VP)
    states = (seqs, count, *one)
    return pl.pallas_call(
        functools.partial(middle_kernel, count, ff),
        grid=(seqs * count,),
        out_shape=[shape((rows, n), LOW) for n in outs]
        + [shape(states, LOW), shape(states, WIDE), shape((seqs, *one), LOW)],
        in_specs=specs,
        out_specs=[row_block(n) for n in outs]
        + [state_block(count)] * 2
        + [seq_block(count)],
        scratch_shapes=[
            VMEM(one, WIDE),
            VMEM(one, LOW),
            VMEM((BLOCK, H * KD), LOW),
            VMEM((H, BLOCK, 128), WIDE),
            VMEM((BLOCK, vp), WIDE),
            VMEM((BLOCK, vp), WIDE),
            VMEM((BLOCK, vp), WIDE),
            VMEM((BLOCK, vp), WIDE),
            VMEM((H + 1, BLOCK, 128), WIDE),
            VMEM((BLOCK, width), WIDE),
            VMEM((3, BLOCK, ff), WIDE),
            VMEM((2, BLOCK, width), WIDE),
            VMEM(states[1:], WIDE),
        ],
        compiler_params=params(60),
        cost_estimate=cost(2 * rows * width * (2 * vp + 6 * ff), 30 * rows * width),
    )(*inputs)


def weight_kernel(plan, count, layout, me_ref, *refs):
    ins, ready, outs, total = refs[:count], refs[count:-3], refs[-3:-1], refs[-1]
    if layout is None:
        outs = refs[-2:-1]
    t = pl.program_id(0)
    last = pl.num_programs(0) - 1
    for left, right, cuts in plan:
        a, b = ins[left], ins[right]
        for source, row, size in cuts:
            add = dot_tn(a[:, source : source + size], b[...])

            @pl.when(t == 0)
            def _():
                total[row : row + size, :] = add

            @pl.when(t > 0)
            def _():
                total[row : row + size, :] += add

    @pl.when(t == last)
    def _():
        used = max(row + size for left, right, cuts in plan for source, row, size in cuts)
        if layout is None:
            outs[0][...] = total[...].astype(LOW)
            return
        for item in ready:
            total[used : used + item.shape[0], :] = item[...].astype(WIDE)
            used += item.shape[0]
        if used < total.shape[0]:
            total[used:, :] = jnp.zeros((total.shape[0] - used, total.shape[1]), WIDE)
        lanes = outs[0].shape[2]
        which, pieces = layout
        rows = outs[0].shape[1] // pieces
        for part in range(2 * outs[0].shape[0]):
            target = outs[part & 1]
            lane = pl.multiple_of(jnp.bitwise_xor(me_ref[0], part) * lanes, lanes)
            for q in range(pieces):
                row = pl.multiple_of(jnp.bitwise_xor(me_ref[which], q) * rows, 16)
                target[part >> 1, q * rows : (q + 1) * rows, :] = total[
                    pl.ds(row, rows), pl.ds(lane, lanes)
                ].astype(LOW)


def weight_grads(arrays, plan, place, shards=2, height=0, layout=None, ready=()):
    rows = arrays[0].shape[0]
    used = max(row + size for left, right, cuts in plan for source, row, size in cuts)
    width = arrays[plan[0][1]].shape[1]
    tile = 2 * BLOCK
    block = lambda n: pl.BlockSpec((tile, n), lambda t: (t, 0))
    dims = [(shards // 2, height, width // shards)] * 2
    if layout is None:
        height, dims = used, [(used, width)]
    full = lambda item: pl.BlockSpec(item, lambda t: (0,) * len(item))
    return pl.pallas_call(
        functools.partial(weight_kernel, plan, len(arrays), layout),
        grid=(rows // tile,),
        out_shape=[shape(item, LOW) for item in dims],
        in_specs=[smem()] + [block(item.shape[1]) for item in arrays]
        + [full(item.shape) for item in ready],
        out_specs=[full(item) for item in dims],
        scratch_shapes=[VMEM((height, width), WIDE)],
        compiler_params=params(48),
        cost_estimate=cost(2 * rows * used * width, 2 * rows * sum(i.shape[1] for i in arrays)),
    )(place, *arrays, *ready)


def back_kernel(count, decay, seg_s, in_last, *refs):
    (q, k, v, gret, cos, sin, seg, seg_row, st, dst, *got) = refs[:13]
    (dq, dk, dv, state, weights, grads) = refs[13:]
    seq = pl.program_id(0) // count
    c = count - 1 - pl.program_id(0) % count

    @pl.when(c == count - 1)
    def _():
        for h in range(H):
            state[h] = entering(decay, count * BLOCK, h, got)

    for b in range(1, count):

        @pl.when(c == b - 1)
        def _():
            prev = seg_s[seq, b * BLOCK - 1]
            first = seg_s[seq, b * BLOCK]
            last = seg_s[seq, (b + 1) * BLOCK - 1]
            joined = jnp.logical_and(first == last, first == prev)
            for h in range(H):
                factor = jnp.exp(jnp.full((1, 1), decay[h] * BLOCK, WIDE))
                state[h] = jnp.where(joined, factor * state[h], 0.0) + dst[h]

    start = c * BLOCK
    before = jnp.where(c > 0, seg_s[seq, jnp.maximum(start - 1, 0)], in_last[seq])
    final = seg_s[seq, start + BLOCK - 1]
    here = (seg[...] == before).astype(WIDE)
    ends = (seg[...] == final).astype(WIDE)
    place = column(BLOCK)
    dqs, dks = [], []
    for h in range(H):
        a = decay[h]
        qh = q[:, h * KD : (h + 1) * KD]
        kh = k[:, h * KD : (h + 1) * KD]
        vh = v[:, h * VP : (h + 1) * VP]
        gh = gret[:, h * VP : (h + 1) * VP]
        qw = jnp.exp(a * (place + 1.0)) * here
        kw = jnp.exp(a * (BLOCK - 1.0 - place)) * ends
        parts = []
        for i in range(BLOCK // TILE):
            top, reach = i * TILE, (i + 1) * TILE
            mix = mixing(a, top, TILE, seg, seg_row)
            s = dot_nt(qh[top:reach, :], kh[:reach, :])
            weights[top:reach, :reach] = (s * mix).astype(LOW)
            gs = (dot_nt(gh[top:reach, :], vh[:reach, :]) * mix).astype(LOW)
            grads[top:reach, :reach] = gs
            parts.append(dot(gs, kh[:reach, :]))
        late = state[h].astype(LOW)
        dqs.append(jnp.concatenate(parts) + qw * dot_nt(gh, st[h]))
        parts, values = [], []
        for i in range(BLOCK // TILE):
            top, reach = i * TILE, (i + 1) * TILE
            parts.append(dot_tn(grads[top:, top:reach], qh[top:, :]))
            values.append(dot_tn(weights[top:, top:reach], gh[top:, :]))
        dks.append(jnp.concatenate(parts) + kw * dot_nt(vh, late))
        dv[:, h * VP : (h + 1) * VP] = (jnp.concatenate(values) + kw * dot(kh, late)).astype(LOW)
    dq[...] = rotated(jnp.concatenate(dqs, axis=1), cos[...], -sin[...]).astype(LOW)
    dk[...] = rotated(jnp.concatenate(dks, axis=1), cos[...], -sin[...]).astype(LOW)


def back(seqs, length, data, cos, sin, seg_col, seg_row, segments, in_last, decay, st, dst, got):
    rows = data[0].shape[0]
    count = length // BLOCK
    turn = lambda t: (t // count) * count + count - 1 - t % count
    block = lambda n: pl.BlockSpec((BLOCK, n), lambda t: (turn(t), 0))
    table = pl.BlockSpec((BLOCK, KD // 2), lambda t: (count - 1 - t % count, 0))
    outs = [H * KD, H * KD, H * VP]
    inputs = [decay, segments, in_last, *data, cos, sin, seg_col, seg_row, st, dst, *got]
    specs = [smem()] * 3 + [block(item.shape[1]) for item in data] + [table, table, block(1)]
    specs += [pl.BlockSpec((None, 1, BLOCK), lambda t: (turn(t), 0, 0))]
    specs += [state_block(count, lambda c: count - 1 - c)]
    specs += [state_block(count, lambda c: jnp.minimum(count - c, count - 1))]
    specs += [seq_block(count)] * 3
    return pl.pallas_call(
        functools.partial(back_kernel, count),
        grid=(seqs * count,),
        out_shape=[shape((rows, n), LOW) for n in outs],
        in_specs=specs,
        out_specs=[block(n) for n in outs],
        scratch_shapes=[
            VMEM((H, KD, VP), WIDE),
            VMEM((BLOCK, BLOCK), LOW),
            VMEM((BLOCK, BLOCK), LOW),
        ],
        compiler_params=params(60),
        cost_estimate=cost(rows * H * 2 * BLOCK * 3 * (KD + VP), 16 * rows * H * VP),
    )(*inputs)


def input_kernel(dq, dk, dv, ggate, tok, glow, w, w_gate, gains, *rest):
    out = rest[-1]
    kd = H * KD
    gh = dot(dq[...], w[:kd, :]) + dot(dk[...], w[kd : 2 * kd, :])
    gh += dot(dv[...], w[2 * kd :, :]) + dot(ggate[...], w_gate[...])
    x = tok[...].astype(WIDE)
    r = lax.rsqrt(jnp.mean(x * x, axis=1, keepdims=True) + EPS)
    xhat = x * r
    gh = gh * gains[0:1, :].astype(WIDE)
    inner_product = jnp.mean(gh * xhat, axis=1, keepdims=True)
    out[...] = (glow[...].astype(WIDE) + r * (gh - xhat * inner_product)).astype(LOW)


def input_grad(first, steps, dq, dk, dv, ggate, tokens, glow, w, w_rest, gains, earlier):
    rows, width = tokens.shape
    parts = rows // BLOCK // steps
    arrays = [dq, dk, dv, ggate, tokens, glow]
    block = lambda item: pl.BlockSpec((BLOCK, item.shape[1]), lambda t: (first + t, 0))
    inputs = [*arrays, w, w_rest, gains]
    specs = [block(item) for item in arrays] + [whole(w.shape)]
    specs += [pl.BlockSpec((H * VP, width), lambda t: (0, 0)), whole(gains.shape)]
    aliases = {}
    if earlier is not None:
        aliases = {len(inputs): 0}
        inputs.append(earlier)
        specs.append(pl.BlockSpec(memory_space=pl.ANY))
    return pl.pallas_call(
        input_kernel,
        grid=(steps,),
        out_shape=shape((rows, width), LOW),
        in_specs=specs,
        out_specs=block(tokens),
        input_output_aliases=aliases,
        compiler_params=params(32),
        cost_estimate=cost(2 * rows * width * (w.shape[0] + H * VP) // parts, 20 * rows * width // parts),
    )(*inputs)


def adam_step(master, moment, second, grad, scale, rate, decay_weight):
    clipped = grad * scale
    moment_new = BETA_ONE * moment + (1.0 - BETA_ONE) * clipped
    second_new = BETA_TWO * second + (1.0 - BETA_TWO) * clipped * clipped
    corrected = (
        moment_new
        * (1.0 / (1.0 - BETA_ONE**STEP))
        / (jnp.sqrt(second_new * (1.0 / (1.0 - BETA_TWO**STEP))) + ADAM_EPS)
    )
    return (master - rate * (corrected + decay_weight * master), moment_new, second_new)


def squares_kernel(vd, ff, layouts, place, *refs):
    halves, (w_qk, w_vg, w_gu, low_gains) = refs[:4], refs[4:8]
    grad_gains, total, early, late = refs[8:]
    kd = H * KD
    for index, target in enumerate((early, late)):
        which, pieces = layouts[index]
        rows = target.shape[0] // pieces
        for q in range(pieces):
            row = pl.multiple_of(jnp.bitwise_xor(place[which], q) * rows, 16)
            source = halves[2 * index + q // (pieces // 2)]
            start = q % (pieces // 2) * rows
            target[pl.ds(row, rows), :] = source[start : start + rows, :]

    def rows(source, start, size):
        return source[start : start + size, :].astype(WIDE)

    def product(weight, grad):
        return jnp.sum(weight.astype(LOW).astype(WIDE) * grad, axis=0, keepdims=True)

    sums = []

    def square(item):
        sums.append(jnp.sum(item * item, axis=0, keepdims=True))
        return item

    first = jnp.zeros((1, low_gains.shape[1]), WIDE)
    for i in range(2):
        grad = square(rows(late, i * kd, kd))
        first += jnp.sum(w_qk[i].astype(LOW).astype(WIDE).T * grad, axis=0, keepdims=True)
    first += product(w_vg[0], square(rows(late, 2 * kd, vd)))
    first += product(w_vg[1], square(rows(early, vd, vd)))
    square(rows(early, 0, vd))
    square(rows(early, 2 * vd, ff))
    second = product(w_gu[0], square(rows(early, 2 * vd + ff, ff)))
    second += product(w_gu[1], square(rows(early, 2 * vd + 2 * ff, ff)))
    gains = jnp.concatenate([first, second]) / low_gains[...].astype(LOW).astype(WIDE)
    grad_gains[...] = gains
    sums.append(jnp.sum(gains * gains, axis=0, keepdims=True))
    total[...] = jnp.broadcast_to(jnp.sum(sum(sums), axis=1, keepdims=True), total.shape)


def squares(vd, ff, layouts, place, grads, w_qk, w_vg, w_gu, gains):
    halves = [half for pair in grads for half in pair]
    vmem = pl.BlockSpec(memory_space=VMEM)
    return pl.pallas_call(
        functools.partial(squares_kernel, vd, ff, layouts),
        out_shape=[shape(gains.shape, WIDE), shape((8, 128), WIDE)]
        + [shape((2 * pair[0].shape[0], pair[0].shape[1]), LOW) for pair in grads],
        in_specs=[smem()] + [vmem] * 8,
        out_specs=[vmem] * 4,
        compiler_params=params(20),
    )(place, *halves, w_qk, w_vg, w_gu, gains)


def update_kernel(vd, ff, *refs):
    totals, (early, late, gain_grads) = refs[:4], refs[4:7]
    sources, targets, norm_out = refs[7:25], refs[25:43], refs[43]
    ins, outs = refs[44:62], refs[62:80]
    arrived, sent = refs[80:]
    kd = H * KD
    order = [4, 3, 2, 1, 0, 5]
    places = [6 * group + place for place in order for group in range(3)]
    fetch = {i: pltpu.make_async_copy(sources[i], ins[i], arrived.at[i]) for i in places}
    send = {i: pltpu.make_async_copy(outs[i], targets[i], sent.at[i]) for i in places}
    for i in places:
        fetch[i].start()
    norm = jnp.sqrt((totals[0][...] + totals[1][...]) + (totals[2][...] + totals[3][...]))
    norm_out[0, 0] = jnp.max(norm)
    scale = jnp.minimum(1.0, CLIP / (norm + 1e-06))[0:1, 0:1]

    def step(place, at, grad, rate, decay_weight):
        results = adam_step(
            ins[place][at], ins[6 + place][at], ins[12 + place][at], grad, scale, rate, decay_weight
        )
        for group, result in enumerate(results):
            outs[6 * group + place][at] = result

    def rows(source, start, size):
        return source[start : start + size, :].astype(WIDE)

    grads = {
        4: [(..., lambda: rows(early, 2 * vd, ff))],
        3: [(i, lambda i=i: rows(early, 2 * vd + (1 + i) * ff, ff)) for i in range(2)],
        2: [(..., lambda: rows(early, 0, vd))],
        1: [(0, lambda: rows(late, 2 * kd, vd)), (1, lambda: rows(early, vd, vd))],
        0: [(i, lambda i=i: rows(late, i * kd, kd).T) for i in range(2)],
        5: [(..., lambda: gain_grads[...])],
    }
    for place in order:
        for group in range(3):
            fetch[6 * group + place].wait()
        rate, decay_weight = (GAIN_RATE, 0.0) if place == 5 else (MATRIX_RATE, DECAY_WEIGHT)
        for at, grad in grads[place]:
            step(place, at, grad(), rate, decay_weight)
        for group in range(3):
            send[6 * group + place].start()
    for i in places:
        send[i].wait()


def update(vd, ff, totals, grads, gain_grads, arrays):
    anywhere = pl.BlockSpec(memory_space=pl.ANY)
    return pl.pallas_call(
        functools.partial(update_kernel, vd, ff),
        out_shape=[shape(item.shape, WIDE) for item in arrays] + [shape((1, 1), WIDE)],
        in_specs=[pl.BlockSpec(memory_space=VMEM)] * 7 + [anywhere] * 18,
        out_specs=[anywhere] * 18 + [smem()],
        scratch_shapes=[VMEM(item.shape, WIDE) for item in arrays] * 2
        + [pltpu.SemaphoreType.DMA((18,))] * 2,
        compiler_params=params(40),
    )(*totals, *grads, gain_grads, *arrays)


def on_device(
    tokens,
    cotangent,
    segments,
    log_decay,
    w_qk,
    w_vg,
    w_out,
    w_gu,
    w_down,
    norm_gains,
    *states,
):
    turned = lambda item: jnp.swapaxes(item, 1, 2)
    shards = lax.axis_size("shard")
    me = lax.axis_index("shard").reshape(1)
    replica = lax.axis_index("dp")
    count = bits_of("dp")
    halved = (tuple(range(count - 1)),) * 2
    numbers = [
        sum(((replica >> bit) & 1) << (len(bits) - 1 - i) for i, bit in enumerate(bits))
        for bits in halved
    ]
    layouts = [(1 + i, 2 ** len(bits)) for i, bits in enumerate(halved)]
    place = jnp.concatenate([me, jnp.stack(numbers)])
    seqs, length, width = tokens.shape
    rows = seqs * length
    kd, vd, ff = H * KD, H * VD, w_down.shape[0]
    vp = H * VP
    vg_t, gu_t = turned(w_vg), turned(w_gu)

    low = lambda item: item.astype(LOW)
    def heads(item):
        return [
            jnp.pad(item[h * VD : (h + 1) * VD], ((0, VP - VD), (0, 0))) for h in range(H)
        ]

    first = jnp.concatenate(
        [
            low(w_qk[0]).T,
            low(w_qk[1]).T,
            low(vg_t[0]),
            jnp.pad(low(norm_gains), ((0, 14), (0, 0))),
        ]
    )
    rest = jnp.concatenate(
        [*heads(low(vg_t[1])), *heads(low(w_out)), low(gu_t[0]), low(gu_t[1]), low(w_down)]
    )
    side = (lax.axis_index("dp") & 1).reshape(1)

    half_width = KD // 2
    freq_rates = jnp.exp(-math.log(10000.0) * jnp.arange(half_width).astype(WIDE) / half_width)
    positions = (lax.axis_index("shard") * length + jnp.arange(length)).astype(WIDE)
    angles = positions[:, None] * freq_rates[None, :]
    cos, sin = jnp.cos(angles), jnp.sin(angles)

    tok = tokens.reshape(rows, width)
    cot = cotangent.reshape(rows, width)
    seg_col = segments.reshape(rows, 1)
    seg_row = segments.reshape(rows // BLOCK, 1, BLOCK)
    in_last = jnp.where(lax.axis_index("shard") > 0, segments[:, 0], -1)
    first_held = gather_shards(first, cos, sin, seg_col, seg_row, in_last, place)
    rest = after(rest, first_held[1][2])
    w_rest = lax.all_gather(rest, "shard", axis=1, tiled=True)
    decay = log_decay

    def tick(*done):
        nonlocal decay, place, gains
        decay, place, gains = lax.optimization_barrier((decay, place, gains, *done))[:3]

    plan = [(0, 0, 0, 2 * kd)] + [(2 * kd + h * VD, 0, 2 * kd + h * VP, VD) for h in range(H)]
    plan += [(2 * kd + vd, 1, 0, 16)]
    fills = [(0, 2 * kd + h * VP + VD, VP - VD) for h in range(H)]
    w_qkv, gains = assemble(first_held, plan, fills, [2 * kd + vp, 16], width, me, side)
    tick(rest)
    hid, k, v, kv, leaving = front(
        seqs, length, tok, seg_col, segments, decay, w_qkv, gains, cos, sin
    )
    passing = Passing(leaving, False)
    tick(leaving)
    tick(passing.turn(decay, length, leaving))
    q, intra = inner(k, v, hid, w_qkv, cos, sin, seg_col, seg_row, decay, length)
    tick(q)
    passing.finish(q)
    gate = gates(after(hid, passing.got[1], q), w_rest)
    tick(gate)
    tokens_out, hid2, prod, dgate, dup, mixed, glow, ggate, gret, st, dst, leaving = middle(
        seqs, length, ff, (intra, gate, q, tok, cot), seg_col, segments, in_last, decay,
        w_rest, gains, passing.got, kv,
    )
    returning = Passing(leaving, True)
    tick(leaving)

    def halves(row):
        return [(h * VP, row + h * VD, VD) for h in range(H)]

    fit = lambda used, layout: used + -used % (16 * layout[1])
    plan = [(0, 1, [(0, 0, ff)]), (2, 3, [(0, ff, ff)]), (4, 3, [(0, 2 * ff, ff)])]
    (made,) = weight_grads([prod, cot, dgate, hid2, dup], plan, place)
    tick(made)
    tick(returning.turn(decay, length, made))
    plan = [(0, 1, halves(0)), (2, 3, halves(vd))]
    made = weight_grads(
        [mixed, glow, ggate, hid], plan, place, shards,
        fit(2 * vd + 3 * ff, layouts[0]), layouts[0], (made,),
    )
    tick(made[0])
    returning.finish(made[0])
    early = Reduction(made[0], after(made[1], returning.got[1]), halved[0])
    tick(early.cross(made[0]))
    dq, dk, dv = back(
        seqs, length, (q, k, v, gret), cos, sin, seg_col, seg_row, segments, in_last, decay,
        st, dst, returning.got,
    )
    tick(dq)
    plan = [(0, 3, [(0, 0, kd)]), (1, 3, [(0, kd, kd)]), (2, 3, halves(2 * kd))]
    made = weight_grads(
        [dq, dk, dv, hid], plan, place, shards, fit(2 * kd + vd, layouts[1]), layouts[1]
    )
    late = Reduction(*made, halved[1])
    tick(made[0])
    tick(early.next(made[0]))
    tick(late.cross(made[0]))
    blocks = rows // BLOCK
    data = (dq, dk, dv, ggate, tok, glow, w_qkv, w_rest)
    grad_input = None
    for part in range(2):
        grad_input = input_grad(part * blocks // 2, blocks // 2, *data, gains, grad_input)
        tick(grad_input)
        tick(late.next(grad_input), early.next(grad_input))
    while early.left() or late.left():
        for item in (late, early):
            if item.left():
                item.next()

    gain_grads, total, *grads = squares(
        vd, ff, layouts, place, [early.result(), late.result()], w_qk, vg_t, gu_t, norm_gains
    )
    others = [
        lax.ppermute(total, "shard", [(i, i ^ mask) for i in range(shards)]) for mask in (1, 2, 3)
    ]
    arrays = []
    for group in ((w_qk, w_vg, w_out, w_gu, w_down, norm_gains), states[:6], states[6:]):
        arrays += [turned(item) if i in (1, 3) else item for i, item in enumerate(group)]
    *results, norm = update(vd, ff, [total, *others], grads, gain_grads, arrays)
    results = [turned(item) if i % 6 in (1, 3) else item for i, item in enumerate(results)]
    return (
        tokens_out.reshape(tokens.shape),
        grad_input.reshape(tokens.shape),
        *results,
        norm.reshape(()),
    )


def solution(mesh):
    split = P("dp", "shard", None)
    rows, columns = P(None, "shard", None), P(None, "shard")
    group = (rows, rows, columns, rows, columns, columns)
    in_specs = (split, split, P("dp", "shard"), P()) + group * 3
    out_specs = (split, split) + group * 3 + (P(),)
    return jax.shard_map(
        on_device, mesh=mesh, in_specs=in_specs, out_specs=out_specs, check_vma=False
    )
```

```python
import functools
import math

import jax
import jax.numpy as jnp
from jax import lax
from jax.experimental import pallas as pl
from jax.experimental.pallas import tpu as pltpu
from jax.sharding import PartitionSpec as P

H = 2
KD = 256
VD = 432
VP = 512
BLOCK = 512
STEP = 10

EPS = 1e-05
ADAM_EPS = 1e-08
BETA_ONE = 0.9
BETA_TWO = 0.95
MATRIX_RATE = 0.15
GAIN_RATE = 1.0
DECAY_WEIGHT = 0.1
CLIP = 1.0

LOW = jnp.bfloat16
WIDE = jnp.float32
VMEM = pltpu.VMEM
SMEM = pltpu.SMEM
MIB = 1024 * 1024


def dot(a, b):
    return jnp.dot(a, b, preferred_element_type=WIDE)


def dot_nt(a, b):
    return lax.dot_general(a, b, (((1,), (1,)), ((), ())), preferred_element_type=WIDE)


def dot_tn(a, b):
    return lax.dot_general(a, b, (((0,), (0,)), ((), ())), preferred_element_type=WIDE)


def params(size):
    return pltpu.CompilerParams(vmem_limit_bytes=size * MIB)


def cost(flops, moved):
    return pl.CostEstimate(flops=int(flops), bytes_accessed=int(moved), transcendentals=0)


def smem():
    return pl.BlockSpec(memory_space=SMEM)


def whole(shape):
    return pl.BlockSpec(shape, lambda *at: (0,) * len(shape), pipeline_mode=pl.Buffered(1))


def shape(dims, kind):
    return jax.ShapeDtypeStruct(dims, kind)


def bits_of(axis):
    return (lax.axis_size(axis) - 1).bit_length()


def exchange(value, axis, bit):
    size = lax.axis_size(axis)
    return lax.ppermute(value, axis, [(i, i ^ (1 << bit)) for i in range(size)])


def gather_shards(own, *others):
    held = [(0, own)]
    for bit in reversed(range(bits_of("shard"))):
        held += [
            (mask | (1 << bit), after(exchange(part, "shard", bit), *others)) for mask, part in held
        ]
    return [(mask, None, part) for mask, part in held]


def add_low(one, two):
    return (one.astype(WIDE) + two.astype(WIDE)).astype(LOW)


class Reduction:
    def __init__(self, keep, send, halved):
        self.keep = keep
        self.near = exchange(send, "shard", 0)
        self.halved = halved
        self.stage = 0

    def cross(self, *done):
        self.near = after(self.near, *done)
        low = add_low(self.keep[1], self.near[1])
        self.got = exchange(low, "shard", 1)
        self.terms = [self.keep[0], self.near[0]]
        return low

    def next(self, *done):
        got = after(self.got, *done)
        count = bits_of("dp")
        rows = got.shape[0]

        def total(at):
            return sum(term[at].astype(WIDE) for term in (*self.terms, got)).astype(LOW)

        bit = self.stage
        if self.stage < count:
            if bit in self.halved:
                sent = total(slice(rows // 2, rows))
                self.terms = [total(slice(0, rows // 2))]
            else:
                sent = total(slice(0, rows))
                self.terms = [sent]
        else:
            bit = self.halved[count - 1 - self.stage]
            if self.stage == count:
                sent = total(slice(0, rows))
            else:
                sent = jnp.concatenate([self.held, got])
            self.held = sent
        self.stage += 1
        self.got = exchange(sent, "dp", bit)
        return sent

    def left(self):
        return bits_of("dp") + len(self.halved) - self.stage

    def result(self):
        return self.held, self.got


class Passing:
    def __init__(self, local, reverse):
        self.local = local
        steps = [[(0, 1), (2, 3)], [(1, 2)], [(2, 3)]]
        if reverse:
            steps = [[(3 - a, 3 - b) for a, b in step] for step in steps]
        self.steps = steps
        self.got = [lax.ppermute(local, "shard", steps[0])]

    def turn(self, decay, length, *done):
        self.got[0] = after(self.got[0], *done)
        total = combine(decay, length, self.local, self.got[0])
        self.got.append(lax.ppermute(total, "shard", self.steps[1]))
        return total

    def finish(self, *done):
        self.got.append(lax.ppermute(after(self.got[1], *done), "shard", self.steps[2]))


def entering(decay, length, h, got):
    factor = jnp.exp(jnp.full((1, 1), decay[h] * length, WIDE))
    wide = [item[h].astype(WIDE) for item in got]
    return wide[0] + wide[1] + factor * wide[2]


def after(value, *others):
    return lax.optimization_barrier((value, *others))[0]


def combine_kernel(length, decay, local, got, out):
    h = pl.program_id(0) % H
    factor = jnp.exp(jnp.full((1, 1), decay[h] * length, WIDE))
    out[...] = (local[...].astype(WIDE) + factor * got[...].astype(WIDE)).astype(LOW)


def combine(decay, length, local, got):
    block = pl.BlockSpec((None, None, KD, VP), lambda i: (i // H, i % H, 0, 0))
    return pl.pallas_call(
        functools.partial(combine_kernel, length),
        grid=(local.shape[0] * H,),
        out_shape=shape(local.shape, LOW),
        in_specs=[smem(), block, block],
        out_specs=block,
        compiler_params=params(60),
        cost_estimate=cost(local.size, 6 * local.size),
    )(decay, local, got)


def assemble_kernel(plan, fills, sources_of, me_ref, side_ref, *refs):
    sources, outs = refs[: len(sources_of)], refs[len(sources_of) :]
    lanes = sources[0].shape[1]
    for index, row, size in fills:
        outs[index][row : row + size, :] = jnp.zeros((size, outs[index].shape[1]), LOW)

    def place(source, lane, low, high):
        for start, index, row, size in plan:
            begin, end = max(start, low), min(start + size, high)
            if begin < end:
                to = row + begin - start
                outs[index][to : to + end - begin, pl.ds(lane, lanes)] = source[
                    begin - low : end - low, :
                ]

    for (mask, half), source in zip(sources_of, sources):
        lane = pl.multiple_of(jnp.bitwise_xor(me_ref[0], mask) * lanes, lanes)
        rows = source.shape[0]
        if half is None:
            place(source, lane, 0, rows)
            continue
        for side in range(2):

            @pl.when(side_ref[0] == side)
            def _():
                low = (side ^ half) * rows
                place(source, lane, low, low + rows)


def assemble(held, plan, fills, heights, width, me, side):
    sources_of = [(mask, half) for mask, half, part in held]
    parts = [part for mask, half, part in held]
    return pl.pallas_call(
        functools.partial(assemble_kernel, plan, fills, sources_of),
        out_shape=[shape((rows, width), LOW) for rows in heights],
        in_specs=[smem()] * 2 + [pl.BlockSpec(memory_space=VMEM)] * len(parts),
        out_specs=[pl.BlockSpec(memory_space=VMEM)] * len(heights),
        compiler_params=params(20),
        cost_estimate=cost(0, 4 * sum(heights) * width),
    )(me, side, *parts)


def rotated(flat, cosine, sine):
    half = KD // 2
    parts = []
    for h in range(H):
        u = flat[:, h * KD : h * KD + half]
        w = flat[:, h * KD + half : (h + 1) * KD]
        parts += [u * cosine - w * sine, w * cosine + u * sine]
    return jnp.concatenate(parts, axis=1)


def column(size):
    return lax.broadcasted_iota(jnp.int32, (size, 1), 0).astype(WIDE)


def front_kernel(count, decay, seg_s, tok, w, gains, cos, sin, seg, *rest):
    hid, k, v, kv, out_state, state = rest
    seq = pl.program_id(0) // count
    c = pl.program_id(0) % count
    x = tok[...].astype(WIDE)
    r = lax.rsqrt(jnp.mean(x * x, axis=1, keepdims=True) + EPS)
    h1 = (x * r * gains[0:1, :].astype(WIDE)).astype(LOW)
    hid[...] = h1
    kd = H * KD
    key = rotated(dot_nt(h1, w[kd : 2 * kd, :]), cos[...], sin[...]).astype(LOW)
    k[...] = key
    val = dot_nt(h1, w[2 * kd :, :]).astype(LOW)
    v[...] = val
    first = seg_s[seq, c * BLOCK]
    last = seg_s[seq, c * BLOCK + BLOCK - 1]
    before = seg_s[seq, jnp.maximum(c * BLOCK - 1, 0)]
    here = (seg[...] == last).astype(WIDE)
    joined = jnp.logical_and(jnp.logical_and(first == last, first == before), c > 0)
    for h in range(H):
        a = decay[h]
        kw = jnp.exp(a * (BLOCK - 1.0 - column(BLOCK))) * here
        kk = (key[:, h * KD : (h + 1) * KD].astype(WIDE) * kw).astype(LOW)
        add = dot_tn(kk, val[:, h * VP : (h + 1) * VP])
        kv[h] = add
        factor = jnp.exp(jnp.full((1, 1), a * BLOCK, WIDE))
        total = jnp.where(joined, factor * state[h], 0.0) + add
        state[h] = total
        out_state[h] = total.astype(LOW)


def row_block(width):
    return pl.BlockSpec((BLOCK, width), lambda t: (t, 0))


def state_block(count, at=lambda c: c):
    return pl.BlockSpec(
        (None, None, H, KD, VP), lambda t: (t // count, at(t % count), 0, 0, 0)
    )


def seq_block(count):
    return pl.BlockSpec((None, H, KD, VP), lambda t: (t // count, 0, 0, 0))


def front(seqs, length, tokens, seg_col, segments, decay, w, gains, cos, sin):
    count = length // BLOCK
    rows, width = tokens.shape
    outs = [width, H * KD, H * VP]
    table = pl.BlockSpec((BLOCK, KD // 2), lambda t: (t % count, 0))
    return pl.pallas_call(
        functools.partial(front_kernel, count),
        grid=(seqs * count,),
        out_shape=[shape((rows, n), LOW) for n in outs]
        + [shape((seqs, count, H, KD, VP), WIDE), shape((seqs, H, KD, VP), LOW)],
        in_specs=[smem(), smem(), row_block(width), whole(w.shape), whole(gains.shape)]
        + [table, table, row_block(1)],
        out_specs=[row_block(n) for n in outs]
        + [state_block(count), seq_block(count)],
        scratch_shapes=[VMEM((H, KD, VP), WIDE)],
        compiler_params=params(60),
        cost_estimate=cost(2 * rows * width * w.shape[0], 12 * rows * width),
    )(decay, segments, tokens, w, gains, cos, sin, seg_col)


def decay_row(a):
    return jnp.exp(-a * lax.broadcasted_iota(jnp.int32, (1, BLOCK), 1).astype(WIDE))


def mixing(a, top, size, seg, seg_row):
    reach = top + size
    rows = jnp.exp(a * (column(size) + float(top)))
    same = seg[top:reach, :] == seg_row[:, :reach]
    n = lax.broadcasted_iota(jnp.int32, (size, reach), 0) + top
    m = lax.broadcasted_iota(jnp.int32, (size, reach), 1)
    return jnp.where(jnp.logical_and(same, n >= m), rows * decay_row(a)[:, :reach], 0.0)


TILE = 256


def inner_kernel(decay, k, v, hid, w, cos, sin, seg, seg_row, q, intra):
    query = rotated(dot_nt(hid[...], w[...]), cos[...], sin[...]).astype(LOW)
    q[...] = query
    for i in range(BLOCK // TILE):
        top, reach = i * TILE, (i + 1) * TILE
        for h in range(H):
            s = dot_nt(query[top:reach, h * KD : (h + 1) * KD], k[:reach, h * KD : (h + 1) * KD])
            weights = (s * mixing(decay[h], top, TILE, seg, seg_row)).astype(LOW)
            intra[top:reach, h * VP : (h + 1) * VP] = dot(
                weights, v[:reach, h * VP : (h + 1) * VP]
            ).astype(LOW)


def inner(k, v, hid, w, cos, sin, seg_col, seg_row, decay, length):
    rows, width = hid.shape
    count = length // BLOCK
    block = lambda n: pl.BlockSpec((BLOCK, n), lambda t: (t, 0))
    table = pl.BlockSpec((BLOCK, KD // 2), lambda t: (t % count, 0))
    return pl.pallas_call(
        inner_kernel,
        grid=(rows // BLOCK,),
        out_shape=[shape((rows, n), LOW) for n in (H * KD, H * VP)],
        in_specs=[
            smem(),
            block(H * KD),
            block(H * VP),
            block(width),
            pl.BlockSpec((H * KD, width), lambda t: (0, 0)),
            table,
            table,
            block(1),
            pl.BlockSpec((None, 1, BLOCK), lambda t: (t, 0, 0)),
        ],
        out_specs=[block(n) for n in (H * KD, H * VP)],
        compiler_params=params(60),
        cost_estimate=cost(rows * (2 * width * 512 + 2 * BLOCK * H * VP), 8 * rows * H * VP),
    )(decay, k, v, hid, w, cos, sin, seg_col, seg_row)


def gate_kernel(hid, w, gate):
    gate[...] = dot_nt(hid[...], w[...]).astype(LOW)


def gates(hid, w):
    rows, width = hid.shape
    vp = H * VP
    return pl.pallas_call(
        gate_kernel,
        grid=(rows // BLOCK,),
        out_shape=shape((rows, vp), LOW),
        in_specs=[row_block(width), pl.BlockSpec((vp, width), lambda t: (0, 0))],
        out_specs=row_block(vp),
        compiler_params=params(60),
        cost_estimate=cost(2 * rows * width * vp, 4 * rows * vp),
    )(hid, w)


CHUNK = 16


def interleaved(first, second):
    steps = [((i + 0.5) / len(first), 0, step) for i, step in enumerate(first)]
    steps += [((i + 0.5) / len(second), 1, step) for i, step in enumerate(second)]
    for place, which, step in sorted(steps, key=lambda item: item[:2]):
        step()


def pieces(width, size=256):
    return [(start, min(start + size, width)) for start in range(0, width, size)]


def across(narrow, width):
    return jnp.concatenate([narrow] * (width // 128), axis=1)


def middle_kernel(count, ff, decay, seg_s, in_last, *refs):
    (intra, gate, q, tok, cot, seg, w, gains, *got, kv) = refs[:12]
    outs, scratch = refs[12:24], refs[24:]
    (tok_out, hid2, prod, dgate, dup, mixed, glow, ggate, gret, st_out, dst, leave) = outs
    (state, now, queries, factors, ret_s, norm_s, silu_s, slope_s, inv_s, res_s, ff_s, low_s, sums) = scratch
    seq = pl.program_id(0) // count
    c = pl.program_id(0) % count
    start = c * BLOCK
    vp = H * VP
    width = tok.shape[1]
    before = jnp.where(c > 0, seg_s[seq, jnp.maximum(start - 1, 0)], in_last[seq])

    @pl.when(c == 0)
    def _():
        for h in range(H):
            total = entering(decay, count * BLOCK, h, got)
            state[h] = total
            now[h] = total.astype(LOW)

    for b in range(1, count):

        @pl.when(c == b)
        def _():
            prev = seg_s[seq, (b - 1) * BLOCK - 1] if b > 1 else in_last[seq]
            joined = jnp.logical_and(
                seg_s[seq, (b - 1) * BLOCK] == seg_s[seq, b * BLOCK - 1],
                seg_s[seq, (b - 1) * BLOCK] == prev,
            )
            for h in range(H):
                factor = jnp.exp(jnp.full((1, 1), decay[h] * BLOCK, WIDE))
                total = jnp.where(joined, factor * state[h], 0.0) + kv[h]
                state[h] = total
                now[h] = total.astype(LOW)

    st_out[...] = now[...]
    here = (seg[...] == before).astype(WIDE)
    for h in range(H):
        qw = jnp.exp(decay[h] * (column(BLOCK) + 1.0)) * here
        factors[h] = jnp.broadcast_to(qw, (BLOCK, 128))

    w_out = (vp, 2 * vp)
    w_gate = (2 * vp, 2 * vp + ff)
    w_up = (2 * vp + ff, 2 * vp + 2 * ff)
    w_down = (2 * vp + 2 * ff, 2 * vp + 3 * ff)
    gain = gains[1:2, :].astype(WIDE)

    def phases(top):
        rs = pl.ds(top, TILE)
        lists = []

        def add(steps):
            lists.append(steps)

        def chunks():
            return [pl.ds(row, CHUNK) for row in range(top, top + TILE, CHUNK)]

        def cross(h, lo, hi):
            ret_s[rs, h * VP + lo : h * VP + hi] = dot(
                q[rs, h * KD : (h + 1) * KD], now[h, :, lo:hi]
            )

        add([functools.partial(cross, h, *piece) for h in range(H) for piece in pieces(VP)])

        def gated(h, r):
            hv = slice(h * VP, (h + 1) * VP)
            hk = slice(h * KD, (h + 1) * KD)
            qw = factors[h, r, :]
            queries[r, hk] = (q[r, hk].astype(WIDE) * across(qw, KD)).astype(LOW)
            ret = intra[r, hv].astype(WIDE) + across(qw, VP) * ret_s[r, hv]
            mean = jnp.sum(ret, axis=1, keepdims=True) * (1.0 / VD)
            centered = ret - mean
            square = jnp.sum(centered * centered, axis=1, keepdims=True)
            var = (square - (VP - VD) * (mean * mean)) * (1.0 / VD)
            inv = lax.rsqrt(var + 1.0 * KD)
            nh = centered * inv
            g = gate[r, hv].astype(WIDE)
            sg = 0.5 * jnp.tanh(0.5 * g) + 0.5
            sl = g * sg
            mixed[r, hv] = (nh * sl).astype(LOW)
            norm_s[r, hv] = nh
            silu_s[r, hv] = sl
            slope_s[r, hv] = nh * (sg + sl * (1.0 - sg))
            inv_s[h, r, :] = jnp.broadcast_to(inv, (CHUNK, 128))

        add([functools.partial(gated, h, r) for r in chunks() for h in range(H)])

        def project(lo, hi):
            res_s[rs, lo:hi] = dot(mixed[rs, :], w[w_out[0] : w_out[1], lo:hi])

        add([functools.partial(project, *piece) for piece in pieces(width)])

        def norm(r):
            resid = tok[r, :].astype(WIDE) + res_s[r, :]
            r2 = lax.rsqrt(jnp.mean(resid * resid, axis=1, keepdims=True) + EPS)
            res_s[r, :] = resid
            hid2[r, :] = (resid * r2 * gain).astype(LOW)
            inv_s[H, r, :] = jnp.broadcast_to(r2, (CHUNK, 128))

        add([functools.partial(norm, r) for r in chunks()])

        def forward(place, source, at, lo, hi):
            ff_s[place, rs, lo:hi] = dot_nt(source[rs, :], w[at[0] + lo : at[0] + hi, :])

        add(
            [
                functools.partial(forward, place, source, at, *piece)
                for piece in pieces(ff)
                for place, source, at in ((0, hid2, w_gate), (1, hid2, w_up), (2, cot, w_down))
            ]
        )

        def gelu(r, lo, hi):
            gf, uf, gp = ff_s[0, r, lo:hi], ff_s[1, r, lo:hi], ff_s[2, r, lo:hi]
            e = jnp.exp(-0.5 * (gf * gf))
            d = 1.0 / (1.0 + (0.3275911 * math.sqrt(0.5)) * jnp.abs(gf))
            poly = d * (
                0.5 * 0.254829592
                + d
                * (
                    0.5 * -0.284496736
                    + d * (0.5 * 1.421413741 + d * (0.5 * -1.453152027 + d * (0.5 * 1.061405429)))
                )
            )
            tail = poly * e
            cdf = jnp.where(gf >= 0.0, 1.0 - tail, tail)
            ge = gf * cdf
            dge = cdf + gf * (e * (1.0 / math.sqrt(2.0 * math.pi)))
            prod[r, lo:hi] = (ge * uf).astype(LOW)
            dgate[r, lo:hi] = (gp * uf * dge).astype(LOW)
            dup[r, lo:hi] = (gp * ge).astype(LOW)

        add([functools.partial(gelu, r, *piece) for r in chunks() for piece in pieces(ff, 512)])

        def down(lo, hi):
            low_s[0, rs, lo:hi] = dot(prod[rs, :], w[w_down[0] : w_down[1], lo:hi])

        def hidden(lo, hi):
            low_s[1, rs, lo:hi] = dot(dgate[rs, :], w[w_gate[0] : w_gate[1], lo:hi]) + dot(
                dup[rs, :], w[w_up[0] : w_up[1], lo:hi]
            )

        add([functools.partial(step, *piece) for piece in pieces(width) for step in (down, hidden)])

        def residual(r):
            resid = res_s[r, :]
            r2 = across(inv_s[H, r, :], width)
            tok_out[r, :] = (resid + low_s[0, r, :]).astype(LOW)
            gh = low_s[1, r, :] * gain
            xhat = resid * r2
            inner_product = jnp.mean(gh * xhat, axis=1, keepdims=True)
            glow[r, :] = (cot[r, :].astype(WIDE) + r2 * (gh - xhat * inner_product)).astype(LOW)

        add([functools.partial(residual, r) for r in chunks()])

        def mix_back(lo, hi):
            ret_s[rs, lo:hi] = dot_nt(glow[rs, :], w[w_out[0] + lo : w_out[0] + hi, :])

        add([functools.partial(mix_back, *piece) for piece in pieces(vp)])

        def gated_back(h, r):
            hv = slice(h * VP, (h + 1) * VP)
            gm = ret_s[r, hv]
            nh = norm_s[r, hv]
            ggate[r, hv] = (gm * slope_s[r, hv]).astype(LOW)
            gn = gm * silu_s[r, hv]
            one = jnp.sum(gn, axis=1, keepdims=True) * (1.0 / VD)
            two = jnp.sum(gn * nh, axis=1, keepdims=True) * (1.0 / VD)
            gret[r, hv] = (across(inv_s[h, r, :], VP) * (gn - one - nh * two)).astype(LOW)

        add([functools.partial(gated_back, h, r) for r in chunks() for h in range(H)])
        return lists

    first, second = phases(0), phases(TILE)
    for k in range(len(first) + 1):
        interleaved(first[k] if k < len(first) else [], second[k - 1] if k else [])
    for h in range(H):
        add = dot_tn(queries[:, h * KD : (h + 1) * KD], gret[:, h * VP : (h + 1) * VP])
        dst[h] = add
        sums[c, h] = add

    @pl.when(c == count - 1)
    def _():
        for h in range(H):
            total = sums[count - 1, h]
            for b in reversed(range(count - 1)):
                prev = seg_s[seq, b * BLOCK - 1] if b > 0 else in_last[seq]
                joined = jnp.logical_and(
                    seg_s[seq, b * BLOCK] == seg_s[seq, (b + 1) * BLOCK - 1],
                    seg_s[seq, b * BLOCK] == prev,
                )
                factor = jnp.exp(jnp.full((1, 1), decay[h] * BLOCK, WIDE))
                total = jnp.where(joined, factor * total, 0.0) + sums[b, h]
            leave[h] = total.astype(LOW)


def middle(seqs, length, ff, data, seg_col, segments, in_last, decay, w, gains, got, kv):
    intra, gate, q, tokens, cotangent = data
    rows, width = tokens.shape
    count = length // BLOCK
    vp = H * VP
    outs = [width, width, ff, ff, ff, vp, width, vp, vp]
    inputs = [decay, segments, in_last, intra, gate, q, tokens, cotangent, seg_col, w, gains, *got, kv]
    specs = [smem()] * 3 + [row_block(n) for n in (vp, vp, H * KD, width, width, 1)]
    specs += [whole(w.shape), whole(gains.shape), *[seq_block(count)] * 3]
    specs += [state_block(count, lambda c: jnp.maximum(c - 1, 0))]
    one = (H, KD, VP)
    states = (seqs, count, *one)
    return pl.pallas_call(
        functools.partial(middle_kernel, count, ff),
        grid=(seqs * count,),
        out_shape=[shape((rows, n), LOW) for n in outs]
        + [shape(states, LOW), shape(states, WIDE), shape((seqs, *one), LOW)],
        in_specs=specs,
        out_specs=[row_block(n) for n in outs]
        + [state_block(count)] * 2
        + [seq_block(count)],
        scratch_shapes=[
            VMEM(one, WIDE),
            VMEM(one, LOW),
            VMEM((BLOCK, H * KD), LOW),
            VMEM((H, BLOCK, 128), WIDE),
            VMEM((BLOCK, vp), WIDE),
            VMEM((BLOCK, vp), WIDE),
            VMEM((BLOCK, vp), WIDE),
            VMEM((BLOCK, vp), WIDE),
            VMEM((H + 1, BLOCK, 128), WIDE),
            VMEM((BLOCK, width), WIDE),
            VMEM((3, BLOCK, ff), WIDE),
            VMEM((2, BLOCK, width), WIDE),
            VMEM(states[1:], WIDE),
        ],
        compiler_params=params(60),
        cost_estimate=cost(2 * rows * width * (2 * vp + 6 * ff), 30 * rows * width),
    )(*inputs)


def weight_kernel(plan, count, layout, me_ref, *refs):
    ins, ready, outs, total = refs[:count], refs[count:-3], refs[-3:-1], refs[-1]
    if layout is None:
        outs = refs[-2:-1]
    t = pl.program_id(0)
    last = pl.num_programs(0) - 1
    for left, right, cuts in plan:
        a, b = ins[left], ins[right]
        for source, row, size in cuts:
            add = dot_tn(a[:, source : source + size], b[...])

            @pl.when(t == 0)
            def _():
                total[row : row + size, :] = add

            @pl.when(t > 0)
            def _():
                total[row : row + size, :] += add

    @pl.when(t == last)
    def _():
        used = max(row + size for left, right, cuts in plan for source, row, size in cuts)
        if layout is None:
            outs[0][...] = total[...].astype(LOW)
            return
        for item in ready:
            total[used : used + item.shape[0], :] = item[...].astype(WIDE)
            used += item.shape[0]
        if used < total.shape[0]:
            total[used:, :] = jnp.zeros((total.shape[0] - used, total.shape[1]), WIDE)
        lanes = outs[0].shape[2]
        which, pieces = layout
        rows = outs[0].shape[1] // pieces
        for part in range(2 * outs[0].shape[0]):
            target = outs[part & 1]
            lane = pl.multiple_of(jnp.bitwise_xor(me_ref[0], part) * lanes, lanes)
            for q in range(pieces):
                row = pl.multiple_of(jnp.bitwise_xor(me_ref[which], q) * rows, 16)
                target[part >> 1, q * rows : (q + 1) * rows, :] = total[
                    pl.ds(row, rows), pl.ds(lane, lanes)
                ].astype(LOW)


def weight_grads(arrays, plan, place, shards=2, height=0, layout=None, ready=()):
    rows = arrays[0].shape[0]
    used = max(row + size for left, right, cuts in plan for source, row, size in cuts)
    width = arrays[plan[0][1]].shape[1]
    tile = 2 * BLOCK
    block = lambda n: pl.BlockSpec((tile, n), lambda t: (t, 0))
    dims = [(shards // 2, height, width // shards)] * 2
    if layout is None:
        height, dims = used, [(used, width)]
    full = lambda item: pl.BlockSpec(item, lambda t: (0,) * len(item))
    return pl.pallas_call(
        functools.partial(weight_kernel, plan, len(arrays), layout),
        grid=(rows // tile,),
        out_shape=[shape(item, LOW) for item in dims],
        in_specs=[smem()] + [block(item.shape[1]) for item in arrays]
        + [full(item.shape) for item in ready],
        out_specs=[full(item) for item in dims],
        scratch_shapes=[VMEM((height, width), WIDE)],
        compiler_params=params(48),
        cost_estimate=cost(2 * rows * used * width, 2 * rows * sum(i.shape[1] for i in arrays)),
    )(place, *arrays, *ready)


def back_kernel(count, decay, seg_s, in_last, *refs):
    (q, k, v, gret, cos, sin, seg, seg_row, st, dst, *got) = refs[:13]
    (dq, dk, dv, state, weights, grads) = refs[13:]
    seq = pl.program_id(0) // count
    c = count - 1 - pl.program_id(0) % count

    @pl.when(c == count - 1)
    def _():
        for h in range(H):
            state[h] = entering(decay, count * BLOCK, h, got)

    for b in range(1, count):

        @pl.when(c == b - 1)
        def _():
            prev = seg_s[seq, b * BLOCK - 1]
            first = seg_s[seq, b * BLOCK]
            last = seg_s[seq, (b + 1) * BLOCK - 1]
            joined = jnp.logical_and(first == last, first == prev)
            for h in range(H):
                factor = jnp.exp(jnp.full((1, 1), decay[h] * BLOCK, WIDE))
                state[h] = jnp.where(joined, factor * state[h], 0.0) + dst[h]

    start = c * BLOCK
    before = jnp.where(c > 0, seg_s[seq, jnp.maximum(start - 1, 0)], in_last[seq])
    final = seg_s[seq, start + BLOCK - 1]
    here = (seg[...] == before).astype(WIDE)
    ends = (seg[...] == final).astype(WIDE)
    place = column(BLOCK)
    dqs, dks = [], []
    for h in range(H):
        a = decay[h]
        qh = q[:, h * KD : (h + 1) * KD]
        kh = k[:, h * KD : (h + 1) * KD]
        vh = v[:, h * VP : (h + 1) * VP]
        gh = gret[:, h * VP : (h + 1) * VP]
        qw = jnp.exp(a * (place + 1.0)) * here
        kw = jnp.exp(a * (BLOCK - 1.0 - place)) * ends
        parts = []
        for i in range(BLOCK // TILE):
            top, reach = i * TILE, (i + 1) * TILE
            mix = mixing(a, top, TILE, seg, seg_row)
            s = dot_nt(qh[top:reach, :], kh[:reach, :])
            weights[top:reach, :reach] = (s * mix).astype(LOW)
            gs = (dot_nt(gh[top:reach, :], vh[:reach, :]) * mix).astype(LOW)
            grads[top:reach, :reach] = gs
            parts.append(dot(gs, kh[:reach, :]))
        late = state[h].astype(LOW)
        dqs.append(jnp.concatenate(parts) + qw * dot_nt(gh, st[h]))
        parts, values = [], []
        for i in range(BLOCK // TILE):
            top, reach = i * TILE, (i + 1) * TILE
            parts.append(dot_tn(grads[top:, top:reach], qh[top:, :]))
            values.append(dot_tn(weights[top:, top:reach], gh[top:, :]))
        dks.append(jnp.concatenate(parts) + kw * dot_nt(vh, late))
        dv[:, h * VP : (h + 1) * VP] = (jnp.concatenate(values) + kw * dot(kh, late)).astype(LOW)
    dq[...] = rotated(jnp.concatenate(dqs, axis=1), cos[...], -sin[...]).astype(LOW)
    dk[...] = rotated(jnp.concatenate(dks, axis=1), cos[...], -sin[...]).astype(LOW)


def back(seqs, length, data, cos, sin, seg_col, seg_row, segments, in_last, decay, st, dst, got):
    rows = data[0].shape[0]
    count = length // BLOCK
    turn = lambda t: (t // count) * count + count - 1 - t % count
    block = lambda n: pl.BlockSpec((BLOCK, n), lambda t: (turn(t), 0))
    table = pl.BlockSpec((BLOCK, KD // 2), lambda t: (count - 1 - t % count, 0))
    outs = [H * KD, H * KD, H * VP]
    inputs = [decay, segments, in_last, *data, cos, sin, seg_col, seg_row, st, dst, *got]
    specs = [smem()] * 3 + [block(item.shape[1]) for item in data] + [table, table, block(1)]
    specs += [pl.BlockSpec((None, 1, BLOCK), lambda t: (turn(t), 0, 0))]
    specs += [state_block(count, lambda c: count - 1 - c)]
    specs += [state_block(count, lambda c: jnp.minimum(count - c, count - 1))]
    specs += [seq_block(count)] * 3
    return pl.pallas_call(
        functools.partial(back_kernel, count),
        grid=(seqs * count,),
        out_shape=[shape((rows, n), LOW) for n in outs],
        in_specs=specs,
        out_specs=[block(n) for n in outs],
        scratch_shapes=[
            VMEM((H, KD, VP), WIDE),
            VMEM((BLOCK, BLOCK), LOW),
            VMEM((BLOCK, BLOCK), LOW),
        ],
        compiler_params=params(60),
        cost_estimate=cost(rows * H * 2 * BLOCK * 3 * (KD + VP), 16 * rows * H * VP),
    )(*inputs)


def input_kernel(dq, dk, dv, ggate, tok, glow, w, w_gate, gains, *rest):
    out = rest[-1]
    kd = H * KD
    gh = dot(dq[...], w[:kd, :]) + dot(dk[...], w[kd : 2 * kd, :])
    gh += dot(dv[...], w[2 * kd :, :]) + dot(ggate[...], w_gate[...])
    x = tok[...].astype(WIDE)
    r = lax.rsqrt(jnp.mean(x * x, axis=1, keepdims=True) + EPS)
    xhat = x * r
    gh = gh * gains[0:1, :].astype(WIDE)
    inner_product = jnp.mean(gh * xhat, axis=1, keepdims=True)
    out[...] = (glow[...].astype(WIDE) + r * (gh - xhat * inner_product)).astype(LOW)


def input_grad(first, steps, dq, dk, dv, ggate, tokens, glow, w, w_rest, gains, earlier, hides):
    rows, width = tokens.shape
    parts = rows // BLOCK // steps
    arrays = [dq, dk, dv, ggate, tokens, glow]
    block = lambda item: pl.BlockSpec((BLOCK, item.shape[1]), lambda t: (first + t, 0))
    inputs = [*arrays, w, w_rest, gains]
    specs = [block(item) for item in arrays] + [whole(w.shape)]
    specs += [pl.BlockSpec((H * VP, width), lambda t: (0, 0)), whole(gains.shape)]
    aliases = {}
    if earlier is not None:
        aliases = {len(inputs): 0}
        inputs.append(earlier)
        specs.append(pl.BlockSpec(memory_space=pl.ANY))
    return pl.pallas_call(
        input_kernel,
        grid=(steps,),
        out_shape=shape((rows, width), LOW),
        in_specs=specs,
        out_specs=block(tokens),
        input_output_aliases=aliases,
        compiler_params=params(32),
        cost_estimate=cost(2 * rows * width * (w.shape[0] + H * VP) // parts, 20 * rows * width // parts)
        if hides
        else cost(1, 1),
    )(*inputs)


def adam_step(master, moment, second, grad, scale, rate, decay_weight):
    clipped = grad * scale
    moment_new = BETA_ONE * moment + (1.0 - BETA_ONE) * clipped
    second_new = BETA_TWO * second + (1.0 - BETA_TWO) * clipped * clipped
    corrected = (
        moment_new
        * (1.0 / (1.0 - BETA_ONE**STEP))
        / (jnp.sqrt(second_new * (1.0 / (1.0 - BETA_TWO**STEP))) + ADAM_EPS)
    )
    return (master - rate * (corrected + decay_weight * master), moment_new, second_new)


def squares_kernel(vd, ff, layouts, place, *refs):
    halves, (w_qk, w_vg, w_gu, low_gains) = refs[:4], refs[4:8]
    grad_gains, total, early, late = refs[8:]
    kd = H * KD
    for index, target in enumerate((early, late)):
        which, pieces = layouts[index]
        rows = target.shape[0] // pieces
        for q in range(pieces):
            row = pl.multiple_of(jnp.bitwise_xor(place[which], q) * rows, 16)
            source = halves[2 * index + q // (pieces // 2)]
            start = q % (pieces // 2) * rows
            target[pl.ds(row, rows), :] = source[start : start + rows, :]

    def rows(source, start, size):
        return source[start : start + size, :].astype(WIDE)

    def product(weight, grad):
        return jnp.sum(weight.astype(LOW).astype(WIDE) * grad, axis=0, keepdims=True)

    sums = []

    def square(item):
        sums.append(jnp.sum(item * item, axis=0, keepdims=True))
        return item

    first = jnp.zeros((1, low_gains.shape[1]), WIDE)
    for i in range(2):
        grad = square(rows(late, i * kd, kd))
        first += jnp.sum(w_qk[i].astype(LOW).astype(WIDE).T * grad, axis=0, keepdims=True)
    first += product(w_vg[0], square(rows(late, 2 * kd, vd)))
    first += product(w_vg[1], square(rows(early, vd, vd)))
    square(rows(early, 0, vd))
    square(rows(early, 2 * vd, ff))
    second = product(w_gu[0], square(rows(early, 2 * vd + ff, ff)))
    second += product(w_gu[1], square(rows(early, 2 * vd + 2 * ff, ff)))
    gains = jnp.concatenate([first, second]) / low_gains[...].astype(LOW).astype(WIDE)
    grad_gains[...] = gains
    sums.append(jnp.sum(gains * gains, axis=0, keepdims=True))
    total[...] = jnp.broadcast_to(jnp.sum(sum(sums), axis=1, keepdims=True), total.shape)


def squares(vd, ff, layouts, place, grads, w_qk, w_vg, w_gu, gains):
    halves = [half for pair in grads for half in pair]
    vmem = pl.BlockSpec(memory_space=VMEM)
    return pl.pallas_call(
        functools.partial(squares_kernel, vd, ff, layouts),
        out_shape=[shape(gains.shape, WIDE), shape((8, 128), WIDE)]
        + [shape((2 * pair[0].shape[0], pair[0].shape[1]), LOW) for pair in grads],
        in_specs=[smem()] + [vmem] * 8,
        out_specs=[vmem] * 4,
        compiler_params=params(20),
    )(place, *halves, w_qk, w_vg, w_gu, gains)


def update_kernel(vd, ff, *refs):
    totals, (early, late, gain_grads) = refs[:4], refs[4:7]
    sources, targets, norm_out = refs[7:25], refs[25:43], refs[43]
    ins, outs = refs[44:62], refs[62:80]
    arrived, sent = refs[80:]
    kd = H * KD
    order = [4, 3, 2, 1, 0, 5]
    places = [6 * group + place for place in order for group in range(3)]
    fetch = {i: pltpu.make_async_copy(sources[i], ins[i], arrived.at[i]) for i in places}
    send = {i: pltpu.make_async_copy(outs[i], targets[i], sent.at[i]) for i in places}
    for i in places:
        fetch[i].start()
    norm = jnp.sqrt((totals[0][...] + totals[1][...]) + (totals[2][...] + totals[3][...]))
    norm_out[0, 0] = jnp.max(norm)
    scale = jnp.minimum(1.0, CLIP / (norm + 1e-06))[0:1, 0:1]

    def step(place, at, grad, rate, decay_weight):
        results = adam_step(
            ins[place][at], ins[6 + place][at], ins[12 + place][at], grad, scale, rate, decay_weight
        )
        for group, result in enumerate(results):
            outs[6 * group + place][at] = result

    def rows(source, start, size):
        return source[start : start + size, :].astype(WIDE)

    grads = {
        4: [(..., lambda: rows(early, 2 * vd, ff))],
        3: [(i, lambda i=i: rows(early, 2 * vd + (1 + i) * ff, ff)) for i in range(2)],
        2: [(..., lambda: rows(early, 0, vd))],
        1: [(0, lambda: rows(late, 2 * kd, vd)), (1, lambda: rows(early, vd, vd))],
        0: [(i, lambda i=i: rows(late, i * kd, kd).T) for i in range(2)],
        5: [(..., lambda: gain_grads[...])],
    }
    for place in order:
        for group in range(3):
            fetch[6 * group + place].wait()
        rate, decay_weight = (GAIN_RATE, 0.0) if place == 5 else (MATRIX_RATE, DECAY_WEIGHT)
        for at, grad in grads[place]:
            step(place, at, grad(), rate, decay_weight)
        for group in range(3):
            send[6 * group + place].start()
    for i in places:
        send[i].wait()


def update(vd, ff, totals, grads, gain_grads, arrays):
    anywhere = pl.BlockSpec(memory_space=pl.ANY)
    return pl.pallas_call(
        functools.partial(update_kernel, vd, ff),
        out_shape=[shape(item.shape, WIDE) for item in arrays] + [shape((1, 1), WIDE)],
        in_specs=[pl.BlockSpec(memory_space=VMEM)] * 7 + [anywhere] * 18,
        out_specs=[anywhere] * 18 + [smem()],
        scratch_shapes=[VMEM(item.shape, WIDE) for item in arrays] * 2
        + [pltpu.SemaphoreType.DMA((18,))] * 2,
        compiler_params=params(40),
    )(*totals, *grads, gain_grads, *arrays)


def on_device(
    tokens,
    cotangent,
    segments,
    log_decay,
    w_qk,
    w_vg,
    w_out,
    w_gu,
    w_down,
    norm_gains,
    *states,
):
    turned = lambda item: jnp.swapaxes(item, 1, 2)
    shards = lax.axis_size("shard")
    me = lax.axis_index("shard").reshape(1)
    replica = lax.axis_index("dp")
    count = bits_of("dp")
    halved = (tuple(range(count - 1)),) * 2
    numbers = [
        sum(((replica >> bit) & 1) << (len(bits) - 1 - i) for i, bit in enumerate(bits))
        for bits in halved
    ]
    layouts = [(1 + i, 2 ** len(bits)) for i, bits in enumerate(halved)]
    place = jnp.concatenate([me, jnp.stack(numbers)])
    seqs, length, width = tokens.shape
    rows = seqs * length
    kd, vd, ff = H * KD, H * VD, w_down.shape[0]
    vp = H * VP
    vg_t, gu_t = turned(w_vg), turned(w_gu)

    low = lambda item: item.astype(LOW)
    def heads(item):
        return [
            jnp.pad(item[h * VD : (h + 1) * VD], ((0, VP - VD), (0, 0))) for h in range(H)
        ]

    first = jnp.concatenate(
        [
            low(w_qk[0]).T,
            low(w_qk[1]).T,
            low(vg_t[0]),
            jnp.pad(low(norm_gains), ((0, 14), (0, 0))),
        ]
    )
    rest = jnp.concatenate(
        [*heads(low(vg_t[1])), *heads(low(w_out)), low(gu_t[0]), low(gu_t[1]), low(w_down)]
    )
    side = (lax.axis_index("dp") & 1).reshape(1)

    half_width = KD // 2
    freq_rates = jnp.exp(-math.log(10000.0) * jnp.arange(half_width).astype(WIDE) / half_width)
    positions = (lax.axis_index("shard") * length + jnp.arange(length)).astype(WIDE)
    angles = positions[:, None] * freq_rates[None, :]
    cos, sin = jnp.cos(angles), jnp.sin(angles)

    tok = tokens.reshape(rows, width)
    cot = cotangent.reshape(rows, width)
    seg_col = segments.reshape(rows, 1)
    seg_row = segments.reshape(rows // BLOCK, 1, BLOCK)
    in_last = jnp.where(lax.axis_index("shard") > 0, segments[:, 0], -1)
    first_held = gather_shards(first, cos, sin, seg_col, seg_row, in_last, place)
    rest = after(rest, first_held[1][2])
    w_rest = lax.all_gather(rest, "shard", axis=1, tiled=True)
    decay = log_decay

    def tick(*done):
        nonlocal decay, place, gains
        decay, place, gains = lax.optimization_barrier((decay, place, gains, *done))[:3]

    plan = [(0, 0, 0, 2 * kd)] + [(2 * kd + h * VD, 0, 2 * kd + h * VP, VD) for h in range(H)]
    plan += [(2 * kd + vd, 1, 0, 16)]
    fills = [(0, 2 * kd + h * VP + VD, VP - VD) for h in range(H)]
    w_qkv, gains = assemble(first_held, plan, fills, [2 * kd + vp, 16], width, me, side)
    tick(rest)
    hid, k, v, kv, leaving = front(
        seqs, length, tok, seg_col, segments, decay, w_qkv, gains, cos, sin
    )
    passing = Passing(leaving, False)
    tick(leaving)
    tick(passing.turn(decay, length, leaving))
    q, intra = inner(k, v, hid, w_qkv, cos, sin, seg_col, seg_row, decay, length)
    tick(q)
    passing.finish(q)
    gate = gates(after(hid, passing.got[1], q), w_rest)
    tick(gate)
    tokens_out, hid2, prod, dgate, dup, mixed, glow, ggate, gret, st, dst, leaving = middle(
        seqs, length, ff, (intra, gate, q, tok, cot), seg_col, segments, in_last, decay,
        w_rest, gains, passing.got, kv,
    )
    returning = Passing(leaving, True)
    tick(leaving)

    def halves(row):
        return [(h * VP, row + h * VD, VD) for h in range(H)]

    fit = lambda used, layout: used + -used % (16 * layout[1])
    plan = [(0, 1, [(0, 0, ff)]), (2, 3, [(0, ff, ff)]), (4, 3, [(0, 2 * ff, ff)])]
    (made,) = weight_grads([prod, cot, dgate, hid2, dup], plan, place)
    tick(made)
    tick(returning.turn(decay, length, made))
    plan = [(0, 1, halves(0)), (2, 3, halves(vd))]
    made = weight_grads(
        [mixed, glow, ggate, hid], plan, place, shards,
        fit(2 * vd + 3 * ff, layouts[0]), layouts[0], (made,),
    )
    tick(made[0])
    returning.finish(made[0])
    early = Reduction(made[0], after(made[1], returning.got[1]), halved[0])
    tick(early.cross(made[0]))
    dq, dk, dv = back(
        seqs, length, (q, k, v, gret), cos, sin, seg_col, seg_row, segments, in_last, decay,
        st, dst, returning.got,
    )
    tick(dq)
    blocks = rows // BLOCK
    data = (dq, dk, dv, ggate, tok, glow, w_qkv, w_rest)
    grad_input = input_grad(0, blocks // 2, *data, gains, None, False)
    tick(grad_input)
    tick(early.next(grad_input))
    plan = [(0, 3, [(0, 0, kd)]), (1, 3, [(0, kd, kd)]), (2, 3, halves(2 * kd))]
    made = weight_grads(
        [dq, dk, dv, hid], plan, place, shards, fit(2 * kd + vd, layouts[1]), layouts[1]
    )
    late = Reduction(*made, halved[1])
    tick(made[0])
    tick(early.next(made[0]))
    tick(late.cross(made[0]))
    grad_input = input_grad(blocks // 2, blocks // 2, *data, gains, grad_input, True)
    tick(grad_input)
    tick(late.next(grad_input), early.next(grad_input))
    while early.left() or late.left():
        for item in (early, late):
            if item.left():
                item.next()

    gain_grads, total, *grads = squares(
        vd, ff, layouts, place, [early.result(), late.result()], w_qk, vg_t, gu_t, norm_gains
    )
    others = [
        lax.ppermute(total, "shard", [(i, i ^ mask) for i in range(shards)]) for mask in (1, 2, 3)
    ]
    arrays = []
    for group in ((w_qk, w_vg, w_out, w_gu, w_down, norm_gains), states[:6], states[6:]):
        arrays += [turned(item) if i in (1, 3) else item for i, item in enumerate(group)]
    *results, norm = update(vd, ff, [total, *others], grads, gain_grads, arrays)
    results = [turned(item) if i % 6 in (1, 3) else item for i, item in enumerate(results)]
    return (
        tokens_out.reshape(tokens.shape),
        grad_input.reshape(tokens.shape),
        *results,
        norm.reshape(()),
    )


def solution(mesh):
    split = P("dp", "shard", None)
    rows, columns = P(None, "shard", None), P(None, "shard")
    group = (rows, rows, columns, rows, columns, columns)
    in_specs = (split, split, P("dp", "shard"), P()) + group * 3
    out_specs = (split, split) + group * 3 + (P(),)
    return jax.shard_map(
        on_device, mesh=mesh, in_specs=in_specs, out_specs=out_specs, check_vma=False
    )
```

```python
import functools
import math

import jax
import jax.numpy as jnp
from jax import lax
from jax.experimental import pallas as pl
from jax.experimental.pallas import tpu as pltpu
from jax.sharding import PartitionSpec as P

H = 2
KD = 256
VD = 432
VP = 512
BLOCK = 512
STEP = 10

EPS = 1e-05
ADAM_EPS = 1e-08
BETA_ONE = 0.9
BETA_TWO = 0.95
MATRIX_RATE = 0.15
GAIN_RATE = 1.0
DECAY_WEIGHT = 0.1
CLIP = 1.0

LOW = jnp.bfloat16
WIDE = jnp.float32
VMEM = pltpu.VMEM
SMEM = pltpu.SMEM
MIB = 1024 * 1024


def dot(a, b):
    return jnp.dot(a, b, preferred_element_type=WIDE)


def dot_nt(a, b):
    return lax.dot_general(a, b, (((1,), (1,)), ((), ())), preferred_element_type=WIDE)


def dot_tn(a, b):
    return lax.dot_general(a, b, (((0,), (0,)), ((), ())), preferred_element_type=WIDE)


def params(size):
    return pltpu.CompilerParams(vmem_limit_bytes=size * MIB)


def cost(flops, moved):
    return pl.CostEstimate(flops=int(flops), bytes_accessed=int(moved), transcendentals=0)


def smem():
    return pl.BlockSpec(memory_space=SMEM)


def whole(shape):
    return pl.BlockSpec(shape, lambda *at: (0,) * len(shape), pipeline_mode=pl.Buffered(1))


def shape(dims, kind):
    return jax.ShapeDtypeStruct(dims, kind)


def bits_of(axis):
    return (lax.axis_size(axis) - 1).bit_length()


def exchange(value, axis, bit):
    size = lax.axis_size(axis)
    return lax.ppermute(value, axis, [(i, i ^ (1 << bit)) for i in range(size)])


def gather_shards(own, *others):
    held = [(0, own)]
    for bit in reversed(range(bits_of("shard"))):
        held += [
            (mask | (1 << bit), after(exchange(part, "shard", bit), *others)) for mask, part in held
        ]
    return [(mask, None, part) for mask, part in held]


def add_low(one, two):
    return (one.astype(WIDE) + two.astype(WIDE)).astype(LOW)


class Reduction:
    def __init__(self, keep, send, halved):
        self.keep = keep
        self.near = exchange(send, "shard", 0)
        self.halved = halved
        self.stage = 0

    def cross(self, *done):
        self.near = after(self.near, *done)
        low = add_low(self.keep[1], self.near[1])
        self.got = exchange(low, "shard", 1)
        self.terms = [self.keep[0], self.near[0]]
        return low

    def next(self, *done):
        got = after(self.got, *done)
        count = bits_of("dp")
        rows = got.shape[0]

        def total(at):
            return sum(term[at].astype(WIDE) for term in (*self.terms, got)).astype(LOW)

        bit = self.stage
        if self.stage < count:
            if bit in self.halved:
                sent = total(slice(rows // 2, rows))
                self.terms = [total(slice(0, rows // 2))]
            else:
                sent = total(slice(0, rows))
                self.terms = [sent]
        else:
            bit = self.halved[count - 1 - self.stage]
            if self.stage == count:
                sent = total(slice(0, rows))
            else:
                sent = jnp.concatenate([self.held, got])
            self.held = sent
        self.stage += 1
        self.got = exchange(sent, "dp", bit)
        return sent

    def left(self):
        return bits_of("dp") + len(self.halved) - self.stage

    def result(self):
        return self.held, self.got


class Passing:
    def __init__(self, local, reverse):
        self.local = local
        steps = [[(0, 1), (2, 3)], [(1, 2)], [(2, 3)]]
        if reverse:
            steps = [[(3 - a, 3 - b) for a, b in step] for step in steps]
        self.steps = steps
        self.got = [lax.ppermute(local, "shard", steps[0])]

    def turn(self, decay, length, *done):
        self.got[0] = after(self.got[0], *done)
        total = combine(decay, length, self.local, self.got[0])
        self.got.append(lax.ppermute(total, "shard", self.steps[1]))
        return total

    def finish(self, *done):
        self.got.append(lax.ppermute(after(self.got[1], *done), "shard", self.steps[2]))


def entering(decay, length, h, got):
    factor = jnp.exp(jnp.full((1, 1), decay[h] * length, WIDE))
    wide = [item[h].astype(WIDE) for item in got]
    return wide[0] + wide[1] + factor * wide[2]


def after(value, *others):
    return lax.optimization_barrier((value, *others))[0]


def combine_kernel(length, decay, local, got, out):
    h = pl.program_id(0) % H
    factor = jnp.exp(jnp.full((1, 1), decay[h] * length, WIDE))
    out[...] = (local[...].astype(WIDE) + factor * got[...].astype(WIDE)).astype(LOW)


def combine(decay, length, local, got):
    block = pl.BlockSpec((None, None, KD, VP), lambda i: (i // H, i % H, 0, 0))
    return pl.pallas_call(
        functools.partial(combine_kernel, length),
        grid=(local.shape[0] * H,),
        out_shape=shape(local.shape, LOW),
        in_specs=[smem(), block, block],
        out_specs=block,
        compiler_params=params(60),
        cost_estimate=cost(local.size, 6 * local.size),
    )(decay, local, got)


def assemble_kernel(plan, fills, sources_of, me_ref, side_ref, *refs):
    sources, outs = refs[: len(sources_of)], refs[len(sources_of) :]
    lanes = sources[0].shape[1]
    for index, row, size in fills:
        outs[index][row : row + size, :] = jnp.zeros((size, outs[index].shape[1]), LOW)

    def place(source, lane, low, high):
        for start, index, row, size in plan:
            begin, end = max(start, low), min(start + size, high)
            if begin < end:
                to = row + begin - start
                outs[index][to : to + end - begin, pl.ds(lane, lanes)] = source[
                    begin - low : end - low, :
                ]

    for (mask, half), source in zip(sources_of, sources):
        lane = pl.multiple_of(jnp.bitwise_xor(me_ref[0], mask) * lanes, lanes)
        rows = source.shape[0]
        if half is None:
            place(source, lane, 0, rows)
            continue
        for side in range(2):

            @pl.when(side_ref[0] == side)
            def _():
                low = (side ^ half) * rows
                place(source, lane, low, low + rows)


def assemble(held, plan, fills, heights, width, me, side):
    sources_of = [(mask, half) for mask, half, part in held]
    parts = [part for mask, half, part in held]
    return pl.pallas_call(
        functools.partial(assemble_kernel, plan, fills, sources_of),
        out_shape=[shape((rows, width), LOW) for rows in heights],
        in_specs=[smem()] * 2 + [pl.BlockSpec(memory_space=VMEM)] * len(parts),
        out_specs=[pl.BlockSpec(memory_space=VMEM)] * len(heights),
        compiler_params=params(20),
        cost_estimate=cost(0, 4 * sum(heights) * width),
    )(me, side, *parts)


def rotated(flat, cosine, sine):
    half = KD // 2
    parts = []
    for h in range(H):
        u = flat[:, h * KD : h * KD + half]
        w = flat[:, h * KD + half : (h + 1) * KD]
        parts += [u * cosine - w * sine, w * cosine + u * sine]
    return jnp.concatenate(parts, axis=1)


def column(size):
    return lax.broadcasted_iota(jnp.int32, (size, 1), 0).astype(WIDE)


def front_kernel(count, decay, seg_s, tok, w, gains, cos, sin, seg, *rest):
    hid, k, v, kv, out_state, state = rest
    seq = pl.program_id(0) // count
    c = pl.program_id(0) % count
    x = tok[...].astype(WIDE)
    r = lax.rsqrt(jnp.mean(x * x, axis=1, keepdims=True) + EPS)
    h1 = (x * r * gains[0:1, :].astype(WIDE)).astype(LOW)
    hid[...] = h1
    kd = H * KD
    key = rotated(dot_nt(h1, w[kd : 2 * kd, :]), cos[...], sin[...]).astype(LOW)
    k[...] = key
    val = dot_nt(h1, w[2 * kd :, :]).astype(LOW)
    v[...] = val
    first = seg_s[seq, c * BLOCK]
    last = seg_s[seq, c * BLOCK + BLOCK - 1]
    before = seg_s[seq, jnp.maximum(c * BLOCK - 1, 0)]
    here = (seg[...] == last).astype(WIDE)
    joined = jnp.logical_and(jnp.logical_and(first == last, first == before), c > 0)
    for h in range(H):
        a = decay[h]
        kw = jnp.exp(a * (BLOCK - 1.0 - column(BLOCK))) * here
        kk = (key[:, h * KD : (h + 1) * KD].astype(WIDE) * kw).astype(LOW)
        add = dot_tn(kk, val[:, h * VP : (h + 1) * VP])
        kv[h] = add
        factor = jnp.exp(jnp.full((1, 1), a * BLOCK, WIDE))
        total = jnp.where(joined, factor * state[h], 0.0) + add
        state[h] = total
        out_state[h] = total.astype(LOW)


def row_block(width):
    return pl.BlockSpec((BLOCK, width), lambda t: (t, 0))


def state_block(count, at=lambda c: c):
    return pl.BlockSpec(
        (None, None, H, KD, VP), lambda t: (t // count, at(t % count), 0, 0, 0)
    )


def seq_block(count):
    return pl.BlockSpec((None, H, KD, VP), lambda t: (t // count, 0, 0, 0))


def front(seqs, length, tokens, seg_col, segments, decay, w, gains, cos, sin):
    count = length // BLOCK
    rows, width = tokens.shape
    outs = [width, H * KD, H * VP]
    table = pl.BlockSpec((BLOCK, KD // 2), lambda t: (t % count, 0))
    return pl.pallas_call(
        functools.partial(front_kernel, count),
        grid=(seqs * count,),
        out_shape=[shape((rows, n), LOW) for n in outs]
        + [shape((seqs, count, H, KD, VP), WIDE), shape((seqs, H, KD, VP), LOW)],
        in_specs=[smem(), smem(), row_block(width), whole(w.shape), whole(gains.shape)]
        + [table, table, row_block(1)],
        out_specs=[row_block(n) for n in outs]
        + [state_block(count), seq_block(count)],
        scratch_shapes=[VMEM((H, KD, VP), WIDE)],
        compiler_params=params(60),
        cost_estimate=cost(2 * rows * width * w.shape[0], 12 * rows * width),
    )(decay, segments, tokens, w, gains, cos, sin, seg_col)


def decay_row(a):
    return jnp.exp(-a * lax.broadcasted_iota(jnp.int32, (1, BLOCK), 1).astype(WIDE))


def mixing(a, top, size, seg, seg_row):
    reach = top + size
    rows = jnp.exp(a * (column(size) + float(top)))
    same = seg[top:reach, :] == seg_row[:, :reach]
    n = lax.broadcasted_iota(jnp.int32, (size, reach), 0) + top
    m = lax.broadcasted_iota(jnp.int32, (size, reach), 1)
    return jnp.where(jnp.logical_and(same, n >= m), rows * decay_row(a)[:, :reach], 0.0)


TILE = 256


def inner_kernel(decay, k, v, hid, w, cos, sin, seg, seg_row, q, intra):
    query = rotated(dot_nt(hid[...], w[...]), cos[...], sin[...]).astype(LOW)
    q[...] = query
    for i in range(BLOCK // TILE):
        top, reach = i * TILE, (i + 1) * TILE
        for h in range(H):
            s = dot_nt(query[top:reach, h * KD : (h + 1) * KD], k[:reach, h * KD : (h + 1) * KD])
            weights = (s * mixing(decay[h], top, TILE, seg, seg_row)).astype(LOW)
            intra[top:reach, h * VP : (h + 1) * VP] = dot(
                weights, v[:reach, h * VP : (h + 1) * VP]
            ).astype(LOW)


def inner(k, v, hid, w, cos, sin, seg_col, seg_row, decay, length):
    rows, width = hid.shape
    count = length // BLOCK
    block = lambda n: pl.BlockSpec((BLOCK, n), lambda t: (t, 0))
    table = pl.BlockSpec((BLOCK, KD // 2), lambda t: (t % count, 0))
    return pl.pallas_call(
        inner_kernel,
        grid=(rows // BLOCK,),
        out_shape=[shape((rows, n), LOW) for n in (H * KD, H * VP)],
        in_specs=[
            smem(),
            block(H * KD),
            block(H * VP),
            block(width),
            pl.BlockSpec((H * KD, width), lambda t: (0, 0)),
            table,
            table,
            block(1),
            pl.BlockSpec((None, 1, BLOCK), lambda t: (t, 0, 0)),
        ],
        out_specs=[block(n) for n in (H * KD, H * VP)],
        compiler_params=params(60),
        cost_estimate=cost(rows * (2 * width * 512 + 2 * BLOCK * H * VP), 8 * rows * H * VP),
    )(decay, k, v, hid, w, cos, sin, seg_col, seg_row)


def gate_kernel(hid, w, gate):
    gate[...] = dot_nt(hid[...], w[...]).astype(LOW)


def gates(hid, w):
    rows, width = hid.shape
    vp = H * VP
    return pl.pallas_call(
        gate_kernel,
        grid=(rows // BLOCK,),
        out_shape=shape((rows, vp), LOW),
        in_specs=[row_block(width), pl.BlockSpec((vp, width), lambda t: (0, 0))],
        out_specs=row_block(vp),
        compiler_params=params(60),
        cost_estimate=cost(2 * rows * width * vp, 4 * rows * vp),
    )(hid, w)


CHUNK = 16


def interleaved(first, second):
    steps = [((i + 0.5) / len(first), 0, step) for i, step in enumerate(first)]
    steps += [((i + 0.5) / len(second), 1, step) for i, step in enumerate(second)]
    for place, which, step in sorted(steps, key=lambda item: item[:2]):
        step()


def pieces(width, size=256):
    return [(start, min(start + size, width)) for start in range(0, width, size)]


def across(narrow, width):
    return jnp.concatenate([narrow] * (width // 128), axis=1)


def middle_kernel(count, ff, decay, seg_s, in_last, *refs):
    (intra, gate, q, tok, cot, seg, w, gains, *got, kv) = refs[:12]
    outs, scratch = refs[12:24], refs[24:]
    (tok_out, hid2, prod, dgate, dup, mixed, glow, ggate, gret, st_out, dst, leave) = outs
    (state, now, queries, factors, ret_s, norm_s, silu_s, slope_s, inv_s, res_s, ff_s, low_s, sums) = scratch
    seq = pl.program_id(0) // count
    c = pl.program_id(0) % count
    start = c * BLOCK
    vp = H * VP
    width = tok.shape[1]
    before = jnp.where(c > 0, seg_s[seq, jnp.maximum(start - 1, 0)], in_last[seq])

    @pl.when(c == 0)
    def _():
        for h in range(H):
            total = entering(decay, count * BLOCK, h, got)
            state[h] = total
            now[h] = total.astype(LOW)

    for b in range(1, count):

        @pl.when(c == b)
        def _():
            prev = seg_s[seq, (b - 1) * BLOCK - 1] if b > 1 else in_last[seq]
            joined = jnp.logical_and(
                seg_s[seq, (b - 1) * BLOCK] == seg_s[seq, b * BLOCK - 1],
                seg_s[seq, (b - 1) * BLOCK] == prev,
            )
            for h in range(H):
                factor = jnp.exp(jnp.full((1, 1), decay[h] * BLOCK, WIDE))
                total = jnp.where(joined, factor * state[h], 0.0) + kv[h]
                state[h] = total
                now[h] = total.astype(LOW)

    st_out[...] = now[...]
    here = (seg[...] == before).astype(WIDE)
    for h in range(H):
        qw = jnp.exp(decay[h] * (column(BLOCK) + 1.0)) * here
        factors[h] = jnp.broadcast_to(qw, (BLOCK, 128))

    w_out = (vp, 2 * vp)
    w_gate = (2 * vp, 2 * vp + ff)
    w_up = (2 * vp + ff, 2 * vp + 2 * ff)
    w_down = (2 * vp + 2 * ff, 2 * vp + 3 * ff)
    gain = gains[1:2, :].astype(WIDE)

    def phases(top):
        rs = pl.ds(top, TILE)
        lists = []

        def add(steps):
            lists.append(steps)

        def chunks():
            return [pl.ds(row, CHUNK) for row in range(top, top + TILE, CHUNK)]

        def cross(h, lo, hi):
            ret_s[rs, h * VP + lo : h * VP + hi] = dot(
                q[rs, h * KD : (h + 1) * KD], now[h, :, lo:hi]
            )

        add([functools.partial(cross, h, *piece) for h in range(H) for piece in pieces(VP)])

        def gated(h, r):
            hv = slice(h * VP, (h + 1) * VP)
            hk = slice(h * KD, (h + 1) * KD)
            qw = factors[h, r, :]
            queries[r, hk] = (q[r, hk].astype(WIDE) * across(qw, KD)).astype(LOW)
            ret = intra[r, hv].astype(WIDE) + across(qw, VP) * ret_s[r, hv]
            mean = jnp.sum(ret, axis=1, keepdims=True) * (1.0 / VD)
            centered = ret - mean
            square = jnp.sum(centered * centered, axis=1, keepdims=True)
            var = (square - (VP - VD) * (mean * mean)) * (1.0 / VD)
            inv = lax.rsqrt(var + 1.0 * KD)
            nh = centered * inv
            g = gate[r, hv].astype(WIDE)
            sg = 0.5 * jnp.tanh(0.5 * g) + 0.5
            sl = g * sg
            mixed[r, hv] = (nh * sl).astype(LOW)
            norm_s[r, hv] = nh
            silu_s[r, hv] = sl
            slope_s[r, hv] = nh * (sg + sl * (1.0 - sg))
            inv_s[h, r, :] = jnp.broadcast_to(inv, (CHUNK, 128))

        add([functools.partial(gated, h, r) for r in chunks() for h in range(H)])

        def project(lo, hi):
            res_s[rs, lo:hi] = dot(mixed[rs, :], w[w_out[0] : w_out[1], lo:hi])

        add([functools.partial(project, *piece) for piece in pieces(width)])

        def norm(r):
            resid = tok[r, :].astype(WIDE) + res_s[r, :]
            r2 = lax.rsqrt(jnp.mean(resid * resid, axis=1, keepdims=True) + EPS)
            res_s[r, :] = resid
            hid2[r, :] = (resid * r2 * gain).astype(LOW)
            inv_s[H, r, :] = jnp.broadcast_to(r2, (CHUNK, 128))

        add([functools.partial(norm, r) for r in chunks()])

        def forward(place, source, at, lo, hi):
            ff_s[place, rs, lo:hi] = dot_nt(source[rs, :], w[at[0] + lo : at[0] + hi, :])

        add(
            [
                functools.partial(forward, place, source, at, *piece)
                for piece in pieces(ff)
                for place, source, at in ((0, hid2, w_gate), (1, hid2, w_up), (2, cot, w_down))
            ]
        )

        def gelu(r, lo, hi):
            gf, uf, gp = ff_s[0, r, lo:hi], ff_s[1, r, lo:hi], ff_s[2, r, lo:hi]
            e = jnp.exp(-0.5 * (gf * gf))
            d = 1.0 / (1.0 + (0.3275911 * math.sqrt(0.5)) * jnp.abs(gf))
            poly = d * (
                0.5 * 0.254829592
                + d
                * (
                    0.5 * -0.284496736
                    + d * (0.5 * 1.421413741 + d * (0.5 * -1.453152027 + d * (0.5 * 1.061405429)))
                )
            )
            tail = poly * e
            cdf = jnp.where(gf >= 0.0, 1.0 - tail, tail)
            ge = gf * cdf
            dge = cdf + gf * (e * (1.0 / math.sqrt(2.0 * math.pi)))
            prod[r, lo:hi] = (ge * uf).astype(LOW)
            dgate[r, lo:hi] = (gp * uf * dge).astype(LOW)
            dup[r, lo:hi] = (gp * ge).astype(LOW)

        add([functools.partial(gelu, r, *piece) for r in chunks() for piece in pieces(ff, 512)])

        def down(lo, hi):
            low_s[0, rs, lo:hi] = dot(prod[rs, :], w[w_down[0] : w_down[1], lo:hi])

        def hidden(lo, hi):
            low_s[1, rs, lo:hi] = dot(dgate[rs, :], w[w_gate[0] : w_gate[1], lo:hi]) + dot(
                dup[rs, :], w[w_up[0] : w_up[1], lo:hi]
            )

        add([functools.partial(step, *piece) for piece in pieces(width) for step in (down, hidden)])

        def residual(r):
            resid = res_s[r, :]
            r2 = across(inv_s[H, r, :], width)
            tok_out[r, :] = (resid + low_s[0, r, :]).astype(LOW)
            gh = low_s[1, r, :] * gain
            xhat = resid * r2
            inner_product = jnp.mean(gh * xhat, axis=1, keepdims=True)
            glow[r, :] = (cot[r, :].astype(WIDE) + r2 * (gh - xhat * inner_product)).astype(LOW)

        add([functools.partial(residual, r) for r in chunks()])

        def mix_back(lo, hi):
            ret_s[rs, lo:hi] = dot_nt(glow[rs, :], w[w_out[0] + lo : w_out[0] + hi, :])

        add([functools.partial(mix_back, *piece) for piece in pieces(vp)])

        def gated_back(h, r):
            hv = slice(h * VP, (h + 1) * VP)
            gm = ret_s[r, hv]
            nh = norm_s[r, hv]
            ggate[r, hv] = (gm * slope_s[r, hv]).astype(LOW)
            gn = gm * silu_s[r, hv]
            one = jnp.sum(gn, axis=1, keepdims=True) * (1.0 / VD)
            two = jnp.sum(gn * nh, axis=1, keepdims=True) * (1.0 / VD)
            gret[r, hv] = (across(inv_s[h, r, :], VP) * (gn - one - nh * two)).astype(LOW)

        add([functools.partial(gated_back, h, r) for r in chunks() for h in range(H)])
        return lists

    first, second = phases(0), phases(TILE)
    for k in range(len(first) + 1):
        interleaved(first[k] if k < len(first) else [], second[k - 1] if k else [])
    for h in range(H):
        add = dot_tn(queries[:, h * KD : (h + 1) * KD], gret[:, h * VP : (h + 1) * VP])
        dst[h] = add
        sums[c, h] = add

    @pl.when(c == count - 1)
    def _():
        for h in range(H):
            total = sums[count - 1, h]
            for b in reversed(range(count - 1)):
                prev = seg_s[seq, b * BLOCK - 1] if b > 0 else in_last[seq]
                joined = jnp.logical_and(
                    seg_s[seq, b * BLOCK] == seg_s[seq, (b + 1) * BLOCK - 1],
                    seg_s[seq, b * BLOCK] == prev,
                )
                factor = jnp.exp(jnp.full((1, 1), decay[h] * BLOCK, WIDE))
                total = jnp.where(joined, factor * total, 0.0) + sums[b, h]
            leave[h] = total.astype(LOW)


def middle(seqs, length, ff, data, seg_col, segments, in_last, decay, w, gains, got, kv):
    intra, gate, q, tokens, cotangent = data
    rows, width = tokens.shape
    count = length // BLOCK
    vp = H * VP
    outs = [width, width, ff, ff, ff, vp, width, vp, vp]
    inputs = [decay, segments, in_last, intra, gate, q, tokens, cotangent, seg_col, w, gains, *got, kv]
    specs = [smem()] * 3 + [row_block(n) for n in (vp, vp, H * KD, width, width, 1)]
    specs += [whole(w.shape), whole(gains.shape), *[seq_block(count)] * 3]
    specs += [state_block(count, lambda c: jnp.maximum(c - 1, 0))]
    one = (H, KD, VP)
    states = (seqs, count, *one)
    return pl.pallas_call(
        functools.partial(middle_kernel, count, ff),
        grid=(seqs * count,),
        out_shape=[shape((rows, n), LOW) for n in outs]
        + [shape(states, LOW), shape(states, WIDE), shape((seqs, *one), LOW)],
        in_specs=specs,
        out_specs=[row_block(n) for n in outs]
        + [state_block(count)] * 2
        + [seq_block(count)],
        scratch_shapes=[
            VMEM(one, WIDE),
            VMEM(one, LOW),
            VMEM((BLOCK, H * KD), LOW),
            VMEM((H, BLOCK, 128), WIDE),
            VMEM((BLOCK, vp), WIDE),
            VMEM((BLOCK, vp), WIDE),
            VMEM((BLOCK, vp), WIDE),
            VMEM((BLOCK, vp), WIDE),
            VMEM((H + 1, BLOCK, 128), WIDE),
            VMEM((BLOCK, width), WIDE),
            VMEM((3, BLOCK, ff), WIDE),
            VMEM((2, BLOCK, width), WIDE),
            VMEM(states[1:], WIDE),
        ],
        compiler_params=params(60),
        cost_estimate=cost(2 * rows * width * (2 * vp + 6 * ff), 30 * rows * width),
    )(*inputs)


def weight_kernel(plan, count, layout, me_ref, *refs):
    ins, ready, outs, total = refs[:count], refs[count:-3], refs[-3:-1], refs[-1]
    if layout is None:
        outs = refs[-2:-1]
    t = pl.program_id(0)
    last = pl.num_programs(0) - 1
    for left, right, cuts in plan:
        a, b = ins[left], ins[right]
        for source, row, size in cuts:
            add = dot_tn(a[:, source : source + size], b[...])

            @pl.when(t == 0)
            def _():
                total[row : row + size, :] = add

            @pl.when(t > 0)
            def _():
                total[row : row + size, :] += add

    @pl.when(t == last)
    def _():
        used = max(row + size for left, right, cuts in plan for source, row, size in cuts)
        if layout is None:
            outs[0][...] = total[...].astype(LOW)
            return
        for item in ready:
            total[used : used + item.shape[0], :] = item[...].astype(WIDE)
            used += item.shape[0]
        if used < total.shape[0]:
            total[used:, :] = jnp.zeros((total.shape[0] - used, total.shape[1]), WIDE)
        lanes = outs[0].shape[2]
        which, pieces = layout
        rows = outs[0].shape[1] // pieces
        for part in range(2 * outs[0].shape[0]):
            target = outs[part & 1]
            lane = pl.multiple_of(jnp.bitwise_xor(me_ref[0], part) * lanes, lanes)
            for q in range(pieces):
                row = pl.multiple_of(jnp.bitwise_xor(me_ref[which], q) * rows, 16)
                target[part >> 1, q * rows : (q + 1) * rows, :] = total[
                    pl.ds(row, rows), pl.ds(lane, lanes)
                ].astype(LOW)


def weight_grads(arrays, plan, place, shards=2, height=0, layout=None, ready=()):
    rows = arrays[0].shape[0]
    used = max(row + size for left, right, cuts in plan for source, row, size in cuts)
    width = arrays[plan[0][1]].shape[1]
    tile = 2 * BLOCK
    block = lambda n: pl.BlockSpec((tile, n), lambda t: (t, 0))
    dims = [(shards // 2, height, width // shards)] * 2
    if layout is None:
        height, dims = used, [(used, width)]
    full = lambda item: pl.BlockSpec(item, lambda t: (0,) * len(item))
    return pl.pallas_call(
        functools.partial(weight_kernel, plan, len(arrays), layout),
        grid=(rows // tile,),
        out_shape=[shape(item, LOW) for item in dims],
        in_specs=[smem()] + [block(item.shape[1]) for item in arrays]
        + [full(item.shape) for item in ready],
        out_specs=[full(item) for item in dims],
        scratch_shapes=[VMEM((height, width), WIDE)],
        compiler_params=params(48),
        cost_estimate=cost(2 * rows * used * width, 2 * rows * sum(i.shape[1] for i in arrays)),
    )(place, *arrays, *ready)


def back_kernel(count, decay, seg_s, in_last, *refs):
    (q, k, v, gret, cos, sin, seg, seg_row, st, dst, *got) = refs[:13]
    (dq, dk, dv, state, weights, grads) = refs[13:]
    seq = pl.program_id(0) // count
    c = count - 1 - pl.program_id(0) % count

    @pl.when(c == count - 1)
    def _():
        for h in range(H):
            state[h] = entering(decay, count * BLOCK, h, got)

    for b in range(1, count):

        @pl.when(c == b - 1)
        def _():
            prev = seg_s[seq, b * BLOCK - 1]
            first = seg_s[seq, b * BLOCK]
            last = seg_s[seq, (b + 1) * BLOCK - 1]
            joined = jnp.logical_and(first == last, first == prev)
            for h in range(H):
                factor = jnp.exp(jnp.full((1, 1), decay[h] * BLOCK, WIDE))
                state[h] = jnp.where(joined, factor * state[h], 0.0) + dst[h]

    start = c * BLOCK
    before = jnp.where(c > 0, seg_s[seq, jnp.maximum(start - 1, 0)], in_last[seq])
    final = seg_s[seq, start + BLOCK - 1]
    here = (seg[...] == before).astype(WIDE)
    ends = (seg[...] == final).astype(WIDE)
    place = column(BLOCK)
    dqs, dks = [], []
    for h in range(H):
        a = decay[h]
        qh = q[:, h * KD : (h + 1) * KD]
        kh = k[:, h * KD : (h + 1) * KD]
        vh = v[:, h * VP : (h + 1) * VP]
        gh = gret[:, h * VP : (h + 1) * VP]
        qw = jnp.exp(a * (place + 1.0)) * here
        kw = jnp.exp(a * (BLOCK - 1.0 - place)) * ends
        parts = []
        for i in range(BLOCK // TILE):
            top, reach = i * TILE, (i + 1) * TILE
            mix = mixing(a, top, TILE, seg, seg_row)
            s = dot_nt(qh[top:reach, :], kh[:reach, :])
            weights[top:reach, :reach] = (s * mix).astype(LOW)
            gs = (dot_nt(gh[top:reach, :], vh[:reach, :]) * mix).astype(LOW)
            grads[top:reach, :reach] = gs
            parts.append(dot(gs, kh[:reach, :]))
        late = state[h].astype(LOW)
        dqs.append(jnp.concatenate(parts) + qw * dot_nt(gh, st[h]))
        parts, values = [], []
        for i in range(BLOCK // TILE):
            top, reach = i * TILE, (i + 1) * TILE
            parts.append(dot_tn(grads[top:, top:reach], qh[top:, :]))
            values.append(dot_tn(weights[top:, top:reach], gh[top:, :]))
        dks.append(jnp.concatenate(parts) + kw * dot_nt(vh, late))
        dv[:, h * VP : (h + 1) * VP] = (jnp.concatenate(values) + kw * dot(kh, late)).astype(LOW)
    dq[...] = rotated(jnp.concatenate(dqs, axis=1), cos[...], -sin[...]).astype(LOW)
    dk[...] = rotated(jnp.concatenate(dks, axis=1), cos[...], -sin[...]).astype(LOW)


def back(seqs, length, data, cos, sin, seg_col, seg_row, segments, in_last, decay, st, dst, got):
    rows = data[0].shape[0]
    count = length // BLOCK
    turn = lambda t: (t // count) * count + count - 1 - t % count
    block = lambda n: pl.BlockSpec((BLOCK, n), lambda t: (turn(t), 0))
    table = pl.BlockSpec((BLOCK, KD // 2), lambda t: (count - 1 - t % count, 0))
    outs = [H * KD, H * KD, H * VP]
    inputs = [decay, segments, in_last, *data, cos, sin, seg_col, seg_row, st, dst, *got]
    specs = [smem()] * 3 + [block(item.shape[1]) for item in data] + [table, table, block(1)]
    specs += [pl.BlockSpec((None, 1, BLOCK), lambda t: (turn(t), 0, 0))]
    specs += [state_block(count, lambda c: count - 1 - c)]
    specs += [state_block(count, lambda c: jnp.minimum(count - c, count - 1))]
    specs += [seq_block(count)] * 3
    return pl.pallas_call(
        functools.partial(back_kernel, count),
        grid=(seqs * count,),
        out_shape=[shape((rows, n), LOW) for n in outs],
        in_specs=specs,
        out_specs=[block(n) for n in outs],
        scratch_shapes=[
            VMEM((H, KD, VP), WIDE),
            VMEM((BLOCK, BLOCK), LOW),
            VMEM((BLOCK, BLOCK), LOW),
        ],
        compiler_params=params(60),
        cost_estimate=cost(rows * H * 2 * BLOCK * 3 * (KD + VP), 16 * rows * H * VP),
    )(*inputs)


def input_kernel(dq, dk, dv, ggate, tok, glow, w, w_gate, gains, *rest):
    out = rest[-1]
    kd = H * KD
    gh = dot(dq[...], w[:kd, :]) + dot(dk[...], w[kd : 2 * kd, :])
    gh += dot(dv[...], w[2 * kd :, :]) + dot(ggate[...], w_gate[...])
    x = tok[...].astype(WIDE)
    r = lax.rsqrt(jnp.mean(x * x, axis=1, keepdims=True) + EPS)
    xhat = x * r
    gh = gh * gains[0:1, :].astype(WIDE)
    inner_product = jnp.mean(gh * xhat, axis=1, keepdims=True)
    out[...] = (glow[...].astype(WIDE) + r * (gh - xhat * inner_product)).astype(LOW)


def input_grad(first, steps, dq, dk, dv, ggate, tokens, glow, w, w_rest, gains, earlier, hides):
    rows, width = tokens.shape
    parts = rows // BLOCK // steps
    arrays = [dq, dk, dv, ggate, tokens, glow]
    block = lambda item: pl.BlockSpec((BLOCK, item.shape[1]), lambda t: (first + t, 0))
    inputs = [*arrays, w, w_rest, gains]
    specs = [block(item) for item in arrays] + [whole(w.shape)]
    specs += [pl.BlockSpec((H * VP, width), lambda t: (0, 0)), whole(gains.shape)]
    aliases = {}
    if earlier is not None:
        aliases = {len(inputs): 0}
        inputs.append(earlier)
        specs.append(pl.BlockSpec(memory_space=pl.ANY))
    return pl.pallas_call(
        input_kernel,
        grid=(steps,),
        out_shape=shape((rows, width), LOW),
        in_specs=specs,
        out_specs=block(tokens),
        input_output_aliases=aliases,
        compiler_params=params(32 if hides else 60),
        cost_estimate=cost(2 * rows * width * (w.shape[0] + H * VP) // parts, 20 * rows * width // parts)
        if hides
        else cost(1, 1),
    )(*inputs)


def adam_step(master, moment, second, grad, scale, rate, decay_weight):
    clipped = grad * scale
    moment_new = BETA_ONE * moment + (1.0 - BETA_ONE) * clipped
    second_new = BETA_TWO * second + (1.0 - BETA_TWO) * clipped * clipped
    corrected = (
        moment_new
        * (1.0 / (1.0 - BETA_ONE**STEP))
        / (jnp.sqrt(second_new * (1.0 / (1.0 - BETA_TWO**STEP))) + ADAM_EPS)
    )
    return (master - rate * (corrected + decay_weight * master), moment_new, second_new)


def squares_kernel(vd, ff, layouts, place, *refs):
    halves, (w_qk, w_vg, w_gu, low_gains) = refs[:4], refs[4:8]
    grad_gains, total, early, late = refs[8:]
    kd = H * KD
    for index, target in enumerate((early, late)):
        which, pieces = layouts[index]
        rows = target.shape[0] // pieces
        for q in range(pieces):
            row = pl.multiple_of(jnp.bitwise_xor(place[which], q) * rows, 16)
            source = halves[2 * index + q // (pieces // 2)]
            start = q % (pieces // 2) * rows
            target[pl.ds(row, rows), :] = source[start : start + rows, :]

    def rows(source, start, size):
        return source[start : start + size, :].astype(WIDE)

    def product(weight, grad):
        return jnp.sum(weight.astype(LOW).astype(WIDE) * grad, axis=0, keepdims=True)

    sums = []

    def square(item):
        sums.append(jnp.sum(item * item, axis=0, keepdims=True))
        return item

    first = jnp.zeros((1, low_gains.shape[1]), WIDE)
    for i in range(2):
        grad = square(rows(late, i * kd, kd))
        first += jnp.sum(w_qk[i].astype(LOW).astype(WIDE).T * grad, axis=0, keepdims=True)
    first += product(w_vg[0], square(rows(late, 2 * kd, vd)))
    first += product(w_vg[1], square(rows(early, vd, vd)))
    square(rows(early, 0, vd))
    square(rows(early, 2 * vd, ff))
    second = product(w_gu[0], square(rows(early, 2 * vd + ff, ff)))
    second += product(w_gu[1], square(rows(early, 2 * vd + 2 * ff, ff)))
    gains = jnp.concatenate([first, second]) / low_gains[...].astype(LOW).astype(WIDE)
    grad_gains[...] = gains
    sums.append(jnp.sum(gains * gains, axis=0, keepdims=True))
    total[...] = jnp.broadcast_to(jnp.sum(sum(sums), axis=1, keepdims=True), total.shape)


def squares(vd, ff, layouts, place, grads, w_qk, w_vg, w_gu, gains):
    halves = [half for pair in grads for half in pair]
    vmem = pl.BlockSpec(memory_space=VMEM)
    return pl.pallas_call(
        functools.partial(squares_kernel, vd, ff, layouts),
        out_shape=[shape(gains.shape, WIDE), shape((8, 128), WIDE)]
        + [shape((2 * pair[0].shape[0], pair[0].shape[1]), LOW) for pair in grads],
        in_specs=[smem()] + [vmem] * 8,
        out_specs=[vmem] * 4,
        compiler_params=params(20),
    )(place, *halves, w_qk, w_vg, w_gu, gains)


def update_kernel(vd, ff, *refs):
    totals, (early, late, gain_grads) = refs[:4], refs[4:7]
    sources, targets, norm_out = refs[7:25], refs[25:43], refs[43]
    ins, outs = refs[44:62], refs[62:80]
    arrived, sent = refs[80:]
    kd = H * KD
    order = [4, 3, 2, 1, 0, 5]
    places = [6 * group + place for place in order for group in range(3)]
    fetch = {i: pltpu.make_async_copy(sources[i], ins[i], arrived.at[i]) for i in places}
    send = {i: pltpu.make_async_copy(outs[i], targets[i], sent.at[i]) for i in places}
    for i in places:
        fetch[i].start()
    norm = jnp.sqrt((totals[0][...] + totals[1][...]) + (totals[2][...] + totals[3][...]))
    norm_out[0, 0] = jnp.max(norm)
    scale = jnp.minimum(1.0, CLIP / (norm + 1e-06))[0:1, 0:1]

    def step(place, at, grad, rate, decay_weight):
        results = adam_step(
            ins[place][at], ins[6 + place][at], ins[12 + place][at], grad, scale, rate, decay_weight
        )
        for group, result in enumerate(results):
            outs[6 * group + place][at] = result

    def rows(source, start, size):
        return source[start : start + size, :].astype(WIDE)

    grads = {
        4: [(..., lambda: rows(early, 2 * vd, ff))],
        3: [(i, lambda i=i: rows(early, 2 * vd + (1 + i) * ff, ff)) for i in range(2)],
        2: [(..., lambda: rows(early, 0, vd))],
        1: [(0, lambda: rows(late, 2 * kd, vd)), (1, lambda: rows(early, vd, vd))],
        0: [(i, lambda i=i: rows(late, i * kd, kd).T) for i in range(2)],
        5: [(..., lambda: gain_grads[...])],
    }
    for place in order:
        for group in range(3):
            fetch[6 * group + place].wait()
        rate, decay_weight = (GAIN_RATE, 0.0) if place == 5 else (MATRIX_RATE, DECAY_WEIGHT)
        for at, grad in grads[place]:
            step(place, at, grad(), rate, decay_weight)
        for group in range(3):
            send[6 * group + place].start()
    for i in places:
        send[i].wait()


def update(vd, ff, totals, grads, gain_grads, arrays):
    anywhere = pl.BlockSpec(memory_space=pl.ANY)
    return pl.pallas_call(
        functools.partial(update_kernel, vd, ff),
        out_shape=[shape(item.shape, WIDE) for item in arrays] + [shape((1, 1), WIDE)],
        in_specs=[pl.BlockSpec(memory_space=VMEM)] * 7 + [anywhere] * 18,
        out_specs=[anywhere] * 18 + [smem()],
        scratch_shapes=[VMEM(item.shape, WIDE) for item in arrays] * 2
        + [pltpu.SemaphoreType.DMA((18,))] * 2,
        compiler_params=params(40),
    )(*totals, *grads, gain_grads, *arrays)


def on_device(
    tokens,
    cotangent,
    segments,
    log_decay,
    w_qk,
    w_vg,
    w_out,
    w_gu,
    w_down,
    norm_gains,
    *states,
):
    turned = lambda item: jnp.swapaxes(item, 1, 2)
    shards = lax.axis_size("shard")
    me = lax.axis_index("shard").reshape(1)
    replica = lax.axis_index("dp")
    count = bits_of("dp")
    halved = (tuple(range(count - 1)),) * 2
    numbers = [
        sum(((replica >> bit) & 1) << (len(bits) - 1 - i) for i, bit in enumerate(bits))
        for bits in halved
    ]
    layouts = [(1 + i, 2 ** len(bits)) for i, bits in enumerate(halved)]
    place = jnp.concatenate([me, jnp.stack(numbers)])
    seqs, length, width = tokens.shape
    rows = seqs * length
    kd, vd, ff = H * KD, H * VD, w_down.shape[0]
    vp = H * VP
    vg_t, gu_t = turned(w_vg), turned(w_gu)

    low = lambda item: item.astype(LOW)
    def heads(item):
        return [
            jnp.pad(item[h * VD : (h + 1) * VD], ((0, VP - VD), (0, 0))) for h in range(H)
        ]

    first = jnp.concatenate(
        [
            low(w_qk[0]).T,
            low(w_qk[1]).T,
            low(vg_t[0]),
            jnp.pad(low(norm_gains), ((0, 14), (0, 0))),
        ]
    )
    rest = jnp.concatenate(
        [*heads(low(vg_t[1])), *heads(low(w_out)), low(gu_t[0]), low(gu_t[1]), low(w_down)]
    )
    side = (lax.axis_index("dp") & 1).reshape(1)

    half_width = KD // 2
    freq_rates = jnp.exp(-math.log(10000.0) * jnp.arange(half_width).astype(WIDE) / half_width)
    positions = (lax.axis_index("shard") * length + jnp.arange(length)).astype(WIDE)
    angles = positions[:, None] * freq_rates[None, :]
    cos, sin = jnp.cos(angles), jnp.sin(angles)

    tok = tokens.reshape(rows, width)
    cot = cotangent.reshape(rows, width)
    seg_col = segments.reshape(rows, 1)
    seg_row = segments.reshape(rows // BLOCK, 1, BLOCK)
    in_last = jnp.where(lax.axis_index("shard") > 0, segments[:, 0], -1)
    first_held = gather_shards(first, cos, sin, seg_col, seg_row, in_last, place)
    rest = after(rest, first_held[1][2])
    w_rest = lax.all_gather(rest, "shard", axis=1, tiled=True)
    decay = log_decay

    def tick(*done):
        nonlocal decay, place, gains
        decay, place, gains = lax.optimization_barrier((decay, place, gains, *done))[:3]

    plan = [(0, 0, 0, 2 * kd)] + [(2 * kd + h * VD, 0, 2 * kd + h * VP, VD) for h in range(H)]
    plan += [(2 * kd + vd, 1, 0, 16)]
    fills = [(0, 2 * kd + h * VP + VD, VP - VD) for h in range(H)]
    w_qkv, gains = assemble(first_held, plan, fills, [2 * kd + vp, 16], width, me, side)
    tick(rest)
    hid, k, v, kv, leaving = front(
        seqs, length, tok, seg_col, segments, decay, w_qkv, gains, cos, sin
    )
    passing = Passing(leaving, False)
    tick(leaving)
    tick(passing.turn(decay, length, leaving))
    q, intra = inner(k, v, hid, w_qkv, cos, sin, seg_col, seg_row, decay, length)
    tick(q)
    passing.finish(q)
    gate = gates(after(hid, passing.got[1], q), w_rest)
    tick(gate)
    tokens_out, hid2, prod, dgate, dup, mixed, glow, ggate, gret, st, dst, leaving = middle(
        seqs, length, ff, (intra, gate, q, tok, cot), seg_col, segments, in_last, decay,
        w_rest, gains, passing.got, kv,
    )
    returning = Passing(leaving, True)
    tick(leaving)

    def halves(row):
        return [(h * VP, row + h * VD, VD) for h in range(H)]

    fit = lambda used, layout: used + -used % (16 * layout[1])
    plan = [(0, 1, [(0, 0, ff)]), (2, 3, [(0, ff, ff)]), (4, 3, [(0, 2 * ff, ff)])]
    (made,) = weight_grads([prod, cot, dgate, hid2, dup], plan, place)
    tick(made)
    tick(returning.turn(decay, length, made))
    plan = [(0, 1, halves(0)), (2, 3, halves(vd))]
    made = weight_grads(
        [mixed, glow, ggate, hid], plan, place, shards,
        fit(2 * vd + 3 * ff, layouts[0]), layouts[0], (made,),
    )
    tick(made[0])
    returning.finish(made[0])
    early = Reduction(made[0], after(made[1], returning.got[1]), halved[0])
    tick(early.cross(made[0]))
    dq, dk, dv = back(
        seqs, length, (q, k, v, gret), cos, sin, seg_col, seg_row, segments, in_last, decay,
        st, dst, returning.got,
    )
    tick(dq)
    blocks = rows // BLOCK
    data = (dq, dk, dv, ggate, tok, glow, w_qkv, w_rest)
    grad_input = input_grad(0, blocks // 2, *data, gains, None, False)
    tick(grad_input)
    tick(early.next(grad_input))
    plan = [(0, 3, [(0, 0, kd)]), (1, 3, [(0, kd, kd)]), (2, 3, halves(2 * kd))]
    made = weight_grads(
        [dq, dk, dv, hid], plan, place, shards, fit(2 * kd + vd, layouts[1]), layouts[1]
    )
    late = Reduction(*made, halved[1])
    tick(made[0])
    tick(early.next(made[0]))
    tick(late.cross(made[0]))
    grad_input = input_grad(blocks // 2, blocks // 2, *data, gains, grad_input, True)
    tick(grad_input)
    sent = late.next(grad_input)
    tick(sent, early.next(grad_input, sent))
    while early.left() or late.left():
        for item in (early, late):
            if item.left():
                item.next()

    gain_grads, total, *grads = squares(
        vd, ff, layouts, place, [early.result(), late.result()], w_qk, vg_t, gu_t, norm_gains
    )
    others = [
        lax.ppermute(total, "shard", [(i, i ^ mask) for i in range(shards)]) for mask in (1, 2, 3)
    ]
    arrays = []
    for group in ((w_qk, w_vg, w_out, w_gu, w_down, norm_gains), states[:6], states[6:]):
        arrays += [turned(item) if i in (1, 3) else item for i, item in enumerate(group)]
    *results, norm = update(vd, ff, [total, *others], grads, gain_grads, arrays)
    results = [turned(item) if i % 6 in (1, 3) else item for i, item in enumerate(results)]
    return (
        tokens_out.reshape(tokens.shape),
        grad_input.reshape(tokens.shape),
        *results,
        norm.reshape(()),
    )


def solution(mesh):
    split = P("dp", "shard", None)
    rows, columns = P(None, "shard", None), P(None, "shard")
    group = (rows, rows, columns, rows, columns, columns)
    in_specs = (split, split, P("dp", "shard"), P()) + group * 3
    out_specs = (split, split) + group * 3 + (P(),)
    return jax.shard_map(
        on_device, mesh=mesh, in_specs=in_specs, out_specs=out_specs, check_vma=False
    )
```

```python
import functools
import math

import jax
import jax.numpy as jnp
from jax import lax
from jax.experimental import pallas as pl
from jax.experimental.pallas import tpu as pltpu
from jax.sharding import PartitionSpec as P

H = 2
KD = 256
VD = 432
VP = 512
BLOCK = 512
STEP = 10

EPS = 1e-05
ADAM_EPS = 1e-08
BETA_ONE = 0.9
BETA_TWO = 0.95
MATRIX_RATE = 0.15
GAIN_RATE = 1.0
DECAY_WEIGHT = 0.1
CLIP = 1.0

LOW = jnp.bfloat16
WIDE = jnp.float32
VMEM = pltpu.VMEM
SMEM = pltpu.SMEM
MIB = 1024 * 1024


def dot(a, b):
    return jnp.dot(a, b, preferred_element_type=WIDE)


def dot_nt(a, b):
    return lax.dot_general(a, b, (((1,), (1,)), ((), ())), preferred_element_type=WIDE)


def dot_tn(a, b):
    return lax.dot_general(a, b, (((0,), (0,)), ((), ())), preferred_element_type=WIDE)


def params(size):
    return pltpu.CompilerParams(vmem_limit_bytes=size * MIB)


def cost(flops, moved):
    return pl.CostEstimate(flops=int(flops), bytes_accessed=int(moved), transcendentals=0)


def smem():
    return pl.BlockSpec(memory_space=SMEM)


def whole(shape):
    return pl.BlockSpec(shape, lambda *at: (0,) * len(shape), pipeline_mode=pl.Buffered(1))


def shape(dims, kind):
    return jax.ShapeDtypeStruct(dims, kind)


def bits_of(axis):
    return (lax.axis_size(axis) - 1).bit_length()


def exchange(value, axis, bit):
    size = lax.axis_size(axis)
    return lax.ppermute(value, axis, [(i, i ^ (1 << bit)) for i in range(size)])


def gather_shards(own, *others):
    held = [(0, own)]
    for bit in reversed(range(bits_of("shard"))):
        held += [
            (mask | (1 << bit), after(exchange(part, "shard", bit), *others)) for mask, part in held
        ]
    return [(mask, None, part) for mask, part in held]


def add_low(one, two):
    return (one.astype(WIDE) + two.astype(WIDE)).astype(LOW)


class Reduction:
    def __init__(self, keep, send, halved):
        self.keep = keep
        self.near = exchange(send, "shard", 0)
        self.halved = halved
        self.stage = 0

    def cross(self, *done):
        self.near = after(self.near, *done)
        low = add_low(self.keep[1], self.near[1])
        self.got = exchange(low, "shard", 1)
        self.terms = [self.keep[0], self.near[0]]
        return low

    def next(self, *done):
        got = after(self.got, *done)
        count = bits_of("dp")
        rows = got.shape[0]

        def total(at):
            return sum(term[at].astype(WIDE) for term in (*self.terms, got)).astype(LOW)

        bit = self.stage
        if self.stage < count:
            if bit in self.halved:
                sent = total(slice(rows // 2, rows))
                self.terms = [total(slice(0, rows // 2))]
            else:
                sent = total(slice(0, rows))
                self.terms = [sent]
        else:
            bit = self.halved[count - 1 - self.stage]
            if self.stage == count:
                sent = total(slice(0, rows))
            else:
                sent = jnp.concatenate([self.held, got])
            self.held = sent
        self.stage += 1
        self.got = exchange(sent, "dp", bit)
        return sent

    def left(self):
        return bits_of("dp") + len(self.halved) - self.stage

    def result(self):
        return self.held, self.got


class Passing:
    def __init__(self, local, reverse):
        self.local = local
        steps = [[(0, 1), (2, 3)], [(1, 2)], [(2, 3)]]
        if reverse:
            steps = [[(3 - a, 3 - b) for a, b in step] for step in steps]
        self.steps = steps
        self.got = [lax.ppermute(local, "shard", steps[0])]

    def turn(self, decay, length, *done):
        self.got[0] = after(self.got[0], *done)
        total = combine(decay, length, self.local, self.got[0])
        self.got.append(lax.ppermute(total, "shard", self.steps[1]))
        return total

    def finish(self, *done):
        self.got.append(lax.ppermute(after(self.got[1], *done), "shard", self.steps[2]))


def entering(decay, length, h, got):
    factor = jnp.exp(jnp.full((1, 1), decay[h] * length, WIDE))
    wide = [item[h].astype(WIDE) for item in got]
    return wide[0] + wide[1] + factor * wide[2]


def after(value, *others):
    return lax.optimization_barrier((value, *others))[0]


def combine_kernel(length, decay, local, got, out):
    h = pl.program_id(0) % H
    factor = jnp.exp(jnp.full((1, 1), decay[h] * length, WIDE))
    out[...] = (local[...].astype(WIDE) + factor * got[...].astype(WIDE)).astype(LOW)


def combine(decay, length, local, got):
    block = pl.BlockSpec((None, None, KD, VP), lambda i: (i // H, i % H, 0, 0))
    return pl.pallas_call(
        functools.partial(combine_kernel, length),
        grid=(local.shape[0] * H,),
        out_shape=shape(local.shape, LOW),
        in_specs=[smem(), block, block],
        out_specs=block,
        compiler_params=params(60),
        cost_estimate=cost(local.size, 6 * local.size),
    )(decay, local, got)


def assemble_kernel(plan, fills, sources_of, me_ref, side_ref, *refs):
    sources, outs = refs[: len(sources_of)], refs[len(sources_of) :]
    lanes = sources[0].shape[1]
    for index, row, size in fills:
        outs[index][row : row + size, :] = jnp.zeros((size, outs[index].shape[1]), LOW)

    def place(source, lane, low, high):
        for start, index, row, size in plan:
            begin, end = max(start, low), min(start + size, high)
            if begin < end:
                to = row + begin - start
                outs[index][to : to + end - begin, pl.ds(lane, lanes)] = source[
                    begin - low : end - low, :
                ]

    for (mask, half), source in zip(sources_of, sources):
        lane = pl.multiple_of(jnp.bitwise_xor(me_ref[0], mask) * lanes, lanes)
        rows = source.shape[0]
        if half is None:
            place(source, lane, 0, rows)
            continue
        for side in range(2):

            @pl.when(side_ref[0] == side)
            def _():
                low = (side ^ half) * rows
                place(source, lane, low, low + rows)


def assemble(held, plan, fills, heights, width, me, side):
    sources_of = [(mask, half) for mask, half, part in held]
    parts = [part for mask, half, part in held]
    return pl.pallas_call(
        functools.partial(assemble_kernel, plan, fills, sources_of),
        out_shape=[shape((rows, width), LOW) for rows in heights],
        in_specs=[smem()] * 2 + [pl.BlockSpec(memory_space=VMEM)] * len(parts),
        out_specs=[pl.BlockSpec(memory_space=VMEM)] * len(heights),
        compiler_params=params(20),
        cost_estimate=cost(0, 4 * sum(heights) * width),
    )(me, side, *parts)


def rotated(flat, cosine, sine):
    half = KD // 2
    parts = []
    for h in range(H):
        u = flat[:, h * KD : h * KD + half]
        w = flat[:, h * KD + half : (h + 1) * KD]
        parts += [u * cosine - w * sine, w * cosine + u * sine]
    return jnp.concatenate(parts, axis=1)


def column(size):
    return lax.broadcasted_iota(jnp.int32, (size, 1), 0).astype(WIDE)


def front_kernel(count, decay, seg_s, tok, w, gains, cos, sin, seg, *rest):
    hid, k, v, kv, out_state, state = rest
    seq = pl.program_id(0) // count
    c = pl.program_id(0) % count
    x = tok[...].astype(WIDE)
    r = lax.rsqrt(jnp.mean(x * x, axis=1, keepdims=True) + EPS)
    h1 = (x * r * gains[0:1, :].astype(WIDE)).astype(LOW)
    hid[...] = h1
    kd = H * KD
    key = rotated(dot_nt(h1, w[kd : 2 * kd, :]), cos[...], sin[...]).astype(LOW)
    k[...] = key
    val = dot_nt(h1, w[2 * kd :, :]).astype(LOW)
    v[...] = val
    first = seg_s[seq, c * BLOCK]
    last = seg_s[seq, c * BLOCK + BLOCK - 1]
    before = seg_s[seq, jnp.maximum(c * BLOCK - 1, 0)]
    here = (seg[...] == last).astype(WIDE)
    joined = jnp.logical_and(jnp.logical_and(first == last, first == before), c > 0)
    for h in range(H):
        a = decay[h]
        kw = jnp.exp(a * (BLOCK - 1.0 - column(BLOCK))) * here
        kk = (key[:, h * KD : (h + 1) * KD].astype(WIDE) * kw).astype(LOW)
        add = dot_tn(kk, val[:, h * VP : (h + 1) * VP])
        kv[h] = add
        factor = jnp.exp(jnp.full((1, 1), a * BLOCK, WIDE))
        total = jnp.where(joined, factor * state[h], 0.0) + add
        state[h] = total
        out_state[h] = total.astype(LOW)


def row_block(width):
    return pl.BlockSpec((BLOCK, width), lambda t: (t, 0))


def state_block(count, at=lambda c: c):
    return pl.BlockSpec(
        (None, None, H, KD, VP), lambda t: (t // count, at(t % count), 0, 0, 0)
    )


def seq_block(count):
    return pl.BlockSpec((None, H, KD, VP), lambda t: (t // count, 0, 0, 0))


def front(seqs, length, tokens, seg_col, segments, decay, w, gains, cos, sin):
    count = length // BLOCK
    rows, width = tokens.shape
    outs = [width, H * KD, H * VP]
    table = pl.BlockSpec((BLOCK, KD // 2), lambda t: (t % count, 0))
    return pl.pallas_call(
        functools.partial(front_kernel, count),
        grid=(seqs * count,),
        out_shape=[shape((rows, n), LOW) for n in outs]
        + [shape((seqs, count, H, KD, VP), WIDE), shape((seqs, H, KD, VP), LOW)],
        in_specs=[smem(), smem(), row_block(width), whole(w.shape), whole(gains.shape)]
        + [table, table, row_block(1)],
        out_specs=[row_block(n) for n in outs]
        + [state_block(count), seq_block(count)],
        scratch_shapes=[VMEM((H, KD, VP), WIDE)],
        compiler_params=params(60),
        cost_estimate=cost(2 * rows * width * w.shape[0], 12 * rows * width),
    )(decay, segments, tokens, w, gains, cos, sin, seg_col)


def decay_row(a):
    return jnp.exp(-a * lax.broadcasted_iota(jnp.int32, (1, BLOCK), 1).astype(WIDE))


def mixing(a, top, size, seg, seg_row):
    reach = top + size
    rows = jnp.exp(a * (column(size) + float(top)))
    same = seg[top:reach, :] == seg_row[:, :reach]
    n = lax.broadcasted_iota(jnp.int32, (size, reach), 0) + top
    m = lax.broadcasted_iota(jnp.int32, (size, reach), 1)
    return jnp.where(jnp.logical_and(same, n >= m), rows * decay_row(a)[:, :reach], 0.0)


TILE = 256


def inner_kernel(decay, k, v, hid, w, cos, sin, seg, seg_row, q, intra):
    query = rotated(dot_nt(hid[...], w[...]), cos[...], sin[...]).astype(LOW)
    q[...] = query
    for i in range(BLOCK // TILE):
        top, reach = i * TILE, (i + 1) * TILE
        for h in range(H):
            s = dot_nt(query[top:reach, h * KD : (h + 1) * KD], k[:reach, h * KD : (h + 1) * KD])
            weights = (s * mixing(decay[h], top, TILE, seg, seg_row)).astype(LOW)
            intra[top:reach, h * VP : (h + 1) * VP] = dot(
                weights, v[:reach, h * VP : (h + 1) * VP]
            ).astype(LOW)


def inner(k, v, hid, w, cos, sin, seg_col, seg_row, decay, length):
    rows, width = hid.shape
    count = length // BLOCK
    block = lambda n: pl.BlockSpec((BLOCK, n), lambda t: (t, 0))
    table = pl.BlockSpec((BLOCK, KD // 2), lambda t: (t % count, 0))
    return pl.pallas_call(
        inner_kernel,
        grid=(rows // BLOCK,),
        out_shape=[shape((rows, n), LOW) for n in (H * KD, H * VP)],
        in_specs=[
            smem(),
            block(H * KD),
            block(H * VP),
            block(width),
            pl.BlockSpec((H * KD, width), lambda t: (0, 0)),
            table,
            table,
            block(1),
            pl.BlockSpec((None, 1, BLOCK), lambda t: (t, 0, 0)),
        ],
        out_specs=[block(n) for n in (H * KD, H * VP)],
        compiler_params=params(60),
        cost_estimate=cost(rows * (2 * width * 512 + 2 * BLOCK * H * VP), 8 * rows * H * VP),
    )(decay, k, v, hid, w, cos, sin, seg_col, seg_row)


def gate_kernel(hid, w, gate):
    gate[...] = dot_nt(hid[...], w[...]).astype(LOW)


def gates(hid, w):
    rows, width = hid.shape
    vp = H * VP
    return pl.pallas_call(
        gate_kernel,
        grid=(rows // BLOCK,),
        out_shape=shape((rows, vp), LOW),
        in_specs=[row_block(width), pl.BlockSpec((vp, width), lambda t: (0, 0))],
        out_specs=row_block(vp),
        compiler_params=params(60),
        cost_estimate=cost(2 * rows * width * vp, 4 * rows * vp),
    )(hid, w)


CHUNK = 16


def interleaved(first, second):
    steps = [((i + 0.5) / len(first), 0, step) for i, step in enumerate(first)]
    steps += [((i + 0.5) / len(second), 1, step) for i, step in enumerate(second)]
    for place, which, step in sorted(steps, key=lambda item: item[:2]):
        step()


def pieces(width, size=256):
    return [(start, min(start + size, width)) for start in range(0, width, size)]


def across(narrow, width):
    return jnp.concatenate([narrow] * (width // 128), axis=1)


def middle_kernel(count, ff, decay, seg_s, in_last, *refs):
    (intra, gate, q, tok, cot, seg, w, gains, *got, kv) = refs[:12]
    outs, scratch = refs[12:24], refs[24:]
    (tok_out, hid2, prod, dgate, dup, mixed, glow, ggate, gret, st_out, dst, leave) = outs
    (state, now, queries, factors, ret_s, norm_s, silu_s, slope_s, inv_s, res_s, ff_s, low_s, sums) = scratch
    seq = pl.program_id(0) // count
    c = pl.program_id(0) % count
    start = c * BLOCK
    vp = H * VP
    width = tok.shape[1]
    before = jnp.where(c > 0, seg_s[seq, jnp.maximum(start - 1, 0)], in_last[seq])

    @pl.when(c == 0)
    def _():
        for h in range(H):
            total = entering(decay, count * BLOCK, h, got)
            state[h] = total
            now[h] = total.astype(LOW)

    for b in range(1, count):

        @pl.when(c == b)
        def _():
            prev = seg_s[seq, (b - 1) * BLOCK - 1] if b > 1 else in_last[seq]
            joined = jnp.logical_and(
                seg_s[seq, (b - 1) * BLOCK] == seg_s[seq, b * BLOCK - 1],
                seg_s[seq, (b - 1) * BLOCK] == prev,
            )
            for h in range(H):
                factor = jnp.exp(jnp.full((1, 1), decay[h] * BLOCK, WIDE))
                total = jnp.where(joined, factor * state[h], 0.0) + kv[h]
                state[h] = total
                now[h] = total.astype(LOW)

    st_out[...] = now[...]
    here = (seg[...] == before).astype(WIDE)
    for h in range(H):
        qw = jnp.exp(decay[h] * (column(BLOCK) + 1.0)) * here
        factors[h] = jnp.broadcast_to(qw, (BLOCK, 128))

    w_out = (vp, 2 * vp)
    w_gate = (2 * vp, 2 * vp + ff)
    w_up = (2 * vp + ff, 2 * vp + 2 * ff)
    w_down = (2 * vp + 2 * ff, 2 * vp + 3 * ff)
    gain = gains[1:2, :].astype(WIDE)

    def phases(top):
        rs = pl.ds(top, TILE)
        lists = []

        def add(steps):
            lists.append(steps)

        def chunks():
            return [pl.ds(row, CHUNK) for row in range(top, top + TILE, CHUNK)]

        def cross(h, lo, hi):
            ret_s[rs, h * VP + lo : h * VP + hi] = dot(
                q[rs, h * KD : (h + 1) * KD], now[h, :, lo:hi]
            )

        add([functools.partial(cross, h, *piece) for h in range(H) for piece in pieces(VP)])

        def gated(h, r):
            hv = slice(h * VP, (h + 1) * VP)
            hk = slice(h * KD, (h + 1) * KD)
            qw = factors[h, r, :]
            queries[r, hk] = (q[r, hk].astype(WIDE) * across(qw, KD)).astype(LOW)
            ret = intra[r, hv].astype(WIDE) + across(qw, VP) * ret_s[r, hv]
            mean = jnp.sum(ret, axis=1, keepdims=True) * (1.0 / VD)
            centered = ret - mean
            square = jnp.sum(centered * centered, axis=1, keepdims=True)
            var = (square - (VP - VD) * (mean * mean)) * (1.0 / VD)
            inv = lax.rsqrt(var + 1.0 * KD)
            nh = centered * inv
            g = gate[r, hv].astype(WIDE)
            sg = 0.5 * jnp.tanh(0.5 * g) + 0.5
            sl = g * sg
            mixed[r, hv] = (nh * sl).astype(LOW)
            norm_s[r, hv] = nh
            silu_s[r, hv] = sl
            slope_s[r, hv] = nh * (sg + sl * (1.0 - sg))
            inv_s[h, r, :] = jnp.broadcast_to(inv, (CHUNK, 128))

        add([functools.partial(gated, h, r) for r in chunks() for h in range(H)])

        def project(lo, hi):
            res_s[rs, lo:hi] = dot(mixed[rs, :], w[w_out[0] : w_out[1], lo:hi])

        add([functools.partial(project, *piece) for piece in pieces(width)])

        def norm(r):
            resid = tok[r, :].astype(WIDE) + res_s[r, :]
            r2 = lax.rsqrt(jnp.mean(resid * resid, axis=1, keepdims=True) + EPS)
            res_s[r, :] = resid
            hid2[r, :] = (resid * r2 * gain).astype(LOW)
            inv_s[H, r, :] = jnp.broadcast_to(r2, (CHUNK, 128))

        add([functools.partial(norm, r) for r in chunks()])

        def forward(place, source, at, lo, hi):
            ff_s[place, rs, lo:hi] = dot_nt(source[rs, :], w[at[0] + lo : at[0] + hi, :])

        add(
            [
                functools.partial(forward, place, source, at, *piece)
                for piece in pieces(ff)
                for place, source, at in ((0, hid2, w_gate), (1, hid2, w_up), (2, cot, w_down))
            ]
        )

        def gelu(r, lo, hi):
            gf, uf, gp = ff_s[0, r, lo:hi], ff_s[1, r, lo:hi], ff_s[2, r, lo:hi]
            e = jnp.exp(-0.5 * (gf * gf))
            d = 1.0 / (1.0 + (0.3275911 * math.sqrt(0.5)) * jnp.abs(gf))
            poly = d * (
                0.5 * 0.254829592
                + d
                * (
                    0.5 * -0.284496736
                    + d * (0.5 * 1.421413741 + d * (0.5 * -1.453152027 + d * (0.5 * 1.061405429)))
                )
            )
            tail = poly * e
            cdf = jnp.where(gf >= 0.0, 1.0 - tail, tail)
            ge = gf * cdf
            dge = cdf + gf * (e * (1.0 / math.sqrt(2.0 * math.pi)))
            prod[r, lo:hi] = (ge * uf).astype(LOW)
            dgate[r, lo:hi] = (gp * uf * dge).astype(LOW)
            dup[r, lo:hi] = (gp * ge).astype(LOW)

        add([functools.partial(gelu, r, *piece) for r in chunks() for piece in pieces(ff, 512)])

        def down(lo, hi):
            low_s[0, rs, lo:hi] = dot(prod[rs, :], w[w_down[0] : w_down[1], lo:hi])

        def hidden(lo, hi):
            low_s[1, rs, lo:hi] = dot(dgate[rs, :], w[w_gate[0] : w_gate[1], lo:hi]) + dot(
                dup[rs, :], w[w_up[0] : w_up[1], lo:hi]
            )

        add([functools.partial(step, *piece) for piece in pieces(width) for step in (down, hidden)])

        def residual(r):
            resid = res_s[r, :]
            r2 = across(inv_s[H, r, :], width)
            tok_out[r, :] = (resid + low_s[0, r, :]).astype(LOW)
            gh = low_s[1, r, :] * gain
            xhat = resid * r2
            inner_product = jnp.mean(gh * xhat, axis=1, keepdims=True)
            glow[r, :] = (cot[r, :].astype(WIDE) + r2 * (gh - xhat * inner_product)).astype(LOW)

        add([functools.partial(residual, r) for r in chunks()])

        def mix_back(lo, hi):
            ret_s[rs, lo:hi] = dot_nt(glow[rs, :], w[w_out[0] + lo : w_out[0] + hi, :])

        add([functools.partial(mix_back, *piece) for piece in pieces(vp)])

        def gated_back(h, r):
            hv = slice(h * VP, (h + 1) * VP)
            gm = ret_s[r, hv]
            nh = norm_s[r, hv]
            ggate[r, hv] = (gm * slope_s[r, hv]).astype(LOW)
            gn = gm * silu_s[r, hv]
            one = jnp.sum(gn, axis=1, keepdims=True) * (1.0 / VD)
            two = jnp.sum(gn * nh, axis=1, keepdims=True) * (1.0 / VD)
            gret[r, hv] = (across(inv_s[h, r, :], VP) * (gn - one - nh * two)).astype(LOW)

        add([functools.partial(gated_back, h, r) for r in chunks() for h in range(H)])
        return lists

    first, second = phases(0), phases(TILE)
    for k in range(len(first) + 1):
        interleaved(first[k] if k < len(first) else [], second[k - 1] if k else [])
    for h in range(H):
        add = dot_tn(queries[:, h * KD : (h + 1) * KD], gret[:, h * VP : (h + 1) * VP])
        dst[h] = add
        sums[c, h] = add

    @pl.when(c == count - 1)
    def _():
        for h in range(H):
            total = sums[count - 1, h]
            for b in reversed(range(count - 1)):
                prev = seg_s[seq, b * BLOCK - 1] if b > 0 else in_last[seq]
                joined = jnp.logical_and(
                    seg_s[seq, b * BLOCK] == seg_s[seq, (b + 1) * BLOCK - 1],
                    seg_s[seq, b * BLOCK] == prev,
                )
                factor = jnp.exp(jnp.full((1, 1), decay[h] * BLOCK, WIDE))
                total = jnp.where(joined, factor * total, 0.0) + sums[b, h]
            leave[h] = total.astype(LOW)


def middle(seqs, length, ff, data, seg_col, segments, in_last, decay, w, gains, got, kv):
    intra, gate, q, tokens, cotangent = data
    rows, width = tokens.shape
    count = length // BLOCK
    vp = H * VP
    outs = [width, width, ff, ff, ff, vp, width, vp, vp]
    inputs = [decay, segments, in_last, intra, gate, q, tokens, cotangent, seg_col, w, gains, *got, kv]
    specs = [smem()] * 3 + [row_block(n) for n in (vp, vp, H * KD, width, width, 1)]
    specs += [whole(w.shape), whole(gains.shape), *[seq_block(count)] * 3]
    specs += [state_block(count, lambda c: jnp.maximum(c - 1, 0))]
    one = (H, KD, VP)
    states = (seqs, count, *one)
    return pl.pallas_call(
        functools.partial(middle_kernel, count, ff),
        grid=(seqs * count,),
        out_shape=[shape((rows, n), LOW) for n in outs]
        + [shape(states, LOW), shape(states, WIDE), shape((seqs, *one), LOW)],
        in_specs=specs,
        out_specs=[row_block(n) for n in outs]
        + [state_block(count)] * 2
        + [seq_block(count)],
        scratch_shapes=[
            VMEM(one, WIDE),
            VMEM(one, LOW),
            VMEM((BLOCK, H * KD), LOW),
            VMEM((H, BLOCK, 128), WIDE),
            VMEM((BLOCK, vp), WIDE),
            VMEM((BLOCK, vp), WIDE),
            VMEM((BLOCK, vp), WIDE),
            VMEM((BLOCK, vp), WIDE),
            VMEM((H + 1, BLOCK, 128), WIDE),
            VMEM((BLOCK, width), WIDE),
            VMEM((3, BLOCK, ff), WIDE),
            VMEM((2, BLOCK, width), WIDE),
            VMEM(states[1:], WIDE),
        ],
        compiler_params=params(60),
        cost_estimate=cost(2 * rows * width * (2 * vp + 6 * ff), 30 * rows * width),
    )(*inputs)


def weight_kernel(plan, count, layout, me_ref, *refs):
    ins, ready, outs, total = refs[:count], refs[count:-3], refs[-3:-1], refs[-1]
    if layout is None:
        outs = refs[-2:-1]
    t = pl.program_id(0)
    last = pl.num_programs(0) - 1
    for left, right, cuts in plan:
        a, b = ins[left], ins[right]
        for source, row, size in cuts:
            add = dot_tn(a[:, source : source + size], b[...])

            @pl.when(t == 0)
            def _():
                total[row : row + size, :] = add

            @pl.when(t > 0)
            def _():
                total[row : row + size, :] += add

    @pl.when(t == last)
    def _():
        used = max(row + size for left, right, cuts in plan for source, row, size in cuts)
        if layout is None:
            outs[0][...] = total[...].astype(LOW)
            return
        for item in ready:
            total[used : used + item.shape[0], :] = item[...].astype(WIDE)
            used += item.shape[0]
        if used < total.shape[0]:
            total[used:, :] = jnp.zeros((total.shape[0] - used, total.shape[1]), WIDE)
        lanes = outs[0].shape[2]
        which, pieces = layout
        rows = outs[0].shape[1] // pieces
        for part in range(2 * outs[0].shape[0]):
            target = outs[part & 1]
            lane = pl.multiple_of(jnp.bitwise_xor(me_ref[0], part) * lanes, lanes)
            for q in range(pieces):
                row = pl.multiple_of(jnp.bitwise_xor(me_ref[which], q) * rows, 16)
                target[part >> 1, q * rows : (q + 1) * rows, :] = total[
                    pl.ds(row, rows), pl.ds(lane, lanes)
                ].astype(LOW)


def weight_grads(arrays, plan, place, shards=2, height=0, layout=None, ready=()):
    rows = arrays[0].shape[0]
    used = max(row + size for left, right, cuts in plan for source, row, size in cuts)
    width = arrays[plan[0][1]].shape[1]
    tile = 2 * BLOCK
    block = lambda n: pl.BlockSpec((tile, n), lambda t: (t, 0))
    dims = [(shards // 2, height, width // shards)] * 2
    if layout is None:
        height, dims = used, [(used, width)]
    full = lambda item: pl.BlockSpec(item, lambda t: (0,) * len(item))
    return pl.pallas_call(
        functools.partial(weight_kernel, plan, len(arrays), layout),
        grid=(rows // tile,),
        out_shape=[shape(item, LOW) for item in dims],
        in_specs=[smem()] + [block(item.shape[1]) for item in arrays]
        + [full(item.shape) for item in ready],
        out_specs=[full(item) for item in dims],
        scratch_shapes=[VMEM((height, width), WIDE)],
        compiler_params=params(48),
        cost_estimate=cost(2 * rows * used * width, 2 * rows * sum(i.shape[1] for i in arrays)),
    )(place, *arrays, *ready)


def back_kernel(count, decay, seg_s, in_last, *refs):
    (q, k, v, gret, cos, sin, seg, seg_row, st, dst, *got) = refs[:13]
    (dq, dk, dv, state, weights, grads) = refs[13:]
    seq = pl.program_id(0) // count
    c = count - 1 - pl.program_id(0) % count

    @pl.when(c == count - 1)
    def _():
        for h in range(H):
            state[h] = entering(decay, count * BLOCK, h, got)

    for b in range(1, count):

        @pl.when(c == b - 1)
        def _():
            prev = seg_s[seq, b * BLOCK - 1]
            first = seg_s[seq, b * BLOCK]
            last = seg_s[seq, (b + 1) * BLOCK - 1]
            joined = jnp.logical_and(first == last, first == prev)
            for h in range(H):
                factor = jnp.exp(jnp.full((1, 1), decay[h] * BLOCK, WIDE))
                state[h] = jnp.where(joined, factor * state[h], 0.0) + dst[h]

    start = c * BLOCK
    before = jnp.where(c > 0, seg_s[seq, jnp.maximum(start - 1, 0)], in_last[seq])
    final = seg_s[seq, start + BLOCK - 1]
    here = (seg[...] == before).astype(WIDE)
    ends = (seg[...] == final).astype(WIDE)
    place = column(BLOCK)
    dqs, dks = [], []
    for h in range(H):
        a = decay[h]
        qh = q[:, h * KD : (h + 1) * KD]
        kh = k[:, h * KD : (h + 1) * KD]
        vh = v[:, h * VP : (h + 1) * VP]
        gh = gret[:, h * VP : (h + 1) * VP]
        qw = jnp.exp(a * (place + 1.0)) * here
        kw = jnp.exp(a * (BLOCK - 1.0 - place)) * ends
        parts = []
        for i in range(BLOCK // TILE):
            top, reach = i * TILE, (i + 1) * TILE
            mix = mixing(a, top, TILE, seg, seg_row)
            s = dot_nt(qh[top:reach, :], kh[:reach, :])
            weights[top:reach, :reach] = (s * mix).astype(LOW)
            gs = (dot_nt(gh[top:reach, :], vh[:reach, :]) * mix).astype(LOW)
            grads[top:reach, :reach] = gs
            parts.append(dot(gs, kh[:reach, :]))
        late = state[h].astype(LOW)
        dqs.append(jnp.concatenate(parts) + qw * dot_nt(gh, st[h]))
        parts, values = [], []
        for i in range(BLOCK // TILE):
            top, reach = i * TILE, (i + 1) * TILE
            parts.append(dot_tn(grads[top:, top:reach], qh[top:, :]))
            values.append(dot_tn(weights[top:, top:reach], gh[top:, :]))
        dks.append(jnp.concatenate(parts) + kw * dot_nt(vh, late))
        dv[:, h * VP : (h + 1) * VP] = (jnp.concatenate(values) + kw * dot(kh, late)).astype(LOW)
    dq[...] = rotated(jnp.concatenate(dqs, axis=1), cos[...], -sin[...]).astype(LOW)
    dk[...] = rotated(jnp.concatenate(dks, axis=1), cos[...], -sin[...]).astype(LOW)


def back(seqs, length, data, cos, sin, seg_col, seg_row, segments, in_last, decay, st, dst, got):
    rows = data[0].shape[0]
    count = length // BLOCK
    turn = lambda t: (t // count) * count + count - 1 - t % count
    block = lambda n: pl.BlockSpec((BLOCK, n), lambda t: (turn(t), 0))
    table = pl.BlockSpec((BLOCK, KD // 2), lambda t: (count - 1 - t % count, 0))
    outs = [H * KD, H * KD, H * VP]
    inputs = [decay, segments, in_last, *data, cos, sin, seg_col, seg_row, st, dst, *got]
    specs = [smem()] * 3 + [block(item.shape[1]) for item in data] + [table, table, block(1)]
    specs += [pl.BlockSpec((None, 1, BLOCK), lambda t: (turn(t), 0, 0))]
    specs += [state_block(count, lambda c: count - 1 - c)]
    specs += [state_block(count, lambda c: jnp.minimum(count - c, count - 1))]
    specs += [seq_block(count)] * 3
    return pl.pallas_call(
        functools.partial(back_kernel, count),
        grid=(seqs * count,),
        out_shape=[shape((rows, n), LOW) for n in outs],
        in_specs=specs,
        out_specs=[block(n) for n in outs],
        scratch_shapes=[
            VMEM((H, KD, VP), WIDE),
            VMEM((BLOCK, BLOCK), LOW),
            VMEM((BLOCK, BLOCK), LOW),
        ],
        compiler_params=params(60),
        cost_estimate=cost(rows * H * 2 * BLOCK * 3 * (KD + VP), 16 * rows * H * VP),
    )(*inputs)


def input_kernel(dq, dk, dv, ggate, tok, glow, w, w_gate, gains, *rest):
    out = rest[-1]
    kd = H * KD
    gh = dot(dq[...], w[:kd, :]) + dot(dk[...], w[kd : 2 * kd, :])
    gh += dot(dv[...], w[2 * kd :, :]) + dot(ggate[...], w_gate[...])
    x = tok[...].astype(WIDE)
    r = lax.rsqrt(jnp.mean(x * x, axis=1, keepdims=True) + EPS)
    xhat = x * r
    gh = gh * gains[0:1, :].astype(WIDE)
    inner_product = jnp.mean(gh * xhat, axis=1, keepdims=True)
    out[...] = (glow[...].astype(WIDE) + r * (gh - xhat * inner_product)).astype(LOW)


def input_grad(first, steps, dq, dk, dv, ggate, tokens, glow, w, w_rest, gains, earlier):
    rows, width = tokens.shape
    parts = rows // BLOCK // steps
    arrays = [dq, dk, dv, ggate, tokens, glow]
    block = lambda item: pl.BlockSpec((BLOCK, item.shape[1]), lambda t: (first + t, 0))
    inputs = [*arrays, w, w_rest, gains]
    specs = [block(item) for item in arrays] + [whole(w.shape)]
    specs += [pl.BlockSpec((H * VP, width), lambda t: (0, 0)), whole(gains.shape)]
    aliases = {}
    if earlier is not None:
        aliases = {len(inputs): 0}
        inputs.append(earlier)
        specs.append(pl.BlockSpec(memory_space=pl.ANY))
    return pl.pallas_call(
        input_kernel,
        grid=(steps,),
        out_shape=shape((rows, width), LOW),
        in_specs=specs,
        out_specs=block(tokens),
        input_output_aliases=aliases,
        compiler_params=params(32),
        cost_estimate=cost(2 * rows * width * (w.shape[0] + H * VP) // parts, 20 * rows * width // parts),
    )(*inputs)


def adam_step(master, moment, second, grad, scale, rate, decay_weight):
    clipped = grad * scale
    moment_new = BETA_ONE * moment + (1.0 - BETA_ONE) * clipped
    second_new = BETA_TWO * second + (1.0 - BETA_TWO) * clipped * clipped
    corrected = (
        moment_new
        * (1.0 / (1.0 - BETA_ONE**STEP))
        / (jnp.sqrt(second_new * (1.0 / (1.0 - BETA_TWO**STEP))) + ADAM_EPS)
    )
    return (master - rate * (corrected + decay_weight * master), moment_new, second_new)


def squares_kernel(vd, ff, layouts, place, *refs):
    halves, (w_qk, w_vg, w_gu, low_gains) = refs[:4], refs[4:8]
    grad_gains, total, early, late = refs[8:]
    kd = H * KD
    for index, target in enumerate((early, late)):
        which, pieces = layouts[index]
        rows = target.shape[0] // pieces
        for q in range(pieces):
            row = pl.multiple_of(jnp.bitwise_xor(place[which], q) * rows, 16)
            source = halves[2 * index + q // (pieces // 2)]
            start = q % (pieces // 2) * rows
            target[pl.ds(row, rows), :] = source[start : start + rows, :]

    def rows(source, start, size):
        return source[start : start + size, :].astype(WIDE)

    def product(weight, grad):
        return jnp.sum(weight.astype(LOW).astype(WIDE) * grad, axis=0, keepdims=True)

    sums = []

    def square(item):
        sums.append(jnp.sum(item * item, axis=0, keepdims=True))
        return item

    first = jnp.zeros((1, low_gains.shape[1]), WIDE)
    for i in range(2):
        grad = square(rows(late, i * kd, kd))
        first += jnp.sum(w_qk[i].astype(LOW).astype(WIDE).T * grad, axis=0, keepdims=True)
    first += product(w_vg[0], square(rows(late, 2 * kd, vd)))
    first += product(w_vg[1], square(rows(early, vd, vd)))
    square(rows(early, 0, vd))
    square(rows(early, 2 * vd, ff))
    second = product(w_gu[0], square(rows(early, 2 * vd + ff, ff)))
    second += product(w_gu[1], square(rows(early, 2 * vd + 2 * ff, ff)))
    gains = jnp.concatenate([first, second]) / low_gains[...].astype(LOW).astype(WIDE)
    grad_gains[...] = gains
    sums.append(jnp.sum(gains * gains, axis=0, keepdims=True))
    total[...] = jnp.broadcast_to(jnp.sum(sum(sums), axis=1, keepdims=True), total.shape)


def squares(vd, ff, layouts, place, grads, w_qk, w_vg, w_gu, gains):
    halves = [half for pair in grads for half in pair]
    vmem = pl.BlockSpec(memory_space=VMEM)
    return pl.pallas_call(
        functools.partial(squares_kernel, vd, ff, layouts),
        out_shape=[shape(gains.shape, WIDE), shape((8, 128), WIDE)]
        + [shape((2 * pair[0].shape[0], pair[0].shape[1]), LOW) for pair in grads],
        in_specs=[smem()] + [vmem] * 8,
        out_specs=[vmem] * 4,
        compiler_params=params(20),
    )(place, *halves, w_qk, w_vg, w_gu, gains)


def update_kernel(vd, ff, *refs):
    totals, (early, late, gain_grads) = refs[:4], refs[4:7]
    sources, targets, norm_out = refs[7:25], refs[25:43], refs[43]
    ins, outs = refs[44:62], refs[62:80]
    arrived, sent = refs[80:]
    kd = H * KD
    order = [4, 3, 2, 1, 0, 5]
    places = [6 * group + place for place in order for group in range(3)]
    fetch = {i: pltpu.make_async_copy(sources[i], ins[i], arrived.at[i]) for i in places}
    send = {i: pltpu.make_async_copy(outs[i], targets[i], sent.at[i]) for i in places}
    for i in places:
        fetch[i].start()
    norm = jnp.sqrt((totals[0][...] + totals[1][...]) + (totals[2][...] + totals[3][...]))
    norm_out[0, 0] = jnp.max(norm)
    scale = jnp.minimum(1.0, CLIP / (norm + 1e-06))[0:1, 0:1]

    def step(place, at, grad, rate, decay_weight):
        results = adam_step(
            ins[place][at], ins[6 + place][at], ins[12 + place][at], grad, scale, rate, decay_weight
        )
        for group, result in enumerate(results):
            outs[6 * group + place][at] = result

    def rows(source, start, size):
        return source[start : start + size, :].astype(WIDE)

    grads = {
        4: [(..., lambda: rows(early, 2 * vd, ff))],
        3: [(i, lambda i=i: rows(early, 2 * vd + (1 + i) * ff, ff)) for i in range(2)],
        2: [(..., lambda: rows(early, 0, vd))],
        1: [(0, lambda: rows(late, 2 * kd, vd)), (1, lambda: rows(early, vd, vd))],
        0: [(i, lambda i=i: rows(late, i * kd, kd).T) for i in range(2)],
        5: [(..., lambda: gain_grads[...])],
    }
    for place in order:
        for group in range(3):
            fetch[6 * group + place].wait()
        rate, decay_weight = (GAIN_RATE, 0.0) if place == 5 else (MATRIX_RATE, DECAY_WEIGHT)
        for at, grad in grads[place]:
            step(place, at, grad(), rate, decay_weight)
        for group in range(3):
            send[6 * group + place].start()
    for i in places:
        send[i].wait()


def update(vd, ff, totals, grads, gain_grads, arrays):
    anywhere = pl.BlockSpec(memory_space=pl.ANY)
    return pl.pallas_call(
        functools.partial(update_kernel, vd, ff),
        out_shape=[shape(item.shape, WIDE) for item in arrays] + [shape((1, 1), WIDE)],
        in_specs=[pl.BlockSpec(memory_space=VMEM)] * 7 + [anywhere] * 18,
        out_specs=[anywhere] * 18 + [smem()],
        scratch_shapes=[VMEM(item.shape, WIDE) for item in arrays] * 2
        + [pltpu.SemaphoreType.DMA((18,))] * 2,
        compiler_params=params(40),
    )(*totals, *grads, gain_grads, *arrays)


def on_device(
    tokens,
    cotangent,
    segments,
    log_decay,
    w_qk,
    w_vg,
    w_out,
    w_gu,
    w_down,
    norm_gains,
    *states,
):
    turned = lambda item: jnp.swapaxes(item, 1, 2)
    shards = lax.axis_size("shard")
    me = lax.axis_index("shard").reshape(1)
    replica = lax.axis_index("dp")
    count = bits_of("dp")
    halved = (tuple(range(count - 1)),) * 2
    numbers = [
        sum(((replica >> bit) & 1) << (len(bits) - 1 - i) for i, bit in enumerate(bits))
        for bits in halved
    ]
    layouts = [(1 + i, 2 ** len(bits)) for i, bits in enumerate(halved)]
    place = jnp.concatenate([me, jnp.stack(numbers)])
    seqs, length, width = tokens.shape
    rows = seqs * length
    kd, vd, ff = H * KD, H * VD, w_down.shape[0]
    vp = H * VP
    vg_t, gu_t = turned(w_vg), turned(w_gu)

    low = lambda item: item.astype(LOW)
    def heads(item):
        return [
            jnp.pad(item[h * VD : (h + 1) * VD], ((0, VP - VD), (0, 0))) for h in range(H)
        ]

    first = jnp.concatenate(
        [
            low(w_qk[0]).T,
            low(w_qk[1]).T,
            low(vg_t[0]),
            jnp.pad(low(norm_gains), ((0, 14), (0, 0))),
        ]
    )
    rest = jnp.concatenate(
        [*heads(low(vg_t[1])), *heads(low(w_out)), low(gu_t[0]), low(gu_t[1]), low(w_down)]
    )
    side = (lax.axis_index("dp") & 1).reshape(1)

    half_width = KD // 2
    freq_rates = jnp.exp(-math.log(10000.0) * jnp.arange(half_width).astype(WIDE) / half_width)
    positions = (lax.axis_index("shard") * length + jnp.arange(length)).astype(WIDE)
    angles = positions[:, None] * freq_rates[None, :]
    cos, sin = jnp.cos(angles), jnp.sin(angles)

    tok = tokens.reshape(rows, width)
    cot = cotangent.reshape(rows, width)
    seg_col = segments.reshape(rows, 1)
    seg_row = segments.reshape(rows // BLOCK, 1, BLOCK)
    in_last = jnp.where(lax.axis_index("shard") > 0, segments[:, 0], -1)
    first_held = gather_shards(first, cos, sin, seg_col, seg_row, in_last, place)
    rest = after(rest, first_held[1][2])
    w_rest = lax.all_gather(rest, "shard", axis=1, tiled=True)
    decay = log_decay

    def tick(*done):
        nonlocal decay, place, gains
        decay, place, gains = lax.optimization_barrier((decay, place, gains, *done))[:3]

    plan = [(0, 0, 0, 2 * kd)] + [(2 * kd + h * VD, 0, 2 * kd + h * VP, VD) for h in range(H)]
    plan += [(2 * kd + vd, 1, 0, 16)]
    fills = [(0, 2 * kd + h * VP + VD, VP - VD) for h in range(H)]
    w_qkv, gains = assemble(first_held, plan, fills, [2 * kd + vp, 16], width, me, side)
    tick(rest)
    hid, k, v, kv, leaving = front(
        seqs, length, tok, seg_col, segments, decay, w_qkv, gains, cos, sin
    )
    passing = Passing(leaving, False)
    tick(leaving)
    tick(passing.turn(decay, length, leaving))
    q, intra = inner(k, v, hid, w_qkv, cos, sin, seg_col, seg_row, decay, length)
    tick(q)
    passing.finish(q)
    gate = gates(after(hid, passing.got[1], q), w_rest)
    tick(gate)
    tokens_out, hid2, prod, dgate, dup, mixed, glow, ggate, gret, st, dst, leaving = middle(
        seqs, length, ff, (intra, gate, q, tok, cot), seg_col, segments, in_last, decay,
        w_rest, gains, passing.got, kv,
    )
    returning = Passing(leaving, True)
    tick(leaving)

    def halves(row):
        return [(h * VP, row + h * VD, VD) for h in range(H)]

    fit = lambda used, layout: used + -used % (16 * layout[1])
    plan = [(0, 1, [(0, 0, ff)]), (2, 3, [(0, ff, ff)]), (4, 3, [(0, 2 * ff, ff)])]
    (made,) = weight_grads([prod, cot, dgate, hid2, dup], plan, place)
    tick(made)
    tick(returning.turn(decay, length, made))
    plan = [(0, 1, halves(0)), (2, 3, halves(vd))]
    made = weight_grads(
        [mixed, glow, ggate, hid], plan, place, shards,
        fit(2 * vd + 3 * ff, layouts[0]), layouts[0], (made,),
    )
    tick(made[0])
    returning.finish(made[0])
    early = Reduction(made[0], after(made[1], returning.got[1]), halved[0])
    tick(early.cross(made[0]))
    dq, dk, dv = back(
        seqs, length, (q, k, v, gret), cos, sin, seg_col, seg_row, segments, in_last, decay,
        st, dst, returning.got,
    )
    tick(dq)
    tick(early.next(dq))
    plan = [(0, 3, [(0, 0, kd)]), (1, 3, [(0, kd, kd)]), (2, 3, halves(2 * kd))]
    made = weight_grads(
        [dq, dk, dv, hid], plan, place, shards, fit(2 * kd + vd, layouts[1]), layouts[1]
    )
    late = Reduction(*made, halved[1])
    tick(made[0])
    tick(early.next(made[0]))
    tick(late.cross(made[0]))
    blocks = rows // BLOCK
    data = (dq, dk, dv, ggate, tok, glow, w_qkv, w_rest)
    grad_input = None
    for part in range(2):
        grad_input = input_grad(part * blocks // 2, blocks // 2, *data, gains, grad_input)
        tick(grad_input)
        sent = (early, late)[part].next(grad_input)
        tick(sent)
    early.next(sent)
    while early.left() or late.left():
        for item in (early, late):
            if item.left():
                item.next()

    gain_grads, total, *grads = squares(
        vd, ff, layouts, place, [early.result(), late.result()], w_qk, vg_t, gu_t, norm_gains
    )
    others = [
        lax.ppermute(total, "shard", [(i, i ^ mask) for i in range(shards)]) for mask in (1, 2, 3)
    ]
    arrays = []
    for group in ((w_qk, w_vg, w_out, w_gu, w_down, norm_gains), states[:6], states[6:]):
        arrays += [turned(item) if i in (1, 3) else item for i, item in enumerate(group)]
    *results, norm = update(vd, ff, [total, *others], grads, gain_grads, arrays)
    results = [turned(item) if i % 6 in (1, 3) else item for i, item in enumerate(results)]
    return (
        tokens_out.reshape(tokens.shape),
        grad_input.reshape(tokens.shape),
        *results,
        norm.reshape(()),
    )


def solution(mesh):
    split = P("dp", "shard", None)
    rows, columns = P(None, "shard", None), P(None, "shard")
    group = (rows, rows, columns, rows, columns, columns)
    in_specs = (split, split, P("dp", "shard"), P()) + group * 3
    out_specs = (split, split) + group * 3 + (P(),)
    return jax.shard_map(
        on_device, mesh=mesh, in_specs=in_specs, out_specs=out_specs, check_vma=False
    )
```
